128 devices in a mesh: batch: 4 (over x), seq: 32 (over z, y, core).
Axes of the slice: x: 4, y: 4, z: 4, core: 2. Of those that a mesh axis runs over, the one named last changes fastest.
Arguments:
- inputs: float32 [4, 2048, 2, 768], P('batch', 'seq'), may hold values from -6 to 6
- cotangent: float32 [4, 2048, 2, 768], P('batch', 'seq'), may hold values from -6 to 6
- lengths: int32 [4, 2], P('batch'), may hold values from 128 to 2048, as said below
- qkv_weight: float32 [2, 3, 768, 768], P(None, None, 'seq'), may hold values from -0.21875 to 0.21875
- qkv_moment: float32 [2, 3, 768, 768], P(None, None, 'seq'), may hold values from -768 to 768
- qkv_average: float32 [2, 3, 768, 768], P(None, None, 'seq'), may hold values from -0.21875 to 0.21875
- out_weight: float32 [2, 768, 768], P(None, 'seq'), may hold values from -0.625 to 0.625
- out_moment: float32 [2, 768, 768], P(None, 'seq'), may hold values from -224 to 224
- out_average: float32 [2, 768, 768], P(None, 'seq'), may hold values from -0.625 to 0.625
- gate_up_weight: float32 [2, 2, 768, 2048], P(None, None, 'seq'), may hold values from -0.21875 to 0.21875
- gate_up_moment: float32 [2, 2, 768, 2048], P(None, None, 'seq'), may hold values from -224 to 224
- gate_up_average: float32 [2, 2, 768, 2048], P(None, None, 'seq'), may hold values from -0.21875 to 0.21875
- down_weight: float32 [2, 2048, 768], P(None, 'seq'), may hold values from -0.125 to 0.125
- down_moment: float32 [2, 2048, 768], P(None, 'seq'), may hold values from -224 to 224
- down_average: float32 [2, 2048, 768], P(None, 'seq'), may hold values from -0.125 to 0.125
- norm_gains: float32 [2, 2, 768], P(None, None, 'seq'), may hold values from 0.5 to 1.5
- gain_moment: float32 [2, 2, 768], P(None, None, 'seq'), may hold values from -768 to 768
- gain_average: float32 [2, 2, 768], P(None, None, 'seq'), may hold values from 0.5 to 1.5
Outputs:
- layer_output: float32 [4, 2048, 2, 768], P('batch', 'seq')
- input_grad: float32 [4, 2048, 2, 768], P('batch', 'seq')
- next_qkv_moment: float32 [2, 3, 768, 768], P(None, None, 'seq')
- next_qkv_weight: float32 [2, 3, 768, 768], P(None, None, 'seq')
- next_qkv_average: float32 [2, 3, 768, 768], P(None, None, 'seq')
- next_out_moment: float32 [2, 768, 768], P(None, 'seq')
- next_out_weight: float32 [2, 768, 768], P(None, 'seq')
- next_out_average: float32 [2, 768, 768], P(None, 'seq')
- next_gate_up_moment: float32 [2, 2, 768, 2048], P(None, None, 'seq')
- next_gate_up_weight: float32 [2, 2, 768, 2048], P(None, None, 'seq')
- next_gate_up_average: float32 [2, 2, 768, 2048], P(None, None, 'seq')
- next_down_moment: float32 [2, 2048, 768], P(None, 'seq')
- next_down_weight: float32 [2, 2048, 768], P(None, 'seq')
- next_down_average: float32 [2, 2048, 768], P(None, 'seq')
- next_gain_moment: float32 [2, 2, 768], P(None, None, 'seq')
- next_norm_gains: float32 [2, 2, 768], P(None, None, 'seq')
- next_gain_average: float32 [2, 2, 768], P(None, None, 'seq')
The draws below stay inside these ranges and needn't reach their ends.
Inputs may be any that keep to these rules, and one draw needn't show every extreme that they name: `lengths`: each slot's live length; in every group one slot is full, with 2048 live places.
All inputs are finite; a program needn't handle non-finite values.
Results may differ from the reference program's by a relative error of at most 0.04.
Values may be sent and summed in bfloat16 or wider, within the bound.
A program may use at most 256 MiB of HBM per device.

```python
import math
import jax
import jax.numpy as jnp
from jax import lax

D = 768
HEADS = 12
HEAD_DIM = 64
FF = 2048
LAYERS = 2
SLOTS = 2
SLOT_LEN = 2048
GROUPS = 4
ALL_TOKENS = 16384


def draw_lengths(key, part):
    key = jax.random.fold_in(key, 7)
    first_key, second_key = jax.random.split(key)
    divisor = jax.random.randint(first_key, (GROUPS, SLOTS), 1, 17)
    ragged = SLOT_LEN // divisor
    chosen = jax.random.randint(second_key, (GROUPS, 1), 0, SLOTS)
    filled = jnp.arange(SLOTS)[None, :] == chosen
    return jnp.where(filled, SLOT_LEN, ragged).astype(jnp.int32)


def levels(rng, shape, shards, low, top_value):
    def one(axis_at, shards_of):
        steps = jax.random.uniform(jax.random.fold_in(jax.random.fold_in(rng, 6), axis_at), (shards_of,), jnp.float32, low / len(shards), top_value / len(shards))
        return jnp.repeat(jnp.exp(steps), shape[axis_at] // shards_of).reshape((-1,) + (1,) * (len(shape) - axis_at - 1))

    factor_of = one(*shards[0])
    for cut in shards[1:]:
        factor_of = factor_of * one(*cut)
    return factor_of


def scatter_about(key, shape, scale, reach, shards=(), held_as=jnp.bfloat16):
    factor_of = levels(key, shape, shards, -0.22, 0.18) if shards else 1.0
    drawn = jax.random.normal(key, shape, jnp.float32) * scale * factor_of
    return jnp.minimum(jnp.maximum(drawn, -reach), reach).astype(held_as)


def setup_inputs(seed: int = 0) -> dict:
    streams_of = jax.random.split(jax.random.key(seed), 19)
    return {
        "inputs": scatter_about(streams_of[0], (GROUPS, SLOT_LEN, SLOTS, D), 1.0, 6.0, ((0, 4), (1, 32)), jnp.float32),
        "cotangent": scatter_about(streams_of[1], (GROUPS, SLOT_LEN, SLOTS, D), 1.0, 6.0, ((0, 4), (1, 32)), jnp.float32),
        "lengths": draw_lengths(jax.random.fold_in(streams_of[18], 71), 0),
        "qkv_weight": scatter_about(streams_of[3], (LAYERS, 3, D, D), D ** -0.5, 0.21875, ((2, 32),), jnp.float32),
        "qkv_moment": scatter_about(streams_of[4], (LAYERS, 3, D, D), (ALL_TOKENS ** 0.5), 768.0, ((2, 32),), jnp.float32),
        "qkv_average": scatter_about(streams_of[5], (LAYERS, 3, D, D), D ** -0.5, 0.21875, ((2, 32),), jnp.float32),
        "out_weight": scatter_about(streams_of[6], (LAYERS, D, D), (D // 8) ** -0.5, 0.625, ((1, 32),), jnp.float32),
        "out_moment": scatter_about(streams_of[7], (LAYERS, D, D), (0.3 * ALL_TOKENS ** 0.5), 224.0, ((1, 32),), jnp.float32),
        "out_average": scatter_about(streams_of[8], (LAYERS, D, D), (D // 8) ** -0.5, 0.625, ((1, 32),), jnp.float32),
        "gate_up_weight": scatter_about(streams_of[9], (LAYERS, 2, D, FF), D ** -0.5, 0.21875, ((2, 32),), jnp.float32),
        "gate_up_moment": scatter_about(streams_of[10], (LAYERS, 2, D, FF), (0.3 * ALL_TOKENS ** 0.5), 224.0, ((2, 32),), jnp.float32),
        "gate_up_average": scatter_about(streams_of[11], (LAYERS, 2, D, FF), D ** -0.5, 0.21875, ((2, 32),), jnp.float32),
        "down_weight": scatter_about(streams_of[12], (LAYERS, FF, D), FF ** -0.5, 0.125, ((1, 32),), jnp.float32),
        "down_moment": scatter_about(streams_of[13], (LAYERS, FF, D), (0.3 * ALL_TOKENS ** 0.5), 224.0, ((1, 32),), jnp.float32),
        "down_average": scatter_about(streams_of[14], (LAYERS, FF, D), FF ** -0.5, 0.125, ((1, 32),), jnp.float32),
        "norm_gains": jnp.clip(1.0 + 0.1 * jax.random.normal(streams_of[15], (LAYERS, 2, D), jnp.float32), 0.5, 1.5),
        "gain_moment": scatter_about(streams_of[16], (LAYERS, 2, D), (ALL_TOKENS ** 0.5), 768.0, ((2, 32),), jnp.float32),
        "gain_average": jnp.clip(0.5 + 1.0 * jax.random.uniform(streams_of[17], (LAYERS, 2, D), jnp.float32) ** levels(streams_of[17], (LAYERS, 2, D), ((2, 32),), -0.2, 0.2), 0.5, 1.5),
    }


@jax.custom_vjp
def low(v):
    return lax.optimization_barrier(v.astype(jnp.bfloat16)).astype(jnp.float32)

@jax.custom_vjp
def low_back(v):
    return v

def low_keep(v):
    return (low(v), None)

def low_pass(kept, grad):
    return (grad,)

def back_keep(v):
    return (v, None)

def back_low(kept, grad):
    return (low(grad),)
low.defvjp(low_keep, low_pass)
low_back.defvjp(back_keep, back_low)
EPSILON = 1e-06
MOMENTUM = 0.5
AVERAGING = 0.5
STEP_RATE = 0.1
MASKED = -1e+30

def product(left, right):
    return jnp.dot(left, right, precision=lax.Precision.HIGHEST, preferred_element_type=jnp.float32)

def angles(places, head_width):
    half_dim = head_width // 2
    frequency = jnp.exp(-math.log(10000.0) * jnp.arange(half_dim).astype(jnp.float32) / half_dim)
    phases = places.astype(jnp.float32)[:, None] * frequency[None, :]
    return (jnp.cos(phases)[:, None, None, :], jnp.sin(phases)[:, None, None, :])

def rotate(values, cosine_table, sine_table):
    half_dim = values.shape[-1] // 2
    front = values[..., :half_dim]
    behind = values[..., half_dim:]
    return jnp.concatenate([front * cosine_table - behind * sine_table, behind * cosine_table + front * sine_table], axis=-1)

def rms_norm(values, norm_gain):
    inverse = lax.rsqrt(lax.optimization_barrier(jnp.mean(values * values, axis=-1, keepdims=True)) + EPSILON)
    return values * inverse * norm_gain

def attend_slot(slot_items):
    queries, key_rows, value_rows, length = slot_items
    scores = low_back(jnp.einsum('qhd,khd->hqk', queries, key_rows, precision=lax.Precision.HIGHEST) * (1.0 / math.sqrt(HEAD_DIM)))
    places = jnp.arange(SLOT_LEN)
    allowed = (places[None, :] <= places[:, None]) & (places[None, :] < length)
    masked = jnp.where(allowed[None], scores, MASKED)
    highest = lax.optimization_barrier(jnp.max(masked, axis=-1, keepdims=True))
    raised = jnp.where(allowed[None], jnp.exp(masked - highest), 0.0)
    attn_probs = raised / lax.optimization_barrier(jnp.sum(raised, axis=-1, keepdims=True))
    return jnp.einsum('hqk,khd->qhd', low(attn_probs), value_rows, precision=lax.Precision.HIGHEST)

def attention_block(source, qkv_low, out_low, slot_lengths, cosine_table, sine_table):
    rows_in = low(source).reshape(SLOT_LEN * SLOTS, D)
    shaped = (SLOT_LEN, SLOTS, HEADS, HEAD_DIM)
    raw_query = low_back(product(rows_in, qkv_low[0])).reshape(shaped)
    raw_key = low_back(product(rows_in, qkv_low[1])).reshape(shaped)
    raw_value = low_back(product(rows_in, qkv_low[2])).reshape(shaped)
    queries = low(rotate(raw_query, cosine_table, sine_table)).transpose(1, 0, 2, 3)
    key_rows = low(rotate(raw_key, cosine_table, sine_table)).transpose(1, 0, 2, 3)
    value_rows = low(raw_value).transpose(1, 0, 2, 3)
    merged = lax.map(jax.checkpoint(attend_slot), (queries, key_rows, value_rows, slot_lengths))
    merged = low(low_back(merged.transpose(1, 0, 2, 3).reshape(SLOT_LEN * SLOTS, D)))
    return low_back(product(merged, out_low)).reshape(SLOT_LEN, SLOTS, D)

def feed_forward(source, gate_up_low, down_low):
    rows_in = low(source).reshape(SLOT_LEN * SLOTS, D)
    gate = low_back(product(rows_in, gate_up_low[0]))
    lifted = low_back(product(rows_in, gate_up_low[1]))
    hidden = low(jax.nn.silu(gate) * lifted)
    return low_back(product(hidden, down_low)).reshape(SLOT_LEN, SLOTS, D)

def forward(stream, qkv_weight, out_weight, gate_up_weight, down_weight, norm_gains, slot_lengths):
    cosine_table, sine_table = angles(jnp.arange(SLOT_LEN), HEAD_DIM)
    qkv_low = low(qkv_weight)
    out_low = low(out_weight)
    gate_up_low = low(gate_up_weight)
    down_low = low(down_weight)
    gains_low = low(norm_gains)
    residual = stream + attention_block(stream, qkv_low[0], out_low[0], slot_lengths, cosine_table, sine_table)
    middle = rms_norm(residual, gains_low[0, 0])
    shallow = rms_norm(middle + feed_forward(middle, gate_up_low[0], down_low[0]), gains_low[0, 1])
    normed = rms_norm(shallow, gains_low[1, 0])
    residual = shallow + attention_block(normed, qkv_low[1], out_low[1], slot_lengths, cosine_table, sine_table)
    return residual + feed_forward(rms_norm(residual, gains_low[1, 1]), gate_up_low[1], down_low[1])

def update(weight_matrix, moment, average, gradient):
    step_size = STEP_RATE / math.sqrt(GROUPS * SLOT_LEN * SLOTS)
    moment_new = MOMENTUM * moment + gradient
    weight_new = weight_matrix - step_size * (gradient + MOMENTUM * moment_new)
    return (moment_new, weight_new, AVERAGING * average + (1.0 - AVERAGING) * weight_new)

def reference(inputs, cotangent, lengths, qkv_weight, qkv_moment, qkv_average, out_weight, out_moment, out_average, gate_up_weight, gate_up_moment, gate_up_average, down_weight, down_moment, down_average, norm_gains, gain_moment, gain_average):
    weight_tensors = (qkv_weight, out_weight, gate_up_weight, down_weight, norm_gains)

    def group_share(running, group_items):
        stream, grad_stream, slot_lengths = group_items

        def apply_layers(source, qkv_part, out_part, gate_up_part, down_part, gain_part):
            return forward(source, qkv_part, out_part, gate_up_part, down_part, gain_part, slot_lengths)
        result, pullback = jax.vjp(apply_layers, stream, *weight_tensors)
        gradients = pullback(grad_stream)
        running = tuple((before + gradient for before, gradient in zip(running, gradients[1:])))
        return (running, (result, gradients[0]))
    empty_slots = tuple((jnp.zeros_like(weight_matrix) for weight_matrix in weight_tensors))
    total_counts, output_rows = lax.scan(group_share, empty_slots, (inputs, cotangent, lengths))
    layer_output, input_grad = output_rows
    qkv_new = update(qkv_weight, qkv_moment, qkv_average, total_counts[0])
    out_new = update(out_weight, out_moment, out_average, total_counts[1])
    gate_up_new = update(gate_up_weight, gate_up_moment, gate_up_average, total_counts[2])
    down_new = update(down_weight, down_moment, down_average, total_counts[3])
    gain_new = update(norm_gains, gain_moment, gain_average, total_counts[4])
    return (layer_output, input_grad, qkv_new[0], qkv_new[1], qkv_new[2], out_new[0], out_new[1], out_new[2], gate_up_new[0], gate_up_new[1], gate_up_new[2], down_new[0], down_new[1], down_new[2], gain_new[0], gain_new[1], gain_new[2])
```

```python
import functools
import math

import jax
import jax.numpy as jnp
from jax import lax
from jax.experimental import pallas as pl
from jax.experimental.pallas import tpu as pltpu
from jax.sharding import PartitionSpec as P

MESH = pl.DeviceIdType.MESH
BF = jnp.bfloat16
F32 = jnp.float32
HEAD_DIM = 64
HEADS = 12
PAIRS = 24
SPAN = 64
LENGTH = 2048
BLOCK = 256
EPSILON = 1e-06
MOMENTUM = 0.5
AVERAGING = 0.5
STEP_RATE = 0.1
MASKED = -1e30
VMEM_BYTES = 60 * 2**20
VMEM = pl.BlockSpec(memory_space=pltpu.VMEM)
ANY = pl.BlockSpec(memory_space=pl.ANY)
SMEM = pl.BlockSpec(memory_space=pltpu.SMEM)
ALL = pl.ds(0, 4)


def params(collective_id):
    return pltpu.CompilerParams(
        collective_id=collective_id, has_side_effects=True, vmem_limit_bytes=VMEM_BYTES
    )


def coordinates():
    seq = lax.axis_index("seq")
    return (
        lax.axis_index("batch"),
        lax.div(seq, 8),
        lax.rem(lax.div(seq, 2), 4),
        lax.rem(seq, 2),
    )


def device(x, z, y, core):
    return (x, (z * 4 + y) * 2 + core)


def shifted(value, by):
    return lax.rem(value + by, 4)


def greet(partners):
    barrier = pltpu.get_barrier_semaphore()
    for partner in partners:
        pl.semaphore_signal(barrier, inc=1, device_id=partner, device_id_type=MESH)
    pl.semaphore_wait(barrier, len(partners))


def remote(source, target, send, receive, where):
    return pltpu.make_async_remote_copy(
        src_ref=source,
        dst_ref=target,
        send_sem=send,
        recv_sem=receive,
        device_id=where,
        device_id_type=MESH,
    )


class Axes:
    def __init__(self, first_is_y):
        x, z, y, core = coordinates()
        self.first_is_y = first_is_y
        self.x, self.z, self.y, self.core = x, z, y, core
        self.m1, self.m2 = (y, z) if first_is_y else (z, y)
        self.partner = device(x, z, y, 1 - core)

    def along_y(self, by):
        return device(self.x, self.z, shifted(self.y, by), self.core)

    def along_z(self, by):
        return device(self.x, shifted(self.z, by), self.y, self.core)

    def first(self, by):
        return self.along_y(by) if self.first_is_y else self.along_z(by)

    def second(self, by):
        return self.along_z(by) if self.first_is_y else self.along_y(by)

    def order(self, i1, i2):
        return (i2, i1) if self.first_is_y else (i1, i2)


def greet_plane():
    axes = Axes(True)
    greet(
        [axes.partner]
        + [axes.along_y(by) for by in (1, 2, 3)]
        + [axes.along_z(by) for by in (1, 2, 3)]
    )


def pipeline(chunks, stages):
    for step in range(len(chunks) + stages - 1):
        for at, chunk in enumerate(chunks):
            if 0 <= step - at < stages:
                for segment in chunk:
                    segment.stage(step - at)


class GatherSegment:
    def __init__(self, first_is_y, view, own, semaphores):
        self.axes = Axes(first_is_y)
        self.view, self.own, self.semaphores = view, own, semaphores

    def block(self, i1, i2):
        return self.view(*self.axes.order(i1, i2))

    def stage(self, number):
        axes, block, sem = self.axes, self.block, self.semaphores
        m1, m2 = axes.m1, axes.m2
        before, after, across = shifted(m2, 3), shifted(m2, 1), shifted(m2, 2)
        if number == 0:
            pltpu.make_async_copy(self.own, block(m1, m2), sem.at[0]).start()
            for by in (1, 3, 2):
                remote(self.own, block(m1, m2), sem.at[1], sem.at[2], axes.first(by)).start()
        elif number == 1:
            pltpu.make_async_copy(self.own, block(m1, m2), sem.at[0]).wait()
            three = block(pl.ds(0, 3), m2)
            remote(three, three, sem.at[1], sem.at[2], axes.partner).wait_recv()
            row = block(ALL, m2)
            remote(row, row, sem.at[3], sem.at[4], axes.second(1)).start()
            remote(row, row, sem.at[3], sem.at[5], axes.second(3)).start()
            remote(row, row, sem.at[8], sem.at[9], axes.partner).start()
        elif number == 2:
            row = block(ALL, m2)
            remote(row, row, sem.at[3], sem.at[4], axes.partner).wait_recv()
            half = block(pl.ds(0, 2), before)
            remote(half, half, sem.at[6], sem.at[7], axes.second(1)).start()
            remote(row, row, sem.at[3], sem.at[5], axes.partner).wait_recv()
            half = block(pl.ds(2, 2), after)
            remote(half, half, sem.at[6], sem.at[7], axes.second(3)).start()
            for other in (before, after):
                row = block(ALL, other)
                remote(row, row, sem.at[8], sem.at[9], axes.partner).start()
        elif number == 3:
            row = block(ALL, across)
            remote(row, row, sem.at[6], sem.at[7], axes.partner).wait_recv()
            remote(row, row, sem.at[8], sem.at[9], axes.partner).start()
        else:
            everything = block(ALL, ALL)
            remote(everything, everything, sem.at[8], sem.at[9], axes.partner).wait()
            three = block(pl.ds(0, 3), m2)
            remote(three, three, sem.at[1], sem.at[2], axes.partner).wait_send()
            two = block(ALL, pl.ds(0, 2))
            remote(two, two, sem.at[3], sem.at[4], axes.partner).wait_send()
            row = block(ALL, m2)
            remote(row, row, sem.at[6], sem.at[7], axes.partner).wait_send()


GATHER_SEMAPHORES = 10


def halves(core, width):
    return pl.ds(pl.multiple_of(core * (width // 2), 128), width // 2)


def gather_kernel(qkv, out, gate_up, down, gains, *rest):
    results, rest = rest[:9], rest[9:]
    their_qkv, their_out, their_gate_up, b_qkv, b_out, b_gate_up, b_down, swap, sems = rest
    axes = Axes(True)
    core = axes.core
    greet_plane()
    swaps = [
        remote(mine, theirs, swap.at[0, at], swap.at[1, at], axes.partner)
        for at, (mine, theirs) in enumerate(
            ((qkv, their_qkv), (out, their_out), (gate_up, their_gate_up))
        )
    ]
    for copy in swaps:
        copy.start()
    b_down[...] = down[...].astype(BF)
    for copy in swaps:
        copy.wait()

    def joined(mine, theirs):
        upper = jnp.where(core == 0, mine, theirs)
        lower = jnp.where(core == 0, theirs, mine)
        return jnp.concatenate([upper, lower], axis=0).astype(BF)

    for layer in range(2):
        for at in range(3):
            b_qkv[layer, at] = joined(qkv[layer, at], their_qkv[layer, at])
        b_out[layer] = joined(out[layer], their_out[layer])
        for at in range(2):
            b_gate_up[layer, at] = joined(gate_up[layer, at], their_gate_up[layer, at])

    narrow, wide = halves(core, 768), halves(core, 2048)
    every = slice(None)
    left, right = pl.ds(0, 384), pl.ds(384, 384)
    chunks = []
    count = 0

    def segment(first_is_y, view, own):
        nonlocal count
        count += 1
        return GatherSegment(first_is_y, view, own, sems.at[count - 1])

    for layer in range(2):
        g_qkv, g_out, g_gate_up, g_down = results[4 * layer : 4 * layer + 4]
        two = pl.ds(0, 2)

        def of_qk(z, y, ref=g_qkv):
            return ref.at[pl.ds(0, 2), z, y, :, narrow]

        def of_v(z, y, ref=g_qkv):
            return ref.at[2, z, y, :, narrow]

        def of_out(z, y, ref=g_out):
            return ref.at[z, y, :, narrow]

        def of_gate(z, y, ref=g_gate_up):
            return ref.at[0, z, y, :, wide]

        def of_up(z, y, ref=g_gate_up):
            return ref.at[1, z, y, :, wide]

        def of_left(z, y, ref=g_down):
            return ref.at[z, y, core, :, left]

        def of_right(z, y, ref=g_down):
            return ref.at[z, y, core, :, right]

        attention = [
            segment(True, of_qk, b_qkv.at[layer, two, :, narrow]),
            segment(False, of_v, b_qkv.at[layer, 2, :, narrow]),
            segment(False, of_out, b_out.at[layer, :, narrow]),
        ]
        if layer == 0:

            def of_gains(z, y, ref=results[8]):
                return ref.at[z, y, core]

            attention.append(segment(True, of_gains, gains))
        chunks.append(attention)
        chunks.append(
            [
                segment(True, of_gate, b_gate_up.at[layer, 0, :, wide]),
                segment(False, of_up, b_gate_up.at[layer, 1, :, wide]),
            ]
        )
        chunks.append(
            [
                segment(True, of_left, b_down.at[layer, :, left]),
                segment(False, of_right, b_down.at[layer, :, right]),
            ]
        )
    pipeline(chunks, 5)


def gather_weights(qkv, out, gate_up, down, gains):
    shape = jax.ShapeDtypeStruct
    one_layer = [
        shape((3, 4, 4, 48, 768), BF),
        shape((4, 4, 48, 768), BF),
        shape((2, 4, 4, 48, 2048), BF),
        shape((4, 4, 2, 64, 768), BF),
    ]
    segments = 15
    results = pl.pallas_call(
        gather_kernel,
        out_shape=one_layer + one_layer + [shape((4, 4, 2, 8, 128), F32)],
        in_specs=[VMEM] * 5,
        out_specs=[ANY] * 9,
        scratch_shapes=[
            pltpu.VMEM((2, 3, 24, 768), F32),
            pltpu.VMEM((2, 24, 768), F32),
            pltpu.VMEM((2, 2, 24, 2048), F32),
            pltpu.VMEM((2, 3, 48, 768), BF),
            pltpu.VMEM((2, 48, 768), BF),
            pltpu.VMEM((2, 2, 48, 2048), BF),
            pltpu.VMEM((2, 64, 768), BF),
            pltpu.SemaphoreType.DMA((2, 3)),
            pltpu.SemaphoreType.DMA((segments, GATHER_SEMAPHORES)),
        ],
        compiler_params=params(1),
        name="gather_weights",
    )(qkv, out, gate_up, down, gains)
    layers = []
    for layer in range(2):
        g_qkv, g_out, g_gate_up, g_down = results[4 * layer : 4 * layer + 4]
        layers.append(
            (
                g_qkv.reshape(3, 768, 768),
                g_out.reshape(768, 768),
                g_gate_up.reshape(2, 768, 2048),
                g_down.reshape(2048, 768),
            )
        )
    return layers, results[8]


class ScatterSegment:
    def __init__(self, first_is_y, view, buffers, semaphores, finish):
        self.axes = Axes(first_is_y)
        self.view, self.semaphores, self.finish = view, semaphores, finish
        self.total, self.theirs, self.ring, self.rows, self.blocks, self.groups = buffers

    def stage(self, number):
        axes, sem, total = self.axes, self.semaphores, self.total
        m1, m2 = axes.m1, axes.m2
        before, after, across = shifted(m2, 3), shifted(m2, 1), shifted(m2, 2)
        low, high = pl.ds(0, 2), pl.ds(2, 2)

        def add(target, source):
            target[...] = (target[...].astype(F32) + source[...].astype(F32)).astype(target.dtype)

        if number == 0:
            for at in range(4):
                z, y = axes.order(ALL, at)
                pltpu.make_async_copy(
                    self.view(z, y, axes.core), total.at[at], sem.at[0]
                ).start()
                remote(
                    self.view(z, y, 1 - axes.core),
                    self.theirs.at[at],
                    sem.at[1],
                    sem.at[2],
                    axes.partner,
                ).start()
        elif number == 1:
            pltpu.make_async_copy(total, total, sem.at[0]).wait()
            remote(total, self.theirs, sem.at[1], sem.at[2], axes.partner).wait()

            def body(at, carry):
                add(total.at[lax.div(at, 4), lax.rem(at, 4)], self.theirs.at[lax.div(at, 4), lax.rem(at, 4)])
                return carry

            lax.fori_loop(0, 16, body, 0)
            remote(
                total.at[across, low], self.ring.at[0], sem.at[3], sem.at[4], axes.second(1)
            ).start()
            remote(
                total.at[across, high], self.ring.at[1], sem.at[3], sem.at[4], axes.second(3)
            ).start()
        elif number == 2:
            row = total.at[m2]
            remote(row, self.ring, sem.at[3], sem.at[4], axes.partner).wait()
            add(total.at[after, low], self.ring.at[0])
            add(total.at[before, high], self.ring.at[1])
            remote(
                total.at[after], self.rows.at[0], sem.at[5], sem.at[6], axes.second(1)
            ).start()
            remote(
                total.at[before], self.rows.at[1], sem.at[5], sem.at[6], axes.second(3)
            ).start()
        elif number == 3:
            remote(self.rows, self.rows, sem.at[5], sem.at[6], axes.partner).wait()

            def body(at, carry):
                total[m2, at] = (
                    total[m2, at].astype(F32)
                    + self.rows[0, at].astype(F32)
                    + self.rows[1, at].astype(F32)
                ).astype(total.dtype)
                return carry

            lax.fori_loop(0, 4, body, 0)
            for by in (1, 3, 2):
                remote(
                    total.at[m2, shifted(m1, by)],
                    self.blocks.at[by - 1],
                    sem.at[7],
                    sem.at[8],
                    axes.first(by),
                ).start()
        elif number == 4:
            remote(self.blocks, self.blocks, sem.at[7], sem.at[8], axes.partner).wait()
            self.groups[axes.x] = (
                total[m2, m1].astype(F32)
                + self.blocks[0].astype(F32)
                + self.blocks[1].astype(F32)
                + self.blocks[2].astype(F32)
            ).astype(total.dtype)
            mine = self.groups.at[axes.x]
            for by in (1, 3, 2):
                remote(
                    mine,
                    mine,
                    sem.at[9],
                    sem.at[10],
                    device(shifted(axes.x, by), axes.z, axes.y, axes.core),
                ).start()
        elif number == 5:
            three = self.groups.at[pl.ds(0, 3)]
            remote(three, three, sem.at[9], sem.at[10], axes.partner).wait()
            summed = self.groups[0].astype(F32)
            for at in range(1, 4):
                summed = summed + self.groups[at].astype(F32)
            self.finish(0, summed)
        else:
            self.finish(1, None)


SCATTER_SEMAPHORES = 13


def scatter_kernel(*refs):
    grads, refs = refs[:9], refs[9:]
    o_qkv, o_out, o_gate_up, o_down, o_gains = refs[:5]
    shapes = scatter_segments()
    buffers, refs = refs[5 : 5 + 6 * len(shapes)], refs[5 + 6 * len(shapes) :]
    swaps, refs = refs[: 2 * SWAPPED], refs[2 * SWAPPED :]
    sems = refs[0]
    axes = Axes(True)
    core = axes.core
    greet(
        [axes.partner]
        + [axes.along_y(by) for by in (1, 2, 3)]
        + [axes.along_z(by) for by in (1, 2, 3)]
        + [device(shifted(axes.x, by), axes.z, axes.y, axes.core) for by in (1, 2, 3)]
    )
    count = 0
    swapped = 0

    def segment(first_is_y, view, finish):
        nonlocal count
        at = count
        count += 1
        return ScatterSegment(
            first_is_y, view, buffers[6 * at : 6 * at + 6], sems.at[at], finish
        )

    def rows_swapped(target, at_sems):
        nonlocal swapped
        mine, theirs = swaps[2 * swapped : 2 * swapped + 2]
        swapped += 1
        sem = sems.at[at_sems]

        def finish(part, summed):
            own_rows = pl.ds(pl.multiple_of(core * 24, 8), 24)
            other_rows = pl.ds(pl.multiple_of((1 - core) * 24, 8), 24)
            lead = (slice(None),) * (len(mine.shape) - 2)
            copy = remote(
                mine.at[lead + (other_rows, slice(None))],
                theirs,
                sem.at[11],
                sem.at[12],
                axes.partner,
            )
            if part == 0:
                mine[...] = summed
                copy.start()
            else:
                copy.wait()
                kept = mine[lead + (own_rows, slice(None))]
                got = theirs[...]
                width = kept.shape[-1]
                target[..., :width] = jnp.where(core == 0, kept, got)
                target[..., width:] = jnp.where(core == 0, got, kept)

        return finish

    def direct(target):
        def finish(part, summed):
            if part == 0:
                target[...] = summed

        return finish

    def columns(which, width):
        return halves(which, width)

    chunks = []
    for layer in (1, 0):
        g_qkv, g_out, g_gate_up, g_down = grads[4 * layer : 4 * layer + 4]

        def of_qk(z, y, which, ref=g_qkv):
            return ref.at[pl.ds(0, 2), z, y, :, columns(which, 768)]

        def of_q(z, y, which, ref=g_qkv):
            return ref.at[0, z, y, :, columns(which, 768)]

        def of_k(z, y, which, ref=g_qkv):
            return ref.at[1, z, y, :, columns(which, 768)]

        def of_v(z, y, which, ref=g_qkv):
            return ref.at[2, z, y, :, columns(which, 768)]

        def of_out(z, y, which, ref=g_out):
            return ref.at[z, y, :, columns(which, 768)]

        def of_gate(z, y, which, ref=g_gate_up):
            return ref.at[0, z, y, :, columns(which, 2048)]

        def of_up(z, y, which, ref=g_gate_up):
            return ref.at[1, z, y, :, columns(which, 2048)]

        def of_left(z, y, which, ref=g_down):
            return ref.at[z, y, which, :, pl.ds(0, 384)]

        def of_right(z, y, which, ref=g_down):
            return ref.at[z, y, which, :, pl.ds(384, 384)]

        chunks.append(
            [
                segment(True, of_gate, rows_swapped(o_gate_up.at[layer, 0], count)),
                segment(False, of_up, rows_swapped(o_gate_up.at[layer, 1], count)),
            ]
        )
        chunks.append(
            [
                segment(True, of_left, direct(o_down.at[layer, :, pl.ds(0, 384)])),
                segment(False, of_right, direct(o_down.at[layer, :, pl.ds(384, 384)])),
            ]
        )
        chunks.append(
            [
                segment(True, of_q, rows_swapped(o_qkv.at[layer, 0], count)),
                segment(True, of_k, rows_swapped(o_qkv.at[layer, 1], count)),
                segment(False, of_v, rows_swapped(o_qkv.at[layer, 2], count)),
                segment(False, of_out, rows_swapped(o_out.at[layer], count)),
            ]
        )

    def of_gains(z, y, which, ref=grads[8]):
        return ref.at[z, y, which]

    chunks[-1].append(segment(True, of_gains, direct(o_gains)))
    pipeline(chunks, 7)


SWAPPED = 12


def scatter_segments():
    layer = [(48, 1024, BF)] * 2 + [(64, 384, BF)] * 2 + [(48, 384, BF)] * 4
    return layer + layer + [(8, 128, F32)]


def scatter_gradients(layers, gains):
    shape = jax.ShapeDtypeStruct
    segments = scatter_segments()
    scratch = []
    for rows, width, kind in segments:
        scratch += [
            pltpu.VMEM((4, 4, rows, width), kind),
            pltpu.VMEM((4, 4, rows, width), kind),
            pltpu.VMEM((2, 2, rows, width), kind),
            pltpu.VMEM((2, 4, rows, width), kind),
            pltpu.VMEM((3, rows, width), kind),
            pltpu.VMEM((4, rows, width), kind),
        ]
    for rows, width, kind in segments:
        if rows == 48:
            scratch += [pltpu.VMEM((48, width), F32), pltpu.VMEM((24, width), F32)]
    operands = []
    for g_qkv, g_out, g_gate_up, g_down in layers:
        operands += [
            g_qkv.reshape(3, 4, 4, 48, 768),
            g_out.reshape(4, 4, 48, 768),
            g_gate_up.reshape(2, 4, 4, 48, 2048),
            g_down.reshape(4, 4, 2, 64, 768),
        ]
    return pl.pallas_call(
        scatter_kernel,
        out_shape=[
            shape((2, 3, 24, 768), F32),
            shape((2, 24, 768), F32),
            shape((2, 2, 24, 2048), F32),
            shape((2, 64, 768), F32),
            shape((8, 128), F32),
        ],
        in_specs=[ANY] * 9,
        out_specs=[VMEM] * 5,
        scratch_shapes=scratch
        + [pltpu.SemaphoreType.DMA((len(segments), SCATTER_SEMAPHORES))],
        compiler_params=params(2),
        name="scatter_gradients",
    )(*operands, gains)


def pair_device(pair):
    if pair < 16:
        return 2 * pair
    z = (pair - 16) // 2
    return 2 * (4 * z + 2 * ((pair - 16) % 2) + z % 2) + 1


def own_pair():
    _, z, y, core = coordinates()
    has_pair = (core == 0) | (lax.rem(z + y, 2) == 0)
    pair = jnp.where(core == 0, 4 * z + y, 16 + 2 * z + lax.div(y, 2))
    return has_pair, pair


def lanes(shape):
    return lax.broadcasted_iota(jnp.int32, shape, len(shape) - 1)


def turned(values, cosine, sine):
    here = lax.rem(lanes(values.shape), 64) < 32
    width = values.shape[-1]
    other = jnp.where(here, pltpu.roll(values, width - 32, 1), pltpu.roll(values, 32, 1))
    return values * cosine + other * sine


def twice(table):
    return jnp.concatenate([table, table], axis=0)


def project_kernel(source, weights, cosine, sine, received, outgoing, send, receive, local):
    x = lax.axis_index("batch")
    me = lax.axis_index("seq")
    has_pair, _ = own_pair()
    barrier = pltpu.get_barrier_semaphore()

    @pl.when(has_pair)
    def _():
        for by in range(1, 32):
            pl.semaphore_signal(
                barrier, inc=1, device_id=(x, lax.rem(me + by, 32)), device_id_type=MESH
            )

    rows = source[...]
    query, key, value = (
        jnp.dot(rows, weights[at], preferred_element_type=F32) for at in range(3)
    )
    cosine_all, sine_all = twice(cosine[...]), twice(sine[...])
    front = lanes((128, 128)) < 64
    for tile in range(6):
        cut = slice(128 * tile, 128 * tile + 128)
        q = turned(query[:, cut], cosine_all, sine_all) * (1.0 / math.sqrt(HEAD_DIM))
        k = turned(key[:, cut], cosine_all, sine_all)
        v = value[:, cut]
        messages = (
            (jnp.where(front, q, 0.0), jnp.where(front, k, pltpu.roll(v, 64, 1))),
            (
                jnp.where(front, pltpu.roll(q, 64, 1), 0.0),
                jnp.where(front, pltpu.roll(k, 64, 1), v),
            ),
        )
        for at, (first, second) in enumerate(messages):
            for slot in range(2):
                span = slice(64 * slot, 64 * slot + 64)
                outgoing[slot * HEADS + 2 * tile + at, :, 0:128] = first[span].astype(BF)
                outgoing[slot * HEADS + 2 * tile + at, :, 128:256] = second[span].astype(BF)

    target = received.at[pl.ds(pl.multiple_of(me * SPAN, SPAN), SPAN)]
    pl.semaphore_wait(barrier, jnp.where(has_pair, PAIRS - 1, PAIRS))
    for pair in range(PAIRS):
        there = pair_device(pair)

        @pl.when(me != there)
        def _(pair=pair, there=there):
            remote(outgoing.at[pair], target, send, receive, (x, there)).start()

        @pl.when(me == there)
        def _(pair=pair):
            pltpu.make_async_copy(outgoing.at[pair], target, local).start()

    @pl.when(has_pair)
    def _():
        pltpu.make_async_copy(outgoing.at[0], target, local).wait()
        others = received.at[pl.ds(0, 31 * SPAN)]
        remote(others, others, send, receive, (x, me)).wait_recv()
        sent = outgoing.at[pl.ds(0, PAIRS - 1)]
        remote(sent, sent, send, receive, (x, me)).wait_send()

    @pl.when(jnp.logical_not(has_pair))
    def _():
        remote(outgoing, outgoing, send, receive, (x, me)).wait_send()


def project(source, weights, cosine, sine):
    return pl.pallas_call(
        project_kernel,
        out_shape=jax.ShapeDtypeStruct((LENGTH, 256), BF),
        in_specs=[VMEM] * 4,
        out_specs=ANY,
        scratch_shapes=[
            pltpu.VMEM((PAIRS, SPAN, 256), BF),
            pltpu.SemaphoreType.DMA(()),
            pltpu.SemaphoreType.DMA(()),
            pltpu.SemaphoreType.DMA(()),
        ],
        compiler_params=params(3),
        name="project",
    )(source, weights, cosine, sine)


def allowed_keys(first_key, first_query, keys, queries, length):
    key = first_key + lax.broadcasted_iota(jnp.int32, (keys, queries), 0)
    query = first_query + lax.broadcasted_iota(jnp.int32, (keys, queries), 1)
    return (key <= query) & (key < length)


def slot_length(lengths, pair):
    return jnp.where(pair < HEADS, lengths[0], lengths[1])


LAST_DIMS = (((1,), (1,)), ((), ()))


def attend_kernel(
    lengths, rows, merged, out_turned, log_total, keys_turned, outgoing, incoming, send, receive, local
):
    x = lax.axis_index("batch")
    me = lax.axis_index("seq")
    has_pair, pair = own_pair()
    barrier = pltpu.get_barrier_semaphore()
    for other in range(PAIRS):
        there = pair_device(other)

        @pl.when(me != there)
        def _(there=there):
            pl.semaphore_signal(barrier, inc=1, device_id=(x, there), device_id_type=MESH)

    @pl.when(has_pair)
    def _():
        length = slot_length(lengths, pair)
        keys_turned[...] = rows[:, 128:256].astype(F32).T.astype(BF)
        pl.semaphore_wait(barrier, 31)
        for at in range(LENGTH // BLOCK):
            count = (at + 1) * BLOCK
            queries = rows[at * BLOCK : count, 0:128]
            keys = rows[0:count, 128:256]
            scores = lax.dot_general(keys, queries, LAST_DIMS, preferred_element_type=F32)
            scores = jnp.where(
                allowed_keys(0, at * BLOCK, count, BLOCK, length), scores, MASKED
            )
            highest = jnp.max(scores, axis=0, keepdims=True)
            raised = jnp.exp(scores - highest)
            total = jnp.sum(raised, axis=0, keepdims=True)
            result = (
                jnp.dot(keys_turned[:, 0:count], raised.astype(BF), preferred_element_type=F32)
                / total
            )
            cut = slice(at * BLOCK, count)
            out_turned[:, cut] = result
            log_total[:, cut] = jnp.broadcast_to(highest + jnp.log(total), (8, BLOCK))
            outgoing[4 * at : 4 * at + 4] = result.T.reshape(4, SPAN, 128).astype(BF)
            for there in range(4 * at, 4 * at + 4):

                @pl.when(me != there)
                def _(there=there):
                    remote(
                        outgoing.at[there], incoming.at[pair], send, receive, (x, there)
                    ).start()

                @pl.when(me == there)
                def _(there=there):
                    pltpu.make_async_copy(outgoing.at[there], incoming.at[pair], local).start()

        pltpu.make_async_copy(outgoing.at[0], incoming.at[0], local).wait()
        sent = outgoing.at[pl.ds(0, 31)]
        remote(sent, sent, send, receive, (x, me)).wait_send()
        got = incoming.at[pl.ds(0, PAIRS - 1)]
        remote(got, got, send, receive, (x, me)).wait_recv()

    @pl.when(jnp.logical_not(has_pair))
    def _():
        remote(incoming, incoming, send, receive, (x, me)).wait_recv()

    front = lanes((SPAN, 128)) < 64
    for slot in range(2):
        for tile in range(6):
            first = incoming[slot * HEADS + 2 * tile].astype(F32)
            second = incoming[slot * HEADS + 2 * tile + 1].astype(F32)
            both = jnp.where(front, pltpu.roll(first, 64, 1), second)
            merged[64 * slot : 64 * slot + 64, 128 * tile : 128 * tile + 128] = both.astype(BF)


def attend(lengths, rows):
    shape = jax.ShapeDtypeStruct
    return pl.pallas_call(
        attend_kernel,
        out_shape=[shape((128, 768), BF), shape((128, LENGTH), F32), shape((8, LENGTH), F32)],
        in_specs=[SMEM, VMEM],
        out_specs=[VMEM] * 3,
        scratch_shapes=[
            pltpu.VMEM((128, LENGTH), BF),
            pltpu.VMEM((32, SPAN, 128), BF),
            pltpu.VMEM((PAIRS, SPAN, 128), BF),
            pltpu.SemaphoreType.DMA(()),
            pltpu.SemaphoreType.DMA(()),
            pltpu.SemaphoreType.DMA(()),
        ],
        compiler_params=params(4),
        name="attend",
    )(lengths, rows)


def attend_back_kernel(
    lengths,
    grad,
    rows,
    out_turned,
    log_total,
    cosine,
    sine,
    result,
    out_grad,
    keys_turned,
    key_grad,
    to_pairs,
    to_places,
    incoming,
    sems,
):
    x = lax.axis_index("batch")
    me = lax.axis_index("seq")
    has_pair, pair = own_pair()
    barrier = pltpu.get_barrier_semaphore()
    places = [pair_device(other) for other in range(PAIRS)]
    for there in places:

        @pl.when(me != there)
        def _(there=there):
            pl.semaphore_signal(barrier, inc=1, device_id=(x, there), device_id_type=MESH)

    @pl.when(has_pair)
    def _():
        for there in range(32):
            if there not in places:
                pl.semaphore_signal(barrier, inc=1, device_id=(x, there), device_id_type=MESH)

    front = lanes((SPAN, 128)) < 64
    for slot in range(2):
        for tile in range(6):
            both = grad[64 * slot : 64 * slot + 64, 128 * tile : 128 * tile + 128].astype(F32)
            at = slot * HEADS + 2 * tile
            to_pairs[at] = jnp.where(front, 0.0, pltpu.roll(both, 64, 1)).astype(BF)
            to_pairs[at + 1] = jnp.where(front, 0.0, both).astype(BF)

    pl.semaphore_wait(barrier, jnp.where(has_pair, 31, PAIRS))
    target = out_grad.at[pl.ds(pl.multiple_of(me * SPAN, SPAN), SPAN)]
    for other, there in enumerate(places):

        @pl.when(me != there)
        def _(other=other, there=there):
            remote(to_pairs.at[other], target, sems.at[0], sems.at[1], (x, there)).start()

        @pl.when(me == there)
        def _(other=other):
            pltpu.make_async_copy(to_pairs.at[other], target, sems.at[2]).start()

    @pl.when(has_pair)
    def _():
        length = slot_length(lengths, pair)
        keys_turned[...] = rows[:, 128:256].astype(F32).T.astype(BF)
        key_grad[...] = jnp.zeros_like(key_grad)
        pltpu.make_async_copy(to_pairs.at[0], target, sems.at[2]).wait()
        others = out_grad.at[pl.ds(0, 31 * SPAN)]
        remote(others, others, sems.at[0], sems.at[1], (x, me)).wait_recv()
        for at in reversed(range(LENGTH // BLOCK)):
            cut = slice(at * BLOCK, (at + 1) * BLOCK)
            queries = rows[cut, 0:128]
            outs = out_grad[cut, :]
            delta = jnp.sum(outs.astype(F32).T * out_turned[:, cut], axis=0, keepdims=True)
            shift = log_total[0:1, cut]
            query_grad = jnp.zeros((128, BLOCK), F32)
            for part in range(at + 1):
                span = slice(part * BLOCK, (part + 1) * BLOCK)
                keys = rows[span, 128:256]
                scores = lax.dot_general(keys, queries, LAST_DIMS, preferred_element_type=F32)
                allowed = allowed_keys(part * BLOCK, at * BLOCK, BLOCK, BLOCK, length)
                probs = jnp.where(allowed, jnp.exp(scores - shift), 0.0)
                probs_grad = lax.dot_general(keys, outs, LAST_DIMS, preferred_element_type=F32)
                score_grad = (probs * (probs_grad - delta)).astype(BF)
                key_grad[span, :] += jnp.dot(
                    score_grad, queries, preferred_element_type=F32
                ) + jnp.dot(probs.astype(BF), outs, preferred_element_type=F32)
                query_grad += jnp.dot(
                    keys_turned[:, span], score_grad, preferred_element_type=F32
                )
            to_places[4 * at : 4 * at + 4, :, 0:128] = query_grad.T.reshape(4, SPAN, 128).astype(BF)
            to_places[4 * at : 4 * at + 4, :, 128:256] = (
                key_grad[cut, :].reshape(4, SPAN, 128).astype(BF)
            )
            for there in range(4 * at, 4 * at + 4):

                @pl.when(me != there)
                def _(there=there):
                    remote(
                        to_places.at[there], incoming.at[pair], sems.at[3], sems.at[4], (x, there)
                    ).start()

                @pl.when(me == there)
                def _(there=there):
                    pltpu.make_async_copy(
                        to_places.at[there], incoming.at[pair], sems.at[5]
                    ).start()

        sent = to_pairs.at[pl.ds(0, PAIRS - 1)]
        remote(sent, sent, sems.at[0], sems.at[1], (x, me)).wait_send()
        pltpu.make_async_copy(to_places.at[0], incoming.at[0], sems.at[5]).wait()
        sent = to_places.at[pl.ds(0, 31)]
        remote(sent, sent, sems.at[3], sems.at[4], (x, me)).wait_send()
        got = incoming.at[pl.ds(0, PAIRS - 1)]
        remote(got, got, sems.at[3], sems.at[4], (x, me)).wait_recv()

    @pl.when(jnp.logical_not(has_pair))
    def _():
        remote(to_pairs, to_pairs, sems.at[0], sems.at[1], (x, me)).wait_send()
        remote(incoming, incoming, sems.at[3], sems.at[4], (x, me)).wait_recv()

    table, wave = cosine[...], -sine[...]
    for slot in range(2):
        span = slice(64 * slot, 64 * slot + 64)
        for tile in range(6):
            cut = slice(128 * tile, 128 * tile + 128)
            at = slot * HEADS + 2 * tile
            first_q, second_q = (incoming[at + n, :, 0:128].astype(F32) for n in (0, 1))
            first_kv, second_kv = (incoming[at + n, :, 128:256].astype(F32) for n in (0, 1))
            q = jnp.where(front, first_q, pltpu.roll(second_q, 64, 1))
            k = jnp.where(front, first_kv, pltpu.roll(second_kv, 64, 1))
            v = jnp.where(front, pltpu.roll(first_kv, 64, 1), second_kv)
            q = turned(q * (1.0 / math.sqrt(HEAD_DIM)), table, wave)
            result[0, span, cut] = q.astype(BF)
            result[1, span, cut] = turned(k, table, wave).astype(BF)
            result[2, span, cut] = v.astype(BF)


def attend_back(lengths, grad, rows, out_turned, log_total, cosine, sine):
    return pl.pallas_call(
        attend_back_kernel,
        out_shape=jax.ShapeDtypeStruct((3, 128, 768), BF),
        in_specs=[SMEM] + [VMEM] * 6,
        out_specs=VMEM,
        scratch_shapes=[
            pltpu.VMEM((LENGTH, 128), BF),
            pltpu.VMEM((128, LENGTH), BF),
            pltpu.VMEM((LENGTH, 128), F32),
            pltpu.VMEM((PAIRS, SPAN, 128), BF),
            pltpu.VMEM((32, SPAN, 256), BF),
            pltpu.VMEM((PAIRS, SPAN, 256), BF),
            pltpu.SemaphoreType.DMA((6,)),
        ],
        compiler_params=params(5),
        name="attend_back",
    )(lengths, grad, rows, out_turned, log_total, cosine, sine)


def angles(places):
    half_dim = HEAD_DIM // 2
    frequency = jnp.exp(-math.log(10000.0) * jnp.arange(half_dim).astype(F32) / half_dim)
    phases = places.astype(F32)[:, None] * frequency[None, :]
    cosine, sine = jnp.cos(phases), jnp.sin(phases)
    return (
        jnp.concatenate([cosine] * 4, axis=1),
        jnp.concatenate([-sine, sine] * 2, axis=1),
    )


def norm_forward(values, norm_gain):
    inverse = lax.rsqrt(jnp.mean(values * values, axis=-1, keepdims=True) + EPSILON)
    return (values * inverse * norm_gain, inverse)


def norm_backward(incoming, values, inverse, norm_gain):
    scaled = incoming * norm_gain
    outgoing = inverse * scaled - values * (inverse * inverse * inverse) * jnp.mean(
        scaled * values, axis=-1, keepdims=True
    )
    return (outgoing, jnp.sum(incoming * values * inverse, axis=0))


def attention_forward(source, weights, tables):
    lengths, cosine, sine = tables
    source_low = source.astype(BF)
    rows = project(source_low, weights[0], cosine, sine)
    merged, out_turned, log_total = attend(lengths, rows)
    mixed = jnp.dot(merged, weights[1], preferred_element_type=F32)
    return mixed, (source_low, rows, merged, out_turned, log_total)


def attention_backward(incoming, saved, weights, tables):
    lengths, cosine, sine = tables
    source_low, rows, merged, out_turned, log_total = saved
    incoming_low = incoming.astype(BF)
    out_grad = jnp.einsum("rd,re->de", merged, incoming_low, preferred_element_type=F32).astype(BF)
    merged_grad = jnp.einsum(
        "re,de->rd", incoming_low, weights[1], preferred_element_type=F32
    ).astype(BF)
    stacked = attend_back(lengths, merged_grad, rows, out_turned, log_total, cosine, sine)
    qkv_grad = jnp.einsum("rd,jre->jde", source_low, stacked, preferred_element_type=F32).astype(BF)
    source_grad = jnp.einsum("jre,jde->rd", stacked, weights[0], preferred_element_type=F32)
    return source_grad, qkv_grad, out_grad


def ffn_forward(source, weights):
    rows_in = source.astype(BF)
    paired = jnp.einsum("rd,jdf->jrf", rows_in, weights[2], preferred_element_type=F32)
    hidden = (jax.nn.silu(paired[0]) * paired[1]).astype(BF)
    result = jnp.dot(hidden, weights[3], preferred_element_type=F32)
    return result, (rows_in, paired, hidden)


def ffn_backward(incoming, saved, weights):
    rows_in, paired, hidden = saved
    incoming_low = incoming.astype(BF)
    down_grad = jnp.einsum("rf,rd->fd", hidden, incoming_low, preferred_element_type=F32).astype(BF)
    hidden_grad = jnp.einsum("rd,fd->rf", incoming_low, weights[3], preferred_element_type=F32)
    gate, lifted = paired[0], paired[1]
    sigmoid = jax.nn.sigmoid(gate)
    gate_grad = hidden_grad * lifted * sigmoid * (1.0 + gate * (1.0 - sigmoid))
    lifted_grad = hidden_grad * gate * sigmoid
    stacked = jnp.stack([gate_grad, lifted_grad]).astype(BF)
    gate_up_grad = jnp.einsum("rd,jrf->jdf", rows_in, stacked, preferred_element_type=F32).astype(BF)
    source_grad = jnp.einsum("jrf,jdf->rd", stacked, weights[2], preferred_element_type=F32)
    return source_grad, gate_up_grad, down_grad


def update(weight_matrix, moment, average, gradient, step_size):
    moment_new = MOMENTUM * moment + gradient
    weight_new = weight_matrix - step_size * (gradient + MOMENTUM * moment_new)
    return (moment_new, weight_new, AVERAGING * average + (1.0 - AVERAGING) * weight_new)


def by_slot(values):
    return values[0].transpose(1, 0, 2).reshape(128, 768)


def by_place(values):
    return values.reshape(2, SPAN, 768).transpose(1, 0, 2)[None]


def on_device(
    inputs,
    cotangent,
    lengths,
    qkv_weight,
    qkv_moment,
    qkv_average,
    out_weight,
    out_moment,
    out_average,
    gate_up_weight,
    gate_up_moment,
    gate_up_average,
    down_weight,
    down_moment,
    down_average,
    norm_gains,
    gain_moment,
    gain_average,
):
    places = lax.axis_index("seq") * SPAN + jnp.arange(SPAN)
    cosine, sine = angles(places)
    tables = (lengths[0], cosine, sine)
    own_gains = jnp.pad(
        norm_gains.astype(BF).astype(F32).reshape(4, 24), ((0, 4), (0, 104))
    )
    (first, second), gathered = gather_weights(
        qkv_weight, out_weight, gate_up_weight, down_weight, own_gains
    )
    gains = gathered.reshape(32, 8, 128)[:, :4, :24].transpose(1, 0, 2).reshape(4, 768)

    stream = by_slot(inputs)
    mixed, attn_0 = attention_forward(stream, first, tables)
    residual_0 = stream + mixed
    middle, inverse_00 = norm_forward(residual_0, gains[0])
    fed, ffn_0 = ffn_forward(middle, first)
    summed_0 = middle + fed
    shallow, inverse_01 = norm_forward(summed_0, gains[1])
    normed, inverse_10 = norm_forward(shallow, gains[2])
    mixed, attn_1 = attention_forward(normed, second, tables)
    residual_1 = shallow + mixed
    normed_two, inverse_11 = norm_forward(residual_1, gains[3])
    fed, ffn_1 = ffn_forward(normed_two, second)
    result = residual_1 + fed
    incoming = by_slot(cotangent)
    normed_grad, gate_up_grad_1, down_grad_1 = ffn_backward(incoming, ffn_1, second)
    through, gain_grad_11 = norm_backward(normed_grad, residual_1, inverse_11, gains[3])
    residual_grad = incoming + through
    normed_grad, qkv_grad_1, out_grad_1 = attention_backward(residual_grad, attn_1, second, tables)
    through, gain_grad_10 = norm_backward(normed_grad, shallow, inverse_10, gains[2])
    shallow_grad = residual_grad + through
    summed_grad, gain_grad_01 = norm_backward(shallow_grad, summed_0, inverse_01, gains[1])
    middle_ffn, gate_up_grad_0, down_grad_0 = ffn_backward(summed_grad, ffn_0, first)
    middle_grad = summed_grad + middle_ffn
    residual_grad, gain_grad_00 = norm_backward(middle_grad, residual_0, inverse_00, gains[0])
    source_grad, qkv_grad_0, out_grad_0 = attention_backward(residual_grad, attn_0, first, tables)
    input_grad = residual_grad + source_grad

    gain_grads = jnp.stack([gain_grad_00, gain_grad_01, gain_grad_10, gain_grad_11])
    gain_parts = jnp.pad(
        gain_grads.reshape(4, 32, 24).transpose(1, 0, 2), ((0, 0), (0, 4), (0, 104))
    ).reshape(4, 4, 2, 8, 128)
    summed = scatter_gradients(
        [
            (qkv_grad_0, out_grad_0, gate_up_grad_0, down_grad_0),
            (qkv_grad_1, out_grad_1, gate_up_grad_1, down_grad_1),
        ],
        gain_parts,
    )
    gain_sum = summed[4][:4, :24].reshape(2, 2, 24)
    step_size = STEP_RATE / math.sqrt(
        lax.axis_size("batch") * SPAN * lax.axis_size("seq") * 2
    )
    qkv_new = update(qkv_weight, qkv_moment, qkv_average, summed[0], step_size)
    out_new = update(out_weight, out_moment, out_average, summed[1], step_size)
    gate_up_new = update(gate_up_weight, gate_up_moment, gate_up_average, summed[2], step_size)
    down_new = update(down_weight, down_moment, down_average, summed[3], step_size)
    gain_new = update(norm_gains, gain_moment, gain_average, gain_sum, step_size)
    return (
        by_place(result),
        by_place(input_grad),
        *qkv_new,
        *out_new,
        *gate_up_new,
        *down_new,
        *gain_new,
    )


def solution(mesh):
    rows = P("batch", "seq", None, None)
    wide = P(None, None, "seq", None)
    flat = P(None, "seq", None)
    gains = P(None, None, "seq")
    state = (wide,) * 3 + (flat,) * 3 + (wide,) * 3 + (flat,) * 3 + (gains,) * 3
    return jax.shard_map(
        on_device,
        mesh=mesh,
        in_specs=(rows, rows, P("batch", None)) + state,
        out_specs=(rows, rows) + state,
        check_vma=False,
    )
```

```python
import functools
import math

import jax
import jax.numpy as jnp
from jax import lax
from jax.experimental import pallas as pl
from jax.experimental.pallas import tpu as pltpu
from jax.sharding import PartitionSpec as P

MESH = pl.DeviceIdType.MESH
BF = jnp.bfloat16
F32 = jnp.float32
HEAD_DIM = 64
HEADS = 12
PAIRS = 24
SPAN = 64
LENGTH = 2048
BLOCK = 256
EPSILON = 1e-06
MOMENTUM = 0.5
AVERAGING = 0.5
STEP_RATE = 0.1
MASKED = -1e30
VMEM_BYTES = 60 * 2**20
VMEM = pl.BlockSpec(memory_space=pltpu.VMEM)
ANY = pl.BlockSpec(memory_space=pl.ANY)
SMEM = pl.BlockSpec(memory_space=pltpu.SMEM)
ALL = pl.ds(0, 4)


def params(collective_id):
    return pltpu.CompilerParams(
        collective_id=collective_id, has_side_effects=True, vmem_limit_bytes=VMEM_BYTES
    )


def coordinates():
    seq = lax.axis_index("seq")
    return (
        lax.axis_index("batch"),
        lax.div(seq, 8),
        lax.rem(lax.div(seq, 2), 4),
        lax.rem(seq, 2),
    )


def device(x, z, y, core):
    return (x, (z * 4 + y) * 2 + core)


def shifted(value, by):
    return lax.rem(value + by, 4)


def signal(partners):
    barrier = pltpu.get_barrier_semaphore()
    for partner in partners:
        pl.semaphore_signal(barrier, inc=1, device_id=partner, device_id_type=MESH)


def greet(partners):
    signal(partners)
    pl.semaphore_wait(pltpu.get_barrier_semaphore(), len(partners))


def remote(source, target, send, receive, where):
    return pltpu.make_async_remote_copy(
        src_ref=source,
        dst_ref=target,
        send_sem=send,
        recv_sem=receive,
        device_id=where,
        device_id_type=MESH,
    )


class Axes:
    def __init__(self, first_is_y):
        x, z, y, core = coordinates()
        self.first_is_y = first_is_y
        self.x, self.z, self.y, self.core = x, z, y, core
        self.m1, self.m2 = (y, z) if first_is_y else (z, y)
        self.partner = device(x, z, y, 1 - core)

    def along_y(self, by):
        return device(self.x, self.z, shifted(self.y, by), self.core)

    def along_z(self, by):
        return device(self.x, shifted(self.z, by), self.y, self.core)

    def first(self, by):
        return self.along_y(by) if self.first_is_y else self.along_z(by)

    def second(self, by):
        return self.along_z(by) if self.first_is_y else self.along_y(by)

    def order(self, i1, i2):
        return (i2, i1) if self.first_is_y else (i1, i2)


def plane():
    axes = Axes(True)
    return (
        [axes.partner]
        + [axes.along_y(by) for by in (1, 2, 3)]
        + [axes.along_z(by) for by in (1, 2, 3)]
    )


def groups():
    axes = Axes(True)
    return [device(shifted(axes.x, by), axes.z, axes.y, axes.core) for by in (1, 2, 3)]


def pipeline(chunks, stages):
    def step(number):
        for at, chunk in enumerate(chunks):
            if 0 <= number - at < stages:
                for segment in chunk:
                    segment.stage(number - at)

    return [functools.partial(step, number) for number in range(len(chunks) + stages - 1)]


class GatherSegment:
    def __init__(self, first_is_y, view, semaphores, own=None):
        self.axes = Axes(first_is_y)
        self.view, self.own, self.semaphores = view, own, semaphores

    def block(self, i1, i2):
        return self.view(*self.axes.order(i1, i2))

    def row(self, by, part=ALL):
        return self.block(part, shifted(self.axes.m2, by))

    def keep(self):
        here = self.block(self.axes.m1, self.axes.m2)
        return pltpu.make_async_copy(self.own, here, self.semaphores.at[3, 0])

    def begin(self, phase):
        axes = self.axes
        sem = [self.semaphores.at[phase, at] for at in range(4)]

        def send(part, where):
            remote(part, part, sem[0], sem[1], where).start()

        def share(part):
            remote(part, part, sem[2], sem[3], axes.partner).start()

        if phase == 0:
            here = self.block(axes.m1, axes.m2)
            source = here if self.own is None else self.own
            for by in (1, 3, 2):
                remote(source, here, sem[0], sem[1], axes.first(by)).start()
        elif phase == 1:
            send(self.row(0), axes.second(1))
            send(self.row(0), axes.second(3))
            share(self.row(0))
        elif phase == 2:
            send(self.row(3, pl.ds(0, 2)), axes.second(1))
            send(self.row(1, pl.ds(2, 2)), axes.second(3))
            share(self.row(3))
            share(self.row(1))
        else:
            share(self.row(2))

    def end(self, phase):
        axes = self.axes
        sem = [self.semaphores.at[phase, at] for at in range(4)]
        one, two = self.row(0), self.block(ALL, pl.ds(0, 2))
        moved = (self.block(pl.ds(0, 3), axes.m2), two, one, None)[phase]
        shared = (None, one, two, one)[phase]
        if moved is not None:
            remote(moved, moved, sem[0], sem[1], axes.partner).wait()
        if shared is not None:
            remote(shared, shared, sem[2], sem[3], axes.partner).wait()


def halves(core, width):
    return pl.ds(pl.multiple_of(core * (width // 2), 128), width // 2)


def weight_views(name, ref):
    core = Axes(True).core
    narrow, wide = halves(core, 768), halves(core, 2048)
    if name == "qkv":
        return [
            (True, lambda z, y: ref.at[pl.ds(0, 2), z, y, :, narrow]),
            (False, lambda z, y: ref.at[2, z, y, :, narrow]),
        ]
    if name == "out":
        return [(False, lambda z, y: ref.at[z, y, :, narrow])]
    if name == "gate_up":
        return [
            (True, lambda z, y: ref.at[0, z, y, :, wide]),
            (False, lambda z, y: ref.at[1, z, y, :, wide]),
        ]
    if name == "down":
        return [
            (True, lambda z, y: ref.at[z, y, core, :, pl.ds(0, 384)]),
            (False, lambda z, y: ref.at[z, y, core, :, pl.ds(384, 384)]),
        ]
    return [(True, lambda z, y: ref.at[z, y, core])]


def own_views(name, ref):
    core = Axes(True).core
    narrow, wide = halves(core, 768), halves(core, 2048)
    if name == "qkv":
        return [ref.at[pl.ds(0, 2), :, narrow], ref.at[2, :, narrow]]
    if name == "out":
        return [ref.at[:, narrow]]
    if name == "gate_up":
        return [ref.at[0, :, wide], ref.at[1, :, wide]]
    if name == "down":
        return [ref.at[:, pl.ds(0, 384)], ref.at[:, pl.ds(384, 384)]]
    return [ref]


WEIGHTS = {
    "qkv": ((3, 4, 4, 48, 768), BF),
    "out": ((4, 4, 48, 768), BF),
    "gate_up": ((2, 4, 4, 48, 2048), BF),
    "down": ((4, 4, 2, 64, 768), BF),
    "gains": ((4, 4, 2, 8, 256), F32),
}
SEGMENTS = {"qkv": 2, "out": 1, "gate_up": 2, "down": 2, "gains": 1}
GATHERED = [(name, layer) for layer in range(2) for name in ("qkv", "out", "gate_up", "down")] + [
    ("gains", 0)
]


def weight_shape(key):
    return jax.ShapeDtypeStruct(*WEIGHTS[key[0]])


class ScatterSegment:
    def __init__(self, first_is_y, view, buffers, semaphores, finish):
        self.axes = Axes(first_is_y)
        self.view, self.semaphores, self.finish = view, semaphores, finish
        self.total, self.theirs, self.ring, self.rows, self.blocks, self.groups = buffers

    def stage(self, number):
        axes, sem, total = self.axes, self.semaphores, self.total
        m1, m2 = axes.m1, axes.m2
        before, after, across = shifted(m2, 3), shifted(m2, 1), shifted(m2, 2)
        low, high = pl.ds(0, 2), pl.ds(2, 2)

        def add(target, source):
            target[...] = (target[...].astype(F32) + source[...].astype(F32)).astype(target.dtype)

        if number == 0:
            for at in range(4):
                z, y = axes.order(ALL, at)
                pltpu.make_async_copy(
                    self.view(z, y, axes.core), total.at[at], sem.at[0]
                ).start()
                remote(
                    self.view(z, y, 1 - axes.core),
                    self.theirs.at[at],
                    sem.at[1],
                    sem.at[2],
                    axes.partner,
                ).start()
        elif number == 1:
            pltpu.make_async_copy(total, total, sem.at[0]).wait()
            remote(total, self.theirs, sem.at[1], sem.at[2], axes.partner).wait()

            def body(at, carry):
                add(total.at[lax.div(at, 4), lax.rem(at, 4)], self.theirs.at[lax.div(at, 4), lax.rem(at, 4)])
                return carry

            lax.fori_loop(0, 16, body, 0)
            remote(
                total.at[across, low], self.ring.at[0], sem.at[3], sem.at[4], axes.second(1)
            ).start()
            remote(
                total.at[across, high], self.ring.at[1], sem.at[3], sem.at[4], axes.second(3)
            ).start()
        elif number == 2:
            row = total.at[m2]
            remote(row, self.ring, sem.at[3], sem.at[4], axes.partner).wait()
            add(total.at[after, low], self.ring.at[0])
            add(total.at[before, high], self.ring.at[1])
            remote(
                total.at[after], self.rows.at[0], sem.at[5], sem.at[6], axes.second(1)
            ).start()
            remote(
                total.at[before], self.rows.at[1], sem.at[5], sem.at[6], axes.second(3)
            ).start()
        elif number == 3:
            remote(self.rows, self.rows, sem.at[5], sem.at[6], axes.partner).wait()

            def body(at, carry):
                total[m2, at] = (
                    total[m2, at].astype(F32)
                    + self.rows[0, at].astype(F32)
                    + self.rows[1, at].astype(F32)
                ).astype(total.dtype)
                return carry

            lax.fori_loop(0, 4, body, 0)
            for by in (1, 3, 2):
                remote(
                    total.at[m2, shifted(m1, by)],
                    self.blocks.at[by - 1],
                    sem.at[7],
                    sem.at[8],
                    axes.first(by),
                ).start()
        elif number == 4:
            remote(self.blocks, self.blocks, sem.at[7], sem.at[8], axes.partner).wait()
            self.groups[axes.x] = (
                total[m2, m1].astype(F32)
                + self.blocks[0].astype(F32)
                + self.blocks[1].astype(F32)
                + self.blocks[2].astype(F32)
            ).astype(total.dtype)
            mine = self.groups.at[axes.x]
            for by in (1, 3, 2):
                remote(
                    mine,
                    mine,
                    sem.at[9],
                    sem.at[10],
                    device(shifted(axes.x, by), axes.z, axes.y, axes.core),
                ).start()
        elif number == 5:
            three = self.groups.at[pl.ds(0, 3)]
            remote(three, three, sem.at[9], sem.at[10], axes.partner).wait()
            summed = self.groups[0].astype(F32)
            for at in range(1, 4):
                summed = summed + self.groups[at].astype(F32)
            self.finish(0, summed)
        else:
            self.finish(1, None)


STAGES = 7
SCATTER_SEMAPHORES = 13
PARTS = {
    "q": (True, 48, 384, BF),
    "k": (False, 48, 384, BF),
    "v": (True, 48, 384, BF),
    "o": (False, 48, 384, BF),
    "gate": (True, 48, 1024, BF),
    "up": (False, 48, 1024, BF),
    "left": (True, 64, 384, BF),
    "right": (False, 64, 384, BF),
    "gains": (False, 8, 128, F32),
}
SOURCE = {
    "q": "qkv", "k": "qkv", "v": "qkv", "o": "out", "gate": "gate_up", "up": "gate_up",
    "left": "down", "right": "down", "gains": "gains",
}
SUMS = {
    "qkv": ((3, 24, 768), F32),
    "out": ((24, 768), F32),
    "gate_up": ((2, 24, 2048), F32),
    "down": ((64, 768), F32),
    "gains": ((8, 128), F32),
}
LEFT, RIGHT = pl.ds(0, 384), pl.ds(384, 384)


def part_view(part, ref):
    def view(z, y, which):
        if part in ("q", "k", "v"):
            return ref.at["qkv".index(part), z, y, :, halves(which, 768)]
        if part == "o":
            return ref.at[z, y, :, halves(which, 768)]
        if part in ("gate", "up"):
            return ref.at[int(part == "up"), z, y, :, halves(which, 2048)]
        if part == "gains":
            return ref.at[z, y, which]
        return ref.at[z, y, which, :, LEFT if part == "left" else RIGHT]

    return view


def part_target(part, ref):
    if part in ("q", "k", "v"):
        return ref.at["qkv".index(part)]
    if part in ("gate", "up"):
        return ref.at[int(part == "up")]
    if part in ("left", "right"):
        return ref.at[:, LEFT if part == "left" else RIGHT]
    return ref


def rows_swapped(target, mine, theirs, sem):
    axes = Axes(True)
    core = axes.core

    def finish(part, summed):
        own_rows = pl.ds(pl.multiple_of(core * 24, 8), 24)
        other_rows = pl.ds(pl.multiple_of((1 - core) * 24, 8), 24)
        copy = remote(mine.at[other_rows, :], theirs, sem.at[11], sem.at[12], axes.partner)
        if part == 0:
            mine[...] = summed
            copy.start()
        else:
            copy.wait()
            kept = mine[own_rows, :]
            got = theirs[...]
            width = kept.shape[-1]
            target[:, :width] = jnp.where(core == 0, kept, got)
            target[:, width:] = jnp.where(core == 0, got, kept)

    return finish


def direct(target):
    def finish(part, summed):
        if part == 0:
            target[...] = summed

    return finish


def scatter_sources(chunks):
    found = []
    for chunk in chunks:
        for part, layer in chunk:
            if (SOURCE[part], layer) not in found:
                found.append((SOURCE[part], layer))
    return found


def scatter_scratch(chunks):
    scratch = []
    for chunk in chunks:
        for part, _ in chunk:
            _, rows, width, kind = PARTS[part]
            scratch += [
                pltpu.VMEM((4, 4, rows, width), kind),
                pltpu.VMEM((4, 4, rows, width), kind),
                pltpu.VMEM((2, 2, rows, width), kind),
                pltpu.VMEM((2, 4, rows, width), kind),
                pltpu.VMEM((3, rows, width), kind),
                pltpu.VMEM((4, rows, width), kind),
                pltpu.VMEM((48, width), F32),
                pltpu.VMEM((24, width), F32),
            ]
    count = sum(len(chunk) for chunk in chunks)
    return scratch + [pltpu.SemaphoreType.DMA((count, SCATTER_SEMAPHORES))]


def scatter_steps(chunks, grads, sums, scratch):
    sources = scatter_sources(chunks)
    sems = scratch[-1]
    at = 0
    built = []
    for chunk in chunks:
        built.append([])
        for part, layer in chunk:
            place = sources.index((SOURCE[part], layer))
            buffers = scratch[8 * at : 8 * at + 8]
            target = part_target(part, sums[place])
            if PARTS[part][1] == 48:
                finish = rows_swapped(target, buffers[6], buffers[7], sems.at[at])
            else:
                finish = direct(target)
            view = part_view(part, grads[place])
            built[-1].append(
                ScatterSegment(PARTS[part][0], view, buffers[:6], sems.at[at], finish)
            )
            at += 1
    return pipeline(built, STAGES)


def scatter_shapes(chunks):
    return [jax.ShapeDtypeStruct(*SUMS[name]) for name, _ in scatter_sources(chunks)]


def split_gradients(name, gradient):
    return gradient.reshape((4, 4, 2, 8, 128) if name == "gains" else WEIGHTS[name][0])


def scatter_kernel(chunks, *refs):
    count = len(scatter_sources(chunks))
    greet(plane() + groups())
    for step in scatter_steps(chunks, refs[:count], refs[count : 2 * count], refs[2 * count :]):
        step()


def scatter_gradients(chunks, grads):
    sources = scatter_sources(chunks)
    results = pl.pallas_call(
        functools.partial(scatter_kernel, chunks),
        out_shape=scatter_shapes(chunks),
        in_specs=[ANY] * len(sources),
        out_specs=[VMEM] * len(sources),
        scratch_shapes=scatter_scratch(chunks),
        compiler_params=params(2),
        name="scatter_gradients",
    )(*[split_gradients(key[0], grads[key]) for key in sources])
    return dict(zip(sources, results))


def pair_device(pair):
    if pair < 16:
        return 2 * pair
    z = (pair - 16) // 2
    return 2 * (4 * z + 2 * ((pair - 16) % 2) + z % 2) + 1


def own_pair():
    _, z, y, core = coordinates()
    has_pair = (core == 0) | (lax.rem(z + y, 2) == 0)
    pair = jnp.where(core == 0, 4 * z + y, 16 + 2 * z + lax.div(y, 2))
    return has_pair, pair


def lanes(shape):
    return lax.broadcasted_iota(jnp.int32, shape, len(shape) - 1)


def turned(values, cosine, sine):
    here = lax.rem(lanes(values.shape), 64) < 32
    width = values.shape[-1]
    other = jnp.where(here, pltpu.roll(values, width - 32, 1), pltpu.roll(values, 32, 1))
    return values * cosine + other * sine


def twice(table):
    return jnp.concatenate([table, table], axis=0)


def allowed_keys(first_key, first_query, keys, queries, length):
    key = first_key + lax.broadcasted_iota(jnp.int32, (keys, queries), 0)
    query = first_query + lax.broadcasted_iota(jnp.int32, (keys, queries), 1)
    return (key <= query) & (key < length)


def slot_length(lengths, pair):
    return jnp.where(pair < HEADS, lengths[0], lengths[1])


LAST_DIMS = (((1,), (1,)), ((), ()))
BLOCKS = LENGTH // BLOCK
MESSAGE = 96


def front_lanes(rows):
    return lanes((rows, 128)) < 64


def pack_heads(both):
    front = front_lanes(32)
    top, bottom = both[0:32], both[32:64]
    return (
        jnp.where(front, top, pltpu.roll(bottom, 64, 1)).astype(BF),
        jnp.where(front, pltpu.roll(top, 64, 1), bottom).astype(BF),
    )


def unpack_heads(first, second):
    front = front_lanes(32)
    first, second = first.astype(F32), second.astype(F32)
    return jnp.concatenate(
        [
            jnp.where(front, first, pltpu.roll(second, 64, 1)),
            jnp.where(front, pltpu.roll(first, 64, 1), second),
        ],
        axis=0,
    )


def unpack_block(packed, to_front):
    packed = packed.astype(F32).reshape(128, 128)
    other = pltpu.roll(packed, 64, 1)
    front = front_lanes(128)
    if to_front:
        top, bottom = jnp.where(front, packed, 0.0), jnp.where(front, other, 0.0)
    else:
        top, bottom = jnp.where(front, 0.0, other), jnp.where(front, 0.0, packed)
    joined = jnp.concatenate([top.reshape(4, 32, 128), bottom.reshape(4, 32, 128)], axis=1)
    return joined.reshape(256, 128).astype(BF)


def pack_turned(turned_values):
    rows = jnp.concatenate([turned_values, turned_values], axis=0).T.reshape(4, 64, 128)
    front = lanes((4, 32, 128)) < 64
    return jnp.where(front, rows[:, 0:32], rows[:, 32:64]).astype(BF)


class Exchange:
    def __init__(self, semaphores):
        self.x, self.me = lax.axis_index("batch"), lax.axis_index("seq")
        self.has_pair, self.pair = own_pair()
        self.send, self.receive, self.local = (semaphores.at[at] for at in range(3))

    def to(self, there, source, target):
        @pl.when(self.me != there)
        def _():
            remote(source, target, self.send, self.receive, (self.x, there)).start()

        @pl.when(self.me == there)
        def _():
            pltpu.make_async_copy(source, target, self.local).start()

    def wait(self, sent, got, where):
        if where == "pairs":
            sends, gets = (sent.shape[0], sent.shape[0] - 1), (None, got.shape[0] - 1)
        else:
            sends, gets = (None, sent.shape[0] - 1), (got.shape[0], got.shape[0] - 1)

        def wait_for(n_sent, n_got):
            if n_got is not None:
                part = got.at[pl.ds(0, n_got)]
                remote(part, part, self.send, self.receive, (self.x, self.me)).wait_recv()
            if n_sent is not None:
                part = sent.at[pl.ds(0, n_sent)]
                remote(part, part, self.send, self.receive, (self.x, self.me)).wait_send()

        @pl.when(self.has_pair)
        def _():
            pltpu.make_async_copy(sent.at[0], got.at[0], self.local).wait()
            wait_for(sends[1], gets[1])

        @pl.when(jnp.logical_not(self.has_pair))
        def _():
            wait_for(sends[0], gets[0])


def send_projections(exchange, query, key, value, cosine, sine, outgoing, rows):
    cosine, sine = twice(cosine), twice(sine)
    front = front_lanes(64)
    for tile in range(6):
        cut = slice(128 * tile, 128 * tile + 128)
        q = turned(query[:, cut], cosine, sine) * (1.0 / math.sqrt(HEAD_DIM))
        k = turned(key[:, cut], cosine, sine)
        v = value[:, cut]
        for slot in range(2):
            span = slice(64 * slot, 64 * slot + 64)
            at = slot * HEADS + 2 * tile
            ks, vs = k[span], v[span]
            outgoing[at, 0:64] = jnp.where(front, ks, pltpu.roll(vs, 64, 1)).astype(BF)
            outgoing[at + 1, 0:64] = jnp.where(front, pltpu.roll(ks, 64, 1), vs).astype(BF)
            outgoing[at, 64:96], outgoing[at + 1, 64:96] = pack_heads(q[span])
    for pair in range(PAIRS):
        exchange.to(pair_device(pair), outgoing.at[pair], rows.at[exchange.me])


def attend_block(exchange, at, length, rows, values_turned, out_turned, log_total, outgoing, incoming):
    count = (at + 1) * BLOCK
    queries = unpack_block(rows[4 * at : 4 * at + 4, 64:96], True)
    keys = rows[0 : 4 * at + 4, 0:64].reshape(count, 128)
    scores = lax.dot_general(keys, queries, LAST_DIMS, preferred_element_type=F32)
    scores = jnp.where(allowed_keys(0, at * BLOCK, count, BLOCK, length), scores, MASKED)
    highest = jnp.max(scores, axis=0, keepdims=True)
    raised = jnp.exp(scores - highest)
    total = jnp.sum(raised, axis=0, keepdims=True)
    result = (
        jnp.dot(values_turned[:, 0:count], raised.astype(BF), preferred_element_type=F32) / total
    )
    cut = slice(at * BLOCK, count)
    out_turned[:, cut] = result
    log_total[:, cut] = jnp.broadcast_to(highest + jnp.log(total), (8, BLOCK))
    outgoing[4 * at : 4 * at + 4] = pack_turned(result)
    for there in range(4 * at, 4 * at + 4):
        exchange.to(there, outgoing.at[there], incoming.at[exchange.pair])


def merge_heads(incoming, merged):
    for slot in range(2):
        for tile in range(6):
            at = slot * HEADS + 2 * tile
            merged[64 * slot : 64 * slot + 64, 128 * tile : 128 * tile + 128] = unpack_heads(
                incoming[at], incoming[at + 1]
            ).astype(BF)


def norm_forward(values, norm_gain):
    inverse = lax.rsqrt(jnp.mean(values * values, axis=-1, keepdims=True) + EPSILON)
    return (values * inverse * norm_gain, inverse)


def feed_forward(rows_in, gate_up, down, paired):
    fed = jnp.zeros((128, 768), F32)
    for z in range(4):
        cut = slice(512 * z, 512 * z + 512)
        gate = jnp.dot(rows_in, gate_up[0, :, :, :, cut].reshape(768, 512), preferred_element_type=F32)
        up = jnp.dot(rows_in, gate_up[1, :, :, :, cut].reshape(768, 512), preferred_element_type=F32)
        paired[0, :, cut] = gate
        paired[1, :, cut] = up
        hidden = (jax.nn.silu(gate) * up).astype(BF)
        fed = fed + jnp.dot(hidden, down[z].reshape(512, 768), preferred_element_type=F32)
    return fed


KEPT = (
    [("result", (128, 768), F32), ("residual_0", (128, 768), F32), ("summed_0", (128, 768), F32)]
    + [("residual_1", (128, 768), F32), ("gains", (8, 768), F32)]
    + [
        (name + "_" + layer, shape, kind)
        for layer in "01"
        for name, shape, kind in (
            ("paired", (2, 128, 2048), F32),
            ("rows", (32, MESSAGE, 128), BF),
            ("merged", (128, 768), BF),
            ("out_turned", (64, LENGTH), F32),
            ("log_total", (8, LENGTH), F32),
        )
    ]
)


def forward_kernel(lengths, qkv, out, gate_up, down, gains, stream, cosine, sine, *refs):
    stored = dict(zip(GATHERED[:-1], refs[:8]))
    kept = {name: ref for (name, _, _), ref in zip(KEPT, refs[8:])}
    refs = refs[8 + len(KEPT) :]
    store, refs = dict(zip(GATHERED, refs[:9])), refs[9:]
    their_qkv, their_out, their_gate_up, b_qkv, b_out, b_gate_up, b_down = refs[:7]
    outgoing, places, incoming, values_turned, swap, sems, local, pair_sems = refs[7:]
    axes = Axes(True)
    core = axes.core
    x, me = lax.axis_index("batch"), lax.axis_index("seq")
    greet([(x, lax.rem(me + by, 32)) for by in range(1, 32)])
    swaps = [
        remote(mine, theirs, swap.at[0, at], swap.at[1, at], axes.partner)
        for at, (mine, theirs) in enumerate(
            (
                (qkv.at[0], their_qkv.at[0]),
                (qkv.at[1], their_qkv.at[1]),
                (out, their_out),
                (gate_up, their_gate_up),
            )
        )
    ]
    for copy in swaps:
        copy.start()

    def joined(mine, theirs):
        upper = jnp.where(core == 0, mine, theirs)
        lower = jnp.where(core == 0, theirs, mine)
        return jnp.concatenate([upper, lower], axis=0).astype(BF)

    segments = {}
    at = 0
    for key in GATHERED:
        name, layer = key
        block = {"qkv": b_qkv, "out": b_out, "gate_up": b_gate_up, "down": b_down}.get(name)
        owns = own_views(name, gains if block is None else block.at[layer])
        segments[key] = []
        for (first_is_y, view), own in zip(weight_views(name, store[key]), owns):
            segments[key].append(GatherSegment(first_is_y, view, sems.at[at], own))
            at += 1

    def each(keys, act):
        for key in keys:
            for segment in segments[key]:
                act(segment)

    def keep(*keys):
        each(keys, lambda segment: segment.keep().start())
        each(keys, lambda segment: segment.keep().wait())

    def begin(phase, *keys):
        each(keys, lambda segment: segment.begin(phase))

    def end(phase, *keys):
        each(keys, lambda segment: segment.end(phase))

    saves = []

    def save(*keys):
        for key in keys:
            copy = pltpu.make_async_copy(store[key], stored[key], local.at[len(saves)])
            copy.start()
            saves.append(copy)

    qkv_0, out_0, wide_0, down_0 = GATHERED[0:4]
    qkv_1, out_1, wide_1, down_1 = GATHERED[4:8]
    gains_0 = GATHERED[8]

    swaps[0].wait()
    for at in range(3):
        b_qkv[0, at] = joined(qkv[0, at], their_qkv[0, at])
    begin(0, qkv_0)
    keep(qkv_0)
    for copy in swaps[1:]:
        copy.wait()
    for at in range(2):
        b_gate_up[0, at] = joined(gate_up[0, at], their_gate_up[0, at])
    begin(0, wide_0)
    keep(wide_0)
    end(0, qkv_0)
    begin(1, qkv_0)
    b_down[0] = down[0].astype(BF)
    b_out[0] = joined(out[0], their_out[0])
    begin(0, out_0, down_0, gains_0)
    keep(out_0, down_0, gains_0)
    for at in range(3):
        b_qkv[1, at] = joined(qkv[1, at], their_qkv[1, at])
    b_out[1] = joined(out[1], their_out[1])
    for at in range(2):
        b_gate_up[1, at] = joined(gate_up[1, at], their_gate_up[1, at])
    b_down[1] = down[1].astype(BF)
    end(1, qkv_0)
    begin(2, qkv_0)
    end(0, wide_0)
    begin(1, wide_0)
    end(2, qkv_0)
    begin(3, qkv_0)
    keep(qkv_1, out_1, wide_1, down_1)
    end(3, qkv_0)
    save(qkv_0)

    def attention(layer, source, before, between):
        weights = store["qkv", layer]
        name = "_" + str(layer)
        rows, merged = kept["rows" + name], kept["merged" + name]
        there = Exchange(pair_sems.at[2 * layer])
        back = Exchange(pair_sems.at[2 * layer + 1])
        low = source.astype(BF)
        query, key, value = (
            jnp.dot(low, weights[at].reshape(768, 768), preferred_element_type=F32)
            for at in range(3)
        )
        send_projections(
            there, query, key, value, cosine[...], sine[...], outgoing.at[layer], rows
        )
        before()
        there.wait(outgoing.at[layer], rows, "pairs")
        length = slot_length(lengths, there.pair)

        @pl.when(there.has_pair)
        def _():
            all_rows = rows[:, 0:64].reshape(LENGTH, 128).astype(F32)
            values_turned[...] = all_rows.T[64:128].astype(BF)

        for at in range(BLOCKS):

            @pl.when(there.has_pair)
            def _(at=at):
                attend_block(
                    back,
                    at,
                    length,
                    rows,
                    values_turned,
                    kept["out_turned" + name],
                    kept["log_total" + name],
                    places.at[layer],
                    incoming.at[layer],
                )

            if at in between:
                between[at]()
        back.wait(places.at[layer], incoming.at[layer], "places")
        merge_heads(incoming.at[layer], merged)
        between["after"]()
        out_matrix = store["out", layer][...].reshape(768, 768)
        return jnp.dot(merged[...], out_matrix, preferred_element_type=F32)

    def before_0():
        end(0, out_0, down_0, gains_0)
        begin(1, out_0, down_0, gains_0)

    def within_0():
        end(1, wide_0)
        begin(2, wide_0)
        begin(0, qkv_1)

    def later_0():
        end(1, out_0, down_0, gains_0)
        begin(2, out_0, down_0, gains_0)

    def last_0():
        end(0, qkv_1)
        begin(1, qkv_1)

    def after_0():
        end(2, wide_0, out_0, down_0, gains_0)
        begin(3, out_0, wide_0, down_0, gains_0)
        begin(0, wide_1)
        end(3, out_0, wide_0, down_0, gains_0)
        save(out_0, wide_0, down_0)
        for device_at in range(32):
            piece = store[gains_0][device_at // 8, device_at // 2 % 4, device_at % 2]
            first = 24 * device_at // 128
            if device_at == 0:
                kept["gains"][...] = jnp.zeros((8, 768), F32)
            width = min(256, 768 - 128 * first)
            kept["gains"][:, 128 * first : 128 * first + width] += piece[:, :width]

    def gain(at):
        return kept["gains"][at : at + 1, :]

    mixed = attention(
        0, stream[...], before_0, {1: within_0, 4: later_0, 7: last_0, "after": after_0}
    )
    residual = stream[...] + mixed
    kept["residual_0"][...] = residual
    middle, _ = norm_forward(residual, gain(0))
    end(1, qkv_1)
    begin(2, qkv_1)
    begin(0, out_1, down_1)
    fed = feed_forward(middle.astype(BF), store[wide_0], store[down_0], kept["paired_0"])
    end(2, qkv_1)
    begin(3, qkv_1)
    end(0, wide_1)
    begin(1, wide_1)
    summed = middle + fed
    kept["summed_0"][...] = summed
    shallow, _ = norm_forward(summed, gain(1))
    normed, _ = norm_forward(shallow, gain(2))
    end(3, qkv_1)
    save(qkv_1)

    def before_1():
        end(0, out_1, down_1)
        begin(1, out_1, down_1)

    def within_1():
        end(1, wide_1)
        begin(2, wide_1)

    def later_1():
        end(1, out_1, down_1)
        begin(2, out_1, down_1)

    def after_1():
        end(2, wide_1, out_1, down_1)
        begin(3, out_1, wide_1, down_1)
        end(3, out_1, wide_1, down_1)
        save(out_1, wide_1, down_1)

    mixed = attention(1, normed, before_1, {1: within_1, 4: later_1, "after": after_1})
    residual = shallow + mixed
    kept["residual_1"][...] = residual
    normed_two, _ = norm_forward(residual, gain(3))
    fed = feed_forward(normed_two.astype(BF), store[wide_1], store[down_1], kept["paired_1"])
    kept["result"][...] = residual + fed
    for copy in saves:
        copy.wait()


def run_forward(lengths, qkv, out, gate_up, down, gains, stream, cosine, sine):
    count = sum(SEGMENTS[name] for name, _ in GATHERED)
    stored = GATHERED[:-1]
    results = pl.pallas_call(
        forward_kernel,
        out_shape=[weight_shape(key) for key in stored]
        + [jax.ShapeDtypeStruct(shape, kind) for _, shape, kind in KEPT],
        in_specs=[SMEM] + [VMEM] * 8,
        out_specs=[ANY] * 8 + [VMEM] * len(KEPT),
        scratch_shapes=[pltpu.VMEM(*WEIGHTS[name]) for name, _ in GATHERED]
        + [
            pltpu.VMEM((2, 3, 24, 768), F32),
            pltpu.VMEM((2, 24, 768), F32),
            pltpu.VMEM((2, 2, 24, 2048), F32),
            pltpu.VMEM((2, 3, 48, 768), BF),
            pltpu.VMEM((2, 48, 768), BF),
            pltpu.VMEM((2, 2, 48, 2048), BF),
            pltpu.VMEM((2, 64, 768), BF),
            pltpu.VMEM((2, PAIRS, MESSAGE, 128), BF),
            pltpu.VMEM((2, 32, 32, 128), BF),
            pltpu.VMEM((2, PAIRS, 32, 128), BF),
            pltpu.VMEM((64, LENGTH), BF),
            pltpu.SemaphoreType.DMA((2, 4)),
            pltpu.SemaphoreType.DMA((count, 4, 4)),
            pltpu.SemaphoreType.DMA((8,)),
            pltpu.SemaphoreType.DMA((4, 3)),
        ],
        compiler_params=params(1),
        name="forward",
    )(lengths, qkv, out, gate_up, down, gains, stream, cosine, sine)
    return dict(zip(stored, results)), {
        name: result for (name, _, _), result in zip(KEPT, results[8:])
    }


def flat_weights(store, layer):
    shapes = {"qkv": (3, 768, 768), "out": (768, 768), "gate_up": (2, 768, 2048), "down": (2048, 768)}
    return {name: store[name, layer].reshape(shape) for name, shape in shapes.items()}


def attend_back_kernel(
    lengths, grad, rows, out_turned, log_total, cosine, sine, result, *refs
):
    out_grad, keys_turned, key_grad, to_pairs, to_places, incoming, sems = refs
    there, back = Exchange(sems.at[0]), Exchange(sems.at[1])
    x, me, has_pair = there.x, there.me, there.has_pair
    barrier = pltpu.get_barrier_semaphore()
    places = [pair_device(other) for other in range(PAIRS)]
    for device_at in places:

        @pl.when(me != device_at)
        def _(device_at=device_at):
            pl.semaphore_signal(barrier, inc=1, device_id=(x, device_at), device_id_type=MESH)

    @pl.when(has_pair)
    def _():
        for device_at in range(32):
            if device_at not in places:
                pl.semaphore_signal(barrier, inc=1, device_id=(x, device_at), device_id_type=MESH)

    for slot in range(2):
        for tile in range(6):
            both = grad[64 * slot : 64 * slot + 64, 128 * tile : 128 * tile + 128].astype(F32)
            at = slot * HEADS + 2 * tile
            to_pairs[at], to_pairs[at + 1] = pack_heads(both)

    pl.semaphore_wait(barrier, jnp.where(has_pair, 31, PAIRS))
    for pair in range(PAIRS):
        there.to(pair_device(pair), to_pairs.at[pair], out_grad.at[me])
    length = slot_length(lengths, there.pair)

    @pl.when(has_pair)
    def _():
        all_rows = rows[:, 0:64].reshape(LENGTH, 128).astype(F32)
        keys_turned[...] = all_rows.T[0:64].astype(BF)
        key_grad[...] = jnp.zeros_like(key_grad)

    there.wait(to_pairs, out_grad, "pairs")
    for at in reversed(range(BLOCKS)):

        @pl.when(has_pair)
        def _(at=at):
            attend_back_block(
                back, at, length, rows, out_grad, out_turned, log_total, keys_turned, key_grad, to_places, incoming
            )

    back.wait(to_places, incoming, "places")
    collect_projections(incoming, cosine[...], sine[...], result)


def attend_back_block(
    exchange, at, length, rows, out_grad, out_turned, log_total, keys_turned, key_grad, outgoing, incoming
):
    cut = slice(at * BLOCK, (at + 1) * BLOCK)
    four = slice(4 * at, 4 * at + 4)
    queries = unpack_block(rows[four, 64:96], True)
    outs = unpack_block(out_grad[four], False)
    outs_turned = outs.astype(F32).T[64:128]
    delta = jnp.sum(outs_turned * out_turned[:, cut], axis=0, keepdims=True)
    shift = log_total[0:1, cut]
    query_grad = jnp.zeros((64, BLOCK), F32)
    for part in range(at + 1):
        span = slice(part * BLOCK, (part + 1) * BLOCK)
        keys = rows[4 * part : 4 * part + 4, 0:64].reshape(BLOCK, 128)
        scores = lax.dot_general(keys, queries, LAST_DIMS, preferred_element_type=F32)
        allowed = allowed_keys(part * BLOCK, at * BLOCK, BLOCK, BLOCK, length)
        probs = jnp.where(allowed, jnp.exp(scores - shift), 0.0)
        probs_grad = lax.dot_general(keys, outs, LAST_DIMS, preferred_element_type=F32)
        score_grad = (probs * (probs_grad - delta)).astype(BF)
        key_grad[span, :] += jnp.dot(score_grad, queries, preferred_element_type=F32) + jnp.dot(
            probs.astype(BF), outs, preferred_element_type=F32
        )
        query_grad += jnp.dot(keys_turned[:, span], score_grad, preferred_element_type=F32)
    outgoing[four, 0:64] = key_grad[cut, :].reshape(4, SPAN, 128).astype(BF)
    outgoing[four, 64:96] = pack_turned(query_grad)
    for there in range(4 * at, 4 * at + 4):
        exchange.to(there, outgoing.at[there], incoming.at[exchange.pair])


def collect_projections(incoming, cosine, sine, result):
    front = front_lanes(64)
    for slot in range(2):
        span = slice(64 * slot, 64 * slot + 64)
        for tile in range(6):
            cut = slice(128 * tile, 128 * tile + 128)
            at = slot * HEADS + 2 * tile
            first, second = (incoming[at + n, 0:64].astype(F32) for n in (0, 1))
            q = unpack_heads(incoming[at, 64:96], incoming[at + 1, 64:96])
            k = jnp.where(front, first, pltpu.roll(second, 64, 1))
            v = jnp.where(front, pltpu.roll(first, 64, 1), second)
            q = turned(q * (1.0 / math.sqrt(HEAD_DIM)), cosine, -sine)
            result[0, span, cut] = q.astype(BF)
            result[1, span, cut] = turned(k, cosine, -sine).astype(BF)
            result[2, span, cut] = v.astype(BF)


def attend_back(lengths, grad, rows, out_turned, log_total, cosine, sine):
    return pl.pallas_call(
        attend_back_kernel,
        out_shape=jax.ShapeDtypeStruct((3, 128, 768), BF),
        in_specs=[SMEM] + [VMEM] * 6,
        out_specs=VMEM,
        scratch_shapes=[
            pltpu.VMEM((32, 32, 128), BF),
            pltpu.VMEM((64, LENGTH), BF),
            pltpu.VMEM((LENGTH, 128), F32),
            pltpu.VMEM((PAIRS, 32, 128), BF),
            pltpu.VMEM((32, MESSAGE, 128), BF),
            pltpu.VMEM((PAIRS, MESSAGE, 128), BF),
            pltpu.SemaphoreType.DMA((2, 3)),
        ],
        compiler_params=params(5),
        name="attend_back",
    )(lengths, grad, rows, out_turned, log_total, cosine, sine)


def angles(places):
    half_dim = HEAD_DIM // 2
    frequency = jnp.exp(-math.log(10000.0) * jnp.arange(half_dim).astype(F32) / half_dim)
    phases = places.astype(F32)[:, None] * frequency[None, :]
    cosine, sine = jnp.cos(phases), jnp.sin(phases)
    return (
        jnp.concatenate([cosine] * 4, axis=1),
        jnp.concatenate([-sine, sine] * 2, axis=1),
    )


def norm_backward(incoming, values, inverse, norm_gain):
    scaled = incoming * norm_gain
    outgoing = inverse * scaled - values * (inverse * inverse * inverse) * jnp.mean(
        scaled * values, axis=-1, keepdims=True
    )
    return (outgoing, jnp.sum(incoming * values * inverse, axis=0))


def attention_backward(incoming, source_low, kept, weights, tables, layer, grads):
    lengths, cosine, sine = tables
    name = "_" + str(layer)
    incoming_low = incoming.astype(BF)
    grads["out", layer] = jnp.einsum(
        "rd,re->de", kept["merged" + name], incoming_low, preferred_element_type=F32
    ).astype(BF)
    merged_grad = jnp.einsum(
        "re,de->rd", incoming_low, weights["out"], preferred_element_type=F32
    ).astype(BF)
    stacked = attend_back(
        lengths,
        merged_grad,
        kept["rows" + name],
        kept["out_turned" + name],
        kept["log_total" + name],
        cosine,
        sine,
    )
    grads["qkv", layer] = jnp.einsum(
        "rd,jre->jde", source_low, stacked, preferred_element_type=F32
    ).astype(BF)
    return jnp.einsum("jre,jde->rd", stacked, weights["qkv"], preferred_element_type=F32)


def ffn_backward(incoming, rows_in, paired, weights, layer, grads):
    incoming_low = incoming.astype(BF)
    gate, lifted = paired[0], paired[1]
    sigmoid = jax.nn.sigmoid(gate)
    hidden = (gate * sigmoid * lifted).astype(BF)
    grads["down", layer] = jnp.einsum(
        "rf,rd->fd", hidden, incoming_low, preferred_element_type=F32
    ).astype(BF)
    hidden_grad = jnp.einsum("rd,fd->rf", incoming_low, weights["down"], preferred_element_type=F32)
    gate_grad = hidden_grad * lifted * sigmoid * (1.0 + gate * (1.0 - sigmoid))
    lifted_grad = hidden_grad * gate * sigmoid
    stacked = jnp.stack([gate_grad, lifted_grad]).astype(BF)
    grads["gate_up", layer] = jnp.einsum(
        "rd,jrf->jdf", rows_in, stacked, preferred_element_type=F32
    ).astype(BF)
    return jnp.einsum("jrf,jdf->rd", stacked, weights["gate_up"], preferred_element_type=F32)


CHUNKS = [
    [("gate", 1), ("up", 1)],
    [("left", 1), ("right", 1)],
    [("q", 1), ("k", 1), ("v", 1), ("o", 1)],
    [("gate", 0), ("up", 0)],
    [("left", 0), ("right", 0)],
    [("q", 0), ("k", 0), ("v", 0), ("o", 0), ("gains", 0)],
]


def update(weight_matrix, moment, average, gradient, step_size):
    moment_new = MOMENTUM * moment + gradient
    weight_new = weight_matrix - step_size * (gradient + MOMENTUM * moment_new)
    return (moment_new, weight_new, AVERAGING * average + (1.0 - AVERAGING) * weight_new)


def by_slot(values):
    return values[0].transpose(1, 0, 2).reshape(128, 768)


def by_place(values):
    return values.reshape(2, SPAN, 768).transpose(1, 0, 2)[None]


def on_device(
    inputs,
    cotangent,
    lengths,
    qkv_weight,
    qkv_moment,
    qkv_average,
    out_weight,
    out_moment,
    out_average,
    gate_up_weight,
    gate_up_moment,
    gate_up_average,
    down_weight,
    down_moment,
    down_average,
    norm_gains,
    gain_moment,
    gain_average,
):
    places = lax.axis_index("seq") * SPAN + jnp.arange(SPAN)
    cosine, sine = angles(places)
    tables = (lengths[0], cosine, sine)
    seq = lax.axis_index("seq")
    own_gains = lax.dynamic_update_slice(
        jnp.zeros((8, 256), F32),
        norm_gains.astype(BF).astype(F32).reshape(4, 24),
        (0, lax.rem(24 * seq, 128)),
    )
    stream = by_slot(inputs)
    store, kept = run_forward(
        lengths[0], qkv_weight, out_weight, gate_up_weight, down_weight, own_gains, stream, cosine, sine
    )
    first, second = flat_weights(store, 0), flat_weights(store, 1)
    gains = kept["gains"]
    result = kept["result"]
    residual_0, summed_0, residual_1 = (kept[n] for n in ("residual_0", "summed_0", "residual_1"))
    middle, inverse_00 = norm_forward(residual_0, gains[0])
    shallow, inverse_01 = norm_forward(summed_0, gains[1])
    normed, inverse_10 = norm_forward(shallow, gains[2])
    normed_two, inverse_11 = norm_forward(residual_1, gains[3])
    grads = {}
    incoming = by_slot(cotangent)
    normed_grad = ffn_backward(
        incoming, normed_two.astype(BF), kept["paired_1"], second, 1, grads
    )
    through, gain_grad_11 = norm_backward(normed_grad, residual_1, inverse_11, gains[3])
    residual_grad = incoming + through
    normed_grad = attention_backward(
        residual_grad, normed.astype(BF), kept, second, tables, 1, grads
    )
    through, gain_grad_10 = norm_backward(normed_grad, shallow, inverse_10, gains[2])
    shallow_grad = residual_grad + through
    summed_grad, gain_grad_01 = norm_backward(shallow_grad, summed_0, inverse_01, gains[1])
    middle_ffn = ffn_backward(
        summed_grad, middle.astype(BF), kept["paired_0"], first, 0, grads
    )
    middle_grad = summed_grad + middle_ffn
    residual_grad, gain_grad_00 = norm_backward(middle_grad, residual_0, inverse_00, gains[0])
    source_grad = attention_backward(
        residual_grad, stream.astype(BF), kept, first, tables, 0, grads
    )
    input_grad = residual_grad + source_grad

    gain_grads = jnp.stack([gain_grad_00, gain_grad_01, gain_grad_10, gain_grad_11])
    grads["gains", 0] = jnp.pad(
        gain_grads.reshape(4, 32, 24).transpose(1, 0, 2), ((0, 0), (0, 4), (0, 104))
    )
    sums = scatter_gradients(CHUNKS, grads)
    gain_sum = sums["gains", 0][:4, :24].reshape(2, 2, 24)

    def both(name):
        return jnp.stack([sums[name, 0], sums[name, 1]])

    step_size = STEP_RATE / math.sqrt(
        lax.axis_size("batch") * SPAN * lax.axis_size("seq") * 2
    )
    qkv_new = update(qkv_weight, qkv_moment, qkv_average, both("qkv"), step_size)
    out_new = update(out_weight, out_moment, out_average, both("out"), step_size)
    gate_up_new = update(gate_up_weight, gate_up_moment, gate_up_average, both("gate_up"), step_size)
    down_new = update(down_weight, down_moment, down_average, both("down"), step_size)
    gain_new = update(norm_gains, gain_moment, gain_average, gain_sum, step_size)
    return (
        by_place(result),
        by_place(input_grad),
        *qkv_new,
        *out_new,
        *gate_up_new,
        *down_new,
        *gain_new,
    )


def solution(mesh):
    rows = P("batch", "seq", None, None)
    wide = P(None, None, "seq", None)
    flat = P(None, "seq", None)
    gains = P(None, None, "seq")
    state = (wide,) * 3 + (flat,) * 3 + (wide,) * 3 + (flat,) * 3 + (gains,) * 3
    return jax.shard_map(
        on_device,
        mesh=mesh,
        in_specs=(rows, rows, P("batch", None)) + state,
        out_specs=(rows, rows) + state,
        check_vma=False,
    )
```

```python
import functools
import math

import jax
import jax.numpy as jnp
from jax import lax
from jax.experimental import pallas as pl
from jax.experimental.pallas import tpu as pltpu
from jax.sharding import PartitionSpec as P

MESH = pl.DeviceIdType.MESH
BF = jnp.bfloat16
F32 = jnp.float32
HEAD_DIM = 64
HEADS = 12
PAIRS = 24
SPAN = 64
LENGTH = 2048
BLOCK = 256
EPSILON = 1e-06
MOMENTUM = 0.5
AVERAGING = 0.5
STEP_RATE = 0.1
MASKED = -1e30
VMEM_BYTES = 61 * 2**20
VMEM = pl.BlockSpec(memory_space=pltpu.VMEM)
ANY = pl.BlockSpec(memory_space=pl.ANY)
SMEM = pl.BlockSpec(memory_space=pltpu.SMEM)
ALL = pl.ds(0, 4)


def params(collective_id):
    return pltpu.CompilerParams(
        collective_id=collective_id, has_side_effects=True, vmem_limit_bytes=VMEM_BYTES
    )


def coordinates():
    seq = lax.axis_index("seq")
    return (
        lax.axis_index("batch"),
        lax.div(seq, 8),
        lax.rem(lax.div(seq, 2), 4),
        lax.rem(seq, 2),
    )


def device(x, z, y, core):
    return (x, (z * 4 + y) * 2 + core)


def shifted(value, by):
    return lax.rem(value + by, 4)


def signal(partners):
    barrier = pltpu.get_barrier_semaphore()
    for partner in partners:
        pl.semaphore_signal(barrier, inc=1, device_id=partner, device_id_type=MESH)


def greet(partners):
    signal(partners)
    pl.semaphore_wait(pltpu.get_barrier_semaphore(), len(partners))


def remote(source, target, send, receive, where):
    return pltpu.make_async_remote_copy(
        src_ref=source,
        dst_ref=target,
        send_sem=send,
        recv_sem=receive,
        device_id=where,
        device_id_type=MESH,
    )


class Axes:
    def __init__(self, first_is_y):
        x, z, y, core = coordinates()
        self.first_is_y = first_is_y
        self.x, self.z, self.y, self.core = x, z, y, core
        self.m1, self.m2 = (y, z) if first_is_y else (z, y)
        self.partner = device(x, z, y, 1 - core)

    def along_y(self, by):
        return device(self.x, self.z, shifted(self.y, by), self.core)

    def along_z(self, by):
        return device(self.x, shifted(self.z, by), self.y, self.core)

    def first(self, by):
        return self.along_y(by) if self.first_is_y else self.along_z(by)

    def second(self, by):
        return self.along_z(by) if self.first_is_y else self.along_y(by)

    def order(self, i1, i2):
        return (i2, i1) if self.first_is_y else (i1, i2)


class GatherSegment:
    def __init__(self, first_is_y, view, semaphores, own=None):
        self.axes = Axes(first_is_y)
        self.view, self.own, self.semaphores = view, own, semaphores

    def block(self, i1, i2):
        return self.view(*self.axes.order(i1, i2))

    def row(self, by, part=ALL):
        return self.block(part, shifted(self.axes.m2, by))

    def keep(self):
        here = self.block(self.axes.m1, self.axes.m2)
        return pltpu.make_async_copy(self.own, here, self.semaphores.at[3, 0])

    def begin(self, phase):
        axes = self.axes
        sem = [self.semaphores.at[phase, at] for at in range(4)]

        def send(part, where):
            remote(part, part, sem[0], sem[1], where).start()

        def share(part):
            remote(part, part, sem[2], sem[3], axes.partner).start()

        if phase == 0:
            here = self.block(axes.m1, axes.m2)
            source = here if self.own is None else self.own
            for by in (1, 3, 2):
                remote(source, here, sem[0], sem[1], axes.first(by)).start()
        elif phase == 1:
            send(self.row(0), axes.second(1))
            send(self.row(0), axes.second(3))
            share(self.row(0))
        elif phase == 2:
            send(self.row(3, pl.ds(0, 2)), axes.second(1))
            send(self.row(1, pl.ds(2, 2)), axes.second(3))
            share(self.row(3))
            share(self.row(1))
        else:
            share(self.row(2))

    def end(self, phase):
        axes = self.axes
        sem = [self.semaphores.at[phase, at] for at in range(4)]
        one, two = self.row(0), self.block(ALL, pl.ds(0, 2))
        moved = (self.block(pl.ds(0, 3), axes.m2), two, one, None)[phase]
        shared = (None, one, two, one)[phase]
        if moved is not None:
            remote(moved, moved, sem[0], sem[1], axes.partner).wait()
        if shared is not None:
            remote(shared, shared, sem[2], sem[3], axes.partner).wait()


class AcrossSegment(GatherSegment):
    def __init__(self, first_is_y, quarters, semaphores, own):
        x = lax.axis_index("batch")
        super().__init__(first_is_y, lambda z, y: quarters(z, y, x, 1), semaphores, own)
        self.quarters = quarters

    def begin(self, phase):
        axes = self.axes
        sem = [self.semaphores.at[phase, at] for at in range(4)]

        def send(part, where):
            remote(part, part, sem[0], sem[1], where).start()

        def share(part):
            remote(part, part, sem[2], sem[3], axes.partner).start()

        if phase == 0:
            here = self.block(axes.m1, axes.m2)
            for by in (1, 3, 2):
                remote(self.own, here, sem[0], sem[1], axes.first(by)).start()
        elif phase == 1:
            send(self.row(0), axes.second(1))
            send(self.row(0), axes.second(3))
        elif phase == 2:
            send(self.row(3, pl.ds(0, 2)), axes.second(1))
            send(self.row(1, pl.ds(2, 2)), axes.second(3))
        elif phase == 3:
            mine = self.block(ALL, ALL)
            for by in (1, 3, 2):
                send(mine, device(shifted(axes.x, by), axes.z, axes.y, axes.core))
            share(mine)
        else:
            for by in (1, 3, 2):
                share(self.quarters(ALL, ALL, shifted(axes.x, by), 1))

    def end(self, phase):
        axes = self.axes
        sem = [self.semaphores.at[phase, at] for at in range(4)]
        three = self.quarters(ALL, ALL, 0, 3)
        mine = self.block(ALL, ALL)
        moved = (
            self.block(pl.ds(0, 3), axes.m2),
            self.block(ALL, pl.ds(0, 2)),
            self.row(0),
            three,
            None,
        )[phase]
        shared = (None, None, None, mine, three)[phase]
        if moved is not None:
            remote(moved, moved, sem[0], sem[1], axes.partner).wait()
        if shared is not None:
            remote(shared, shared, sem[2], sem[3], axes.partner).wait()


def across_views(name, ref):
    core = Axes(True).core

    def columns(first, count):
        return pl.ds(pl.multiple_of(core * 1024 + first * 256, 128), 256 * count)

    def rows(first, count):
        return pl.ds(pl.multiple_of(first * 16, 16), 16 * count)

    if name == "wide":
        return [
            (True, lambda z, y, first, count: ref.at[0, z, y, :, columns(first, count)]),
            (False, lambda z, y, first, count: ref.at[1, z, y, :, columns(first, count)]),
        ]
    return [
        (True, lambda z, y, first, count: ref.at[z, y, core, rows(first, count), pl.ds(0, 384)]),
        (False, lambda z, y, first, count: ref.at[z, y, core, rows(first, count), pl.ds(384, 384)]),
    ]


def across_owns(name, ref):
    axes = Axes(True)
    if name == "wide":
        columns = pl.ds(pl.multiple_of(axes.core * 1024 + axes.x * 256, 128), 256)
        return [ref.at[0, :, columns], ref.at[1, :, columns]]
    rows = pl.ds(pl.multiple_of(axes.x * 16, 16), 16)
    return [ref.at[rows, pl.ds(0, 384)], ref.at[rows, pl.ds(384, 384)]]


ACROSS = (("wide", 1), ("down", 0))


def halves(core, width):
    return pl.ds(pl.multiple_of(core * (width // 2), 128), width // 2)


def weight_views(name, ref):
    core = Axes(True).core
    narrow, wide = halves(core, 768), halves(core, 2048)
    if name == "qkv":
        return [
            (True, lambda z, y: ref.at[pl.ds(0, 2), z, y, :, narrow]),
            (False, lambda z, y: ref.at[2, z, y, :, narrow]),
        ]
    if name == "out":
        return [(False, lambda z, y: ref.at[z, y, :, narrow])]
    if name == "wide":
        return [
            (True, lambda z, y: ref.at[0, z, y, :, wide]),
            (False, lambda z, y: ref.at[1, z, y, :, wide]),
        ]
    if name == "down":
        return [
            (True, lambda z, y: ref.at[z, y, core, :, pl.ds(0, 384)]),
            (False, lambda z, y: ref.at[z, y, core, :, pl.ds(384, 384)]),
        ]
    return [(True, lambda z, y: ref.at[z, y, core])]


def own_views(name, ref):
    core = Axes(True).core
    narrow, wide = halves(core, 768), halves(core, 2048)
    if name == "qkv":
        return [ref.at[pl.ds(0, 2), :, narrow], ref.at[2, :, narrow]]
    if name == "out":
        return [ref.at[:, narrow]]
    if name == "wide":
        return [ref.at[0, :, wide], ref.at[1, :, wide]]
    if name == "down":
        return [ref.at[:, pl.ds(0, 384)], ref.at[:, pl.ds(384, 384)]]
    return [ref]


WEIGHTS = {
    "qkv": ((3, 4, 4, 48, 768), BF),
    "out": ((4, 4, 48, 768), BF),
    "wide": ((2, 4, 4, 48, 2048), BF),
    "down": ((4, 4, 2, 64, 768), BF),
    "gain": ((4, 4, 2, 8, 256), F32),
}
SEGMENTS = {"qkv": 2, "out": 1, "wide": 2, "down": 2, "gain": 1}
GATHERED = [(name, layer) for layer in range(2) for name in ("qkv", "out", "wide", "down")] + [
    ("gain", 0)
]


def weight_shape(key):
    return jax.ShapeDtypeStruct(*WEIGHTS[key[0]])


class ScatterPart:
    def __init__(self, first_is_y, total, rows, ring, blocks, groups, semaphores, finish):
        self.axes = Axes(first_is_y)
        self.total, self.rows, self.ring, self.blocks, self.groups = total, rows, ring, blocks, groups
        self.semaphores, self.finish = semaphores, finish

    def fill(self, z, value):
        if self.axes.first_is_y:
            self.total[z] = value
        else:
            self.total[:, z] = value

    def stage(self, number):
        axes, sem, total = self.axes, self.semaphores, self.total
        m1, m2 = axes.m1, axes.m2
        before, after, across = shifted(m2, 3), shifted(m2, 1), shifted(m2, 2)
        low, high = pl.ds(0, 2), pl.ds(2, 2)

        def add(target, source):
            target[...] = (target[...].astype(F32) + source[...].astype(F32)).astype(target.dtype)

        if number == 1:
            remote(
                total.at[across, low], self.ring.at[0], sem.at[0], sem.at[1], axes.second(1)
            ).start()
            remote(
                total.at[across, high], self.ring.at[1], sem.at[0], sem.at[1], axes.second(3)
            ).start()
        elif number == 2:
            row = total.at[m2]
            remote(row, self.ring, sem.at[0], sem.at[1], axes.partner).wait()
            add(total.at[after, low], self.ring.at[0])
            add(total.at[before, high], self.ring.at[1])
            remote(
                total.at[after], self.rows.at[0], sem.at[2], sem.at[3], axes.second(1)
            ).start()
            remote(
                total.at[before], self.rows.at[1], sem.at[2], sem.at[3], axes.second(3)
            ).start()
        elif number == 3:
            remote(self.rows, self.rows, sem.at[2], sem.at[3], axes.partner).wait()
            for at in range(4):
                total[m2, at] = (
                    total[m2, at].astype(F32)
                    + self.rows[0, at].astype(F32)
                    + self.rows[1, at].astype(F32)
                ).astype(total.dtype)
            for by in (1, 3, 2):
                remote(
                    total.at[m2, shifted(m1, by)],
                    self.blocks.at[by - 1],
                    sem.at[4],
                    sem.at[5],
                    axes.first(by),
                ).start()
        elif number == 4:
            remote(self.blocks, self.blocks, sem.at[4], sem.at[5], axes.partner).wait()
            self.groups[axes.x] = (
                total[m2, m1].astype(F32)
                + self.blocks[0].astype(F32)
                + self.blocks[1].astype(F32)
                + self.blocks[2].astype(F32)
            ).astype(total.dtype)
            mine = self.groups.at[axes.x]
            for by in (1, 3, 2):
                remote(
                    mine,
                    mine,
                    sem.at[6],
                    sem.at[7],
                    device(shifted(axes.x, by), axes.z, axes.y, axes.core),
                ).start()
        elif number == 5:
            three = self.groups.at[pl.ds(0, 3)]
            remote(three, three, sem.at[6], sem.at[7], axes.partner).wait()
            summed = self.groups[0].astype(F32)
            for at in range(1, 4):
                summed = summed + self.groups[at].astype(F32)
            self.finish(0, summed)
        else:
            self.finish(1, None)


class AcrossPart(ScatterPart):
    def __init__(self, first_is_y, whole, quarter, came, rows, ring, blocks, groups, semaphores, finish):
        super().__init__(first_is_y, quarter, rows, ring, blocks, groups, semaphores, finish)
        self.whole, self.came = whole, came

    def fill(self, z, value):
        if self.axes.first_is_y:
            self.whole[z] = value
        else:
            self.whole[:, z] = value

    def columns(self, at):
        return pl.ds(pl.multiple_of(at * 256, 128), 256)

    def stage(self, number):
        axes, sem = self.axes, self.semaphores
        if number == 0:
            for by in (1, 3, 2):
                there = shifted(axes.x, by)
                remote(
                    self.whole.at[:, :, :, self.columns(there)],
                    self.came.at[by - 1],
                    sem.at[10],
                    sem.at[11],
                    device(there, axes.z, axes.y, axes.core),
                ).start()
            return
        if number == 1:
            remote(self.came, self.came, sem.at[10], sem.at[11], axes.partner).wait()
            for at in range(4):
                summed = self.whole[at, :, :, self.columns(axes.x)].astype(F32)
                for by in range(3):
                    summed = summed + self.came[by, at].astype(F32)
                self.total[at] = summed.astype(BF)
        if number == 5:
            three = self.groups.at[pl.ds(0, 3)]
            remote(three, three, sem.at[6], sem.at[7], axes.partner).wait()
            quarters = [self.groups[at].astype(F32) for at in range(4)]
            self.finish(0, jnp.concatenate(quarters, axis=1))
            return
        super().stage(number)


SCATTER_SEMAPHORES = 12
ACROSS_PARTS = (("gate", 0), ("up", 0))
PARTS = {
    "gate": (True, 48, 1024, BF),
    "up": (False, 48, 1024, BF),
    "left": (True, 64, 384, BF),
    "right": (False, 64, 384, BF),
    "o": (False, 48, 384, BF),
    "q": (True, 48, 384, BF),
    "k": (False, 48, 384, BF),
    "v": (True, 48, 384, BF),
    "gain": (False, 8, 256, F32),
}
SOURCE = {
    "q": "qkv", "k": "qkv", "v": "qkv", "o": "out", "gate": "wide", "up": "wide",
    "left": "down", "right": "down", "gain": "gain",
}
SUMS = {
    "qkv": ((2, 3, 24, 768), F32),
    "out": ((2, 24, 768), F32),
    "wide": ((2, 2, 24, 2048), F32),
    "down": ((2, 64, 768), F32),
    "gain": ((1, 8, 256), F32),
}
LEFT, RIGHT = pl.ds(0, 384), pl.ds(384, 384)


def part_target(part, ref):
    if part in ("q", "k", "v"):
        return ref.at["qkv".index(part)]
    if part in ("gate", "up"):
        return ref.at[int(part == "up")]
    if part in ("left", "right"):
        return ref.at[:, LEFT if part == "left" else RIGHT]
    return ref


def rows_swapped(target, mine, theirs, sem):
    axes = Axes(True)
    core = axes.core

    def finish(part, summed):
        own_rows = pl.ds(pl.multiple_of(core * 24, 8), 24)
        other_rows = pl.ds(pl.multiple_of((1 - core) * 24, 8), 24)
        copy = remote(mine.at[other_rows, :], theirs, sem.at[8], sem.at[9], axes.partner)
        if part == 0:
            mine[...] = summed
            copy.start()
        else:
            copy.wait()
            kept = mine[own_rows, :]
            got = theirs[...]
            width = kept.shape[-1]
            target[:, :width] = jnp.where(core == 0, kept, got)
            target[:, width:] = jnp.where(core == 0, got, kept)

    return finish


def direct(target):
    def finish(part, summed):
        if part == 0:
            target[...] = summed

    return finish


def part_scratch():
    shared, own = [], []
    for part, (_, rows, width, kind) in PARTS.items():
        shared += [
            pltpu.VMEM((4, 4, rows, width), kind),
            pltpu.VMEM((2, 4, rows, width), kind),
            pltpu.VMEM((48, width), F32) if rows == 48 else pltpu.VMEM((8, 128), F32),
        ]
        for layer in range(1 if part == "gain" else 2):
            across = (part, layer) in ACROSS_PARTS
            if across:
                own += [
                    pltpu.VMEM((4, 4, rows, width // 4), kind),
                    pltpu.VMEM((3, 4, 4, rows, width // 4), kind),
                    pltpu.VMEM((2, 4, rows, width // 4), kind),
                ]
            narrow = width // 4 if across else width
            own += [
                pltpu.VMEM((2, 2, rows, narrow), kind),
                pltpu.VMEM((3, rows, narrow), kind),
                pltpu.VMEM((4, rows, narrow), kind),
                pltpu.VMEM((24, width), F32) if rows == 48 else pltpu.VMEM((8, 128), F32),
            ]
    return shared, own


def build_parts(shared, own, sems, sums):
    parts = {}
    count = 0
    own = list(own)

    def take(number):
        taken = own[:number]
        del own[:number]
        return taken

    for at, (part, (first_is_y, rows, _, _)) in enumerate(PARTS.items()):
        total, rows_in, mine = shared[3 * at : 3 * at + 3]
        for layer in (0,) if part == "gain" else (0, 1):
            if (part, layer) in ACROSS_PARTS:
                quarter, came, rows_here = take(3)
            ring, blocks, groups, theirs = take(4)
            target = part_target(part, sums[SOURCE[part]].at[layer])
            sem = sems.at[count]
            finish = rows_swapped(target, mine, theirs, sem) if rows == 48 else direct(target)
            if (part, layer) in ACROSS_PARTS:
                parts[part, layer] = AcrossPart(
                    first_is_y, total, quarter, came, rows_here, ring, blocks, groups, sem, finish
                )
            else:
                parts[part, layer] = ScatterPart(
                    first_is_y, total, rows_in, ring, blocks, groups, sem, finish
                )
            count += 1
    return parts


def pair_device(pair):
    if pair < 16:
        return 2 * pair
    z = (pair - 16) // 2
    return 2 * (4 * z + 2 * ((pair - 16) % 2) + z % 2) + 1


def own_pair():
    _, z, y, core = coordinates()
    has_pair = (core == 0) | (lax.rem(z + y, 2) == 0)
    pair = jnp.where(core == 0, 4 * z + y, 16 + 2 * z + lax.div(y, 2))
    return has_pair, pair


def lanes(shape):
    return lax.broadcasted_iota(jnp.int32, shape, len(shape) - 1)


def turned(values, cosine, sine):
    here = lax.rem(lanes(values.shape), 64) < 32
    width = values.shape[-1]
    other = jnp.where(here, pltpu.roll(values, width - 32, 1), pltpu.roll(values, 32, 1))
    return values * cosine + other * sine


def twice(table):
    return jnp.concatenate([table, table], axis=0)


def allowed_keys(first_key, first_query, keys, queries, length):
    key = first_key + lax.broadcasted_iota(jnp.int32, (keys, queries), 0)
    query = first_query + lax.broadcasted_iota(jnp.int32, (keys, queries), 1)
    return (key <= query) & (key < length)


def slot_length(lengths, pair):
    return jnp.where(pair < HEADS, lengths[0], lengths[1])


LAST_DIMS = (((1,), (1,)), ((), ()))
BLOCKS = LENGTH // BLOCK
MESSAGE = 96


def front_lanes(rows):
    return lanes((rows, 128)) < 64


def pack_heads(both):
    front = front_lanes(32)
    top, bottom = both[0:32], both[32:64]
    return (
        jnp.where(front, top, pltpu.roll(bottom, 64, 1)).astype(BF),
        jnp.where(front, pltpu.roll(top, 64, 1), bottom).astype(BF),
    )


def unpack_heads(first, second):
    front = front_lanes(32)
    first, second = first.astype(F32), second.astype(F32)
    return jnp.concatenate(
        [
            jnp.where(front, first, pltpu.roll(second, 64, 1)),
            jnp.where(front, pltpu.roll(first, 64, 1), second),
        ],
        axis=0,
    )


def unpack_block(packed, to_front):
    packed = packed.astype(F32).reshape(128, 128)
    other = pltpu.roll(packed, 64, 1)
    front = front_lanes(128)
    if to_front:
        top, bottom = jnp.where(front, packed, 0.0), jnp.where(front, other, 0.0)
    else:
        top, bottom = jnp.where(front, 0.0, other), jnp.where(front, 0.0, packed)
    joined = jnp.concatenate([top.reshape(4, 32, 128), bottom.reshape(4, 32, 128)], axis=1)
    return joined.reshape(256, 128).astype(BF)


def pack_turned(turned_values):
    rows = jnp.concatenate([turned_values, turned_values], axis=0).T.reshape(4, 64, 128)
    front = lanes((4, 32, 128)) < 64
    return jnp.where(front, rows[:, 0:32], rows[:, 32:64]).astype(BF)


class Exchange:
    def __init__(self, semaphores):
        self.x, self.me = lax.axis_index("batch"), lax.axis_index("seq")
        self.has_pair, self.pair = own_pair()
        self.send, self.receive, self.local = (semaphores.at[at] for at in range(3))

    def to(self, there, source, target):
        @pl.when(self.me != there)
        def _():
            remote(source, target, self.send, self.receive, (self.x, there)).start()

        @pl.when(self.me == there)
        def _():
            pltpu.make_async_copy(source, target, self.local).start()

    def wait(self, sent, got, where):
        if where == "pairs":
            sends, gets = (sent.shape[0], sent.shape[0] - 1), (None, got.shape[0] - 1)
        else:
            sends, gets = (None, sent.shape[0] - 1), (got.shape[0], got.shape[0] - 1)

        def wait_for(n_sent, n_got):
            if n_got is not None:
                part = got.at[pl.ds(0, n_got)]
                remote(part, part, self.send, self.receive, (self.x, self.me)).wait_recv()
            if n_sent is not None:
                part = sent.at[pl.ds(0, n_sent)]
                remote(part, part, self.send, self.receive, (self.x, self.me)).wait_send()

        @pl.when(self.has_pair)
        def _():
            pltpu.make_async_copy(sent.at[0], got.at[0], self.local).wait()
            wait_for(sends[1], gets[1])

        @pl.when(jnp.logical_not(self.has_pair))
        def _():
            wait_for(sends[0], gets[0])


def send_projections(exchange, query, key, value, cosine, sine, outgoing, rows):
    cosine, sine = twice(cosine), twice(sine)
    front = front_lanes(64)
    for tile in range(6):
        cut = slice(128 * tile, 128 * tile + 128)
        q = turned(query[:, cut], cosine, sine) * (1.0 / math.sqrt(HEAD_DIM))
        k = turned(key[:, cut], cosine, sine)
        v = value[:, cut]
        for slot in range(2):
            span = slice(64 * slot, 64 * slot + 64)
            at = slot * HEADS + 2 * tile
            ks, vs = k[span], v[span]
            outgoing[at, 0:64] = jnp.where(front, ks, pltpu.roll(vs, 64, 1)).astype(BF)
            outgoing[at + 1, 0:64] = jnp.where(front, pltpu.roll(ks, 64, 1), vs).astype(BF)
            outgoing[at, 64:96], outgoing[at + 1, 64:96] = pack_heads(q[span])
    for pair in range(PAIRS):
        exchange.to(pair_device(pair), outgoing.at[pair], rows.at[exchange.me])


def attend_block(exchange, at, length, rows, values_turned, out_turned, log_total, outgoing, incoming):
    count = (at + 1) * BLOCK
    queries = unpack_block(rows[4 * at : 4 * at + 4, 64:96], True)
    keys = rows[0 : 4 * at + 4, 0:64].reshape(count, 128)
    scores = lax.dot_general(keys, queries, LAST_DIMS, preferred_element_type=F32)
    scores = jnp.where(allowed_keys(0, at * BLOCK, count, BLOCK, length), scores, MASKED)
    highest = jnp.max(scores, axis=0, keepdims=True)
    raised = jnp.exp(scores - highest)
    total = jnp.sum(raised, axis=0, keepdims=True)
    result = (
        jnp.dot(values_turned[:, 0:count], raised.astype(BF), preferred_element_type=F32) / total
    )
    cut = slice(at * BLOCK, count)
    out_turned[:, cut] = result
    log_total[:, cut] = jnp.broadcast_to(highest + jnp.log(total), (8, BLOCK))
    outgoing[4 * at : 4 * at + 4] = pack_turned(result)
    for there in range(4 * at, 4 * at + 4):
        exchange.to(there, outgoing.at[there], incoming.at[exchange.pair])


def merge_heads(incoming, merged):
    for slot in range(2):
        for tile in range(6):
            at = slot * HEADS + 2 * tile
            merged[64 * slot : 64 * slot + 64, 128 * tile : 128 * tile + 128] = unpack_heads(
                incoming[at], incoming[at + 1]
            ).astype(BF)


def norm_forward(values, norm_gain):
    inverse = lax.rsqrt(jnp.mean(values * values, axis=-1, keepdims=True) + EPSILON)
    return (values * inverse * norm_gain, inverse)


def feed_forward(rows_in, gate_up, down, paired):
    fed = jnp.zeros((128, 768), F32)
    for z in range(4):
        cut = slice(512 * z, 512 * z + 512)
        gate = jnp.dot(rows_in, gate_up[0, :, :, :, cut].reshape(768, 512), preferred_element_type=F32)
        up = jnp.dot(rows_in, gate_up[1, :, :, :, cut].reshape(768, 512), preferred_element_type=F32)
        paired[0, :, cut] = gate
        paired[1, :, cut] = up
        hidden = (jax.nn.silu(gate) * up).astype(BF)
        fed = fed + jnp.dot(hidden, down[z].reshape(512, 768), preferred_element_type=F32)
    return fed


KEPT = (
    [("result", (128, 768), F32), ("mid_0", (128, 768), F32), ("summed_0", (128, 768), F32)]
    + [("mid_1", (128, 768), F32), ("gain", (8, 768), F32)]
    + [("stream", (128, 768), BF), ("cotangent", (128, 768), F32)]
    + [
        (name + "_" + layer, shape, kind)
        for layer in "01"
        for name, shape, kind in (
            ("paired", (2, 128, 2048), F32),
            ("rows", (32, MESSAGE, 128), BF),
            ("merged", (128, 768), BF),
            ("turned", (64, LENGTH), F32),
            ("total", (8, LENGTH), F32),
        )
    ]
)


def forward_kernel(
    lengths, qkv, out, gate_up, down, gains, inputs, cotangents, cosine, sine, *refs
):
    stored = dict(zip(GATHERED[:-1], refs[:8]))
    kept = {name: ref for (name, _, _), ref in zip(KEPT, refs[8:])}
    refs = refs[8 + len(KEPT) :]
    store, refs = dict(zip(GATHERED, refs[:9])), refs[9:]
    their_qkv, their_out, their_gate_up, b_qkv, b_out, b_gate_up, b_down = refs[:7]
    outgoing, places, incoming, values_turned, stream, swap, sems, local, pair_sems = refs[7:]
    axes = Axes(True)
    core = axes.core
    x, me = lax.axis_index("batch"), lax.axis_index("seq")
    greet(
        [(x, lax.rem(me + by, 32)) for by in range(1, 32)]
        + [device(shifted(x, by), axes.z, axes.y, core) for by in (1, 2, 3)]
    )
    swaps = [
        remote(mine, theirs, swap.at[0, at], swap.at[1, at], axes.partner)
        for at, (mine, theirs) in enumerate(
            (
                (qkv.at[0], their_qkv.at[0]),
                (qkv.at[1], their_qkv.at[1]),
                (out, their_out),
                (gate_up, their_gate_up),
            )
        )
    ]
    for copy in swaps:
        copy.start()
    for slot in range(2):
        stream[64 * slot : 64 * slot + 64] = inputs[:, slot, :]
        kept["cotangent"][64 * slot : 64 * slot + 64] = cotangents[:, slot, :]
    kept["stream"][...] = stream[...].astype(BF)

    def joined(mine, theirs):
        upper = jnp.where(core == 0, mine, theirs)
        lower = jnp.where(core == 0, theirs, mine)
        return jnp.concatenate([upper, lower], axis=0).astype(BF)

    segments = {}
    at = 0
    for key in GATHERED:
        name, layer = key
        block = {"qkv": b_qkv, "out": b_out, "wide": b_gate_up, "down": b_down}.get(name)
        block = gains if block is None else block.at[layer]
        kind, views, owns = GatherSegment, weight_views, own_views
        if key in ACROSS:
            kind, views, owns = AcrossSegment, across_views, across_owns
        segments[key] = []
        for (first_is_y, view), own in zip(views(name, store[key]), owns(name, block)):
            segments[key].append(kind(first_is_y, view, sems.at[at], own))
            at += 1

    def each(keys, act):
        for key in keys:
            for segment in segments[key]:
                act(segment)

    def keep(*keys):
        each(keys, lambda segment: segment.keep().start())
        each(keys, lambda segment: segment.keep().wait())

    def begin(phase, *keys):
        each(keys, lambda segment: segment.begin(phase))

    def end(phase, *keys):
        each(keys, lambda segment: segment.end(phase))

    saves = []

    def save(*keys):
        for key in keys:
            copy = pltpu.make_async_copy(store[key], stored[key], local.at[len(saves)])
            copy.start()
            saves.append(copy)

    qkv_0, out_0, wide_0, down_0 = GATHERED[0:4]
    qkv_1, out_1, wide_1, down_1 = GATHERED[4:8]
    gains_0 = GATHERED[8]

    swaps[0].wait()
    for at in range(3):
        b_qkv[0, at] = joined(qkv[0, at], their_qkv[0, at])
    begin(0, qkv_0)
    keep(qkv_0)
    b_down[0] = down[0].astype(BF)
    begin(0, down_0)
    keep(down_0)
    for copy in swaps[1:]:
        copy.wait()
    for at in range(2):
        b_gate_up[0, at] = joined(gate_up[0, at], their_gate_up[0, at])
    begin(0, wide_0)
    keep(wide_0)
    end(0, qkv_0)
    begin(1, qkv_0)
    end(0, down_0)
    begin(1, down_0)
    b_out[0] = joined(out[0], their_out[0])
    for at in range(2):
        b_gate_up[1, at] = joined(gate_up[1, at], their_gate_up[1, at])
    begin(0, out_0, gains_0, wide_1)
    keep(out_0, gains_0, wide_1)
    for at in range(3):
        b_qkv[1, at] = joined(qkv[1, at], their_qkv[1, at])
    b_out[1] = joined(out[1], their_out[1])
    b_down[1] = down[1].astype(BF)
    end(1, qkv_0)
    begin(2, qkv_0)
    end(1, down_0)
    begin(2, down_0)
    end(0, wide_0)
    begin(1, wide_0)
    end(2, qkv_0)
    begin(3, qkv_0)
    keep(qkv_1, out_1, down_1)
    end(2, down_0)
    begin(3, down_0)
    end(0, out_0, gains_0, wide_1)
    begin(1, wide_1)
    end(3, qkv_0)
    save(qkv_0)

    def attention(layer, source, before, between):
        weights = store["qkv", layer]
        name = "_" + str(layer)
        rows, merged = kept["rows" + name], kept["merged" + name]
        there = Exchange(pair_sems.at[2 * layer])
        back = Exchange(pair_sems.at[2 * layer + 1])
        low = source.astype(BF)
        query, key, value = (
            jnp.dot(low, weights[at].reshape(768, 768), preferred_element_type=F32)
            for at in range(3)
        )
        send_projections(
            there, query, key, value, cosine[...], sine[...], outgoing.at[layer], rows
        )
        before()
        there.wait(outgoing.at[layer], rows, "pairs")
        length = slot_length(lengths, there.pair)

        @pl.when(there.has_pair)
        def _():
            all_rows = rows[:, 0:64].reshape(LENGTH, 128).astype(F32)
            values_turned[...] = all_rows.T[64:128].astype(BF)

        for at in range(BLOCKS):

            @pl.when(there.has_pair)
            def _(at=at):
                attend_block(
                    back,
                    at,
                    length,
                    rows,
                    values_turned,
                    kept["turned" + name],
                    kept["total" + name],
                    places.at[layer],
                    incoming.at[layer],
                )

            if at in between:
                between[at]()
        back.wait(places.at[layer], incoming.at[layer], "places")
        merge_heads(incoming.at[layer], merged)
        between["after"]()
        out_matrix = store["out", layer][...].reshape(768, 768)
        return jnp.dot(merged[...], out_matrix, preferred_element_type=F32)

    def before_0():
        begin(1, out_0, gains_0)
        end(1, wide_1)
        begin(2, wide_1)

    def within_0():
        end(1, wide_0)
        begin(2, wide_0)
        end(2, wide_1)
        begin(3, wide_1)
        begin(0, qkv_1)

    def later_0():
        end(1, out_0, gains_0)
        begin(2, out_0, gains_0)

    def last_0():
        end(0, qkv_1)
        begin(1, qkv_1)

    def after_0():
        end(3, down_0)
        begin(4, down_0)
        end(2, wide_0, out_0, gains_0)
        begin(3, out_0, wide_0, gains_0)
        begin(0, out_1, down_1)
        end(3, out_0, wide_0, gains_0)
        end(4, down_0)
        save(out_0, wide_0, down_0)
        for device_at in range(32):
            piece = store[gains_0][device_at // 8, device_at // 2 % 4, device_at % 2]
            first = 24 * device_at // 128
            if device_at == 0:
                kept["gain"][...] = jnp.zeros((8, 768), F32)
            width = min(256, 768 - 128 * first)
            kept["gain"][:, 128 * first : 128 * first + width] += piece[:, :width]

    def gain(at):
        return kept["gain"][at : at + 1, :]

    mixed = attention(
        0, stream[...], before_0, {1: within_0, 4: later_0, 7: last_0, "after": after_0}
    )
    residual = stream[...] + mixed
    kept["mid_0"][...] = residual
    middle, _ = norm_forward(residual, gain(0))
    end(1, qkv_1)
    begin(2, qkv_1)
    fed = feed_forward(middle.astype(BF), store[wide_0], store[down_0], kept["paired_0"])
    end(2, qkv_1)
    begin(3, qkv_1)
    end(0, out_1, down_1)
    begin(1, out_1, down_1)
    summed = middle + fed
    kept["summed_0"][...] = summed
    shallow, _ = norm_forward(summed, gain(1))
    normed, _ = norm_forward(shallow, gain(2))
    end(3, qkv_1)
    save(qkv_1)

    def before_1():
        pass

    def within_1():
        end(1, out_1, down_1)
        begin(2, out_1, down_1)

    def later_1():
        end(3, wide_1)
        begin(4, wide_1)

    def after_1():
        end(2, out_1, down_1)
        begin(3, out_1, down_1)
        end(3, out_1, down_1)
        end(4, wide_1)
        save(out_1, wide_1, down_1)

    mixed = attention(1, normed, before_1, {1: within_1, 7: later_1, "after": after_1})
    residual = shallow + mixed
    kept["mid_1"][...] = residual
    normed_two, _ = norm_forward(residual, gain(3))
    fed = feed_forward(normed_two.astype(BF), store[wide_1], store[down_1], kept["paired_1"])
    kept["result"][...] = residual + fed
    for copy in saves:
        copy.wait()


def run_forward(*operands):
    count = sum(SEGMENTS[name] for name, _ in GATHERED)
    stored = GATHERED[:-1]
    results = pl.pallas_call(
        forward_kernel,
        out_shape=[weight_shape(key) for key in stored]
        + [jax.ShapeDtypeStruct(shape, kind) for _, shape, kind in KEPT],
        in_specs=[SMEM] + [VMEM] * 9,
        out_specs=[ANY] * 8 + [VMEM] * len(KEPT),
        scratch_shapes=[pltpu.VMEM(*WEIGHTS[name]) for name, _ in GATHERED]
        + [
            pltpu.VMEM((2, 3, 24, 768), F32),
            pltpu.VMEM((2, 24, 768), F32),
            pltpu.VMEM((2, 2, 24, 2048), F32),
            pltpu.VMEM((2, 3, 48, 768), BF),
            pltpu.VMEM((2, 48, 768), BF),
            pltpu.VMEM((2, 2, 48, 2048), BF),
            pltpu.VMEM((2, 64, 768), BF),
            pltpu.VMEM((2, PAIRS, MESSAGE, 128), BF),
            pltpu.VMEM((2, 32, 32, 128), BF),
            pltpu.VMEM((2, PAIRS, 32, 128), BF),
            pltpu.VMEM((64, LENGTH), BF),
            pltpu.VMEM((128, 768), F32),
            pltpu.SemaphoreType.DMA((2, 4)),
            pltpu.SemaphoreType.DMA((count, 5, 4)),
            pltpu.SemaphoreType.DMA((8,)),
            pltpu.SemaphoreType.DMA((4, 3)),
        ],
        compiler_params=params(1),
        name="forward",
    )(*operands)
    return dict(zip(stored, results)), {
        name: result for (name, _, _), result in zip(KEPT, results[8:])
    }


def attend_back_block(
    exchange, at, length, rows, out_grad, out_turned, log_total, keys_turned, key_grad, outgoing, incoming
):
    cut = slice(at * BLOCK, (at + 1) * BLOCK)
    four = slice(4 * at, 4 * at + 4)
    queries = unpack_block(rows[four, 64:96], True)
    outs = unpack_block(out_grad[four], False)
    outs_turned = outs.astype(F32).T[64:128]
    delta = jnp.sum(outs_turned * out_turned[:, cut], axis=0, keepdims=True)
    shift = log_total[0:1, cut]
    query_grad = jnp.zeros((64, BLOCK), F32)
    for part in range(at + 1):
        span = slice(part * BLOCK, (part + 1) * BLOCK)
        keys = rows[4 * part : 4 * part + 4, 0:64].reshape(BLOCK, 128)
        scores = lax.dot_general(keys, queries, LAST_DIMS, preferred_element_type=F32)
        allowed = allowed_keys(part * BLOCK, at * BLOCK, BLOCK, BLOCK, length)
        probs = jnp.where(allowed, jnp.exp(scores - shift), 0.0)
        probs_grad = lax.dot_general(keys, outs, LAST_DIMS, preferred_element_type=F32)
        score_grad = (probs * (probs_grad - delta)).astype(BF)
        key_grad[span, :] += jnp.dot(score_grad, queries, preferred_element_type=F32) + jnp.dot(
            probs.astype(BF), outs, preferred_element_type=F32
        )
        query_grad += jnp.dot(keys_turned[:, span], score_grad, preferred_element_type=F32)
    outgoing[four, 0:64] = key_grad[cut, :].reshape(4, SPAN, 128).astype(BF)
    outgoing[four, 64:96] = pack_turned(query_grad)
    for there in range(4 * at, 4 * at + 4):
        exchange.to(there, outgoing.at[there], incoming.at[exchange.pair])


def collect_projections(incoming, cosine, sine, result):
    front = front_lanes(64)
    for slot in range(2):
        span = slice(64 * slot, 64 * slot + 64)
        for tile in range(6):
            cut = slice(128 * tile, 128 * tile + 128)
            at = slot * HEADS + 2 * tile
            first, second = (incoming[at + n, 0:64].astype(F32) for n in (0, 1))
            q = unpack_heads(incoming[at, 64:96], incoming[at + 1, 64:96])
            k = jnp.where(front, first, pltpu.roll(second, 64, 1))
            v = jnp.where(front, pltpu.roll(first, 64, 1), second)
            q = turned(q * (1.0 / math.sqrt(HEAD_DIM)), cosine, -sine)
            result[0, span, cut] = q.astype(BF)
            result[1, span, cut] = turned(k, cosine, -sine).astype(BF)
            result[2, span, cut] = v.astype(BF)


def norm_backward(incoming, values, norm_gain):
    inverse = lax.rsqrt(jnp.mean(values * values, axis=-1, keepdims=True) + EPSILON)
    scaled = incoming * norm_gain
    outgoing = inverse * scaled - values * (inverse * inverse * inverse) * jnp.mean(
        scaled * values, axis=-1, keepdims=True
    )
    return outgoing, jnp.sum(incoming * values * inverse, axis=0, keepdims=True)


def feed_back(incoming, paired, gate_up, down, gate_grads, up_grads, hidden_turned):
    source_grad = jnp.zeros((128, 768), F32)
    for z in range(4):
        cut = slice(512 * z, 512 * z + 512)
        hidden_grad = lax.dot_general(
            incoming, down[z].reshape(512, 768), LAST_DIMS, preferred_element_type=F32
        )
        gate, up = paired[0, :, cut], paired[1, :, cut]
        sigmoid = jax.nn.sigmoid(gate)
        hidden = (gate * sigmoid * up).T.astype(BF).reshape(4, 2, 64, 128)
        hidden_turned[0, z] = hidden[:, 0]
        hidden_turned[1, z] = hidden[:, 1]
        gate_grad = (hidden_grad * up * sigmoid * (1.0 + gate * (1.0 - sigmoid))).astype(BF)
        up_grad = (hidden_grad * gate * sigmoid).astype(BF)
        part = slice(512 * (z % 2), 512 * (z % 2) + 512)
        gate_grads[z // 2, :, part] = gate_grad
        up_grads[z // 2, :, part] = up_grad
        for at, value in enumerate((gate_grad, up_grad)):
            source_grad = source_grad + lax.dot_general(
                value, gate_up[at, :, :, :, cut].reshape(768, 512), LAST_DIMS, preferred_element_type=F32
            )
    return source_grad


def turned_low(values):
    return values.astype(F32).T.astype(BF)


def fill_part(part, rows, left_of, right):
    for z in range(4):
        value = jnp.dot(left_of(z), right, preferred_element_type=F32).astype(BF)
        part.fill(z, value.reshape(4, rows, right.shape[1]))


def beside(first, second, rows):
    def left_of(z):
        cut = slice(4 * rows * z, 4 * rows * (z + 1))
        return jnp.concatenate([first[cut], second[cut]], axis=1)

    return left_of


SHARED = {
    "source": ((768, 128), (768, 128)),
    "gate": ((2, 128, 1024), (128, 1024)),
    "up": ((2, 128, 1024), (128, 1024)),
    "hidden": ((2, 4, 4, 64, 128), (4, 4, 64, 128)),
    "fed": ((128, 768), (128, 768)),
    "merged": ((768, 128), (768, 128)),
    "mixed": ((2, 128, 384), (128, 384)),
    "norm": ((768, 128), (768, 128)),
    "low": ((2, 3, 128, 384), (3, 128, 384)),
}
KEPT_0 = ("rows_0", "merged_0", "turned_0", "total_0")
KEPT_1 = tuple(name[:-1] + "1" for name in KEPT_0)
KEPT_TYPES = {name: (shape, kind) for name, shape, kind in KEPT}
WEIGHT_ORDER = ("down", "wide", "out", "qkv")


def backward_kernel(lengths, *refs):
    refs = list(refs)

    def take(count):
        taken = refs[:count]
        del refs[:count]
        return taken

    cotangent, stream, residual_0, summed_0, residual_1, gains, cosine, sine = take(8)
    kept = dict(zip(KEPT_1, take(4)))
    far = dict(zip(KEPT_0, take(4)))
    paired_far = dict(zip((0, 1), take(2)))
    stored = dict(zip(GATHERED[:-1], take(8)))
    (input_grad,) = take(1)
    sums = dict(zip(SUMS, take(len(SUMS))))
    kept.update(zip(KEPT_0, take(4)))
    (paired,) = take(1)
    weights = dict(zip(WEIGHT_ORDER, take(4)))
    shared, own = part_scratch()
    shared, own = take(len(shared)), take(len(own))
    given = dict(zip(SHARED, take(len(SHARED))))
    got = [dict(zip(SHARED, take(len(SHARED)))) for _ in range(2)]
    out_grads, to_pairs, to_places, incoming = take(4)
    keys_turned, key_grad, gain_grads, their_gains, stacked = take(5)
    part_sems, give_sems, load_sems, pair_sems = take(4)
    parts = build_parts(shared, own, part_sems, sums)
    axes = Axes(True)
    core = axes.core
    x, me = lax.axis_index("batch"), lax.axis_index("seq")
    barrier = pltpu.get_barrier_semaphore()
    neighbours = [(x, lax.rem(me + by, 32)) for by in range(1, 32)]
    neighbours += [device(shifted(x, by), axes.z, axes.y, core) for by in (1, 2, 3)]
    for where in neighbours:
        pl.semaphore_signal(barrier, inc=1, device_id=where, device_id_type=MESH)

    def load(name, layer):
        at = WEIGHT_ORDER.index(name)
        return pltpu.make_async_copy(stored[name, layer], weights[name], load_sems.at[at])

    def load_paired(layer):
        return pltpu.make_async_copy(paired_far[layer], paired, load_sems.at[8])

    load_paired(1).start()
    for name in WEIGHT_ORDER:
        load(name, 1).start()
    loads = [
        pltpu.make_async_copy(far[name], kept[name], load_sems.at[4 + at])
        for at, name in enumerate(KEPT_0)
    ]
    for copy in loads:
        copy.start()

    def gain(at):
        return gains[at : at + 1, :]

    def stages(*work):
        for names, layer, number in work:
            for name in names:
                parts[name, layer].stage(number)

    def share(layer, names):
        copies = []
        for name in names:
            at = list(SHARED).index(name)
            source = given[name]
            if SHARED[name][0] != SHARED[name][1]:
                source = source.at[1 - core]
            copies.append(
                remote(
                    source,
                    got[layer][name],
                    give_sems.at[layer, at, 0],
                    give_sems.at[layer, at, 1],
                    axes.partner,
                )
            )
        return copies

    def start(copies):
        for copy in copies:
            copy.start()

    def finish(copies):
        for copy in copies:
            copy.wait()

    wide, narrow = ("gate", "up"), ("left", "right", "o")

    def wide_grads(layer):
        left_of = beside(given["source"], got[layer]["source"], 48)
        for name in wide:
            right = jnp.concatenate([given[name][core], got[layer][name][...]], axis=0)
            fill_part(parts[name, layer], 48, left_of, right)

    def narrow_grads(layer):
        def left_of(z):
            mine = given["hidden"][core, z].reshape(256, 128)
            return jnp.concatenate([mine, got[layer]["hidden"][z].reshape(256, 128)], axis=1)

        right = jnp.concatenate([given["fed"][...], got[layer]["fed"][...]], axis=0)
        fill_part(parts["left", layer], 64, left_of, right[:, :384])
        fill_part(parts["right", layer], 64, left_of, right[:, 384:])
        right = jnp.concatenate([given["mixed"][core], got[layer]["mixed"][...]], axis=0)
        left_of = beside(given["merged"], got[layer]["merged"], 48)
        fill_part(parts["o", layer], 48, left_of, right)

    def projection_grads(layer):
        left_of = beside(given["norm"], got[layer]["norm"], 48)
        for at, name in enumerate("qkv"):
            right = jnp.concatenate([given["low"][core, at], got[layer]["low"][at]], axis=0)
            fill_part(parts[name, layer], 48, left_of, right)

    FED = ("source", "gate", "up", "hidden", "fed")
    MIXED = ("merged", "mixed")
    PROJECTED = ("norm", "low")

    def feed(layer, source, grad):
        load("down", layer).wait()
        load("wide", layer).wait()
        load_paired(layer).wait()
        low = grad.astype(BF)
        given["fed"][...] = low
        given["source"][...] = turned_low(source.astype(BF))
        return feed_back(
            low,
            paired,
            weights["wide"],
            weights["down"],
            given["gate"],
            given["up"],
            given["hidden"],
        )

    def send_out_grad(layer, grad):
        load("out", layer).wait()
        low = grad.astype(BF)
        given["mixed"][0] = low[:, :384]
        given["mixed"][1] = low[:, 384:]
        given["merged"][...] = turned_low(kept["merged_" + str(layer)][...])
        merged_grad = (
            lax.dot_general(
                low, weights["out"][...].reshape(768, 768), LAST_DIMS, preferred_element_type=F32
            )
            .astype(BF)
            .astype(F32)
        )
        exchange = Exchange(pair_sems.at[2 * layer])
        to = to_pairs
        for slot in range(2):
            for tile in range(6):
                at = slot * HEADS + 2 * tile
                both = merged_grad[64 * slot : 64 * slot + 64, 128 * tile : 128 * tile + 128]
                to[at], to[at + 1] = pack_heads(both)
        for pair in range(PAIRS):
            exchange.to(pair_device(pair), to.at[pair], out_grads.at[layer, me])
        return exchange

    def attention(layer, exchange, between):
        name = "_" + str(layer)
        rows = kept["rows" + name]
        length = slot_length(lengths, exchange.pair)

        @pl.when(exchange.has_pair)
        def _():
            all_rows = rows[:, 0:64].reshape(LENGTH, 128).astype(F32)
            keys_turned[...] = all_rows.T[0:64].astype(BF)
            key_grad[...] = jnp.zeros_like(key_grad)

        exchange.wait(to_pairs, out_grads.at[layer], "pairs")
        back = Exchange(pair_sems.at[2 * layer + 1])
        for at in reversed(range(BLOCKS)):

            @pl.when(exchange.has_pair)
            def _(at=at):
                attend_back_block(
                    back,
                    at,
                    length,
                    rows,
                    out_grads.at[layer],
                    kept["turned" + name],
                    kept["total" + name],
                    keys_turned,
                    key_grad,
                    to_places,
                    incoming.at[layer],
                )

            stages(*between.get(at, ()))
        stages(*between.get("sent", ()))
        back.wait(to_places, incoming.at[layer], "places")
        collect_projections(incoming.at[layer], cosine[...], sine[...], stacked)

    def source_gradient(layer, source):
        load("qkv", layer).wait()
        given["norm"][...] = turned_low(source.astype(BF))
        for at in range(3):
            given["low"][0, at] = stacked[at, :, 0:384]
            given["low"][1, at] = stacked[at, :, 384:768]
        copies = share(layer, PROJECTED)
        start(copies)
        result = jnp.zeros((128, 768), F32)
        for at in range(3):
            result = result + lax.dot_general(
                stacked[at],
                weights["qkv"][at].reshape(768, 768),
                LAST_DIMS,
                preferred_element_type=F32,
            )
        return result, copies

    normed_two, _ = norm_forward(residual_1[...], gain(3))
    fed_grad = feed(1, normed_two, cotangent[...])
    for name in ("down", "wide"):
        load(name, 0).start()
    load_paired(0).start()
    through, gain_grad = norm_backward(fed_grad, residual_1[...], gain(3))
    gain_grads[...] = jnp.zeros_like(gain_grads)
    gain_grads[3:4, :] = gain_grad
    residual_grad = cotangent[...] + through
    pl.semaphore_wait(barrier, len(neighbours))
    exchange = send_out_grad(1, residual_grad)
    load("out", 0).start()
    copies = share(1, FED + MIXED)
    start(copies)
    finish(copies)
    wide_grads(1)
    stages((wide, 1, 1))
    narrow_grads(1)
    stages((narrow, 1, 1))
    attention(
        1,
        exchange,
        {6: [(wide, 1, 2)], 4: [(narrow, 1, 2)], "sent": [(wide, 1, 3), (narrow, 1, 3)]},
    )
    shallow, _ = norm_forward(summed_0[...], gain(1))
    normed, _ = norm_forward(shallow, gain(2))
    normed_grad, copies = source_gradient(1, normed)
    load("qkv", 0).start()
    stages((wide, 1, 4), (narrow, 1, 4))
    through, gain_grad = norm_backward(normed_grad, shallow, gain(2))
    gain_grads[2:3, :] = gain_grad
    shallow_grad = residual_grad + through
    summed_grad, gain_grad = norm_backward(shallow_grad, summed_0[...], gain(1))
    gain_grads[1:2, :] = gain_grad

    finish(loads)
    finish(copies)
    projection_grads(1)
    stages(("qkv", 1, 1))
    middle, _ = norm_forward(residual_0[...], gain(0))
    fed_grad = feed(0, middle, summed_grad)
    middle_grad = summed_grad + fed_grad
    residual_grad, gain_grad = norm_backward(middle_grad, residual_0[...], gain(0))
    gain_grads[0:1, :] = gain_grad
    exchange = send_out_grad(0, residual_grad)
    copies = share(0, FED + MIXED)
    start(copies)
    stages(("qkv", 1, 2), (wide, 1, 5), (narrow, 1, 5))
    finish(copies)
    wide_grads(0)
    stages((wide, 0, 0))
    narrow_grads(0)
    stages((narrow, 0, 1), (wide, 1, 6), (narrow, 1, 6))
    attention(
        0,
        exchange,
        {
            6: [("qkv", 1, 3)],
            4: [(narrow, 0, 2)],
            0: [("qkv", 1, 4)],
            "sent": [(narrow, 0, 3)],
        },
    )
    source_grad, copies = source_gradient(0, stream[...])
    swap = remote(
        gain_grads, their_gains, give_sems.at[0, len(SHARED), 0], give_sems.at[0, len(SHARED), 1], axes.partner
    )
    swap.start()
    input_grad[...] = residual_grad + source_grad
    stages(("qkv", 1, 5))
    finish(copies)
    projection_grads(0)
    swap.wait()
    gain_total = gain_grads[...] + their_gains[...]
    gain_total = jnp.concatenate([gain_total, jnp.zeros((8, 128), F32)], axis=1)
    for z in range(4):
        for y in range(4):
            first, second = (24 * (8 * z + 2 * y + which) // 128 * 128 for which in (0, 1))
            parts["gain", 0].total[y, z] = jnp.where(
                core == 0, gain_total[:, first : first + 256], gain_total[:, second : second + 256]
            )
    last = ("q", "k", "v", "gain")
    stages((last, 0, 1), (narrow, 0, 4), ("qkv", 1, 6), (wide, 0, 1))
    stages((last, 0, 2), (wide, 0, 2), (narrow, 0, 5))
    stages((last, 0, 3), (wide, 0, 3), (narrow, 0, 6))
    stages((last, 0, 4), (wide, 0, 4), (last, 0, 5), (wide, 0, 5), (last, 0, 6), (wide, 0, 6))


def run_backward(lengths, kept, store, cosine, sine):
    near = [kept["cotangent"], kept["stream"]] + [
        kept[name] for name in ("mid_0", "summed_0", "mid_1", "gain")
    ]
    near += [cosine, sine] + [kept[name] for name in KEPT_1]
    away = [kept[name] for name in KEPT_0 + ("paired_0", "paired_1")] + [store[key] for key in GATHERED[:-1]]
    shared, own = part_scratch()
    results = pl.pallas_call(
        backward_kernel,
        out_shape=[jax.ShapeDtypeStruct((128, 768), F32)]
        + [jax.ShapeDtypeStruct(*shape) for shape in SUMS.values()],
        in_specs=[SMEM] + [VMEM] * len(near) + [ANY] * len(away),
        out_specs=[VMEM] * (1 + len(SUMS)),
        scratch_shapes=[pltpu.VMEM(*KEPT_TYPES[name]) for name in KEPT_0 + ("paired_0",)]
        + [pltpu.VMEM(*WEIGHTS[name]) for name in WEIGHT_ORDER]
        + shared
        + own
        + [pltpu.VMEM(here, BF) for here, _ in SHARED.values()]
        + [pltpu.VMEM(there, BF) for _, there in SHARED.values()] * 2
        + [
            pltpu.VMEM((2, 32, 32, 128), BF),
            pltpu.VMEM((PAIRS, 32, 128), BF),
            pltpu.VMEM((32, MESSAGE, 128), BF),
            pltpu.VMEM((2, PAIRS, MESSAGE, 128), BF),
            pltpu.VMEM((64, LENGTH), BF),
            pltpu.VMEM((LENGTH, 128), F32),
            pltpu.VMEM((8, 768), F32),
            pltpu.VMEM((8, 768), F32),
            pltpu.VMEM((3, 128, 768), BF),
            pltpu.SemaphoreType.DMA((2 * len(PARTS), SCATTER_SEMAPHORES)),
            pltpu.SemaphoreType.DMA((2, len(SHARED) + 1, 2)),
            pltpu.SemaphoreType.DMA((9,)),
            pltpu.SemaphoreType.DMA((4, 3)),
        ],
        compiler_params=params(2),
        name="backward",
    )(lengths, *near, *away)
    return results[0], dict(zip(SUMS, results[1:]))


def angles(places):
    half_dim = HEAD_DIM // 2
    frequency = jnp.exp(-math.log(10000.0) * jnp.arange(half_dim).astype(F32) / half_dim)
    phases = places.astype(F32)[:, None] * frequency[None, :]
    cosine, sine = jnp.cos(phases), jnp.sin(phases)
    return (
        jnp.concatenate([cosine] * 4, axis=1),
        jnp.concatenate([-sine, sine] * 2, axis=1),
    )


def update(weight_matrix, moment, average, gradient, step_size):
    moment_new = MOMENTUM * moment + gradient
    weight_new = weight_matrix - step_size * (gradient + MOMENTUM * moment_new)
    return (moment_new, weight_new, AVERAGING * average + (1.0 - AVERAGING) * weight_new)


def by_place(values):
    return values.reshape(2, SPAN, 768).transpose(1, 0, 2)[None]


def on_device(
    inputs,
    cotangent,
    lengths,
    qkv_weight,
    qkv_moment,
    qkv_average,
    out_weight,
    out_moment,
    out_average,
    gate_up_weight,
    gate_up_moment,
    gate_up_average,
    down_weight,
    down_moment,
    down_average,
    norm_gains,
    gain_moment,
    gain_average,
):
    places = lax.axis_index("seq") * SPAN + jnp.arange(SPAN)
    cosine, sine = angles(places)
    seq = lax.axis_index("seq")
    own_gains = lax.dynamic_update_slice(
        jnp.zeros((8, 256), F32),
        norm_gains.astype(BF).astype(F32).reshape(4, 24),
        (0, lax.rem(24 * seq, 128)),
    )
    store, kept = run_forward(
        lengths[0],
        qkv_weight,
        out_weight,
        gate_up_weight,
        down_weight,
        own_gains,
        inputs[0],
        cotangent[0],
        cosine,
        sine,
    )
    input_grad, sums = run_backward(
        lengths[0], kept, store, cosine, sine
    )
    gain_sum = lax.dynamic_slice(
        sums["gain"][0], (0, lax.rem(24 * seq, 128)), (4, 24)
    ).reshape(2, 2, 24)

    step_size = STEP_RATE / math.sqrt(
        lax.axis_size("batch") * SPAN * lax.axis_size("seq") * 2
    )
    qkv_new = update(qkv_weight, qkv_moment, qkv_average, sums["qkv"], step_size)
    out_new = update(out_weight, out_moment, out_average, sums["out"], step_size)
    gate_up_new = update(gate_up_weight, gate_up_moment, gate_up_average, sums["wide"], step_size)
    down_new = update(down_weight, down_moment, down_average, sums["down"], step_size)
    gain_new = update(norm_gains, gain_moment, gain_average, gain_sum, step_size)
    return (
        by_place(kept["result"]),
        by_place(input_grad),
        *qkv_new,
        *out_new,
        *gate_up_new,
        *down_new,
        *gain_new,
    )


def solution(mesh):
    rows = P("batch", "seq", None, None)
    wide = P(None, None, "seq", None)
    flat = P(None, "seq", None)
    gains = P(None, None, "seq")
    state = (wide,) * 3 + (flat,) * 3 + (wide,) * 3 + (flat,) * 3 + (gains,) * 3
    return jax.shard_map(
        on_device,
        mesh=mesh,
        in_specs=(rows, rows, P("batch", None)) + state,
        out_specs=(rows, rows) + state,
        check_vma=False,
    )
```

```python
import functools
import math

import jax
import jax.numpy as jnp
from jax import lax
from jax.experimental import pallas as pl
from jax.experimental.pallas import tpu as pltpu
from jax.sharding import PartitionSpec as P

MESH = pl.DeviceIdType.MESH
BF = jnp.bfloat16
F32 = jnp.float32
BATCH, SEQ = "batch", "seq"
HEAD_DIM = 64
HEADS = 12
PAIRS = 24
SPAN = 64
LENGTH = 2048
BLOCK = 256
EPSILON = 1e-06
MOMENTUM = 0.5
AVERAGING = 0.5
STEP_RATE = 0.1
MASKED = -1e30
VMEM_BYTES = 62 * 2**20
VMEM = pl.BlockSpec(memory_space=pltpu.VMEM)
ANY = pl.BlockSpec(memory_space=pl.ANY)
SMEM = pl.BlockSpec(memory_space=pltpu.SMEM)
ALL = pl.ds(0, 4)


def params(collective_id):
    return pltpu.CompilerParams(
        collective_id=collective_id, has_side_effects=True, vmem_limit_bytes=VMEM_BYTES
    )


def coordinates():
    seq = lax.axis_index(SEQ)
    return (
        lax.axis_index(BATCH),
        lax.div(seq, 8),
        lax.rem(lax.div(seq, 2), 4),
        lax.rem(seq, 2),
    )


def device(x, z, y, core):
    return (x, (z * 4 + y) * 2 + core)


def shifted(value, by):
    return lax.rem(value + by, 4)


def signal(partners):
    barrier = pltpu.get_barrier_semaphore()
    for partner in partners:
        pl.semaphore_signal(barrier, inc=1, device_id=partner, device_id_type=MESH)


def greet(partners):
    signal(partners)
    pl.semaphore_wait(pltpu.get_barrier_semaphore(), len(partners))


def remote(source, target, send, receive, where):
    return pltpu.make_async_remote_copy(
        src_ref=source,
        dst_ref=target,
        send_sem=send,
        recv_sem=receive,
        device_id=where,
        device_id_type=MESH,
    )


class Axes:
    def __init__(self, first_is_y):
        x, z, y, core = coordinates()
        self.first_is_y = first_is_y
        self.x, self.z, self.y, self.core = x, z, y, core
        self.m1, self.m2 = (y, z) if first_is_y else (z, y)
        self.partner = device(x, z, y, 1 - core)

    def along_y(self, by):
        return device(self.x, self.z, shifted(self.y, by), self.core)

    def along_z(self, by):
        return device(self.x, shifted(self.z, by), self.y, self.core)

    def first(self, by):
        return self.along_y(by) if self.first_is_y else self.along_z(by)

    def second(self, by):
        return self.along_z(by) if self.first_is_y else self.along_y(by)

    def order(self, i1, i2):
        return (i2, i1) if self.first_is_y else (i1, i2)


class GatherSegment:
    def __init__(self, first_is_y, view, semaphores, own=None):
        self.axes = Axes(first_is_y)
        self.view, self.own, self.semaphores = view, own, semaphores

    def block(self, i1, i2):
        return self.view(*self.axes.order(i1, i2))

    def row(self, by, part=ALL):
        return self.block(part, shifted(self.axes.m2, by))

    def keep(self):
        here = self.block(self.axes.m1, self.axes.m2)
        return pltpu.make_async_copy(self.own, here, self.semaphores.at[3, 0])

    def begin(self, phase):
        axes = self.axes
        sem = [self.semaphores.at[phase, at] for at in range(4)]

        def send(part, where):
            remote(part, part, sem[0], sem[1], where).start()

        def share(part):
            remote(part, part, sem[2], sem[3], axes.partner).start()

        if phase == 0:
            here = self.block(axes.m1, axes.m2)
            source = here if self.own is None else self.own
            for by in (1, 3, 2):
                remote(source, here, sem[0], sem[1], axes.first(by)).start()
        elif phase == 1:
            send(self.row(0), axes.second(1))
            send(self.row(0), axes.second(3))
            share(self.row(0))
        elif phase == 2:
            send(self.row(3, pl.ds(0, 2)), axes.second(1))
            send(self.row(1, pl.ds(2, 2)), axes.second(3))
            share(self.row(3))
            share(self.row(1))
        else:
            share(self.row(2))

    def end(self, phase):
        axes = self.axes
        sem = [self.semaphores.at[phase, at] for at in range(4)]
        one, two = self.row(0), self.block(ALL, pl.ds(0, 2))
        moved = (self.block(pl.ds(0, 3), axes.m2), two, one, None)[phase]
        shared = (None, one, two, one)[phase]
        if moved is not None:
            remote(moved, moved, sem[0], sem[1], axes.partner).wait()
        if shared is not None:
            remote(shared, shared, sem[2], sem[3], axes.partner).wait()


class AcrossSegment(GatherSegment):
    def __init__(self, first_is_y, quarters, semaphores, own):
        x = lax.axis_index(BATCH)
        super().__init__(first_is_y, lambda z, y: quarters(z, y, x, 1), semaphores, own)
        self.quarters = quarters

    def begin(self, phase):
        axes = self.axes
        sem = [self.semaphores.at[phase, at] for at in range(4)]

        def send(part, where):
            remote(part, part, sem[0], sem[1], where).start()

        def share(part):
            remote(part, part, sem[2], sem[3], axes.partner).start()

        if phase == 0:
            here = self.block(axes.m1, axes.m2)
            for by in (1, 3, 2):
                remote(self.own, here, sem[0], sem[1], axes.first(by)).start()
        elif phase == 1:
            send(self.row(0), axes.second(1))
            send(self.row(0), axes.second(3))
        elif phase == 2:
            send(self.row(3, pl.ds(0, 2)), axes.second(1))
            send(self.row(1, pl.ds(2, 2)), axes.second(3))
        elif phase == 3:
            mine = self.block(ALL, ALL)
            for by in (1, 3, 2):
                send(mine, device(shifted(axes.x, by), axes.z, axes.y, axes.core))
            share(mine)
        else:
            for by in (1, 3, 2):
                share(self.quarters(ALL, ALL, shifted(axes.x, by), 1))

    def end(self, phase):
        axes = self.axes
        sem = [self.semaphores.at[phase, at] for at in range(4)]
        three = self.quarters(ALL, ALL, 0, 3)
        mine = self.block(ALL, ALL)
        moved = (
            self.block(pl.ds(0, 3), axes.m2),
            self.block(ALL, pl.ds(0, 2)),
            self.row(0),
            three,
            None,
        )[phase]
        shared = (None, None, None, mine, three)[phase]
        if moved is not None:
            remote(moved, moved, sem[0], sem[1], axes.partner).wait()
        if shared is not None:
            remote(shared, shared, sem[2], sem[3], axes.partner).wait()


def across_views(name, ref):
    core = Axes(True).core

    def columns(first, count):
        return pl.ds(pl.multiple_of(core * 1024 + first * 256, 128), 256 * count)

    def rows(first, count):
        return pl.ds(pl.multiple_of(first * 16, 16), 16 * count)

    if name == "wide":
        return [
            (True, lambda z, y, first, count: ref.at[0, z, y, :, columns(first, count)]),
            (False, lambda z, y, first, count: ref.at[1, z, y, :, columns(first, count)]),
        ]
    return [
        (True, lambda z, y, first, count: ref.at[z, y, core, rows(first, count), pl.ds(0, 384)]),
        (False, lambda z, y, first, count: ref.at[z, y, core, rows(first, count), pl.ds(384, 384)]),
    ]


def across_owns(name, ref):
    axes = Axes(True)
    if name == "wide":
        columns = pl.ds(pl.multiple_of(axes.core * 1024 + axes.x * 256, 128), 256)
        return [ref.at[0, :, columns], ref.at[1, :, columns]]
    rows = pl.ds(pl.multiple_of(axes.x * 16, 16), 16)
    return [ref.at[rows, pl.ds(0, 384)], ref.at[rows, pl.ds(384, 384)]]


ACROSS = (("wide", 1), ("down", 0))


def halves(core, width):
    return pl.ds(pl.multiple_of(core * (width // 2), 128), width // 2)


def weight_views(name, ref):
    core = Axes(True).core
    narrow, wide = halves(core, 768), halves(core, 2048)
    if name == "qkv":
        return [
            (True, lambda z, y: ref.at[pl.ds(0, 2), z, y, :, narrow]),
            (False, lambda z, y: ref.at[2, z, y, :, narrow]),
        ]
    if name == "out":
        return [(False, lambda z, y: ref.at[z, y, :, narrow])]
    if name == "wide":
        return [
            (True, lambda z, y: ref.at[0, z, y, :, wide]),
            (False, lambda z, y: ref.at[1, z, y, :, wide]),
        ]
    if name == "down":
        return [
            (True, lambda z, y: ref.at[z, y, core, :, pl.ds(0, 384)]),
            (False, lambda z, y: ref.at[z, y, core, :, pl.ds(384, 384)]),
        ]
    return [(True, lambda z, y: ref.at[z, y, core])]


def own_views(name, ref):
    core = Axes(True).core
    narrow, wide = halves(core, 768), halves(core, 2048)
    if name == "qkv":
        return [ref.at[pl.ds(0, 2), :, narrow], ref.at[2, :, narrow]]
    if name == "out":
        return [ref.at[:, narrow]]
    if name == "wide":
        return [ref.at[0, :, wide], ref.at[1, :, wide]]
    if name == "down":
        return [ref.at[:, pl.ds(0, 384)], ref.at[:, pl.ds(384, 384)]]
    return [ref]


WEIGHTS = {
    "qkv": ((3, 4, 4, 48, 768), BF),
    "out": ((4, 4, 48, 768), BF),
    "wide": ((2, 4, 4, 48, 2048), BF),
    "down": ((4, 4, 2, 64, 768), BF),
    "gain": ((4, 4, 2, 8, 256), F32),
}
SEGMENTS = {"qkv": 2, "out": 1, "wide": 2, "down": 2, "gain": 1}
GATHERED = [(name, layer) for layer in range(2) for name in ("qkv", "out", "wide", "down")] + [
    ("gain", 0)
]


def weight_shape(key):
    return jax.ShapeDtypeStruct(*WEIGHTS[key[0]])


class ScatterPart:
    def __init__(self, first_is_y, total, rows, ring, blocks, groups, semaphores, finish):
        self.axes = Axes(first_is_y)
        self.total, self.rows, self.ring, self.blocks, self.groups = total, rows, ring, blocks, groups
        self.semaphores, self.finish = semaphores, finish

    def fill(self, z, value):
        if self.axes.first_is_y:
            self.total[z] = value
        else:
            self.total[:, z] = value

    def spread(self):
        axes, sem = self.axes, self.semaphores
        for by in (1, 3, 2):
            remote(
                self.total.at[axes.m2, shifted(axes.m1, by)],
                self.blocks.at[by - 1],
                sem.at[4],
                sem.at[5],
                axes.first(by),
            ).start()

    def stage(self, number):
        axes, sem, total = self.axes, self.semaphores, self.total
        m1, m2 = axes.m1, axes.m2
        before, after, across = shifted(m2, 3), shifted(m2, 1), shifted(m2, 2)
        low, high = pl.ds(0, 2), pl.ds(2, 2)

        def add(target, source):
            target[...] = (target[...].astype(F32) + source[...].astype(F32)).astype(target.dtype)

        if number == 1:
            remote(
                total.at[across, low], self.ring.at[0], sem.at[0], sem.at[1], axes.second(1)
            ).start()
            remote(
                total.at[across, high], self.ring.at[1], sem.at[0], sem.at[1], axes.second(3)
            ).start()
        elif number == 2:
            row = total.at[m2]
            remote(row, self.ring, sem.at[0], sem.at[1], axes.partner).wait()
            add(total.at[after, low], self.ring.at[0])
            add(total.at[before, high], self.ring.at[1])
            remote(
                total.at[after], self.rows.at[0], sem.at[2], sem.at[3], axes.second(1)
            ).start()
            remote(
                total.at[before], self.rows.at[1], sem.at[2], sem.at[3], axes.second(3)
            ).start()
        elif number == 3:
            remote(self.rows, self.rows, sem.at[2], sem.at[3], axes.partner).wait()
            for at in range(4):
                total[m2, at] = (
                    total[m2, at].astype(F32)
                    + self.rows[0, at].astype(F32)
                    + self.rows[1, at].astype(F32)
                ).astype(total.dtype)
            self.spread()
        elif number == 4:
            remote(self.blocks, self.blocks, sem.at[4], sem.at[5], axes.partner).wait()
            self.groups[axes.x] = (
                total[m2, m1].astype(F32)
                + self.blocks[0].astype(F32)
                + self.blocks[1].astype(F32)
                + self.blocks[2].astype(F32)
            ).astype(total.dtype)
            mine = self.groups.at[axes.x]
            for by in (1, 3, 2):
                remote(
                    mine,
                    mine,
                    sem.at[6],
                    sem.at[7],
                    device(shifted(axes.x, by), axes.z, axes.y, axes.core),
                ).start()
        elif number == 5:
            three = self.groups.at[pl.ds(0, 3)]
            remote(three, three, sem.at[6], sem.at[7], axes.partner).wait()
            summed = self.groups[0].astype(F32)
            for at in range(1, 4):
                summed = summed + self.groups[at].astype(F32)
            self.finish(0, summed)
        else:
            self.finish(1, None)


class AcrossPart(ScatterPart):
    def __init__(self, first_is_y, whole, quarter, came, rows, ring, blocks, groups, semaphores, finish):
        super().__init__(first_is_y, quarter, rows, ring, blocks, groups, semaphores, finish)
        self.whole, self.came = whole, came

    def fill(self, z, value):
        if self.axes.first_is_y:
            self.whole[z] = value
        else:
            self.whole[:, z] = value

    def columns(self, at):
        return pl.ds(pl.multiple_of(at * 256, 128), 256)

    def stage(self, number):
        axes, sem = self.axes, self.semaphores
        if number == 0:
            for by in (1, 3, 2):
                there = shifted(axes.x, by)
                remote(
                    self.whole.at[:, :, :, self.columns(there)],
                    self.came.at[by - 1],
                    sem.at[10],
                    sem.at[11],
                    device(there, axes.z, axes.y, axes.core),
                ).start()
            return
        if number == 1:
            remote(self.came, self.came, sem.at[10], sem.at[11], axes.partner).wait()
            for at in range(4):
                summed = self.whole[at, :, :, self.columns(axes.x)].astype(F32)
                for by in range(3):
                    summed = summed + self.came[by, at].astype(F32)
                self.total[at] = summed.astype(BF)
        if number == 5:
            three = self.groups.at[pl.ds(0, 3)]
            remote(three, three, sem.at[6], sem.at[7], axes.partner).wait()
            quarters = [self.groups[at].astype(F32) for at in range(4)]
            self.finish(0, jnp.concatenate(quarters, axis=1))
            return
        super().stage(number)


class StraightPart(ScatterPart):
    def stage(self, number):
        axes, sem = self.axes, self.semaphores
        m2 = axes.m2
        if number == 1:
            for by in (1, 3, 2):
                remote(
                    self.total.at[shifted(m2, by)],
                    self.rows.at[by - 1],
                    sem.at[2],
                    sem.at[3],
                    axes.second(by),
                ).start()
        elif number == 2:
            remote(self.rows, self.rows, sem.at[2], sem.at[3], axes.partner).wait()
            for at in range(4):
                summed = self.total[m2, at].astype(F32)
                for by in range(3):
                    summed = summed + self.rows[by, at].astype(F32)
                self.total[m2, at] = summed.astype(self.total.dtype)
            self.spread()
        elif number != 3:
            super().stage(number)


SCATTER_SEMAPHORES = 12
ACROSS_PARTS = (("gate", 0), ("up", 0), ("gate", 1), ("up", 1))
LAST_PARTS = (("q", 0), ("k", 0), ("v", 0), ("gain", 0))
PARTS = {
    "gate": (True, 48, 1024, BF),
    "up": (False, 48, 1024, BF),
    "left": (True, 64, 384, BF),
    "right": (False, 64, 384, BF),
    "o": (False, 48, 384, BF),
    "q": (True, 48, 384, BF),
    "k": (False, 48, 384, BF),
    "v": (True, 48, 384, BF),
    "gain": (False, 8, 256, F32),
}
SOURCE = {
    "q": "qkv", "k": "qkv", "v": "qkv", "o": "out", "gate": "wide", "up": "wide",
    "left": "down", "right": "down", "gain": "gain",
}
SUMS = {
    "qkv": ((2, 3, 24, 768), F32),
    "out": ((2, 24, 768), F32),
    "wide": ((2, 2, 24, 2048), F32),
    "down": ((2, 64, 768), F32),
    "gain": ((1, 8, 256), F32),
}
LEFT, RIGHT = pl.ds(0, 384), pl.ds(384, 384)


def part_target(part, ref):
    if part in ("q", "k", "v"):
        return ref.at["qkv".index(part)]
    if part in ("gate", "up"):
        return ref.at[int(part == "up")]
    if part in ("left", "right"):
        return ref.at[:, LEFT if part == "left" else RIGHT]
    return ref


def rows_swapped(target, mine, theirs, sem):
    axes = Axes(True)
    core = axes.core

    def finish(part, summed):
        own_rows = pl.ds(pl.multiple_of(core * 24, 8), 24)
        other_rows = pl.ds(pl.multiple_of((1 - core) * 24, 8), 24)
        copy = remote(mine.at[other_rows, :], theirs, sem.at[8], sem.at[9], axes.partner)
        if part == 0:
            mine[...] = summed
            copy.start()
        else:
            copy.wait()
            kept = mine[own_rows, :]
            got = theirs[...]
            width = kept.shape[-1]
            target[:, :width] = jnp.where(core == 0, kept, got)
            target[:, width:] = jnp.where(core == 0, got, kept)

    return finish


def direct(target):
    def finish(part, summed):
        if part == 0:
            target[...] = summed

    return finish


def part_scratch():
    shared, own = [], []
    for part, (_, rows, width, kind) in PARTS.items():
        shared += [
            pltpu.VMEM((4, 4, rows, width), kind),
            pltpu.VMEM((8, 128) if part in ("gate", "up", "gain") else (2, 4, rows, width), kind),
            pltpu.VMEM((48, width), F32) if rows == 48 else pltpu.VMEM((8, 128), F32),
        ]
        for layer in range(1 if part == "gain" else 2):
            across = (part, layer) in ACROSS_PARTS
            if across:
                own += [
                    pltpu.VMEM((4, 4, rows, width // 4), kind),
                    pltpu.VMEM((3, 4, 4, rows, width // 4), kind),
                    pltpu.VMEM((2, 4, rows, width // 4), kind),
                ]
            narrow = width // 4 if across else width
            straight = (part, layer) in LAST_PARTS
            own += [
                pltpu.VMEM((3, 4, rows, width) if straight else (2, 2, rows, narrow), kind),
                pltpu.VMEM((3, rows, narrow), kind),
                pltpu.VMEM((4, rows, narrow), kind),
                pltpu.VMEM((24, width), F32) if rows == 48 else pltpu.VMEM((8, 128), F32),
            ]
    return shared, own


def build_parts(shared, own, sems, sums):
    parts = {}
    count = 0
    own = list(own)

    def take(number):
        taken = own[:number]
        del own[:number]
        return taken

    for at, (part, (first_is_y, rows, _, _)) in enumerate(PARTS.items()):
        total, rows_in, mine = shared[3 * at : 3 * at + 3]
        for layer in (0,) if part == "gain" else (0, 1):
            if (part, layer) in ACROSS_PARTS:
                quarter, came, rows_here = take(3)
            ring, blocks, groups, theirs = take(4)
            target = part_target(part, sums[SOURCE[part]].at[layer])
            sem = sems.at[count]
            finish = rows_swapped(target, mine, theirs, sem) if rows == 48 else direct(target)
            if (part, layer) in ACROSS_PARTS:
                parts[part, layer] = AcrossPart(
                    first_is_y, total, quarter, came, rows_here, ring, blocks, groups, sem, finish
                )
            elif (part, layer) in LAST_PARTS:
                parts[part, layer] = StraightPart(
                    first_is_y, total, ring, None, blocks, groups, sem, finish
                )
            else:
                parts[part, layer] = ScatterPart(
                    first_is_y, total, rows_in, ring, blocks, groups, sem, finish
                )
            count += 1
    return parts


def pair_device(pair):
    if pair < 16:
        return 2 * pair
    z = (pair - 16) // 2
    return 2 * (4 * z + 2 * ((pair - 16) % 2) + z % 2) + 1


def own_pair():
    _, z, y, core = coordinates()
    has_pair = (core == 0) | (lax.rem(z + y, 2) == 0)
    pair = jnp.where(core == 0, 4 * z + y, 16 + 2 * z + lax.div(y, 2))
    return has_pair, pair


def lanes(shape):
    return lax.broadcasted_iota(jnp.int32, shape, len(shape) - 1)


def turned(values, cosine, sine):
    here = lax.rem(lanes(values.shape), 64) < 32
    width = values.shape[-1]
    other = jnp.where(here, pltpu.roll(values, width - 32, 1), pltpu.roll(values, 32, 1))
    return values * cosine + other * sine


def twice(table):
    return jnp.concatenate([table, table], axis=0)


def allowed_keys(first_key, first_query, keys, queries, length):
    key = first_key + lax.broadcasted_iota(jnp.int32, (keys, queries), 0)
    query = first_query + lax.broadcasted_iota(jnp.int32, (keys, queries), 1)
    return (key <= query) & (key < length)


def slot_length(lengths, pair):
    return jnp.where(pair < HEADS, lengths[0], lengths[1])


LAST_DIMS = (((1,), (1,)), ((), ()))
BLOCKS = LENGTH // BLOCK
MESSAGE = 96


def front_lanes(rows):
    return lanes((rows, 128)) < 64


def pack_heads(both):
    front = front_lanes(32)
    top, bottom = both[0:32], both[32:64]
    return (
        jnp.where(front, top, pltpu.roll(bottom, 64, 1)).astype(BF),
        jnp.where(front, pltpu.roll(top, 64, 1), bottom).astype(BF),
    )


def unpack_heads(first, second):
    front = front_lanes(32)
    first, second = first.astype(F32), second.astype(F32)
    return jnp.concatenate(
        [
            jnp.where(front, first, pltpu.roll(second, 64, 1)),
            jnp.where(front, pltpu.roll(first, 64, 1), second),
        ],
        axis=0,
    )


def unpack_block(packed, to_front):
    packed = packed.astype(F32).reshape(128, 128)
    other = pltpu.roll(packed, 64, 1)
    front = front_lanes(128)
    if to_front:
        top, bottom = jnp.where(front, packed, 0.0), jnp.where(front, other, 0.0)
    else:
        top, bottom = jnp.where(front, 0.0, other), jnp.where(front, 0.0, packed)
    joined = jnp.concatenate([top.reshape(4, 32, 128), bottom.reshape(4, 32, 128)], axis=1)
    return joined.reshape(256, 128).astype(BF)


def pack_turned(turned_values):
    rows = jnp.concatenate([turned_values, turned_values], axis=0).T.reshape(4, 64, 128)
    front = lanes((4, 32, 128)) < 64
    return jnp.where(front, rows[:, 0:32], rows[:, 32:64]).astype(BF)


class Exchange:
    def __init__(self, semaphores):
        self.x, self.me = lax.axis_index(BATCH), lax.axis_index(SEQ)
        self.has_pair, self.pair = own_pair()
        self.send, self.receive, self.local = (semaphores.at[at] for at in range(3))

    def to(self, there, source, target):
        @pl.when(self.me != there)
        def _():
            remote(source, target, self.send, self.receive, (self.x, there)).start()

        @pl.when(self.me == there)
        def _():
            pltpu.make_async_copy(source, target, self.local).start()

    def wait(self, sent, got, where):
        if where == "pairs":
            sends, gets = (sent.shape[0], sent.shape[0] - 1), (None, got.shape[0] - 1)
        else:
            sends, gets = (None, sent.shape[0] - 1), (got.shape[0], got.shape[0] - 1)

        def wait_for(n_sent, n_got):
            if n_got is not None:
                part = got.at[pl.ds(0, n_got)]
                remote(part, part, self.send, self.receive, (self.x, self.me)).wait_recv()
            if n_sent is not None:
                part = sent.at[pl.ds(0, n_sent)]
                remote(part, part, self.send, self.receive, (self.x, self.me)).wait_send()

        @pl.when(self.has_pair)
        def _():
            pltpu.make_async_copy(sent.at[0], got.at[0], self.local).wait()
            wait_for(sends[1], gets[1])

        @pl.when(jnp.logical_not(self.has_pair))
        def _():
            wait_for(sends[0], gets[0])


def send_projections(exchange, query, key, value, cosine, sine, outgoing, rows):
    cosine, sine = twice(cosine), twice(sine)
    front = front_lanes(64)
    for tile in range(6):
        cut = slice(128 * tile, 128 * tile + 128)
        q = turned(query[:, cut], cosine, sine) * (1.0 / math.sqrt(HEAD_DIM))
        k = turned(key[:, cut], cosine, sine)
        v = value[:, cut]
        for slot in range(2):
            span = slice(64 * slot, 64 * slot + 64)
            at = slot * HEADS + 2 * tile
            ks, vs = k[span], v[span]
            outgoing[at, 0:64] = jnp.where(front, ks, pltpu.roll(vs, 64, 1)).astype(BF)
            outgoing[at + 1, 0:64] = jnp.where(front, pltpu.roll(ks, 64, 1), vs).astype(BF)
            outgoing[at, 64:96], outgoing[at + 1, 64:96] = pack_heads(q[span])
    for pair in range(PAIRS):
        exchange.to(pair_device(pair), outgoing.at[pair], rows.at[exchange.me])


def attend_block(exchange, at, length, rows, values_turned, out_turned, log_total, outgoing, incoming):
    count = (at + 1) * BLOCK
    queries = unpack_block(rows[4 * at : 4 * at + 4, 64:96], True)
    keys = rows[0 : 4 * at + 4, 0:64].reshape(count, 128)
    scores = lax.dot_general(keys, queries, LAST_DIMS, preferred_element_type=F32)
    scores = jnp.where(allowed_keys(0, at * BLOCK, count, BLOCK, length), scores, MASKED)
    highest = jnp.max(scores, axis=0, keepdims=True)
    raised = jnp.exp(scores - highest)
    total = jnp.sum(raised, axis=0, keepdims=True)
    result = (
        jnp.dot(values_turned[:, 0:count], raised.astype(BF), preferred_element_type=F32) / total
    )
    cut = slice(at * BLOCK, count)
    out_turned[:, cut] = result
    log_total[:, cut] = jnp.broadcast_to(highest + jnp.log(total), (8, BLOCK))
    outgoing[4 * at : 4 * at + 4] = pack_turned(result)
    for there in range(4 * at, 4 * at + 4):
        exchange.to(there, outgoing.at[there], incoming.at[exchange.pair])


def merge_heads(incoming, merged):
    for slot in range(2):
        for tile in range(6):
            at = slot * HEADS + 2 * tile
            merged[64 * slot : 64 * slot + 64, 128 * tile : 128 * tile + 128] = unpack_heads(
                incoming[at], incoming[at + 1]
            ).astype(BF)


def norm_forward(values, norm_gain):
    inverse = lax.rsqrt(jnp.mean(values * values, axis=-1, keepdims=True) + EPSILON)
    return (values * inverse * norm_gain, inverse)


def feed_forward(rows_in, gate_up, down, paired):
    fed = jnp.zeros((128, 768), F32)
    for z in range(4):
        cut = slice(512 * z, 512 * z + 512)
        gate = jnp.dot(rows_in, gate_up[0, :, :, :, cut].reshape(768, 512), preferred_element_type=F32)
        up = jnp.dot(rows_in, gate_up[1, :, :, :, cut].reshape(768, 512), preferred_element_type=F32)
        paired[0, :, cut] = gate
        paired[1, :, cut] = up
        hidden = (jax.nn.silu(gate) * up).astype(BF)
        fed = fed + jnp.dot(hidden, down[z].reshape(512, 768), preferred_element_type=F32)
    return fed


KEPT = (
    [("result", (128, 768), F32), ("mid_0", (128, 768), F32), ("summed_0", (128, 768), F32)]
    + [("mid_1", (128, 768), F32), ("gain", (8, 768), F32)]
    + [("stream", (128, 768), BF), ("cotangent", (128, 768), F32)]
    + [
        (name + "_" + layer, shape, kind)
        for layer in "01"
        for name, shape, kind in (
            ("paired", (2, 128, 2048), F32),
            ("rows", (32, MESSAGE, 128), BF),
            ("merged", (128, 768), BF),
            ("turned", (64, LENGTH), F32),
            ("total", (8, LENGTH), F32),
        )
    ]
)


def forward_kernel(
    lengths, qkv, out, gate_up, down, gains, inputs, cotangents, cosine, sine, *refs
):
    stored = dict(zip(GATHERED[:-1], refs[:8]))
    kept = {name: ref for (name, _, _), ref in zip(KEPT, refs[8:])}
    refs = refs[8 + len(KEPT) :]
    store, refs = dict(zip(GATHERED, refs[:9])), refs[9:]
    their_qkv, their_out, their_gate_up, b_qkv, b_out, b_gate_up, b_down = refs[:7]
    outgoing, places, incoming, values_turned, stream, swap, sems, local, pair_sems = refs[7:]
    axes = Axes(True)
    core = axes.core
    x, me = lax.axis_index(BATCH), lax.axis_index(SEQ)
    greet(
        [(x, lax.rem(me + by, 32)) for by in range(1, 32)]
        + [device(shifted(x, by), axes.z, axes.y, core) for by in (1, 2, 3)]
    )
    swaps = [
        remote(mine, theirs, swap.at[0, at], swap.at[1, at], axes.partner)
        for at, (mine, theirs) in enumerate(
            (
                (qkv.at[0], their_qkv.at[0]),
                (qkv.at[1], their_qkv.at[1]),
                (out, their_out),
                (gate_up, their_gate_up),
            )
        )
    ]
    for copy in swaps:
        copy.start()
    for slot in range(2):
        stream[64 * slot : 64 * slot + 64] = inputs[:, slot, :]
        kept["cotangent"][64 * slot : 64 * slot + 64] = cotangents[:, slot, :]
    kept["stream"][...] = stream[...].astype(BF)

    def joined(mine, theirs):
        upper = jnp.where(core == 0, mine, theirs)
        lower = jnp.where(core == 0, theirs, mine)
        return jnp.concatenate([upper, lower], axis=0).astype(BF)

    segments = {}
    at = 0
    for key in GATHERED:
        name, layer = key
        block = {"qkv": b_qkv, "out": b_out, "wide": b_gate_up, "down": b_down}.get(name)
        block = gains if block is None else block.at[layer]
        kind, views, owns = GatherSegment, weight_views, own_views
        if key in ACROSS:
            kind, views, owns = AcrossSegment, across_views, across_owns
        segments[key] = []
        for (first_is_y, view), own in zip(views(name, store[key]), owns(name, block)):
            segments[key].append(kind(first_is_y, view, sems.at[at], own))
            at += 1

    def each(keys, act):
        for key in keys:
            for segment in segments[key]:
                act(segment)

    def keep(*keys):
        each(keys, lambda segment: segment.keep().start())
        each(keys, lambda segment: segment.keep().wait())

    def begin(phase, *keys):
        each(keys, lambda segment: segment.begin(phase))

    def end(phase, *keys):
        each(keys, lambda segment: segment.end(phase))

    saves = []

    def save(*keys):
        for key in keys:
            copy = pltpu.make_async_copy(store[key], stored[key], local.at[len(saves)])
            copy.start()
            saves.append(copy)

    qkv_0, out_0, wide_0, down_0 = GATHERED[0:4]
    qkv_1, out_1, wide_1, down_1 = GATHERED[4:8]
    gains_0 = GATHERED[8]

    swaps[0].wait()
    for at in range(3):
        b_qkv[0, at] = joined(qkv[0, at], their_qkv[0, at])
    begin(0, qkv_0)
    keep(qkv_0)
    b_down[0] = down[0].astype(BF)
    begin(0, down_0)
    keep(down_0)
    for copy in swaps[1:]:
        copy.wait()
    for at in range(2):
        b_gate_up[0, at] = joined(gate_up[0, at], their_gate_up[0, at])
    begin(0, wide_0)
    keep(wide_0)
    end(0, qkv_0)
    begin(1, qkv_0)
    end(0, down_0)
    begin(1, down_0)
    b_out[0] = joined(out[0], their_out[0])
    for at in range(2):
        b_gate_up[1, at] = joined(gate_up[1, at], their_gate_up[1, at])
    begin(0, out_0, gains_0, wide_1)
    keep(out_0, gains_0, wide_1)
    for at in range(3):
        b_qkv[1, at] = joined(qkv[1, at], their_qkv[1, at])
    b_out[1] = joined(out[1], their_out[1])
    b_down[1] = down[1].astype(BF)
    end(1, qkv_0)
    begin(2, qkv_0)
    end(1, down_0)
    begin(2, down_0)
    end(0, wide_0)
    begin(1, wide_0)
    end(2, qkv_0)
    begin(3, qkv_0)
    keep(qkv_1, out_1, down_1)
    end(2, down_0)
    begin(3, down_0)
    end(0, out_0, gains_0, wide_1)
    begin(1, wide_1)
    end(3, qkv_0)
    save(qkv_0)

    def attention(layer, source, before, between):
        weights = store["qkv", layer]
        name = "_" + str(layer)
        rows, merged = kept["rows" + name], kept["merged" + name]
        there = Exchange(pair_sems.at[2 * layer])
        back = Exchange(pair_sems.at[2 * layer + 1])
        low = source.astype(BF)
        query, key, value = (
            jnp.dot(low, weights[at].reshape(768, 768), preferred_element_type=F32)
            for at in range(3)
        )
        send_projections(
            there, query, key, value, cosine[...], sine[...], outgoing.at[layer], rows
        )
        before()
        there.wait(outgoing.at[layer], rows, "pairs")
        length = slot_length(lengths, there.pair)

        @pl.when(there.has_pair)
        def _():
            all_rows = rows[:, 0:64].reshape(LENGTH, 128).astype(F32)
            values_turned[...] = all_rows.T[64:128].astype(BF)

        for at in range(BLOCKS):

            @pl.when(there.has_pair)
            def _(at=at):
                attend_block(
                    back,
                    at,
                    length,
                    rows,
                    values_turned,
                    kept["turned" + name],
                    kept["total" + name],
                    places.at[layer],
                    incoming.at[layer],
                )

            if at in between:
                between[at]()
        back.wait(places.at[layer], incoming.at[layer], "places")
        merge_heads(incoming.at[layer], merged)
        between["after"]()
        out_matrix = store["out", layer][...].reshape(768, 768)
        return jnp.dot(merged[...], out_matrix, preferred_element_type=F32)

    def before_0():
        begin(1, out_0, gains_0)
        end(1, wide_1)
        begin(2, wide_1)

    def within_0():
        end(1, wide_0)
        begin(2, wide_0)
        end(2, wide_1)
        begin(3, wide_1)
        begin(0, qkv_1)

    def later_0():
        end(1, out_0, gains_0)
        begin(2, out_0, gains_0)

    def last_0():
        end(0, qkv_1)
        begin(1, qkv_1)

    def after_0():
        end(3, down_0)
        begin(4, down_0)
        end(2, wide_0, out_0, gains_0)
        begin(3, out_0, wide_0, gains_0)
        begin(0, out_1, down_1)
        end(3, out_0, wide_0, gains_0)
        end(4, down_0)
        save(out_0, wide_0, down_0)
        for device_at in range(32):
            piece = store[gains_0][device_at // 8, device_at // 2 % 4, device_at % 2]
            first = 24 * device_at // 128
            if device_at == 0:
                kept["gain"][...] = jnp.zeros((8, 768), F32)
            width = min(256, 768 - 128 * first)
            kept["gain"][:, 128 * first : 128 * first + width] += piece[:, :width]

    def gain(at):
        return kept["gain"][at : at + 1, :]

    mixed = attention(
        0, stream[...], before_0, {1: within_0, 4: later_0, 7: last_0, "after": after_0}
    )
    residual = stream[...] + mixed
    kept["mid_0"][...] = residual
    middle, _ = norm_forward(residual, gain(0))
    end(1, qkv_1)
    begin(2, qkv_1)
    fed = feed_forward(middle.astype(BF), store[wide_0], store[down_0], kept["paired_0"])
    end(2, qkv_1)
    begin(3, qkv_1)
    end(0, out_1, down_1)
    begin(1, out_1, down_1)
    summed = middle + fed
    kept["summed_0"][...] = summed
    shallow, _ = norm_forward(summed, gain(1))
    normed, _ = norm_forward(shallow, gain(2))
    end(3, qkv_1)
    save(qkv_1)

    def before_1():
        pass

    def within_1():
        end(1, out_1, down_1)
        begin(2, out_1, down_1)

    def later_1():
        end(3, wide_1)
        begin(4, wide_1)

    def after_1():
        end(2, out_1, down_1)
        begin(3, out_1, down_1)
        end(3, out_1, down_1)
        end(4, wide_1)
        save(out_1, wide_1, down_1)

    mixed = attention(1, normed, before_1, {1: within_1, 7: later_1, "after": after_1})
    residual = shallow + mixed
    kept["mid_1"][...] = residual
    normed_two, _ = norm_forward(residual, gain(3))
    fed = feed_forward(normed_two.astype(BF), store[wide_1], store[down_1], kept["paired_1"])
    kept["result"][...] = residual + fed
    for copy in saves:
        copy.wait()


def run_forward(*operands):
    count = sum(SEGMENTS[name] for name, _ in GATHERED)
    stored = GATHERED[:-1]
    results = pl.pallas_call(
        forward_kernel,
        out_shape=[weight_shape(key) for key in stored]
        + [jax.ShapeDtypeStruct(shape, kind) for _, shape, kind in KEPT],
        in_specs=[SMEM] + [VMEM] * 9,
        out_specs=[ANY] * 8 + [VMEM] * len(KEPT),
        scratch_shapes=[pltpu.VMEM(*WEIGHTS[name]) for name, _ in GATHERED]
        + [
            pltpu.VMEM((2, 3, 24, 768), F32),
            pltpu.VMEM((2, 24, 768), F32),
            pltpu.VMEM((2, 2, 24, 2048), F32),
            pltpu.VMEM((2, 3, 48, 768), BF),
            pltpu.VMEM((2, 48, 768), BF),
            pltpu.VMEM((2, 2, 48, 2048), BF),
            pltpu.VMEM((2, 64, 768), BF),
            pltpu.VMEM((2, PAIRS, MESSAGE, 128), BF),
            pltpu.VMEM((2, 32, 32, 128), BF),
            pltpu.VMEM((2, PAIRS, 32, 128), BF),
            pltpu.VMEM((64, LENGTH), BF),
            pltpu.VMEM((128, 768), F32),
            pltpu.SemaphoreType.DMA((2, 4)),
            pltpu.SemaphoreType.DMA((count, 5, 4)),
            pltpu.SemaphoreType.DMA((8,)),
            pltpu.SemaphoreType.DMA((4, 3)),
        ],
        compiler_params=params(1),
        name="forward",
    )(*operands)
    return dict(zip(stored, results)), {
        name: result for (name, _, _), result in zip(KEPT, results[8:])
    }


def attend_back_block(
    exchange, at, length, rows, out_grad, out_turned, log_total, keys_turned, key_grad, outgoing, incoming
):
    cut = slice(at * BLOCK, (at + 1) * BLOCK)
    four = slice(4 * at, 4 * at + 4)
    queries = unpack_block(rows[four, 64:96], True)
    outs = unpack_block(out_grad[four], False)
    outs_turned = outs.astype(F32).T[64:128]
    delta = jnp.sum(outs_turned * out_turned[:, cut], axis=0, keepdims=True)
    shift = log_total[0:1, cut]
    query_grad = jnp.zeros((64, BLOCK), F32)
    for part in range(at + 1):
        span = slice(part * BLOCK, (part + 1) * BLOCK)
        keys = rows[4 * part : 4 * part + 4, 0:64].reshape(BLOCK, 128)
        scores = lax.dot_general(keys, queries, LAST_DIMS, preferred_element_type=F32)
        allowed = allowed_keys(part * BLOCK, at * BLOCK, BLOCK, BLOCK, length)
        probs = jnp.where(allowed, jnp.exp(scores - shift), 0.0)
        probs_grad = lax.dot_general(keys, outs, LAST_DIMS, preferred_element_type=F32)
        score_grad = (probs * (probs_grad - delta)).astype(BF)
        key_grad[span, :] += jnp.dot(score_grad, queries, preferred_element_type=F32) + jnp.dot(
            probs.astype(BF), outs, preferred_element_type=F32
        )
        query_grad += jnp.dot(keys_turned[:, span], score_grad, preferred_element_type=F32)
    outgoing[four, 0:64] = key_grad[cut, :].reshape(4, SPAN, 128).astype(BF)
    outgoing[four, 64:96] = pack_turned(query_grad)
    for there in range(4 * at, 4 * at + 4):
        exchange.to(there, outgoing.at[there], incoming.at[exchange.pair])


def collect_projections(incoming, cosine, sine, result):
    front = front_lanes(64)
    for slot in range(2):
        span = slice(64 * slot, 64 * slot + 64)
        for tile in range(6):
            cut = slice(128 * tile, 128 * tile + 128)
            at = slot * HEADS + 2 * tile
            first, second = (incoming[at + n, 0:64].astype(F32) for n in (0, 1))
            q = unpack_heads(incoming[at, 64:96], incoming[at + 1, 64:96])
            k = jnp.where(front, first, pltpu.roll(second, 64, 1))
            v = jnp.where(front, pltpu.roll(first, 64, 1), second)
            q = turned(q * (1.0 / math.sqrt(HEAD_DIM)), cosine, -sine)
            result[0, span, cut] = q.astype(BF)
            result[1, span, cut] = turned(k, cosine, -sine).astype(BF)
            result[2, span, cut] = v.astype(BF)


def norm_backward(incoming, values, norm_gain):
    inverse = lax.rsqrt(jnp.mean(values * values, axis=-1, keepdims=True) + EPSILON)
    scaled = incoming * norm_gain
    outgoing = inverse * scaled - values * (inverse * inverse * inverse) * jnp.mean(
        scaled * values, axis=-1, keepdims=True
    )
    return outgoing, jnp.sum(incoming * values * inverse, axis=0, keepdims=True)


def feed_back(incoming, paired, gate_up, down, gate_grads, up_grads, hidden_turned):
    source_grad = jnp.zeros((128, 768), F32)
    for z in range(4):
        cut = slice(512 * z, 512 * z + 512)
        hidden_grad = lax.dot_general(
            incoming, down[z].reshape(512, 768), LAST_DIMS, preferred_element_type=F32
        )
        gate, up = paired[0, :, cut], paired[1, :, cut]
        sigmoid = jax.nn.sigmoid(gate)
        hidden = (gate * sigmoid * up).T.astype(BF).reshape(4, 2, 64, 128)
        hidden_turned[0, z] = hidden[:, 0]
        hidden_turned[1, z] = hidden[:, 1]
        gate_grad = (hidden_grad * up * sigmoid * (1.0 + gate * (1.0 - sigmoid))).astype(BF)
        up_grad = (hidden_grad * gate * sigmoid).astype(BF)
        part = slice(512 * (z % 2), 512 * (z % 2) + 512)
        gate_grads[z // 2, :, part] = gate_grad
        up_grads[z // 2, :, part] = up_grad
        for at, value in enumerate((gate_grad, up_grad)):
            source_grad = source_grad + lax.dot_general(
                value, gate_up[at, :, :, :, cut].reshape(768, 512), LAST_DIMS, preferred_element_type=F32
            )
    return source_grad


def turned_low(values):
    return values.astype(F32).T.astype(BF)


def fill_part(part, rows, left_of, right):
    for z in range(4):
        value = jnp.dot(left_of(z), right, preferred_element_type=F32).astype(BF)
        part.fill(z, value.reshape(4, rows, right.shape[1]))


def beside(first, second, rows):
    def left_of(z):
        cut = slice(4 * rows * z, 4 * rows * (z + 1))
        return jnp.concatenate([first[cut], second[cut]], axis=1)

    return left_of


SHARED = {
    "source": ((768, 128), (768, 128)),
    "gate": ((2, 128, 1024), (128, 1024)),
    "up": ((2, 128, 1024), (128, 1024)),
    "hidden": ((2, 4, 4, 64, 128), (4, 4, 64, 128)),
    "fed": ((128, 768), (128, 768)),
    "merged": ((768, 128), (768, 128)),
    "mixed": ((2, 128, 384), (128, 384)),
    "norm": ((768, 128), (768, 128)),
    "low": ((2, 3, 128, 384), (3, 128, 384)),
}
KEPT_NAMES = ("paired", "rows", "merged", "turned", "total")
KEPT_TYPES = {name: (shape, kind) for name, shape, kind in KEPT}
WEIGHT_ORDER = ("down", "wide", "out", "qkv")


def backward_kernel(lengths, *refs):
    refs = list(refs)

    def take(count):
        taken = refs[:count]
        del refs[:count]
        return taken

    cotangent, stream, residual_0, summed_0, residual_1, gains, cosine, sine = take(8)
    far = [dict(zip(KEPT_NAMES, take(len(KEPT_NAMES)))) for _ in range(2)]
    stored = dict(zip(GATHERED[:-1], take(8)))
    (input_grad,) = take(1)
    sums = dict(zip(SUMS, take(len(SUMS))))
    kept = dict(zip(KEPT_NAMES, take(len(KEPT_NAMES))))
    weights = dict(zip(WEIGHT_ORDER, take(4)))
    shared, own = part_scratch()
    shared, own = take(len(shared)), take(len(own))
    given = dict(zip(SHARED, take(len(SHARED))))
    got = [dict(zip(SHARED, take(len(SHARED)))) for _ in range(2)]
    out_grads, to_pairs, to_places, incoming = take(4)
    keys_turned, key_grad, gain_grads, their_gains, stacked = take(5)
    part_sems, give_sems, load_sems, pair_sems = take(4)
    parts = build_parts(shared, own, part_sems, sums)
    axes = Axes(True)
    core = axes.core
    x, me = lax.axis_index(BATCH), lax.axis_index(SEQ)
    barrier = pltpu.get_barrier_semaphore()
    neighbours = [(x, lax.rem(me + by, 32)) for by in range(1, 32)]
    neighbours += [device(shifted(x, by), axes.z, axes.y, core) for by in (1, 2, 3)]
    for where in neighbours:
        pl.semaphore_signal(barrier, inc=1, device_id=where, device_id_type=MESH)

    def load(name, layer):
        at = WEIGHT_ORDER.index(name)
        return pltpu.make_async_copy(stored[name, layer], weights[name], load_sems.at[at])

    def recall(name, layer):
        at = KEPT_NAMES.index(name)
        return pltpu.make_async_copy(far[layer][name], kept[name], load_sems.at[4 + at])

    recall("paired", 1).start()
    for name in WEIGHT_ORDER:
        load(name, 1).start()
    for name in KEPT_NAMES[1:]:
        recall(name, 1).start()

    def gain(at):
        return gains[at : at + 1, :]

    def stages(*work):
        for names, layer, number in work:
            for name in names:
                parts[name, layer].stage(number)

    def share(layer, names):
        copies = []
        for name in names:
            at = list(SHARED).index(name)
            source = given[name]
            if SHARED[name][0] != SHARED[name][1]:
                source = source.at[1 - core]
            copies.append(
                remote(
                    source,
                    got[layer][name],
                    give_sems.at[layer, at, 0],
                    give_sems.at[layer, at, 1],
                    axes.partner,
                )
            )
        return copies

    def start(copies):
        for copy in copies:
            copy.start()

    def finish(copies):
        for copy in copies:
            copy.wait()

    wide, narrow = ("gate", "up"), ("left", "right", "o")

    def wide_grads(layer):
        left_of = beside(given["source"], got[layer]["source"], 48)
        for name in wide:
            right = jnp.concatenate([given[name][core], got[layer][name][...]], axis=0)
            fill_part(parts[name, layer], 48, left_of, right)

    def narrow_grads(layer):
        def left_of(z):
            mine = given["hidden"][core, z].reshape(256, 128)
            return jnp.concatenate([mine, got[layer]["hidden"][z].reshape(256, 128)], axis=1)

        right = jnp.concatenate([given["fed"][...], got[layer]["fed"][...]], axis=0)
        fill_part(parts["left", layer], 64, left_of, right[:, :384])
        fill_part(parts["right", layer], 64, left_of, right[:, 384:])
        right = jnp.concatenate([given["mixed"][core], got[layer]["mixed"][...]], axis=0)
        left_of = beside(given["merged"], got[layer]["merged"], 48)
        fill_part(parts["o", layer], 48, left_of, right)

    def projection_grads(layer):
        left_of = beside(given["norm"], got[layer]["norm"], 48)
        for at, name in enumerate("qkv"):
            right = jnp.concatenate([given["low"][core, at], got[layer]["low"][at]], axis=0)
            fill_part(parts[name, layer], 48, left_of, right)

    FED = ("source", "gate", "up", "hidden", "fed")
    MIXED = ("merged", "mixed")
    PROJECTED = ("norm", "low")

    def feed(layer, source, grad):
        load("down", layer).wait()
        load("wide", layer).wait()
        recall("paired", layer).wait()
        low = grad.astype(BF)
        given["fed"][...] = low
        given["source"][...] = turned_low(source.astype(BF))
        return feed_back(
            low,
            kept["paired"],
            weights["wide"],
            weights["down"],
            given["gate"],
            given["up"],
            given["hidden"],
        )

    def send_out_grad(layer, grad):
        load("out", layer).wait()
        low = grad.astype(BF)
        given["mixed"][0] = low[:, :384]
        given["mixed"][1] = low[:, 384:]
        for name in KEPT_NAMES[1:]:
            recall(name, layer).wait()
        given["merged"][...] = turned_low(kept["merged"][...])
        merged_grad = (
            lax.dot_general(
                low, weights["out"][...].reshape(768, 768), LAST_DIMS, preferred_element_type=F32
            )
            .astype(BF)
            .astype(F32)
        )
        exchange = Exchange(pair_sems.at[2 * layer])
        to = to_pairs
        for slot in range(2):
            for tile in range(6):
                at = slot * HEADS + 2 * tile
                both = merged_grad[64 * slot : 64 * slot + 64, 128 * tile : 128 * tile + 128]
                to[at], to[at + 1] = pack_heads(both)
        for pair in range(PAIRS):
            exchange.to(pair_device(pair), to.at[pair], out_grads.at[layer, me])
        return exchange

    def attention(layer, exchange, between):
        rows = kept["rows"]
        length = slot_length(lengths, exchange.pair)

        @pl.when(exchange.has_pair)
        def _():
            all_rows = rows[:, 0:64].reshape(LENGTH, 128).astype(F32)
            keys_turned[...] = all_rows.T[0:64].astype(BF)
            key_grad[...] = jnp.zeros_like(key_grad)

        exchange.wait(to_pairs, out_grads.at[layer], "pairs")
        back = Exchange(pair_sems.at[2 * layer + 1])
        for at in reversed(range(BLOCKS)):

            @pl.when(exchange.has_pair)
            def _(at=at):
                attend_back_block(
                    back,
                    at,
                    length,
                    rows,
                    out_grads.at[layer],
                    kept["turned"],
                    kept["total"],
                    keys_turned,
                    key_grad,
                    to_places,
                    incoming.at[layer],
                )

            stages(*between.get(at, ()))
        stages(*between.get("sent", ()))
        back.wait(to_places, incoming.at[layer], "places")
        collect_projections(incoming.at[layer], cosine[...], sine[...], stacked)

    def source_gradient(layer, source):
        load("qkv", layer).wait()
        given["norm"][...] = turned_low(source.astype(BF))
        for at in range(3):
            given["low"][0, at] = stacked[at, :, 0:384]
            given["low"][1, at] = stacked[at, :, 384:768]
        copies = share(layer, PROJECTED)
        start(copies)
        result = jnp.zeros((128, 768), F32)
        for at in range(3):
            result = result + lax.dot_general(
                stacked[at],
                weights["qkv"][at].reshape(768, 768),
                LAST_DIMS,
                preferred_element_type=F32,
            )
        return result, copies

    normed_two, _ = norm_forward(residual_1[...], gain(3))
    fed_grad = feed(1, normed_two, cotangent[...])
    for name in ("down", "wide"):
        load(name, 0).start()
    recall("paired", 0).start()
    through, gain_grad = norm_backward(fed_grad, residual_1[...], gain(3))
    gain_grads[...] = jnp.zeros_like(gain_grads)
    gain_grads[3:4, :] = gain_grad
    residual_grad = cotangent[...] + through
    pl.semaphore_wait(barrier, len(neighbours))
    exchange = send_out_grad(1, residual_grad)
    load("out", 0).start()
    copies = share(1, FED + MIXED)
    start(copies)
    finish(copies)
    wide_grads(1)
    stages((wide, 1, 0))
    narrow_grads(1)
    stages((narrow, 1, 1))
    attention(1, exchange, {6: [(narrow, 1, 2)], "sent": [(narrow, 1, 3)]})
    for name in KEPT_NAMES[1:]:
        recall(name, 0).start()
    shallow, _ = norm_forward(summed_0[...], gain(1))
    normed, _ = norm_forward(shallow, gain(2))
    normed_grad, copies = source_gradient(1, normed)
    load("qkv", 0).start()
    stages((narrow, 1, 4))
    through, gain_grad = norm_backward(normed_grad, shallow, gain(2))
    gain_grads[2:3, :] = gain_grad
    shallow_grad = residual_grad + through
    summed_grad, gain_grad = norm_backward(shallow_grad, summed_0[...], gain(1))
    gain_grads[1:2, :] = gain_grad

    finish(copies)
    projection_grads(1)
    stages(("qkv", 1, 1))
    middle, _ = norm_forward(residual_0[...], gain(0))
    fed_grad = feed(0, middle, summed_grad)
    middle_grad = summed_grad + fed_grad
    residual_grad, gain_grad = norm_backward(middle_grad, residual_0[...], gain(0))
    gain_grads[0:1, :] = gain_grad
    exchange = send_out_grad(0, residual_grad)
    copies = share(0, FED + MIXED)
    start(copies)
    stages(("qkv", 1, 2), (narrow, 1, 5), (wide, 1, 1))
    finish(copies)
    wide_grads(0)
    stages((wide, 0, 0))
    narrow_grads(0)
    stages((narrow, 0, 1), (narrow, 1, 6))
    attention(
        0,
        exchange,
        {
            6: [("qkv", 1, 3), (wide, 1, 2)],
            4: [(narrow, 0, 2)],
            2: [(wide, 1, 3)],
            0: [("qkv", 1, 4)],
            "sent": [(narrow, 0, 3), (wide, 1, 4)],
        },
    )
    source_grad, copies = source_gradient(0, stream[...])
    swap = remote(
        gain_grads, their_gains, give_sems.at[0, len(SHARED), 0], give_sems.at[0, len(SHARED), 1], axes.partner
    )
    swap.start()
    input_grad[...] = residual_grad + source_grad
    stages(("qkv", 1, 5), (wide, 1, 5))
    finish(copies)
    projection_grads(0)
    swap.wait()
    gain_total = gain_grads[...] + their_gains[...]
    gain_total = jnp.concatenate([gain_total, jnp.zeros((8, 128), F32)], axis=1)
    for z in range(4):
        for y in range(4):
            first, second = (24 * (8 * z + 2 * y + which) // 128 * 128 for which in (0, 1))
            parts["gain", 0].total[y, z] = jnp.where(
                core == 0, gain_total[:, first : first + 256], gain_total[:, second : second + 256]
            )
    last = ("q", "k", "v", "gain")
    stages((last, 0, 1), (narrow, 0, 4), ("qkv", 1, 6), (wide, 1, 6), (wide, 0, 1))
    stages((last, 0, 2), (wide, 0, 2), (narrow, 0, 5), (wide, 0, 3), (narrow, 0, 6))
    stages((last, 0, 4), (wide, 0, 4), (last, 0, 5), (wide, 0, 5), (last, 0, 6), (wide, 0, 6))


def run_backward(lengths, kept, store, cosine, sine):
    near = [kept["cotangent"], kept["stream"]] + [
        kept[name] for name in ("mid_0", "summed_0", "mid_1", "gain")
    ]
    near += [cosine, sine]
    away = [kept[name + layer] for layer in ("_0", "_1") for name in KEPT_NAMES]
    away += [store[key] for key in GATHERED[:-1]]
    shared, own = part_scratch()
    results = pl.pallas_call(
        backward_kernel,
        out_shape=[jax.ShapeDtypeStruct((128, 768), F32)]
        + [jax.ShapeDtypeStruct(*shape) for shape in SUMS.values()],
        in_specs=[SMEM] + [VMEM] * len(near) + [ANY] * len(away),
        out_specs=[VMEM] * (1 + len(SUMS)),
        scratch_shapes=[pltpu.VMEM(*KEPT_TYPES[name + "_0"]) for name in KEPT_NAMES]
        + [pltpu.VMEM(*WEIGHTS[name]) for name in WEIGHT_ORDER]
        + shared
        + own
        + [pltpu.VMEM(here, BF) for here, _ in SHARED.values()]
        + [pltpu.VMEM(there, BF) for _, there in SHARED.values()] * 2
        + [
            pltpu.VMEM((2, 32, 32, 128), BF),
            pltpu.VMEM((PAIRS, 32, 128), BF),
            pltpu.VMEM((32, MESSAGE, 128), BF),
            pltpu.VMEM((2, PAIRS, MESSAGE, 128), BF),
            pltpu.VMEM((64, LENGTH), BF),
            pltpu.VMEM((LENGTH, 128), F32),
            pltpu.VMEM((8, 768), F32),
            pltpu.VMEM((8, 768), F32),
            pltpu.VMEM((3, 128, 768), BF),
            pltpu.SemaphoreType.DMA((2 * len(PARTS), SCATTER_SEMAPHORES)),
            pltpu.SemaphoreType.DMA((2, len(SHARED) + 1, 2)),
            pltpu.SemaphoreType.DMA((9,)),
            pltpu.SemaphoreType.DMA((4, 3)),
        ],
        compiler_params=params(2),
        name="backward",
    )(lengths, *near, *away)
    return results[0], dict(zip(SUMS, results[1:]))


def angles(places):
    half_dim = HEAD_DIM // 2
    frequency = jnp.exp(-math.log(10000.0) * jnp.arange(half_dim).astype(F32) / half_dim)
    phases = places.astype(F32)[:, None] * frequency[None, :]
    cosine, sine = jnp.cos(phases), jnp.sin(phases)
    return (
        jnp.concatenate([cosine] * 4, axis=1),
        jnp.concatenate([-sine, sine] * 2, axis=1),
    )


def update(weight_matrix, moment, average, gradient, step_size):
    moment_new = MOMENTUM * moment + gradient
    weight_new = weight_matrix - step_size * (gradient + MOMENTUM * moment_new)
    return (moment_new, weight_new, AVERAGING * average + (1.0 - AVERAGING) * weight_new)


STEPPED = ("qkv", "out", "wide", "down")


def update_kernel(step_size, *refs):
    count = len(STEPPED)
    sources, refs = refs[: 4 * count + 2], refs[4 * count + 2 :]
    targets, refs = refs[: 3 * count + 2], refs[3 * count + 2 :]
    held, (loads, stores) = refs[:-2], refs[-2:]
    placed, held = held[-2:], held[:-2]
    fetches = [
        pltpu.make_async_copy(source, here, loads.at[at])
        for at, (source, here) in enumerate(zip(sources, held))
    ]
    for copy in fetches:
        copy.start()
    saves = []

    def save(here, at):
        copy = pltpu.make_async_copy(here, targets[at], stores.at[at])
        copy.start()
        saves.append(copy)

    for at in range(count):
        for copy in fetches[4 * at : 4 * at + 4]:
            copy.wait()
        gradient, weight_matrix, moment, average = held[4 * at : 4 * at + 4]
        stepped = update(weight_matrix[...], moment[...], average[...], gradient[...], step_size)
        for n, (here, value) in enumerate(zip((moment, weight_matrix, average), stepped)):
            here[...] = value
            save(here, 3 * at + n)
    for at in range(2):
        fetches[4 * count + at].wait()
        for slot in range(2):
            placed[at][:, slot, :] = held[4 * count + at][64 * slot : 64 * slot + 64]
        save(placed[at], 3 * count + at)
    for copy in saves:
        copy.wait()


def run_update(step_size, sums, states, activations):
    shapes = {name: jax.ShapeDtypeStruct(*SUMS[name]) for name in STEPPED}
    operands = []
    for name in STEPPED:
        operands += [sums[name], *states[name]]
    operands += activations
    by_place = jax.ShapeDtypeStruct((SPAN, 2, 768), F32)
    results = pl.pallas_call(
        functools.partial(update_kernel, step_size),
        out_shape=[shapes[name] for name in STEPPED for _ in range(3)] + [by_place] * 2,
        in_specs=[ANY] * len(operands),
        out_specs=[ANY] * (3 * len(STEPPED) + 2),
        scratch_shapes=[pltpu.VMEM(operand.shape, F32) for operand in operands]
        + [pltpu.VMEM((SPAN, 2, 768), F32)] * 2
        + [
            pltpu.SemaphoreType.DMA((len(operands),)),
            pltpu.SemaphoreType.DMA((3 * len(STEPPED) + 2,)),
        ],
        compiler_params=pltpu.CompilerParams(vmem_limit_bytes=VMEM_BYTES),
        name="step",
    )(*operands)
    return results[: 3 * len(STEPPED)], results[3 * len(STEPPED) :]


def on_device(
    inputs,
    cotangent,
    lengths,
    qkv_weight,
    qkv_moment,
    qkv_average,
    out_weight,
    out_moment,
    out_average,
    gate_up_weight,
    gate_up_moment,
    gate_up_average,
    down_weight,
    down_moment,
    down_average,
    norm_gains,
    gain_moment,
    gain_average,
):
    places = lax.axis_index(SEQ) * SPAN + jnp.arange(SPAN)
    cosine, sine = angles(places)
    seq = lax.axis_index(SEQ)
    own_gains = lax.dynamic_update_slice(
        jnp.zeros((8, 256), F32),
        norm_gains.astype(BF).astype(F32).reshape(4, 24),
        (0, lax.rem(24 * seq, 128)),
    )
    store, kept = run_forward(
        lengths[0],
        qkv_weight,
        out_weight,
        gate_up_weight,
        down_weight,
        own_gains,
        inputs[0],
        cotangent[0],
        cosine,
        sine,
    )
    input_grad, sums = run_backward(
        lengths[0], kept, store, cosine, sine
    )
    gain_sum = lax.dynamic_slice(
        sums["gain"][0], (0, lax.rem(24 * seq, 128)), (4, 24)
    ).reshape(2, 2, 24)

    step_size = STEP_RATE / math.sqrt(
        lax.axis_size(BATCH) * SPAN * lax.axis_size(SEQ) * 2
    )
    stepped, (result, input_grad) = run_update(
        step_size,
        sums,
        {
            "qkv": (qkv_weight, qkv_moment, qkv_average),
            "out": (out_weight, out_moment, out_average),
            "wide": (gate_up_weight, gate_up_moment, gate_up_average),
            "down": (down_weight, down_moment, down_average),
        },
        [kept["result"], input_grad],
    )
    gain_new = update(norm_gains, gain_moment, gain_average, gain_sum, step_size)
    return (result[None], input_grad[None], *stepped, *gain_new)


def solution(mesh):
    rows = P(BATCH, SEQ, None, None)
    wide = P(None, None, SEQ, None)
    flat = P(None, SEQ, None)
    gains = P(None, None, SEQ)
    state = (wide,) * 3 + (flat,) * 3 + (wide,) * 3 + (flat,) * 3 + (gains,) * 3
    return jax.shard_map(
        on_device,
        mesh=mesh,
        in_specs=(rows, rows, P(BATCH, None)) + state,
        out_specs=(rows, rows) + state,
        check_vma=False,
    )
```

```python
import functools
import math

import jax
import jax.numpy as jnp
from jax import lax
from jax.experimental import pallas as pl
from jax.experimental.pallas import tpu as pltpu
from jax.sharding import PartitionSpec as P

MESH = pl.DeviceIdType.MESH
BF = jnp.bfloat16
F32 = jnp.float32
BATCH, SEQ = "batch", "seq"
HEAD_DIM = 64
HEADS = 12
PAIRS = 24
SPAN = 64
LENGTH = 2048
BLOCK = 256
EPSILON = 1e-06
MOMENTUM = 0.5
AVERAGING = 0.5
STEP_RATE = 0.1
MASKED = -1e30
VMEM_BYTES = 62 * 2**20
VMEM = pl.BlockSpec(memory_space=pltpu.VMEM)
ANY = pl.BlockSpec(memory_space=pl.ANY)
SMEM = pl.BlockSpec(memory_space=pltpu.SMEM)
ALL = pl.ds(0, 4)


def params(collective_id):
    return pltpu.CompilerParams(
        collective_id=collective_id, has_side_effects=True, vmem_limit_bytes=VMEM_BYTES
    )


def coordinates():
    seq = lax.axis_index(SEQ)
    return (
        lax.axis_index(BATCH),
        lax.div(seq, 8),
        lax.rem(lax.div(seq, 2), 4),
        lax.rem(seq, 2),
    )


def device(x, z, y, core):
    return (x, (z * 4 + y) * 2 + core)


def shifted(value, by):
    return lax.rem(value + by, 4)


def signal(partners):
    barrier = pltpu.get_barrier_semaphore()
    for partner in partners:
        pl.semaphore_signal(barrier, inc=1, device_id=partner, device_id_type=MESH)


def greet(partners):
    signal(partners)
    pl.semaphore_wait(pltpu.get_barrier_semaphore(), len(partners))


def remote(source, target, send, receive, where):
    return pltpu.make_async_remote_copy(
        src_ref=source,
        dst_ref=target,
        send_sem=send,
        recv_sem=receive,
        device_id=where,
        device_id_type=MESH,
    )


class Axes:
    def __init__(self, first_is_y):
        x, z, y, core = coordinates()
        self.first_is_y = first_is_y
        self.x, self.z, self.y, self.core = x, z, y, core
        self.m1, self.m2 = (y, z) if first_is_y else (z, y)
        self.partner = device(x, z, y, 1 - core)

    def along_y(self, by):
        return device(self.x, self.z, shifted(self.y, by), self.core)

    def along_z(self, by):
        return device(self.x, shifted(self.z, by), self.y, self.core)

    def first(self, by):
        return self.along_y(by) if self.first_is_y else self.along_z(by)

    def second(self, by):
        return self.along_z(by) if self.first_is_y else self.along_y(by)

    def order(self, i1, i2):
        return (i2, i1) if self.first_is_y else (i1, i2)


class GatherSegment:
    def __init__(self, first_is_y, view, semaphores, own=None):
        self.axes = Axes(first_is_y)
        self.view, self.own, self.semaphores = view, own, semaphores

    def block(self, i1, i2):
        return self.view(*self.axes.order(i1, i2))

    def row(self, by, part=ALL):
        return self.block(part, shifted(self.axes.m2, by))

    def keep(self):
        here = self.block(self.axes.m1, self.axes.m2)
        return pltpu.make_async_copy(self.own, here, self.semaphores.at[3, 0])

    def begin(self, phase):
        axes = self.axes
        sem = [self.semaphores.at[phase, at] for at in range(4)]

        def send(part, where):
            remote(part, part, sem[0], sem[1], where).start()

        def share(part):
            remote(part, part, sem[2], sem[3], axes.partner).start()

        if phase == 0:
            here = self.block(axes.m1, axes.m2)
            source = here if self.own is None else self.own
            for by in (1, 3, 2):
                remote(source, here, sem[0], sem[1], axes.first(by)).start()
        elif phase == 1:
            send(self.row(0), axes.second(1))
            send(self.row(0), axes.second(3))
            share(self.row(0))
        elif phase == 2:
            send(self.row(3, pl.ds(0, 2)), axes.second(1))
            send(self.row(1, pl.ds(2, 2)), axes.second(3))
            share(self.row(3))
            share(self.row(1))
        else:
            share(self.row(2))

    def end(self, phase):
        axes = self.axes
        sem = [self.semaphores.at[phase, at] for at in range(4)]
        one, two = self.row(0), self.block(ALL, pl.ds(0, 2))
        moved = (self.block(pl.ds(0, 3), axes.m2), two, one, None)[phase]
        shared = (None, one, two, one)[phase]
        if moved is not None:
            remote(moved, moved, sem[0], sem[1], axes.partner).wait()
        if shared is not None:
            remote(shared, shared, sem[2], sem[3], axes.partner).wait()


class AcrossSegment(GatherSegment):
    def __init__(self, first_is_y, quarters, semaphores, own):
        x = lax.axis_index(BATCH)
        super().__init__(first_is_y, lambda z, y: quarters(z, y, x, 1), semaphores, own)
        self.quarters = quarters

    def begin(self, phase):
        axes = self.axes
        sem = [self.semaphores.at[phase, at] for at in range(4)]

        def send(part, where):
            remote(part, part, sem[0], sem[1], where).start()

        def share(part):
            remote(part, part, sem[2], sem[3], axes.partner).start()

        if phase == 0:
            here = self.block(axes.m1, axes.m2)
            for by in (1, 3, 2):
                remote(self.own, here, sem[0], sem[1], axes.first(by)).start()
        elif phase == 1:
            send(self.row(0), axes.second(1))
            send(self.row(0), axes.second(3))
        elif phase == 2:
            send(self.row(3, pl.ds(0, 2)), axes.second(1))
            send(self.row(1, pl.ds(2, 2)), axes.second(3))
        elif phase == 3:
            mine = self.block(ALL, ALL)
            for by in (1, 3):
                send(mine, self.plane(by))
            far = [self.semaphores.at[4, at] for at in range(2)]
            remote(mine, mine, far[0], far[1], self.plane(2)).start()
            share(mine)
        elif phase == 4:
            for by in (1, 3):
                share(self.quarters(ALL, ALL, shifted(axes.x, by), 1))
        else:
            self.last_share().start()

    def plane(self, by):
        axes = self.axes
        return device(shifted(axes.x, by), axes.z, axes.y, axes.core)

    def last_share(self):
        part = self.quarters(ALL, ALL, shifted(self.axes.x, 2), 1)
        sem = [self.semaphores.at[2, at] for at in (2, 3)]
        return remote(part, part, sem[0], sem[1], self.axes.partner)

    def end(self, phase):
        axes = self.axes
        if phase == 5:
            self.last_share().wait()
            return
        sem = [self.semaphores.at[phase, at] for at in range(4)]
        two = self.quarters(ALL, ALL, 0, 2)
        mine = self.block(ALL, ALL)
        moved = (
            self.block(pl.ds(0, 3), axes.m2),
            self.block(ALL, pl.ds(0, 2)),
            self.row(0),
            two,
            mine,
        )[phase]
        shared = (None, None, None, mine, two)[phase]
        remote(moved, moved, sem[0], sem[1], axes.partner).wait()
        if shared is not None:
            remote(shared, shared, sem[2], sem[3], axes.partner).wait()


def across_views(name, ref):
    core = Axes(True).core

    def columns(first, count):
        return pl.ds(pl.multiple_of(core * 1024 + first * 256, 128), 256 * count)

    def rows(first, count):
        return pl.ds(pl.multiple_of(first * 16, 16), 16 * count)

    if name == "wide":
        return [
            (True, lambda z, y, first, count: ref.at[0, z, y, :, columns(first, count)]),
            (False, lambda z, y, first, count: ref.at[1, z, y, :, columns(first, count)]),
        ]
    return [
        (True, lambda z, y, first, count: ref.at[z, y, core, rows(first, count), pl.ds(0, 384)]),
        (False, lambda z, y, first, count: ref.at[z, y, core, rows(first, count), pl.ds(384, 384)]),
    ]


def across_owns(name, ref):
    axes = Axes(True)
    if name == "wide":
        columns = pl.ds(pl.multiple_of(axes.core * 1024 + axes.x * 256, 128), 256)
        return [ref.at[0, :, columns], ref.at[1, :, columns]]
    rows = pl.ds(pl.multiple_of(axes.x * 16, 16), 16)
    return [ref.at[rows, pl.ds(0, 384)], ref.at[rows, pl.ds(384, 384)]]


ACROSS = (("wide", 1), ("down", 0))


def halves(core, width):
    return pl.ds(pl.multiple_of(core * (width // 2), 128), width // 2)


def weight_views(name, ref):
    core = Axes(True).core
    narrow, wide = halves(core, 768), halves(core, 2048)
    if name == "qkv":
        return [
            (True, lambda z, y: ref.at[pl.ds(0, 2), z, y, :, narrow]),
            (False, lambda z, y: ref.at[2, z, y, :, narrow]),
        ]
    if name == "out":
        return [(False, lambda z, y: ref.at[z, y, :, narrow])]
    if name == "wide":
        return [
            (True, lambda z, y: ref.at[0, z, y, :, wide]),
            (False, lambda z, y: ref.at[1, z, y, :, wide]),
        ]
    if name == "down":
        return [
            (True, lambda z, y: ref.at[z, y, core, :, pl.ds(0, 384)]),
            (False, lambda z, y: ref.at[z, y, core, :, pl.ds(384, 384)]),
        ]
    return [(True, lambda z, y: ref.at[z, y, core])]


def own_views(name, ref):
    core = Axes(True).core
    narrow, wide = halves(core, 768), halves(core, 2048)
    if name == "qkv":
        return [ref.at[pl.ds(0, 2), :, narrow], ref.at[2, :, narrow]]
    if name == "out":
        return [ref.at[:, narrow]]
    if name == "wide":
        return [ref.at[0, :, wide], ref.at[1, :, wide]]
    if name == "down":
        return [ref.at[:, pl.ds(0, 384)], ref.at[:, pl.ds(384, 384)]]
    return [ref]


WEIGHTS = {
    "qkv": ((3, 4, 4, 48, 768), BF),
    "out": ((4, 4, 48, 768), BF),
    "wide": ((2, 4, 4, 48, 2048), BF),
    "down": ((4, 4, 2, 64, 768), BF),
    "gain": ((4, 4, 2, 8, 256), F32),
}
SEGMENTS = {"qkv": 2, "out": 1, "wide": 2, "down": 2, "gain": 1}
GATHERED = [(name, layer) for layer in range(2) for name in ("qkv", "out", "wide", "down")] + [
    ("gain", 0)
]


def weight_shape(key):
    return jax.ShapeDtypeStruct(*WEIGHTS[key[0]])


class ScatterPart:
    def __init__(self, first_is_y, total, rows, ring, blocks, groups, semaphores, finish):
        self.axes = Axes(first_is_y)
        self.total, self.rows, self.ring, self.blocks, self.groups = total, rows, ring, blocks, groups
        self.semaphores, self.finish = semaphores, finish

    def fill(self, z, value):
        if self.axes.first_is_y:
            self.total[z] = value
        else:
            self.total[:, z] = value

    def spread(self):
        axes, sem = self.axes, self.semaphores
        for by in (1, 3, 2):
            remote(
                self.total.at[axes.m2, shifted(axes.m1, by)],
                self.blocks.at[by - 1],
                sem.at[4],
                sem.at[5],
                axes.first(by),
            ).start()

    def stage(self, number):
        axes, sem, total = self.axes, self.semaphores, self.total
        m1, m2 = axes.m1, axes.m2
        before, after, across = shifted(m2, 3), shifted(m2, 1), shifted(m2, 2)
        low, high = pl.ds(0, 2), pl.ds(2, 2)

        def add(target, source):
            target[...] = (target[...].astype(F32) + source[...].astype(F32)).astype(target.dtype)

        if number == 1:
            remote(
                total.at[across, low], self.ring.at[0], sem.at[0], sem.at[1], axes.second(1)
            ).start()
            remote(
                total.at[across, high], self.ring.at[1], sem.at[0], sem.at[1], axes.second(3)
            ).start()
        elif number == 2:
            row = total.at[m2]
            remote(row, self.ring, sem.at[0], sem.at[1], axes.partner).wait()
            add(total.at[after, low], self.ring.at[0])
            add(total.at[before, high], self.ring.at[1])
            remote(
                total.at[after], self.rows.at[0], sem.at[2], sem.at[3], axes.second(1)
            ).start()
            remote(
                total.at[before], self.rows.at[1], sem.at[2], sem.at[3], axes.second(3)
            ).start()
        elif number == 3:
            remote(self.rows, self.rows, sem.at[2], sem.at[3], axes.partner).wait()
            for at in range(4):
                total[m2, at] = (
                    total[m2, at].astype(F32)
                    + self.rows[0, at].astype(F32)
                    + self.rows[1, at].astype(F32)
                ).astype(total.dtype)
            self.spread()
        elif number == 4:
            remote(self.blocks, self.blocks, sem.at[4], sem.at[5], axes.partner).wait()
            self.groups[axes.x] = (
                total[m2, m1].astype(F32)
                + self.blocks[0].astype(F32)
                + self.blocks[1].astype(F32)
                + self.blocks[2].astype(F32)
            ).astype(total.dtype)
            mine = self.groups.at[axes.x]
            for by in (1, 3, 2):
                remote(
                    mine,
                    mine,
                    sem.at[6],
                    sem.at[7],
                    device(shifted(axes.x, by), axes.z, axes.y, axes.core),
                ).start()
        elif number == 5:
            three = self.groups.at[pl.ds(0, 3)]
            remote(three, three, sem.at[6], sem.at[7], axes.partner).wait()
            summed = self.groups[0].astype(F32)
            for at in range(1, 4):
                summed = summed + self.groups[at].astype(F32)
            self.finish(0, summed)
        else:
            self.finish(1, None)


class AcrossPart(ScatterPart):
    def __init__(self, first_is_y, whole, quarter, came, rows, ring, blocks, groups, semaphores, finish):
        super().__init__(first_is_y, quarter, rows, ring, blocks, groups, semaphores, finish)
        self.whole, self.came = whole, came
        self.by_rows = whole.shape[2] == 64

    def fill(self, z, value):
        if self.axes.first_is_y:
            self.whole[z] = value
        else:
            self.whole[:, z] = value

    def quarter(self, at):
        if self.by_rows:
            return pl.ds(pl.multiple_of(at * 16, 16), 16), slice(None)
        return slice(None), pl.ds(pl.multiple_of(at * 256, 128), 256)

    def stage(self, number):
        axes, sem = self.axes, self.semaphores
        if number == 0:
            for by in (1, 3, 2):
                there = shifted(axes.x, by)
                remote(
                    self.whole.at[(slice(None), slice(None)) + self.quarter(there)],
                    self.came.at[by - 1],
                    sem.at[10],
                    sem.at[11],
                    device(there, axes.z, axes.y, axes.core),
                ).start()
            return
        if number == 1:
            remote(self.came, self.came, sem.at[10], sem.at[11], axes.partner).wait()
            for at in range(4):
                summed = self.whole[(at, slice(None)) + self.quarter(axes.x)].astype(F32)
                for by in range(3):
                    summed = summed + self.came[by, at].astype(F32)
                self.total[at] = summed.astype(BF)
        if number == 5:
            three = self.groups.at[pl.ds(0, 3)]
            remote(three, three, sem.at[6], sem.at[7], axes.partner).wait()
            quarters = [self.groups[at].astype(F32) for at in range(4)]
            self.finish(0, jnp.concatenate(quarters, axis=0 if self.by_rows else 1))
            return
        super().stage(number)


class StraightPart(ScatterPart):
    def stage(self, number):
        axes, sem = self.axes, self.semaphores
        m2 = axes.m2
        if number == 1:
            for by in (1, 3, 2):
                remote(
                    self.total.at[shifted(m2, by)],
                    self.rows.at[by - 1],
                    sem.at[2],
                    sem.at[3],
                    axes.second(by),
                ).start()
        elif number == 2:
            remote(self.rows, self.rows, sem.at[2], sem.at[3], axes.partner).wait()
            for at in range(4):
                summed = self.total[m2, at].astype(F32)
                for by in range(3):
                    summed = summed + self.rows[by, at].astype(F32)
                self.total[m2, at] = summed.astype(self.total.dtype)
            self.spread()
        elif number != 3:
            super().stage(number)


SCATTER_SEMAPHORES = 12
ACROSS_PARTS = (("left", 0), ("right", 0), ("gate", 1), ("up", 1))
LAST_PARTS = (("q", 0), ("k", 0), ("v", 0), ("gain", 0))
PARTS = {
    "gate": (True, 48, 1024, BF),
    "up": (False, 48, 1024, BF),
    "left": (True, 64, 384, BF),
    "right": (False, 64, 384, BF),
    "o": (False, 48, 384, BF),
    "q": (True, 48, 384, BF),
    "k": (False, 48, 384, BF),
    "v": (True, 48, 384, BF),
    "gain": (False, 8, 256, F32),
}
SOURCE = {
    "q": "qkv", "k": "qkv", "v": "qkv", "o": "out", "gate": "wide", "up": "wide",
    "left": "down", "right": "down", "gain": "gain",
}
SUMS = {
    "qkv": ((2, 3, 24, 768), F32),
    "out": ((2, 24, 768), F32),
    "wide": ((2, 2, 24, 2048), F32),
    "down": ((2, 64, 768), F32),
    "gain": ((1, 8, 256), F32),
}
LEFT, RIGHT = pl.ds(0, 384), pl.ds(384, 384)


def part_target(part, ref):
    if part in ("q", "k", "v"):
        return ref.at["qkv".index(part)]
    if part in ("gate", "up"):
        return ref.at[int(part == "up")]
    if part in ("left", "right"):
        return ref.at[:, LEFT if part == "left" else RIGHT]
    return ref


def rows_swapped(target, mine, theirs, sem):
    axes = Axes(True)
    core = axes.core

    def finish(part, summed):
        own_rows = pl.ds(pl.multiple_of(core * 24, 8), 24)
        other_rows = pl.ds(pl.multiple_of((1 - core) * 24, 8), 24)
        copy = remote(mine.at[other_rows, :], theirs, sem.at[8], sem.at[9], axes.partner)
        if part == 0:
            mine[...] = summed
            copy.start()
        else:
            copy.wait()
            kept = mine[own_rows, :]
            got = theirs[...]
            width = kept.shape[-1]
            target[:, :width] = jnp.where(core == 0, kept, got)
            target[:, width:] = jnp.where(core == 0, got, kept)

    return finish


def direct(target):
    def finish(part, summed):
        if part == 0:
            target[...] = summed

    return finish


def part_scratch():
    shared, own = [], []
    for part, (_, rows, width, kind) in PARTS.items():
        shared += [
            pltpu.VMEM((4, 4, rows, width), kind),
            pltpu.VMEM((8, 128) if part == "gain" else (2, 4, rows, width), kind),
            pltpu.VMEM((48, width), F32) if rows == 48 else pltpu.VMEM((8, 128), F32),
        ]
        for layer in range(1 if part == "gain" else 2):
            across = (part, layer) in ACROSS_PARTS
            block = (rows, width)
            if across:
                block = (16, width) if rows == 64 else (rows, width // 4)
                own += [
                    pltpu.VMEM((4, 4) + block, kind),
                    pltpu.VMEM((3, 4, 4) + block, kind),
                    pltpu.VMEM((2, 4) + block, kind),
                ]
            straight = (part, layer) in LAST_PARTS
            own += [
                pltpu.VMEM(((3, 4) if straight else (2, 2)) + block, kind),
                pltpu.VMEM((3,) + block, kind),
                pltpu.VMEM((4,) + block, kind),
                pltpu.VMEM((24, width), F32) if rows == 48 else pltpu.VMEM((8, 128), F32),
            ]
    return shared, own


def build_parts(shared, own, sems, sums):
    parts = {}
    count = 0
    own = list(own)

    def take(number):
        taken = own[:number]
        del own[:number]
        return taken

    for at, (part, (first_is_y, rows, _, _)) in enumerate(PARTS.items()):
        total, rows_in, mine = shared[3 * at : 3 * at + 3]
        for layer in (0,) if part == "gain" else (0, 1):
            if (part, layer) in ACROSS_PARTS:
                quarter, came, rows_here = take(3)
            ring, blocks, groups, theirs = take(4)
            target = part_target(part, sums[SOURCE[part]].at[layer])
            sem = sems.at[count]
            finish = rows_swapped(target, mine, theirs, sem) if rows == 48 else direct(target)
            if (part, layer) in ACROSS_PARTS:
                parts[part, layer] = AcrossPart(
                    first_is_y, total, quarter, came, rows_here, ring, blocks, groups, sem, finish
                )
            elif (part, layer) in LAST_PARTS:
                parts[part, layer] = StraightPart(
                    first_is_y, total, ring, None, blocks, groups, sem, finish
                )
            else:
                parts[part, layer] = ScatterPart(
                    first_is_y, total, rows_in, ring, blocks, groups, sem, finish
                )
            count += 1
    return parts


def pair_device(pair):
    if pair < 16:
        return 2 * pair
    z = (pair - 16) // 2
    return 2 * (4 * z + 2 * ((pair - 16) % 2) + z % 2) + 1


def own_pair():
    _, z, y, core = coordinates()
    has_pair = (core == 0) | (lax.rem(z + y, 2) == 0)
    pair = jnp.where(core == 0, 4 * z + y, 16 + 2 * z + lax.div(y, 2))
    return has_pair, pair


def lanes(shape):
    return lax.broadcasted_iota(jnp.int32, shape, len(shape) - 1)


def turned(values, cosine, sine):
    here = lax.rem(lanes(values.shape), 64) < 32
    width = values.shape[-1]
    other = jnp.where(here, pltpu.roll(values, width - 32, 1), pltpu.roll(values, 32, 1))
    return values * cosine + other * sine


def twice(table):
    return jnp.concatenate([table, table], axis=0)


def allowed_keys(first_key, first_query, keys, queries, length):
    key = first_key + lax.broadcasted_iota(jnp.int32, (keys, queries), 0)
    query = first_query + lax.broadcasted_iota(jnp.int32, (keys, queries), 1)
    return (key <= query) & (key < length)


def slot_length(lengths, pair):
    return jnp.where(pair < HEADS, lengths[0], lengths[1])


LAST_DIMS = (((1,), (1,)), ((), ()))
BLOCKS = LENGTH // BLOCK
MESSAGE = 96


def front_lanes(rows):
    return lanes((rows, 128)) < 64


def pack_heads(both):
    front = front_lanes(32)
    top, bottom = both[0:32], both[32:64]
    return (
        jnp.where(front, top, pltpu.roll(bottom, 64, 1)).astype(BF),
        jnp.where(front, pltpu.roll(top, 64, 1), bottom).astype(BF),
    )


def unpack_heads(first, second):
    front = front_lanes(32)
    first, second = first.astype(F32), second.astype(F32)
    return jnp.concatenate(
        [
            jnp.where(front, first, pltpu.roll(second, 64, 1)),
            jnp.where(front, pltpu.roll(first, 64, 1), second),
        ],
        axis=0,
    )


def unpack_block(packed, to_front):
    packed = packed.astype(F32).reshape(128, 128)
    other = pltpu.roll(packed, 64, 1)
    front = front_lanes(128)
    if to_front:
        top, bottom = jnp.where(front, packed, 0.0), jnp.where(front, other, 0.0)
    else:
        top, bottom = jnp.where(front, 0.0, other), jnp.where(front, 0.0, packed)
    joined = jnp.concatenate([top.reshape(4, 32, 128), bottom.reshape(4, 32, 128)], axis=1)
    return joined.reshape(256, 128).astype(BF)


def pack_turned(turned_values):
    rows = jnp.concatenate([turned_values, turned_values], axis=0).T.reshape(4, 64, 128)
    front = lanes((4, 32, 128)) < 64
    return jnp.where(front, rows[:, 0:32], rows[:, 32:64]).astype(BF)


class Exchange:
    def __init__(self, semaphores):
        self.x, self.me = lax.axis_index(BATCH), lax.axis_index(SEQ)
        self.has_pair, self.pair = own_pair()
        self.send, self.receive, self.local = (semaphores.at[at] for at in range(3))

    def to(self, there, source, target):
        @pl.when(self.me != there)
        def _():
            remote(source, target, self.send, self.receive, (self.x, there)).start()

        @pl.when(self.me == there)
        def _():
            pltpu.make_async_copy(source, target, self.local).start()

    def wait(self, sent, got, where):
        if where == "pairs":
            sends, gets = (sent.shape[0], sent.shape[0] - 1), (None, got.shape[0] - 1)
        else:
            sends, gets = (None, sent.shape[0] - 1), (got.shape[0], got.shape[0] - 1)

        def wait_for(n_sent, n_got):
            if n_got is not None:
                part = got.at[pl.ds(0, n_got)]
                remote(part, part, self.send, self.receive, (self.x, self.me)).wait_recv()
            if n_sent is not None:
                part = sent.at[pl.ds(0, n_sent)]
                remote(part, part, self.send, self.receive, (self.x, self.me)).wait_send()

        @pl.when(self.has_pair)
        def _():
            pltpu.make_async_copy(sent.at[0], got.at[0], self.local).wait()
            wait_for(sends[1], gets[1])

        @pl.when(jnp.logical_not(self.has_pair))
        def _():
            wait_for(sends[0], gets[0])


def send_projections(exchange, query, key, value, cosine, sine, outgoing, rows):
    cosine, sine = twice(cosine), twice(sine)
    front = front_lanes(64)
    for tile in range(6):
        cut = slice(128 * tile, 128 * tile + 128)
        q = turned(query[:, cut], cosine, sine) * (1.0 / math.sqrt(HEAD_DIM))
        k = turned(key[:, cut], cosine, sine)
        v = value[:, cut]
        for slot in range(2):
            span = slice(64 * slot, 64 * slot + 64)
            at = slot * HEADS + 2 * tile
            ks, vs = k[span], v[span]
            outgoing[at, 0:64] = jnp.where(front, ks, pltpu.roll(vs, 64, 1)).astype(BF)
            outgoing[at + 1, 0:64] = jnp.where(front, pltpu.roll(ks, 64, 1), vs).astype(BF)
            outgoing[at, 64:96], outgoing[at + 1, 64:96] = pack_heads(q[span])
    for pair in range(PAIRS):
        exchange.to(pair_device(pair), outgoing.at[pair], rows.at[exchange.me])


def attend_block(exchange, at, length, rows, values_turned, out_turned, log_total, outgoing, incoming):
    count = (at + 1) * BLOCK
    queries = unpack_block(rows[4 * at : 4 * at + 4, 64:96], True)
    keys = rows[0 : 4 * at + 4, 0:64].reshape(count, 128)
    scores = lax.dot_general(keys, queries, LAST_DIMS, preferred_element_type=F32)
    scores = jnp.where(allowed_keys(0, at * BLOCK, count, BLOCK, length), scores, MASKED)
    highest = jnp.max(scores, axis=0, keepdims=True)
    raised = jnp.exp(scores - highest)
    total = jnp.sum(raised, axis=0, keepdims=True)
    result = (
        jnp.dot(values_turned[:, 0:count], raised.astype(BF), preferred_element_type=F32) / total
    )
    cut = slice(at * BLOCK, count)
    out_turned[:, cut] = result
    log_total[:, cut] = jnp.broadcast_to(highest + jnp.log(total), (8, BLOCK))
    outgoing[4 * at : 4 * at + 4] = pack_turned(result)
    for there in range(4 * at, 4 * at + 4):
        exchange.to(there, outgoing.at[there], incoming.at[exchange.pair])


def merge_heads(incoming, merged):
    for slot in range(2):
        for tile in range(6):
            at = slot * HEADS + 2 * tile
            merged[64 * slot : 64 * slot + 64, 128 * tile : 128 * tile + 128] = unpack_heads(
                incoming[at], incoming[at + 1]
            ).astype(BF)


def norm_forward(values, norm_gain):
    inverse = lax.rsqrt(jnp.mean(values * values, axis=-1, keepdims=True) + EPSILON)
    return (values * inverse * norm_gain, inverse)


def feed_forward(rows_in, gate_up, down, paired):
    fed = jnp.zeros((128, 768), F32)
    for z in range(4):
        cut = slice(512 * z, 512 * z + 512)
        gate = jnp.dot(rows_in, gate_up[0, :, :, :, cut].reshape(768, 512), preferred_element_type=F32)
        up = jnp.dot(rows_in, gate_up[1, :, :, :, cut].reshape(768, 512), preferred_element_type=F32)
        paired[0, :, cut] = gate
        paired[1, :, cut] = up
        hidden = (jax.nn.silu(gate) * up).astype(BF)
        fed = fed + jnp.dot(hidden, down[z].reshape(512, 768), preferred_element_type=F32)
    return fed


KEPT = (
    [("result", (128, 768), F32), ("mid_0", (128, 768), F32), ("summed_0", (128, 768), F32)]
    + [("mid_1", (128, 768), F32), ("gain", (8, 768), F32)]
    + [("stream", (128, 768), BF), ("cotangent", (128, 768), F32)]
    + [
        (name + "_" + layer, shape, kind)
        for layer in "01"
        for name, shape, kind in (
            ("paired", (2, 128, 2048), F32),
            ("rows", (32, MESSAGE, 128), BF),
            ("merged", (128, 768), BF),
            ("turned", (64, LENGTH), F32),
            ("total", (8, LENGTH), F32),
        )
    ]
)


def forward_kernel(
    lengths, qkv, out, gate_up, down, gains, inputs, cotangents, cosine, sine, *refs
):
    stored = dict(zip(GATHERED[:-1], refs[:8]))
    kept = {name: ref for (name, _, _), ref in zip(KEPT, refs[8:])}
    refs = refs[8 + len(KEPT) :]
    store, refs = dict(zip(GATHERED, refs[:9])), refs[9:]
    their_qkv, their_out, their_gate_up, b_qkv, b_out, b_gate_up, b_down = refs[:7]
    outgoing, places, incoming, values_turned, stream, swap, sems, local, pair_sems = refs[7:]
    axes = Axes(True)
    core = axes.core
    x, me = lax.axis_index(BATCH), lax.axis_index(SEQ)
    greet(
        [(x, lax.rem(me + by, 32)) for by in range(1, 32)]
        + [device(shifted(x, by), axes.z, axes.y, core) for by in (1, 2, 3)]
    )
    swaps = [
        remote(mine, theirs, swap.at[0, at], swap.at[1, at], axes.partner)
        for at, (mine, theirs) in enumerate(
            (
                (qkv.at[0], their_qkv.at[0]),
                (qkv.at[1], their_qkv.at[1]),
                (out, their_out),
                (gate_up, their_gate_up),
            )
        )
    ]
    for copy in swaps:
        copy.start()
    for slot in range(2):
        stream[64 * slot : 64 * slot + 64] = inputs[:, slot, :]
        kept["cotangent"][64 * slot : 64 * slot + 64] = cotangents[:, slot, :]
    kept["stream"][...] = stream[...].astype(BF)

    def joined(mine, theirs):
        upper = jnp.where(core == 0, mine, theirs)
        lower = jnp.where(core == 0, theirs, mine)
        return jnp.concatenate([upper, lower], axis=0).astype(BF)

    segments = {}
    at = 0
    for key in GATHERED:
        name, layer = key
        block = {"qkv": b_qkv, "out": b_out, "wide": b_gate_up, "down": b_down}.get(name)
        block = gains if block is None else block.at[layer]
        kind, views, owns = GatherSegment, weight_views, own_views
        if key in ACROSS:
            kind, views, owns = AcrossSegment, across_views, across_owns
        segments[key] = []
        for (first_is_y, view), own in zip(views(name, store[key]), owns(name, block)):
            segments[key].append(kind(first_is_y, view, sems.at[at], own))
            at += 1

    def each(keys, act):
        for key in keys:
            for segment in segments[key]:
                act(segment)

    def keep(*keys):
        each(keys, lambda segment: segment.keep().start())
        each(keys, lambda segment: segment.keep().wait())

    def begin(phase, *keys):
        each(keys, lambda segment: segment.begin(phase))

    def end(phase, *keys):
        each(keys, lambda segment: segment.end(phase))

    saves = []

    def save(*keys):
        for key in keys:
            copy = pltpu.make_async_copy(store[key], stored[key], local.at[len(saves)])
            copy.start()
            saves.append(copy)

    qkv_0, out_0, wide_0, down_0 = GATHERED[0:4]
    qkv_1, out_1, wide_1, down_1 = GATHERED[4:8]
    gains_0 = GATHERED[8]

    swaps[0].wait()
    for at in range(3):
        b_qkv[0, at] = joined(qkv[0, at], their_qkv[0, at])
    begin(0, qkv_0)
    keep(qkv_0)
    b_down[0] = down[0].astype(BF)
    begin(0, down_0)
    keep(down_0)
    for copy in swaps[1:]:
        copy.wait()
    for at in range(2):
        b_gate_up[0, at] = joined(gate_up[0, at], their_gate_up[0, at])
    begin(0, wide_0)
    keep(wide_0)
    end(0, qkv_0)
    begin(1, qkv_0)
    end(0, down_0)
    begin(1, down_0)
    b_out[0] = joined(out[0], their_out[0])
    for at in range(2):
        b_gate_up[1, at] = joined(gate_up[1, at], their_gate_up[1, at])
    begin(0, out_0, gains_0, wide_1)
    keep(out_0, gains_0, wide_1)
    for at in range(3):
        b_qkv[1, at] = joined(qkv[1, at], their_qkv[1, at])
    b_out[1] = joined(out[1], their_out[1])
    b_down[1] = down[1].astype(BF)
    end(1, qkv_0)
    begin(2, qkv_0)
    end(1, down_0)
    begin(2, down_0)
    end(0, wide_0)
    begin(1, wide_0)
    end(2, qkv_0)
    begin(3, qkv_0)
    keep(qkv_1, out_1, down_1)
    end(2, down_0)
    begin(3, down_0)
    end(0, out_0, gains_0, wide_1)
    begin(1, wide_1)
    end(3, qkv_0)
    save(qkv_0)

    def attention(layer, source, before, between):
        weights = store["qkv", layer]
        name = "_" + str(layer)
        rows, merged = kept["rows" + name], kept["merged" + name]
        there = Exchange(pair_sems.at[2 * layer])
        back = Exchange(pair_sems.at[2 * layer + 1])
        low = source.astype(BF)
        query, key, value = (
            jnp.dot(low, weights[at].reshape(768, 768), preferred_element_type=F32)
            for at in range(3)
        )
        send_projections(
            there, query, key, value, cosine[...], sine[...], outgoing.at[layer], rows
        )
        before()
        there.wait(outgoing.at[layer], rows, "pairs")
        length = slot_length(lengths, there.pair)

        @pl.when(there.has_pair)
        def _():
            all_rows = rows[:, 0:64].reshape(LENGTH, 128).astype(F32)
            values_turned[...] = all_rows.T[64:128].astype(BF)

        for at in range(BLOCKS):

            @pl.when(there.has_pair)
            def _(at=at):
                attend_block(
                    back,
                    at,
                    length,
                    rows,
                    values_turned,
                    kept["turned" + name],
                    kept["total" + name],
                    places.at[layer],
                    incoming.at[layer],
                )

            if at in between:
                between[at]()
        back.wait(places.at[layer], incoming.at[layer], "places")
        merge_heads(incoming.at[layer], merged)
        between["after"]()
        out_matrix = store["out", layer][...].reshape(768, 768)
        return jnp.dot(merged[...], out_matrix, preferred_element_type=F32)

    def before_0():
        begin(1, out_0, gains_0)
        end(1, wide_1)
        begin(2, wide_1)

    def within_0():
        end(1, wide_0)
        begin(2, wide_0)
        end(2, wide_1)
        begin(3, wide_1)
        begin(0, qkv_1)

    def later_0():
        end(1, out_0, gains_0)
        begin(2, out_0, gains_0)

    def last_0():
        end(0, qkv_1)
        begin(1, qkv_1)
        end(3, down_0)
        begin(4, down_0)

    def after_0():
        end(4, down_0)
        begin(5, down_0)
        end(2, wide_0, out_0, gains_0)
        begin(3, out_0, wide_0, gains_0)
        begin(0, out_1, down_1)
        end(3, out_0, wide_0, gains_0)
        end(5, down_0)
        save(out_0, wide_0, down_0)
        for device_at in range(32):
            piece = store[gains_0][device_at // 8, device_at // 2 % 4, device_at % 2]
            first = 24 * device_at // 128
            if device_at == 0:
                kept["gain"][...] = jnp.zeros((8, 768), F32)
            width = min(256, 768 - 128 * first)
            kept["gain"][:, 128 * first : 128 * first + width] += piece[:, :width]

    def gain(at):
        return kept["gain"][at : at + 1, :]

    mixed = attention(
        0, stream[...], before_0, {1: within_0, 4: later_0, 7: last_0, "after": after_0}
    )
    residual = stream[...] + mixed
    kept["mid_0"][...] = residual
    middle, _ = norm_forward(residual, gain(0))
    end(1, qkv_1)
    begin(2, qkv_1)
    fed = feed_forward(middle.astype(BF), store[wide_0], store[down_0], kept["paired_0"])
    end(2, qkv_1)
    begin(3, qkv_1)
    end(0, out_1, down_1)
    begin(1, out_1, down_1)
    summed = middle + fed
    kept["summed_0"][...] = summed
    shallow, _ = norm_forward(summed, gain(1))
    normed, _ = norm_forward(shallow, gain(2))
    end(3, qkv_1)
    save(qkv_1)

    def before_1():
        pass

    def within_1():
        end(1, out_1, down_1)
        begin(2, out_1, down_1)
        end(3, wide_1)
        begin(4, wide_1)

    def later_1():
        end(4, wide_1)
        begin(5, wide_1)

    def after_1():
        end(2, out_1, down_1)
        begin(3, out_1, down_1)
        end(3, out_1, down_1)
        end(5, wide_1)
        save(out_1, wide_1, down_1)

    mixed = attention(1, normed, before_1, {1: within_1, 7: later_1, "after": after_1})
    residual = shallow + mixed
    kept["mid_1"][...] = residual
    normed_two, _ = norm_forward(residual, gain(3))
    fed = feed_forward(normed_two.astype(BF), store[wide_1], store[down_1], kept["paired_1"])
    kept["result"][...] = residual + fed
    for copy in saves:
        copy.wait()


def run_forward(*operands):
    count = sum(SEGMENTS[name] for name, _ in GATHERED)
    stored = GATHERED[:-1]
    results = pl.pallas_call(
        forward_kernel,
        out_shape=[weight_shape(key) for key in stored]
        + [jax.ShapeDtypeStruct(shape, kind) for _, shape, kind in KEPT],
        in_specs=[SMEM] + [VMEM] * 9,
        out_specs=[ANY] * 8 + [VMEM] * len(KEPT),
        scratch_shapes=[pltpu.VMEM(*WEIGHTS[name]) for name, _ in GATHERED]
        + [
            pltpu.VMEM((2, 3, 24, 768), F32),
            pltpu.VMEM((2, 24, 768), F32),
            pltpu.VMEM((2, 2, 24, 2048), F32),
            pltpu.VMEM((2, 3, 48, 768), BF),
            pltpu.VMEM((2, 48, 768), BF),
            pltpu.VMEM((2, 2, 48, 2048), BF),
            pltpu.VMEM((2, 64, 768), BF),
            pltpu.VMEM((2, PAIRS, MESSAGE, 128), BF),
            pltpu.VMEM((2, 32, 32, 128), BF),
            pltpu.VMEM((2, PAIRS, 32, 128), BF),
            pltpu.VMEM((64, LENGTH), BF),
            pltpu.VMEM((128, 768), F32),
            pltpu.SemaphoreType.DMA((2, 4)),
            pltpu.SemaphoreType.DMA((count, 5, 4)),
            pltpu.SemaphoreType.DMA((8,)),
            pltpu.SemaphoreType.DMA((4, 3)),
        ],
        compiler_params=params(1),
        name="forward",
    )(*operands)
    return dict(zip(stored, results)), {
        name: result for (name, _, _), result in zip(KEPT, results[8:])
    }


def attend_back_block(
    exchange, at, length, rows, out_grad, out_turned, log_total, keys_turned, key_grad, outgoing, incoming
):
    cut = slice(at * BLOCK, (at + 1) * BLOCK)
    four = slice(4 * at, 4 * at + 4)
    queries = unpack_block(rows[four, 64:96], True)
    outs = unpack_block(out_grad[four], False)
    outs_turned = outs.astype(F32).T[64:128]
    delta = jnp.sum(outs_turned * out_turned[:, cut], axis=0, keepdims=True)
    shift = log_total[0:1, cut]
    query_grad = jnp.zeros((64, BLOCK), F32)
    for part in range(at + 1):
        span = slice(part * BLOCK, (part + 1) * BLOCK)
        keys = rows[4 * part : 4 * part + 4, 0:64].reshape(BLOCK, 128)
        scores = lax.dot_general(keys, queries, LAST_DIMS, preferred_element_type=F32)
        allowed = allowed_keys(part * BLOCK, at * BLOCK, BLOCK, BLOCK, length)
        probs = jnp.where(allowed, jnp.exp(scores - shift), 0.0)
        probs_grad = lax.dot_general(keys, outs, LAST_DIMS, preferred_element_type=F32)
        score_grad = (probs * (probs_grad - delta)).astype(BF)
        key_grad[span, :] += jnp.dot(score_grad, queries, preferred_element_type=F32) + jnp.dot(
            probs.astype(BF), outs, preferred_element_type=F32
        )
        query_grad += jnp.dot(keys_turned[:, span], score_grad, preferred_element_type=F32)
    outgoing[four, 0:64] = key_grad[cut, :].reshape(4, SPAN, 128).astype(BF)
    outgoing[four, 64:96] = pack_turned(query_grad)
    for there in range(4 * at, 4 * at + 4):
        exchange.to(there, outgoing.at[there], incoming.at[exchange.pair])


def collect_projections(incoming, cosine, sine, result):
    front = front_lanes(64)
    for slot in range(2):
        span = slice(64 * slot, 64 * slot + 64)
        for tile in range(6):
            cut = slice(128 * tile, 128 * tile + 128)
            at = slot * HEADS + 2 * tile
            first, second = (incoming[at + n, 0:64].astype(F32) for n in (0, 1))
            q = unpack_heads(incoming[at, 64:96], incoming[at + 1, 64:96])
            k = jnp.where(front, first, pltpu.roll(second, 64, 1))
            v = jnp.where(front, pltpu.roll(first, 64, 1), second)
            q = turned(q * (1.0 / math.sqrt(HEAD_DIM)), cosine, -sine)
            result[0, span, cut] = q.astype(BF)
            result[1, span, cut] = turned(k, cosine, -sine).astype(BF)
            result[2, span, cut] = v.astype(BF)


def norm_backward(incoming, values, norm_gain):
    inverse = lax.rsqrt(jnp.mean(values * values, axis=-1, keepdims=True) + EPSILON)
    scaled = incoming * norm_gain
    outgoing = inverse * scaled - values * (inverse * inverse * inverse) * jnp.mean(
        scaled * values, axis=-1, keepdims=True
    )
    return outgoing, jnp.sum(incoming * values * inverse, axis=0, keepdims=True)


def feed_back(incoming, paired, gate_up, down, gate_grads, up_grads, hidden_turned):
    source_grad = jnp.zeros((128, 768), F32)
    for z in range(4):
        cut = slice(512 * z, 512 * z + 512)
        hidden_grad = lax.dot_general(
            incoming, down[z].reshape(512, 768), LAST_DIMS, preferred_element_type=F32
        )
        gate, up = paired[0, :, cut], paired[1, :, cut]
        sigmoid = jax.nn.sigmoid(gate)
        hidden = (gate * sigmoid * up).T.astype(BF).reshape(4, 2, 64, 128)
        hidden_turned[0, z] = hidden[:, 0]
        hidden_turned[1, z] = hidden[:, 1]
        gate_grad = (hidden_grad * up * sigmoid * (1.0 + gate * (1.0 - sigmoid))).astype(BF)
        up_grad = (hidden_grad * gate * sigmoid).astype(BF)
        part = slice(512 * (z % 2), 512 * (z % 2) + 512)
        gate_grads[z // 2, :, part] = gate_grad
        up_grads[z // 2, :, part] = up_grad
        for at, value in enumerate((gate_grad, up_grad)):
            source_grad = source_grad + lax.dot_general(
                value, gate_up[at, :, :, :, cut].reshape(768, 512), LAST_DIMS, preferred_element_type=F32
            )
    return source_grad


def turned_low(values):
    return values.astype(F32).T.astype(BF)


def fill_part(part, rows, left_of, right):
    for z in range(4):
        value = jnp.dot(left_of(z), right, preferred_element_type=F32).astype(BF)
        part.fill(z, value.reshape(4, rows, right.shape[1]))


def beside(first, second, rows):
    def left_of(z):
        cut = slice(4 * rows * z, 4 * rows * (z + 1))
        return jnp.concatenate([first[cut], second[cut]], axis=1)

    return left_of


SHARED = {
    "source": ((768, 128), (768, 128)),
    "gate": ((2, 128, 1024), (128, 1024)),
    "up": ((2, 128, 1024), (128, 1024)),
    "hidden": ((2, 4, 4, 64, 128), (4, 4, 64, 128)),
    "fed": ((128, 768), (128, 768)),
    "merged": ((768, 128), (768, 128)),
    "mixed": ((2, 128, 384), (128, 384)),
    "norm": ((768, 128), (768, 128)),
    "low": ((2, 3, 128, 384), (3, 128, 384)),
}
KEPT_NAMES = ("paired", "rows", "merged", "turned", "total")
KEPT_TYPES = {name: (shape, kind) for name, shape, kind in KEPT}
WEIGHT_ORDER = ("down", "wide", "out", "qkv")


def backward_kernel(lengths, *refs):
    refs = list(refs)

    def take(count):
        taken = refs[:count]
        del refs[:count]
        return taken

    cotangent, stream, residual_0, summed_0, residual_1, gains, cosine, sine = take(8)
    far = [dict(zip(KEPT_NAMES, take(len(KEPT_NAMES)))) for _ in range(2)]
    stored = dict(zip(GATHERED[:-1], take(8)))
    (input_grad,) = take(1)
    sums = dict(zip(SUMS, take(len(SUMS))))
    kept = dict(zip(KEPT_NAMES, take(len(KEPT_NAMES))))
    weights = dict(zip(WEIGHT_ORDER, take(4)))
    shared, own = part_scratch()
    shared, own = take(len(shared)), take(len(own))
    given = dict(zip(SHARED, take(len(SHARED))))
    got = [dict(zip(SHARED, take(len(SHARED)))) for _ in range(2)]
    out_grads, to_pairs, to_places, incoming = take(4)
    keys_turned, key_grad, gain_grads, their_gains, stacked = take(5)
    part_sems, give_sems, load_sems, pair_sems = take(4)
    parts = build_parts(shared, own, part_sems, sums)
    axes = Axes(True)
    core = axes.core
    x, me = lax.axis_index(BATCH), lax.axis_index(SEQ)
    barrier = pltpu.get_barrier_semaphore()
    neighbours = [(x, lax.rem(me + by, 32)) for by in range(1, 32)]
    neighbours += [device(shifted(x, by), axes.z, axes.y, core) for by in (1, 2, 3)]
    for where in neighbours:
        pl.semaphore_signal(barrier, inc=1, device_id=where, device_id_type=MESH)

    def load(name, layer):
        at = WEIGHT_ORDER.index(name)
        return pltpu.make_async_copy(stored[name, layer], weights[name], load_sems.at[at])

    def recall(name, layer):
        at = KEPT_NAMES.index(name)
        return pltpu.make_async_copy(far[layer][name], kept[name], load_sems.at[4 + at])

    recall("paired", 1).start()
    for name in WEIGHT_ORDER:
        load(name, 1).start()
    for name in KEPT_NAMES[1:]:
        recall(name, 1).start()

    def gain(at):
        return gains[at : at + 1, :]

    def stages(*work):
        for names, layer, number in work:
            for name in names:
                parts[name, layer].stage(number)

    def share(layer, names):
        copies = []
        for name in names:
            at = list(SHARED).index(name)
            source = given[name]
            if SHARED[name][0] != SHARED[name][1]:
                source = source.at[1 - core]
            copies.append(
                remote(
                    source,
                    got[layer][name],
                    give_sems.at[layer, at, 0],
                    give_sems.at[layer, at, 1],
                    axes.partner,
                )
            )
        return copies

    def start(copies):
        for copy in copies:
            copy.start()

    def finish(copies):
        for copy in copies:
            copy.wait()

    wide, narrow, down = ("gate", "up"), ("left", "right", "o"), ("left", "right")

    def wide_grads(layer):
        left_of = beside(given["source"], got[layer]["source"], 48)
        for name in wide:
            right = jnp.concatenate([given[name][core], got[layer][name][...]], axis=0)
            fill_part(parts[name, layer], 48, left_of, right)

    def narrow_grads(layer):
        def left_of(z):
            mine = given["hidden"][core, z].reshape(256, 128)
            return jnp.concatenate([mine, got[layer]["hidden"][z].reshape(256, 128)], axis=1)

        right = jnp.concatenate([given["fed"][...], got[layer]["fed"][...]], axis=0)
        fill_part(parts["left", layer], 64, left_of, right[:, :384])
        fill_part(parts["right", layer], 64, left_of, right[:, 384:])
        right = jnp.concatenate([given["mixed"][core], got[layer]["mixed"][...]], axis=0)
        left_of = beside(given["merged"], got[layer]["merged"], 48)
        fill_part(parts["o", layer], 48, left_of, right)

    def projection_grads(layer):
        left_of = beside(given["norm"], got[layer]["norm"], 48)
        for at, name in enumerate("qkv"):
            right = jnp.concatenate([given["low"][core, at], got[layer]["low"][at]], axis=0)
            fill_part(parts[name, layer], 48, left_of, right)

    FED = ("source", "gate", "up", "hidden", "fed")
    MIXED = ("merged", "mixed")
    PROJECTED = ("norm", "low")

    def feed(layer, source, grad):
        load("down", layer).wait()
        load("wide", layer).wait()
        recall("paired", layer).wait()
        low = grad.astype(BF)
        given["fed"][...] = low
        given["source"][...] = turned_low(source.astype(BF))
        return feed_back(
            low,
            kept["paired"],
            weights["wide"],
            weights["down"],
            given["gate"],
            given["up"],
            given["hidden"],
        )

    def send_out_grad(layer, grad):
        load("out", layer).wait()
        low = grad.astype(BF)
        given["mixed"][0] = low[:, :384]
        given["mixed"][1] = low[:, 384:]
        for name in KEPT_NAMES[1:]:
            recall(name, layer).wait()
        given["merged"][...] = turned_low(kept["merged"][...])
        merged_grad = (
            lax.dot_general(
                low, weights["out"][...].reshape(768, 768), LAST_DIMS, preferred_element_type=F32
            )
            .astype(BF)
            .astype(F32)
        )
        exchange = Exchange(pair_sems.at[2 * layer])
        to = to_pairs
        for slot in range(2):
            for tile in range(6):
                at = slot * HEADS + 2 * tile
                both = merged_grad[64 * slot : 64 * slot + 64, 128 * tile : 128 * tile + 128]
                to[at], to[at + 1] = pack_heads(both)
        for pair in range(PAIRS):
            exchange.to(pair_device(pair), to.at[pair], out_grads.at[layer, me])
        return exchange

    def attention(layer, exchange, between):
        rows = kept["rows"]
        length = slot_length(lengths, exchange.pair)

        @pl.when(exchange.has_pair)
        def _():
            all_rows = rows[:, 0:64].reshape(LENGTH, 128).astype(F32)
            keys_turned[...] = all_rows.T[0:64].astype(BF)
            key_grad[...] = jnp.zeros_like(key_grad)

        exchange.wait(to_pairs, out_grads.at[layer], "pairs")
        back = Exchange(pair_sems.at[2 * layer + 1])
        for at in reversed(range(BLOCKS)):

            @pl.when(exchange.has_pair)
            def _(at=at):
                attend_back_block(
                    back,
                    at,
                    length,
                    rows,
                    out_grads.at[layer],
                    kept["turned"],
                    kept["total"],
                    keys_turned,
                    key_grad,
                    to_places,
                    incoming.at[layer],
                )

            stages(*between.get(at, ()))
        stages(*between.get("sent", ()))
        back.wait(to_places, incoming.at[layer], "places")
        collect_projections(incoming.at[layer], cosine[...], sine[...], stacked)

    def source_gradient(layer, source):
        load("qkv", layer).wait()
        given["norm"][...] = turned_low(source.astype(BF))
        for at in range(3):
            given["low"][0, at] = stacked[at, :, 0:384]
            given["low"][1, at] = stacked[at, :, 384:768]
        copies = share(layer, PROJECTED)
        start(copies)
        result = jnp.zeros((128, 768), F32)
        for at in range(3):
            result = result + lax.dot_general(
                stacked[at],
                weights["qkv"][at].reshape(768, 768),
                LAST_DIMS,
                preferred_element_type=F32,
            )
        return result, copies

    normed_two, _ = norm_forward(residual_1[...], gain(3))
    fed_grad = feed(1, normed_two, cotangent[...])
    for name in ("down", "wide"):
        load(name, 0).start()
    recall("paired", 0).start()
    through, gain_grad = norm_backward(fed_grad, residual_1[...], gain(3))
    gain_grads[...] = jnp.zeros_like(gain_grads)
    gain_grads[3:4, :] = gain_grad
    residual_grad = cotangent[...] + through
    pl.semaphore_wait(barrier, len(neighbours))
    exchange = send_out_grad(1, residual_grad)
    load("out", 0).start()
    copies = share(1, FED + MIXED)
    start(copies)
    finish(copies)
    wide_grads(1)
    stages((wide, 1, 0))
    narrow_grads(1)
    stages((narrow, 1, 1))
    attention(1, exchange, {6: [(narrow, 1, 2)], "sent": [(narrow, 1, 3)]})
    for name in KEPT_NAMES[1:]:
        recall(name, 0).start()
    shallow, _ = norm_forward(summed_0[...], gain(1))
    normed, _ = norm_forward(shallow, gain(2))
    normed_grad, copies = source_gradient(1, normed)
    load("qkv", 0).start()
    stages((narrow, 1, 4))
    through, gain_grad = norm_backward(normed_grad, shallow, gain(2))
    gain_grads[2:3, :] = gain_grad
    shallow_grad = residual_grad + through
    summed_grad, gain_grad = norm_backward(shallow_grad, summed_0[...], gain(1))
    gain_grads[1:2, :] = gain_grad

    finish(copies)
    projection_grads(1)
    stages(("qkv", 1, 1))
    middle, _ = norm_forward(residual_0[...], gain(0))
    fed_grad = feed(0, middle, summed_grad)
    middle_grad = summed_grad + fed_grad
    residual_grad, gain_grad = norm_backward(middle_grad, residual_0[...], gain(0))
    gain_grads[0:1, :] = gain_grad
    exchange = send_out_grad(0, residual_grad)
    copies = share(0, FED + MIXED)
    start(copies)
    stages(("qkv", 1, 2), (narrow, 1, 5), (wide, 1, 1))
    finish(copies)
    narrow_grads(0)
    stages((down, 0, 0))
    wide_grads(0)
    stages((wide, 0, 1), ("o", 0, 1), (narrow, 1, 6))
    attention(
        0,
        exchange,
        {
            6: [("qkv", 1, 3), (wide, 1, 2)],
            3: [(wide, 1, 3)],
            0: [("qkv", 1, 4)],
            "sent": [(wide, 0, 2), ("o", 0, 2), (wide, 1, 4)],
        },
    )
    source_grad, copies = source_gradient(0, stream[...])
    swap = remote(
        gain_grads, their_gains, give_sems.at[0, len(SHARED), 0], give_sems.at[0, len(SHARED), 1], axes.partner
    )
    swap.start()
    input_grad[...] = residual_grad + source_grad
    stages(("qkv", 1, 5), (wide, 1, 5))
    finish(copies)
    projection_grads(0)
    swap.wait()
    gain_total = gain_grads[...] + their_gains[...]
    gain_total = jnp.concatenate([gain_total, jnp.zeros((8, 128), F32)], axis=1)
    for z in range(4):
        for y in range(4):
            first, second = (24 * (8 * z + 2 * y + which) // 128 * 128 for which in (0, 1))
            parts["gain", 0].total[y, z] = jnp.where(
                core == 0, gain_total[:, first : first + 256], gain_total[:, second : second + 256]
            )
    last = ("q", "k", "v", "gain")
    stages((last, 0, 1), (down, 0, 1), (wide, 0, 3), ("o", 0, 3), ("qkv", 1, 6), (wide, 1, 6))
    stages((last, 0, 2), (down, 0, 2), (wide, 0, 4), ("o", 0, 4), (down, 0, 3))
    stages((last, 0, 4), (down, 0, 4), (wide, 0, 5), ("o", 0, 5), (last, 0, 5), (down, 0, 5))
    stages((wide, 0, 6), ("o", 0, 6), (last, 0, 6), (down, 0, 6))


def run_backward(lengths, kept, store, cosine, sine):
    near = [kept["cotangent"], kept["stream"]] + [
        kept[name] for name in ("mid_0", "summed_0", "mid_1", "gain")
    ]
    near += [cosine, sine]
    away = [kept[name + layer] for layer in ("_0", "_1") for name in KEPT_NAMES]
    away += [store[key] for key in GATHERED[:-1]]
    shared, own = part_scratch()
    results = pl.pallas_call(
        backward_kernel,
        out_shape=[jax.ShapeDtypeStruct((128, 768), F32)]
        + [jax.ShapeDtypeStruct(*shape) for shape in SUMS.values()],
        in_specs=[SMEM] + [VMEM] * len(near) + [ANY] * len(away),
        out_specs=[VMEM] * (1 + len(SUMS)),
        scratch_shapes=[pltpu.VMEM(*KEPT_TYPES[name + "_0"]) for name in KEPT_NAMES]
        + [pltpu.VMEM(*WEIGHTS[name]) for name in WEIGHT_ORDER]
        + shared
        + own
        + [pltpu.VMEM(here, BF) for here, _ in SHARED.values()]
        + [pltpu.VMEM(there, BF) for _, there in SHARED.values()] * 2
        + [
            pltpu.VMEM((2, 32, 32, 128), BF),
            pltpu.VMEM((PAIRS, 32, 128), BF),
            pltpu.VMEM((32, MESSAGE, 128), BF),
            pltpu.VMEM((2, PAIRS, MESSAGE, 128), BF),
            pltpu.VMEM((64, LENGTH), BF),
            pltpu.VMEM((LENGTH, 128), F32),
            pltpu.VMEM((8, 768), F32),
            pltpu.VMEM((8, 768), F32),
            pltpu.VMEM((3, 128, 768), BF),
            pltpu.SemaphoreType.DMA((2 * len(PARTS), SCATTER_SEMAPHORES)),
            pltpu.SemaphoreType.DMA((2, len(SHARED) + 1, 2)),
            pltpu.SemaphoreType.DMA((9,)),
            pltpu.SemaphoreType.DMA((4, 3)),
        ],
        compiler_params=params(2),
        name="backward",
    )(lengths, *near, *away)
    return results[0], dict(zip(SUMS, results[1:]))


def angles(places):
    half_dim = HEAD_DIM // 2
    frequency = jnp.exp(-math.log(10000.0) * jnp.arange(half_dim).astype(F32) / half_dim)
    phases = places.astype(F32)[:, None] * frequency[None, :]
    cosine, sine = jnp.cos(phases), jnp.sin(phases)
    return (
        jnp.concatenate([cosine] * 4, axis=1),
        jnp.concatenate([-sine, sine] * 2, axis=1),
    )


def update(weight_matrix, moment, average, gradient, step_size):
    moment_new = MOMENTUM * moment + gradient
    weight_new = weight_matrix - step_size * (gradient + MOMENTUM * moment_new)
    return (moment_new, weight_new, AVERAGING * average + (1.0 - AVERAGING) * weight_new)


STEPPED = ("qkv", "out", "wide", "down")


def update_kernel(step_size, *refs):
    count = len(STEPPED)
    sources, refs = refs[: 4 * count + 2], refs[4 * count + 2 :]
    targets, refs = refs[: 3 * count + 2], refs[3 * count + 2 :]
    held, (loads, stores) = refs[:-2], refs[-2:]
    placed, held = held[-2:], held[:-2]
    fetches = [
        pltpu.make_async_copy(source, here, loads.at[at])
        for at, (source, here) in enumerate(zip(sources, held))
    ]
    for copy in fetches:
        copy.start()
    saves = []

    def save(here, at):
        copy = pltpu.make_async_copy(here, targets[at], stores.at[at])
        copy.start()
        saves.append(copy)

    for at in range(count):
        for copy in fetches[4 * at : 4 * at + 4]:
            copy.wait()
        gradient, weight_matrix, moment, average = held[4 * at : 4 * at + 4]
        stepped = update(weight_matrix[...], moment[...], average[...], gradient[...], step_size)
        for n, (here, value) in enumerate(zip((moment, weight_matrix, average), stepped)):
            here[...] = value
            save(here, 3 * at + n)
    for at in range(2):
        fetches[4 * count + at].wait()
        for slot in range(2):
            placed[at][:, slot, :] = held[4 * count + at][64 * slot : 64 * slot + 64]
        save(placed[at], 3 * count + at)
    for copy in saves:
        copy.wait()


def run_update(step_size, sums, states, activations):
    shapes = {name: jax.ShapeDtypeStruct(*SUMS[name]) for name in STEPPED}
    operands = []
    for name in STEPPED:
        operands += [sums[name], *states[name]]
    operands += activations
    by_place = jax.ShapeDtypeStruct((SPAN, 2, 768), F32)
    results = pl.pallas_call(
        functools.partial(update_kernel, step_size),
        out_shape=[shapes[name] for name in STEPPED for _ in range(3)] + [by_place] * 2,
        in_specs=[ANY] * len(operands),
        out_specs=[ANY] * (3 * len(STEPPED) + 2),
        scratch_shapes=[pltpu.VMEM(operand.shape, F32) for operand in operands]
        + [pltpu.VMEM((SPAN, 2, 768), F32)] * 2
        + [
            pltpu.SemaphoreType.DMA((len(operands),)),
            pltpu.SemaphoreType.DMA((3 * len(STEPPED) + 2,)),
        ],
        compiler_params=pltpu.CompilerParams(vmem_limit_bytes=VMEM_BYTES),
        name="step",
    )(*operands)
    return results[: 3 * len(STEPPED)], results[3 * len(STEPPED) :]


def on_device(
    inputs,
    cotangent,
    lengths,
    qkv_weight,
    qkv_moment,
    qkv_average,
    out_weight,
    out_moment,
    out_average,
    gate_up_weight,
    gate_up_moment,
    gate_up_average,
    down_weight,
    down_moment,
    down_average,
    norm_gains,
    gain_moment,
    gain_average,
):
    places = lax.axis_index(SEQ) * SPAN + jnp.arange(SPAN)
    cosine, sine = angles(places)
    seq = lax.axis_index(SEQ)
    own_gains = lax.dynamic_update_slice(
        jnp.zeros((8, 256), F32),
        norm_gains.astype(BF).astype(F32).reshape(4, 24),
        (0, lax.rem(24 * seq, 128)),
    )
    store, kept = run_forward(
        lengths[0],
        qkv_weight,
        out_weight,
        gate_up_weight,
        down_weight,
        own_gains,
        inputs[0],
        cotangent[0],
        cosine,
        sine,
    )
    input_grad, sums = run_backward(
        lengths[0], kept, store, cosine, sine
    )
    gain_sum = lax.dynamic_slice(
        sums["gain"][0], (0, lax.rem(24 * seq, 128)), (4, 24)
    ).reshape(2, 2, 24)

    step_size = STEP_RATE / math.sqrt(
        lax.axis_size(BATCH) * SPAN * lax.axis_size(SEQ) * 2
    )
    stepped, (result, input_grad) = run_update(
        step_size,
        sums,
        {
            "qkv": (qkv_weight, qkv_moment, qkv_average),
            "out": (out_weight, out_moment, out_average),
            "wide": (gate_up_weight, gate_up_moment, gate_up_average),
            "down": (down_weight, down_moment, down_average),
        },
        [kept["result"], input_grad],
    )
    gain_new = update(norm_gains, gain_moment, gain_average, gain_sum, step_size)
    return (result[None], input_grad[None], *stepped, *gain_new)


def solution(mesh):
    rows = P(BATCH, SEQ, None, None)
    wide = P(None, None, SEQ, None)
    flat = P(None, SEQ, None)
    gains = P(None, None, SEQ)
    state = (wide,) * 3 + (flat,) * 3 + (wide,) * 3 + (flat,) * 3 + (gains,) * 3
    return jax.shard_map(
        on_device,
        mesh=mesh,
        in_specs=(rows, rows, P(BATCH, None)) + state,
        out_specs=(rows, rows) + state,
        check_vma=False,
    )
```

```python
import functools
import math

import jax
import jax.numpy as jnp
from jax import lax
from jax.experimental import pallas as pl
from jax.experimental.pallas import tpu as pltpu
from jax.sharding import PartitionSpec as P

MESH = pl.DeviceIdType.MESH
BF = jnp.bfloat16
F32 = jnp.float32
BATCH, SEQ = "batch", "seq"
HEAD_DIM = 64
HEADS = 12
PAIRS = 24
SPAN = 64
LENGTH = 2048
BLOCK = 256
EPSILON = 1e-06
MOMENTUM = 0.5
AVERAGING = 0.5
STEP_RATE = 0.1
MASKED = -1e30
VMEM_BYTES = 62 * 2**20
VMEM = pl.BlockSpec(memory_space=pltpu.VMEM)
ANY = pl.BlockSpec(memory_space=pl.ANY)
SMEM = pl.BlockSpec(memory_space=pltpu.SMEM)
ALL = pl.ds(0, 4)


def params(collective_id):
    return pltpu.CompilerParams(
        collective_id=collective_id, has_side_effects=True, vmem_limit_bytes=VMEM_BYTES
    )


def coordinates():
    seq = lax.axis_index(SEQ)
    return (
        lax.axis_index(BATCH),
        lax.div(seq, 8),
        lax.rem(lax.div(seq, 2), 4),
        lax.rem(seq, 2),
    )


def device(x, z, y, core):
    return (x, (z * 4 + y) * 2 + core)


def shifted(value, by):
    return lax.rem(value + by, 4)


def signal(partners):
    barrier = pltpu.get_barrier_semaphore()
    for partner in partners:
        pl.semaphore_signal(barrier, inc=1, device_id=partner, device_id_type=MESH)


def greet(partners):
    signal(partners)
    pl.semaphore_wait(pltpu.get_barrier_semaphore(), len(partners))


def remote(source, target, send, receive, where):
    return pltpu.make_async_remote_copy(
        src_ref=source,
        dst_ref=target,
        send_sem=send,
        recv_sem=receive,
        device_id=where,
        device_id_type=MESH,
    )


class Axes:
    def __init__(self, first_is_y):
        x, z, y, core = coordinates()
        self.first_is_y = first_is_y
        self.x, self.z, self.y, self.core = x, z, y, core
        self.m1, self.m2 = (y, z) if first_is_y else (z, y)
        self.partner = device(x, z, y, 1 - core)

    def along_y(self, by):
        return device(self.x, self.z, shifted(self.y, by), self.core)

    def along_z(self, by):
        return device(self.x, shifted(self.z, by), self.y, self.core)

    def first(self, by):
        return self.along_y(by) if self.first_is_y else self.along_z(by)

    def second(self, by):
        return self.along_z(by) if self.first_is_y else self.along_y(by)

    def order(self, i1, i2):
        return (i2, i1) if self.first_is_y else (i1, i2)


class GatherSegment:
    def __init__(self, first_is_y, view, semaphores, own=None):
        self.axes = Axes(first_is_y)
        self.view, self.own, self.semaphores = view, own, semaphores

    def block(self, i1, i2):
        return self.view(*self.axes.order(i1, i2))

    def row(self, by, part=ALL):
        return self.block(part, shifted(self.axes.m2, by))

    def keep(self):
        here = self.block(self.axes.m1, self.axes.m2)
        return pltpu.make_async_copy(self.own, here, self.semaphores.at[3, 0])

    def begin(self, phase):
        axes = self.axes
        sem = [self.semaphores.at[phase, at] for at in range(4)]

        def send(part, where):
            remote(part, part, sem[0], sem[1], where).start()

        def share(part):
            remote(part, part, sem[2], sem[3], axes.partner).start()

        if phase == 0:
            here = self.block(axes.m1, axes.m2)
            source = here if self.own is None else self.own
            for by in (1, 3, 2):
                remote(source, here, sem[0], sem[1], axes.first(by)).start()
        elif phase == 1:
            send(self.row(0), axes.second(1))
            send(self.row(0), axes.second(3))
            share(self.row(0))
        elif phase == 2:
            send(self.row(3, pl.ds(0, 2)), axes.second(1))
            send(self.row(1, pl.ds(2, 2)), axes.second(3))
            share(self.row(3))
            share(self.row(1))
        else:
            share(self.row(2))

    def end(self, phase):
        axes = self.axes
        sem = [self.semaphores.at[phase, at] for at in range(4)]
        one, two = self.row(0), self.block(ALL, pl.ds(0, 2))
        moved = (self.block(pl.ds(0, 3), axes.m2), two, one, None)[phase]
        shared = (None, one, two, one)[phase]
        if moved is not None:
            remote(moved, moved, sem[0], sem[1], axes.partner).wait()
        if shared is not None:
            remote(shared, shared, sem[2], sem[3], axes.partner).wait()


class AcrossSegment(GatherSegment):
    def __init__(self, first_is_y, quarters, semaphores, own):
        x = lax.axis_index(BATCH)
        super().__init__(first_is_y, lambda z, y: quarters(z, y, x, 1), semaphores, own)
        self.quarters = quarters

    def begin(self, phase):
        axes = self.axes
        sem = [self.semaphores.at[phase, at] for at in range(4)]

        def send(part, where):
            remote(part, part, sem[0], sem[1], where).start()

        def share(part):
            remote(part, part, sem[2], sem[3], axes.partner).start()

        if phase == 0:
            here = self.block(axes.m1, axes.m2)
            for by in (1, 3, 2):
                remote(self.own, here, sem[0], sem[1], axes.first(by)).start()
        elif phase == 1:
            send(self.row(0), axes.second(1))
            send(self.row(0), axes.second(3))
        elif phase == 2:
            send(self.row(3, pl.ds(0, 2)), axes.second(1))
            send(self.row(1, pl.ds(2, 2)), axes.second(3))
        elif phase == 3:
            mine = self.block(ALL, ALL)
            for by in (1, 3):
                send(mine, self.plane(by))
            far = [self.semaphores.at[4, at] for at in range(2)]
            remote(mine, mine, far[0], far[1], self.plane(2)).start()
            share(mine)
        elif phase == 4:
            for by in (1, 3):
                share(self.quarters(ALL, ALL, shifted(axes.x, by), 1))
        else:
            self.last_share().start()

    def plane(self, by):
        axes = self.axes
        return device(shifted(axes.x, by), axes.z, axes.y, axes.core)

    def last_share(self):
        part = self.quarters(ALL, ALL, shifted(self.axes.x, 2), 1)
        sem = [self.semaphores.at[2, at] for at in (2, 3)]
        return remote(part, part, sem[0], sem[1], self.axes.partner)

    def end(self, phase):
        axes = self.axes
        if phase == 5:
            self.last_share().wait()
            return
        sem = [self.semaphores.at[phase, at] for at in range(4)]
        two = self.quarters(ALL, ALL, 0, 2)
        mine = self.block(ALL, ALL)
        moved = (
            self.block(pl.ds(0, 3), axes.m2),
            self.block(ALL, pl.ds(0, 2)),
            self.row(0),
            two,
            mine,
        )[phase]
        shared = (None, None, None, mine, two)[phase]
        remote(moved, moved, sem[0], sem[1], axes.partner).wait()
        if shared is not None:
            remote(shared, shared, sem[2], sem[3], axes.partner).wait()


def across_views(name, ref):
    core = Axes(True).core

    def columns(first, count):
        return pl.ds(pl.multiple_of(core * 1024 + first * 256, 128), 256 * count)

    def rows(first, count):
        return pl.ds(pl.multiple_of(first * 16, 16), 16 * count)

    if name == "wide":
        return [
            (True, lambda z, y, first, count: ref.at[0, z, y, :, columns(first, count)]),
            (False, lambda z, y, first, count: ref.at[1, z, y, :, columns(first, count)]),
        ]
    return [
        (True, lambda z, y, first, count: ref.at[z, y, core, rows(first, count), pl.ds(0, 384)]),
        (False, lambda z, y, first, count: ref.at[z, y, core, rows(first, count), pl.ds(384, 384)]),
    ]


def across_owns(name, ref):
    axes = Axes(True)
    if name == "wide":
        columns = pl.ds(pl.multiple_of(axes.core * 1024 + axes.x * 256, 128), 256)
        return [ref.at[0, :, columns], ref.at[1, :, columns]]
    rows = pl.ds(pl.multiple_of(axes.x * 16, 16), 16)
    return [ref.at[rows, pl.ds(0, 384)], ref.at[rows, pl.ds(384, 384)]]


ACROSS = (("wide", 1), ("down", 0))


def halves(core, width):
    return pl.ds(pl.multiple_of(core * (width // 2), 128), width // 2)


def weight_views(name, ref):
    core = Axes(True).core
    narrow, wide = halves(core, 768), halves(core, 2048)
    if name == "qkv":
        return [
            (True, lambda z, y: ref.at[pl.ds(0, 2), z, y, :, narrow]),
            (False, lambda z, y: ref.at[2, z, y, :, narrow]),
        ]
    if name == "out":
        return [(False, lambda z, y: ref.at[z, y, :, narrow])]
    if name == "wide":
        return [
            (True, lambda z, y: ref.at[0, z, y, :, wide]),
            (False, lambda z, y: ref.at[1, z, y, :, wide]),
        ]
    if name == "down":
        return [
            (True, lambda z, y: ref.at[z, y, core, :, pl.ds(0, 384)]),
            (False, lambda z, y: ref.at[z, y, core, :, pl.ds(384, 384)]),
        ]
    return [(True, lambda z, y: ref.at[z, y, core])]


def own_views(name, ref):
    core = Axes(True).core
    narrow, wide = halves(core, 768), halves(core, 2048)
    if name == "qkv":
        return [ref.at[pl.ds(0, 2), :, narrow], ref.at[2, :, narrow]]
    if name == "out":
        return [ref.at[:, narrow]]
    if name == "wide":
        return [ref.at[0, :, wide], ref.at[1, :, wide]]
    if name == "down":
        return [ref.at[:, pl.ds(0, 384)], ref.at[:, pl.ds(384, 384)]]
    return [ref]


WEIGHTS = {
    "qkv": ((3, 4, 4, 48, 768), BF),
    "out": ((4, 4, 48, 768), BF),
    "wide": ((2, 4, 4, 48, 2048), BF),
    "down": ((4, 4, 2, 64, 768), BF),
    "gain": ((4, 4, 2, 8, 256), F32),
}
SEGMENTS = {"qkv": 2, "out": 1, "wide": 2, "down": 2, "gain": 1}
GATHERED = [(name, layer) for layer in range(2) for name in ("qkv", "out", "wide", "down")] + [
    ("gain", 0)
]


def weight_shape(key):
    return jax.ShapeDtypeStruct(*WEIGHTS[key[0]])


class ScatterPart:
    def __init__(self, first_is_y, total, rows, ring, blocks, groups, semaphores, finish):
        self.axes = Axes(first_is_y)
        self.total, self.rows, self.ring, self.blocks, self.groups = total, rows, ring, blocks, groups
        self.semaphores, self.finish = semaphores, finish

    def fill(self, z, value):
        if self.axes.first_is_y:
            self.total[z] = value
        else:
            self.total[:, z] = value

    def spread(self):
        axes, sem = self.axes, self.semaphores
        for by in (1, 3, 2):
            remote(
                self.total.at[axes.m2, shifted(axes.m1, by)],
                self.blocks.at[by - 1],
                sem.at[4],
                sem.at[5],
                axes.first(by),
            ).start()

    def stage(self, number):
        axes, sem, total = self.axes, self.semaphores, self.total
        m1, m2 = axes.m1, axes.m2
        before, after, across = shifted(m2, 3), shifted(m2, 1), shifted(m2, 2)
        low, high = pl.ds(0, 2), pl.ds(2, 2)

        def add(target, source):
            target[...] = (target[...].astype(F32) + source[...].astype(F32)).astype(target.dtype)

        if number == 1:
            remote(
                total.at[across, low], self.ring.at[0], sem.at[0], sem.at[1], axes.second(1)
            ).start()
            remote(
                total.at[across, high], self.ring.at[1], sem.at[0], sem.at[1], axes.second(3)
            ).start()
        elif number == 2:
            row = total.at[m2]
            remote(row, self.ring, sem.at[0], sem.at[1], axes.partner).wait()
            add(total.at[after, low], self.ring.at[0])
            add(total.at[before, high], self.ring.at[1])
            remote(
                total.at[after], self.rows.at[0], sem.at[2], sem.at[3], axes.second(1)
            ).start()
            remote(
                total.at[before], self.rows.at[1], sem.at[2], sem.at[3], axes.second(3)
            ).start()
        elif number == 3:
            remote(self.rows, self.rows, sem.at[2], sem.at[3], axes.partner).wait()
            for at in range(4):
                total[m2, at] = (
                    total[m2, at].astype(F32)
                    + self.rows[0, at].astype(F32)
                    + self.rows[1, at].astype(F32)
                ).astype(total.dtype)
            self.spread()
        elif number == 4:
            remote(self.blocks, self.blocks, sem.at[4], sem.at[5], axes.partner).wait()
            self.groups[axes.x] = (
                total[m2, m1].astype(F32)
                + self.blocks[0].astype(F32)
                + self.blocks[1].astype(F32)
                + self.blocks[2].astype(F32)
            ).astype(total.dtype)
            mine = self.groups.at[axes.x]
            for by in (1, 3, 2):
                remote(
                    mine,
                    mine,
                    sem.at[6],
                    sem.at[7],
                    device(shifted(axes.x, by), axes.z, axes.y, axes.core),
                ).start()
        elif number == 5:
            three = self.groups.at[pl.ds(0, 3)]
            remote(three, three, sem.at[6], sem.at[7], axes.partner).wait()
            summed = self.groups[0].astype(F32)
            for at in range(1, 4):
                summed = summed + self.groups[at].astype(F32)
            self.finish(0, summed)
        else:
            self.finish(1, None)


class AcrossPart(ScatterPart):
    def __init__(self, first_is_y, whole, quarter, came, rows, ring, blocks, groups, semaphores, finish):
        super().__init__(first_is_y, quarter, rows, ring, blocks, groups, semaphores, finish)
        self.whole, self.came = whole, came
        self.by_rows = whole.shape[2] == 64

    def fill(self, z, value):
        if self.axes.first_is_y:
            self.whole[z] = value
        else:
            self.whole[:, z] = value

    def quarter(self, at):
        if self.by_rows:
            return pl.ds(pl.multiple_of(at * 16, 16), 16), slice(None)
        return slice(None), pl.ds(pl.multiple_of(at * 256, 128), 256)

    def stage(self, number):
        axes, sem = self.axes, self.semaphores
        if number == 0:
            for by in (1, 3, 2):
                there = shifted(axes.x, by)
                remote(
                    self.whole.at[(slice(None), slice(None)) + self.quarter(there)],
                    self.came.at[by - 1],
                    sem.at[10],
                    sem.at[11],
                    device(there, axes.z, axes.y, axes.core),
                ).start()
            return
        if number == 1:
            remote(self.came, self.came, sem.at[10], sem.at[11], axes.partner).wait()
            for at in range(4):
                summed = self.whole[(at, slice(None)) + self.quarter(axes.x)].astype(F32)
                for by in range(3):
                    summed = summed + self.came[by, at].astype(F32)
                self.total[at] = summed.astype(BF)
        if number == 5:
            three = self.groups.at[pl.ds(0, 3)]
            remote(three, three, sem.at[6], sem.at[7], axes.partner).wait()
            quarters = [self.groups[at].astype(F32) for at in range(4)]
            self.finish(0, jnp.concatenate(quarters, axis=0 if self.by_rows else 1))
            return
        super().stage(number)


class StraightPart(ScatterPart):
    def stage(self, number):
        axes, sem = self.axes, self.semaphores
        m2 = axes.m2
        if number == 1:
            for by in (1, 3, 2):
                remote(
                    self.total.at[shifted(m2, by)],
                    self.rows.at[by - 1],
                    sem.at[2],
                    sem.at[3],
                    axes.second(by),
                ).start()
        elif number == 2:
            remote(self.rows, self.rows, sem.at[2], sem.at[3], axes.partner).wait()
            for at in range(4):
                summed = self.total[m2, at].astype(F32)
                for by in range(3):
                    summed = summed + self.rows[by, at].astype(F32)
                self.total[m2, at] = summed.astype(self.total.dtype)
            self.spread()
        elif number != 3:
            super().stage(number)


SCATTER_SEMAPHORES = 12
ACROSS_PARTS = (("left", 0), ("right", 0), ("gate", 1), ("up", 1))
LAST_PARTS = (("q", 0), ("k", 0), ("v", 0), ("gain", 0))
PARTS = {
    "gate": (True, 48, 1024, BF),
    "up": (False, 48, 1024, BF),
    "left": (True, 64, 384, BF),
    "right": (False, 64, 384, BF),
    "o": (False, 48, 384, BF),
    "q": (True, 48, 384, BF),
    "k": (False, 48, 384, BF),
    "v": (True, 48, 384, BF),
    "gain": (False, 8, 256, F32),
}
SOURCE = {
    "q": "qkv", "k": "qkv", "v": "qkv", "o": "out", "gate": "wide", "up": "wide",
    "left": "down", "right": "down", "gain": "gain",
}
SUMS = {
    "qkv": ((2, 3, 24, 768), F32),
    "out": ((2, 24, 768), F32),
    "wide": ((2, 2, 24, 2048), F32),
    "down": ((2, 64, 768), F32),
    "gain": ((1, 8, 256), F32),
}
LEFT, RIGHT = pl.ds(0, 384), pl.ds(384, 384)


def part_target(part, ref):
    if part in ("q", "k", "v"):
        return ref.at["qkv".index(part)]
    if part in ("gate", "up"):
        return ref.at[int(part == "up")]
    if part in ("left", "right"):
        return ref.at[:, LEFT if part == "left" else RIGHT]
    return ref


def rows_swapped(target, mine, theirs, sem):
    axes = Axes(True)
    core = axes.core

    def finish(part, summed):
        own_rows = pl.ds(pl.multiple_of(core * 24, 8), 24)
        other_rows = pl.ds(pl.multiple_of((1 - core) * 24, 8), 24)
        copy = remote(mine.at[other_rows, :], theirs, sem.at[8], sem.at[9], axes.partner)
        if part == 0:
            mine[...] = summed
            copy.start()
        else:
            copy.wait()
            kept = mine[own_rows, :]
            got = theirs[...]
            width = kept.shape[-1]
            target[:, :width] = jnp.where(core == 0, kept, got)
            target[:, width:] = jnp.where(core == 0, got, kept)

    return finish


def direct(target):
    def finish(part, summed):
        if part == 0:
            target[...] = summed

    return finish


def part_scratch():
    shared, own = [], []
    for part, (_, rows, width, kind) in PARTS.items():
        shared += [
            pltpu.VMEM((4, 4, rows, width), kind),
            pltpu.VMEM((8, 128) if part == "gain" else (2, 4, rows, width), kind),
            pltpu.VMEM((48, width), F32) if rows == 48 else pltpu.VMEM((8, 128), F32),
        ]
        for layer in range(1 if part == "gain" else 2):
            across = (part, layer) in ACROSS_PARTS
            block = (rows, width)
            if across:
                block = (16, width) if rows == 64 else (rows, width // 4)
                own += [
                    pltpu.VMEM((4, 4) + block, kind),
                    pltpu.VMEM((3, 4, 4) + block, kind),
                    pltpu.VMEM((2, 4) + block, kind),
                ]
            straight = (part, layer) in LAST_PARTS
            own += [
                pltpu.VMEM(((3, 4) if straight else (2, 2)) + block, kind),
                pltpu.VMEM((3,) + block, kind),
                pltpu.VMEM((4,) + block, kind),
                pltpu.VMEM((24, width), F32) if rows == 48 else pltpu.VMEM((8, 128), F32),
            ]
    return shared, own


def build_parts(shared, own, sems, sums):
    parts = {}
    count = 0
    own = list(own)

    def take(number):
        taken = own[:number]
        del own[:number]
        return taken

    for at, (part, (first_is_y, rows, _, _)) in enumerate(PARTS.items()):
        total, rows_in, mine = shared[3 * at : 3 * at + 3]
        for layer in (0,) if part == "gain" else (0, 1):
            if (part, layer) in ACROSS_PARTS:
                quarter, came, rows_here = take(3)
            ring, blocks, groups, theirs = take(4)
            target = part_target(part, sums[SOURCE[part]].at[layer])
            sem = sems.at[count]
            finish = rows_swapped(target, mine, theirs, sem) if rows == 48 else direct(target)
            if (part, layer) in ACROSS_PARTS:
                parts[part, layer] = AcrossPart(
                    first_is_y, total, quarter, came, rows_here, ring, blocks, groups, sem, finish
                )
            elif (part, layer) in LAST_PARTS:
                parts[part, layer] = StraightPart(
                    first_is_y, total, ring, None, blocks, groups, sem, finish
                )
            else:
                parts[part, layer] = ScatterPart(
                    first_is_y, total, rows_in, ring, blocks, groups, sem, finish
                )
            count += 1
    return parts


def pair_device(pair):
    if pair < 16:
        return 2 * pair
    z = (pair - 16) // 2
    return 2 * (4 * z + 2 * ((pair - 16) % 2) + z % 2) + 1


def own_pair():
    _, z, y, core = coordinates()
    has_pair = (core == 0) | (lax.rem(z + y, 2) == 0)
    pair = jnp.where(core == 0, 4 * z + y, 16 + 2 * z + lax.div(y, 2))
    return has_pair, pair


def lanes(shape):
    return lax.broadcasted_iota(jnp.int32, shape, len(shape) - 1)


def turned(values, cosine, sine):
    here = lax.rem(lanes(values.shape), 64) < 32
    width = values.shape[-1]
    other = jnp.where(here, pltpu.roll(values, width - 32, 1), pltpu.roll(values, 32, 1))
    return values * cosine + other * sine


def twice(table):
    return jnp.concatenate([table, table], axis=0)


def allowed_keys(first_key, first_query, keys, queries, length):
    key = first_key + lax.broadcasted_iota(jnp.int32, (keys, queries), 0)
    query = first_query + lax.broadcasted_iota(jnp.int32, (keys, queries), 1)
    return (key <= query) & (key < length)


def slot_length(lengths, pair):
    return jnp.where(pair < HEADS, lengths[0], lengths[1])


LAST_DIMS = (((1,), (1,)), ((), ()))
BLOCKS = LENGTH // BLOCK
MESSAGE = 96


def front_lanes(rows):
    return lanes((rows, 128)) < 64


def pack_heads(both):
    front = front_lanes(32)
    top, bottom = both[0:32], both[32:64]
    return (
        jnp.where(front, top, pltpu.roll(bottom, 64, 1)).astype(BF),
        jnp.where(front, pltpu.roll(top, 64, 1), bottom).astype(BF),
    )


def unpack_heads(first, second):
    front = front_lanes(32)
    first, second = first.astype(F32), second.astype(F32)
    return jnp.concatenate(
        [
            jnp.where(front, first, pltpu.roll(second, 64, 1)),
            jnp.where(front, pltpu.roll(first, 64, 1), second),
        ],
        axis=0,
    )


def unpack_block(packed, to_front):
    packed = packed.astype(F32).reshape(128, 128)
    other = pltpu.roll(packed, 64, 1)
    front = front_lanes(128)
    if to_front:
        top, bottom = jnp.where(front, packed, 0.0), jnp.where(front, other, 0.0)
    else:
        top, bottom = jnp.where(front, 0.0, other), jnp.where(front, 0.0, packed)
    joined = jnp.concatenate([top.reshape(4, 32, 128), bottom.reshape(4, 32, 128)], axis=1)
    return joined.reshape(256, 128).astype(BF)


def pack_turned(turned_values):
    rows = jnp.concatenate([turned_values, turned_values], axis=0).T.reshape(4, 64, 128)
    front = lanes((4, 32, 128)) < 64
    return jnp.where(front, rows[:, 0:32], rows[:, 32:64]).astype(BF)


class Exchange:
    def __init__(self, semaphores):
        self.x, self.me = lax.axis_index(BATCH), lax.axis_index(SEQ)
        self.has_pair, self.pair = own_pair()
        self.send, self.receive, self.local = (semaphores.at[at] for at in range(3))

    def to(self, there, source, target):
        @pl.when(self.me != there)
        def _():
            remote(source, target, self.send, self.receive, (self.x, there)).start()

        @pl.when(self.me == there)
        def _():
            pltpu.make_async_copy(source, target, self.local).start()

    def wait(self, sent, got, where):
        if where == "pairs":
            sends, gets = (sent.shape[0], sent.shape[0] - 1), (None, got.shape[0] - 1)
        else:
            sends, gets = (None, sent.shape[0] - 1), (got.shape[0], got.shape[0] - 1)

        def wait_for(n_sent, n_got):
            if n_got is not None:
                part = got.at[pl.ds(0, n_got)]
                remote(part, part, self.send, self.receive, (self.x, self.me)).wait_recv()
            if n_sent is not None:
                part = sent.at[pl.ds(0, n_sent)]
                remote(part, part, self.send, self.receive, (self.x, self.me)).wait_send()

        @pl.when(self.has_pair)
        def _():
            pltpu.make_async_copy(sent.at[0], got.at[0], self.local).wait()
            wait_for(sends[1], gets[1])

        @pl.when(jnp.logical_not(self.has_pair))
        def _():
            wait_for(sends[0], gets[0])


def send_projections(exchange, query, key, value, cosine, sine, outgoing, rows):
    cosine, sine = twice(cosine), twice(sine)
    front = front_lanes(64)
    for tile in range(6):
        cut = slice(128 * tile, 128 * tile + 128)
        q = turned(query[:, cut], cosine, sine) * (1.0 / math.sqrt(HEAD_DIM))
        k = turned(key[:, cut], cosine, sine)
        v = value[:, cut]
        for slot in range(2):
            span = slice(64 * slot, 64 * slot + 64)
            at = slot * HEADS + 2 * tile
            ks, vs = k[span], v[span]
            outgoing[at, 0:64] = jnp.where(front, ks, pltpu.roll(vs, 64, 1)).astype(BF)
            outgoing[at + 1, 0:64] = jnp.where(front, pltpu.roll(ks, 64, 1), vs).astype(BF)
            outgoing[at, 64:96], outgoing[at + 1, 64:96] = pack_heads(q[span])
    for pair in range(PAIRS):
        exchange.to(pair_device(pair), outgoing.at[pair], rows.at[exchange.me])


def attend_block(exchange, at, length, rows, values_turned, out_turned, log_total, outgoing, incoming):
    count = (at + 1) * BLOCK
    queries = unpack_block(rows[4 * at : 4 * at + 4, 64:96], True)
    keys = rows[0 : 4 * at + 4, 0:64].reshape(count, 128)
    scores = lax.dot_general(keys, queries, LAST_DIMS, preferred_element_type=F32)
    scores = jnp.where(allowed_keys(0, at * BLOCK, count, BLOCK, length), scores, MASKED)
    highest = jnp.max(scores, axis=0, keepdims=True)
    raised = jnp.exp(scores - highest)
    total = jnp.sum(raised, axis=0, keepdims=True)
    result = (
        jnp.dot(values_turned[:, 0:count], raised.astype(BF), preferred_element_type=F32) / total
    )
    cut = slice(at * BLOCK, count)
    out_turned[:, cut] = result
    log_total[:, cut] = jnp.broadcast_to(highest + jnp.log(total), (8, BLOCK))
    outgoing[4 * at : 4 * at + 4] = pack_turned(result)
    for there in range(4 * at, 4 * at + 4):
        exchange.to(there, outgoing.at[there], incoming.at[exchange.pair])


def merge_heads(incoming, merged):
    for slot in range(2):
        for tile in range(6):
            at = slot * HEADS + 2 * tile
            merged[64 * slot : 64 * slot + 64, 128 * tile : 128 * tile + 128] = unpack_heads(
                incoming[at], incoming[at + 1]
            ).astype(BF)


def norm_forward(values, norm_gain):
    inverse = lax.rsqrt(jnp.mean(values * values, axis=-1, keepdims=True) + EPSILON)
    return (values * inverse * norm_gain, inverse)


def feed_forward(rows_in, gate_up, down, paired):
    fed = jnp.zeros((128, 768), F32)
    for z in range(4):
        cut = slice(512 * z, 512 * z + 512)
        gate = jnp.dot(rows_in, gate_up[0, :, :, :, cut].reshape(768, 512), preferred_element_type=F32)
        up = jnp.dot(rows_in, gate_up[1, :, :, :, cut].reshape(768, 512), preferred_element_type=F32)
        paired[0, :, cut] = gate
        paired[1, :, cut] = up
        hidden = (jax.nn.silu(gate) * up).astype(BF)
        fed = fed + jnp.dot(hidden, down[z].reshape(512, 768), preferred_element_type=F32)
    return fed


KEPT = (
    [("result", (128, 768), F32), ("mid_0", (128, 768), F32), ("summed_0", (128, 768), F32)]
    + [("mid_1", (128, 768), F32), ("gain", (8, 768), F32)]
    + [("stream", (128, 768), BF), ("cotangent", (128, 768), F32)]
    + [
        (name + "_" + layer, shape, kind)
        for layer in "01"
        for name, shape, kind in (
            ("paired", (2, 128, 2048), F32),
            ("rows", (32, MESSAGE, 128), BF),
            ("merged", (128, 768), BF),
            ("turned", (64, LENGTH), F32),
            ("total", (8, LENGTH), F32),
        )
    ]
)


def forward_kernel(
    lengths, qkv, out, gate_up, down, gains, inputs, cotangents, cosine, sine, *refs
):
    stored = dict(zip(GATHERED[:-1], refs[:8]))
    kept = {name: ref for (name, _, _), ref in zip(KEPT, refs[8:])}
    refs = refs[8 + len(KEPT) :]
    store, refs = dict(zip(GATHERED, refs[:9])), refs[9:]
    their_qkv, their_out, their_gate_up, b_qkv, b_out, b_gate_up, b_down = refs[:7]
    outgoing, places, incoming, values_turned, stream, swap, sems, local, pair_sems = refs[7:]
    axes = Axes(True)
    core = axes.core
    x, me = lax.axis_index(BATCH), lax.axis_index(SEQ)
    greet(
        [(x, lax.rem(me + by, 32)) for by in range(1, 32)]
        + [device(shifted(x, by), axes.z, axes.y, core) for by in (1, 2, 3)]
    )
    swaps = [
        remote(mine, theirs, swap.at[0, at], swap.at[1, at], axes.partner)
        for at, (mine, theirs) in enumerate(
            (
                (qkv.at[0], their_qkv.at[0]),
                (qkv.at[1], their_qkv.at[1]),
                (out, their_out),
                (gate_up, their_gate_up),
            )
        )
    ]
    for copy in swaps:
        copy.start()
    for slot in range(2):
        stream[64 * slot : 64 * slot + 64] = inputs[:, slot, :]
        kept["cotangent"][64 * slot : 64 * slot + 64] = cotangents[:, slot, :]
    kept["stream"][...] = stream[...].astype(BF)

    def joined(mine, theirs):
        upper = jnp.where(core == 0, mine, theirs)
        lower = jnp.where(core == 0, theirs, mine)
        return jnp.concatenate([upper, lower], axis=0).astype(BF)

    segments = {}
    at = 0
    for key in GATHERED:
        name, layer = key
        block = {"qkv": b_qkv, "out": b_out, "wide": b_gate_up, "down": b_down}.get(name)
        block = gains if block is None else block.at[layer]
        kind, views, owns = GatherSegment, weight_views, own_views
        if key in ACROSS:
            kind, views, owns = AcrossSegment, across_views, across_owns
        segments[key] = []
        for (first_is_y, view), own in zip(views(name, store[key]), owns(name, block)):
            segments[key].append(kind(first_is_y, view, sems.at[at], own))
            at += 1

    def each(keys, act):
        for key in keys:
            for segment in segments[key]:
                act(segment)

    def keep(*keys):
        each(keys, lambda segment: segment.keep().start())
        each(keys, lambda segment: segment.keep().wait())

    def begin(phase, *keys):
        each(keys, lambda segment: segment.begin(phase))

    def end(phase, *keys):
        each(keys, lambda segment: segment.end(phase))

    saves = []

    def save(*keys):
        for key in keys:
            copy = pltpu.make_async_copy(store[key], stored[key], local.at[len(saves)])
            copy.start()
            saves.append(copy)

    qkv_0, out_0, wide_0, down_0 = GATHERED[0:4]
    qkv_1, out_1, wide_1, down_1 = GATHERED[4:8]
    gains_0 = GATHERED[8]

    swaps[0].wait()
    for at in range(3):
        b_qkv[0, at] = joined(qkv[0, at], their_qkv[0, at])
    begin(0, qkv_0)
    keep(qkv_0)
    b_down[0] = down[0].astype(BF)
    begin(0, down_0)
    keep(down_0)
    for copy in swaps[1:]:
        copy.wait()
    for at in range(2):
        b_gate_up[0, at] = joined(gate_up[0, at], their_gate_up[0, at])
    begin(0, wide_0)
    keep(wide_0)
    end(0, qkv_0)
    begin(1, qkv_0)
    end(0, down_0)
    begin(1, down_0)
    b_out[0] = joined(out[0], their_out[0])
    for at in range(2):
        b_gate_up[1, at] = joined(gate_up[1, at], their_gate_up[1, at])
    begin(0, out_0, gains_0, wide_1)
    keep(out_0, gains_0, wide_1)
    for at in range(3):
        b_qkv[1, at] = joined(qkv[1, at], their_qkv[1, at])
    b_out[1] = joined(out[1], their_out[1])
    b_down[1] = down[1].astype(BF)
    end(1, qkv_0)
    begin(2, qkv_0)
    end(1, down_0)
    begin(2, down_0)
    end(0, wide_0)
    begin(1, wide_0)
    end(2, qkv_0)
    begin(3, qkv_0)
    keep(qkv_1, out_1, down_1)
    begin(0, qkv_1)
    end(2, down_0)
    begin(3, down_0)
    end(0, out_0, gains_0, wide_1)
    begin(1, wide_1)
    end(3, qkv_0)
    save(qkv_0)

    def attention(layer, source, before, between):
        weights = store["qkv", layer]
        name = "_" + str(layer)
        rows, merged = kept["rows" + name], kept["merged" + name]
        there = Exchange(pair_sems.at[2 * layer])
        back = Exchange(pair_sems.at[2 * layer + 1])
        low = source.astype(BF)
        query, key, value = (
            jnp.dot(low, weights[at].reshape(768, 768), preferred_element_type=F32)
            for at in range(3)
        )
        send_projections(
            there, query, key, value, cosine[...], sine[...], outgoing.at[layer], rows
        )
        before()
        there.wait(outgoing.at[layer], rows, "pairs")
        length = slot_length(lengths, there.pair)

        @pl.when(there.has_pair)
        def _():
            all_rows = rows[:, 0:64].reshape(LENGTH, 128).astype(F32)
            values_turned[...] = all_rows.T[64:128].astype(BF)

        for at in range(BLOCKS):

            @pl.when(there.has_pair)
            def _(at=at):
                attend_block(
                    back,
                    at,
                    length,
                    rows,
                    values_turned,
                    kept["turned" + name],
                    kept["total" + name],
                    places.at[layer],
                    incoming.at[layer],
                )

            if at in between:
                between[at]()
        back.wait(places.at[layer], incoming.at[layer], "places")
        merge_heads(incoming.at[layer], merged)
        between["after"]()
        out_matrix = store["out", layer][...].reshape(768, 768)
        return jnp.dot(merged[...], out_matrix, preferred_element_type=F32)

    def before_0():
        begin(1, out_0, gains_0)
        end(1, wide_1)
        begin(2, wide_1)
        end(0, qkv_1)
        begin(1, qkv_1)

    def within_0():
        end(1, wide_0)
        begin(2, wide_0)
        end(2, wide_1)
        begin(3, wide_1)

    def later_0():
        end(1, out_0, gains_0)
        begin(2, out_0, gains_0)

    def last_0():
        end(1, qkv_1)
        begin(2, qkv_1)
        end(3, down_0)
        begin(4, down_0)

    def after_0():
        end(4, down_0)
        begin(5, down_0)
        end(2, wide_0, out_0, gains_0)
        begin(3, out_0, wide_0, gains_0)
        begin(0, out_1, down_1)
        end(3, out_0, wide_0, gains_0)
        end(5, down_0)
        save(out_0, wide_0, down_0)
        for device_at in range(32):
            piece = store[gains_0][device_at // 8, device_at // 2 % 4, device_at % 2]
            first = 24 * device_at // 128
            if device_at == 0:
                kept["gain"][...] = jnp.zeros((8, 768), F32)
            width = min(256, 768 - 128 * first)
            kept["gain"][:, 128 * first : 128 * first + width] += piece[:, :width]

    def gain(at):
        return kept["gain"][at : at + 1, :]

    mixed = attention(
        0, stream[...], before_0, {1: within_0, 4: later_0, 7: last_0, "after": after_0}
    )
    residual = stream[...] + mixed
    kept["mid_0"][...] = residual
    middle, _ = norm_forward(residual, gain(0))
    end(2, qkv_1)
    begin(3, qkv_1)
    fed = feed_forward(middle.astype(BF), store[wide_0], store[down_0], kept["paired_0"])
    end(0, out_1, down_1)
    summed = middle + fed
    kept["summed_0"][...] = summed
    shallow, _ = norm_forward(summed, gain(1))
    normed, _ = norm_forward(shallow, gain(2))
    end(3, qkv_1)
    save(qkv_1)

    def before_1():
        begin(1, out_1, down_1)

    def within_1():
        end(3, wide_1)
        begin(4, wide_1)

    def later_1():
        end(1, out_1, down_1)
        begin(2, out_1, down_1)
        end(4, wide_1)
        begin(5, wide_1)

    def after_1():
        end(2, out_1, down_1)
        begin(3, out_1, down_1)
        end(3, out_1, down_1)
        end(5, wide_1)
        save(out_1, wide_1, down_1)

    mixed = attention(1, normed, before_1, {1: within_1, 7: later_1, "after": after_1})
    residual = shallow + mixed
    kept["mid_1"][...] = residual
    normed_two, _ = norm_forward(residual, gain(3))
    fed = feed_forward(normed_two.astype(BF), store[wide_1], store[down_1], kept["paired_1"])
    kept["result"][...] = residual + fed
    for copy in saves:
        copy.wait()


def run_forward(*operands):
    count = sum(SEGMENTS[name] for name, _ in GATHERED)
    stored = GATHERED[:-1]
    results = pl.pallas_call(
        forward_kernel,
        out_shape=[weight_shape(key) for key in stored]
        + [jax.ShapeDtypeStruct(shape, kind) for _, shape, kind in KEPT],
        in_specs=[SMEM] + [VMEM] * 9,
        out_specs=[ANY] * 8 + [VMEM] * len(KEPT),
        scratch_shapes=[pltpu.VMEM(*WEIGHTS[name]) for name, _ in GATHERED]
        + [
            pltpu.VMEM((2, 3, 24, 768), F32),
            pltpu.VMEM((2, 24, 768), F32),
            pltpu.VMEM((2, 2, 24, 2048), F32),
            pltpu.VMEM((2, 3, 48, 768), BF),
            pltpu.VMEM((2, 48, 768), BF),
            pltpu.VMEM((2, 2, 48, 2048), BF),
            pltpu.VMEM((2, 64, 768), BF),
            pltpu.VMEM((2, PAIRS, MESSAGE, 128), BF),
            pltpu.VMEM((2, 32, 32, 128), BF),
            pltpu.VMEM((2, PAIRS, 32, 128), BF),
            pltpu.VMEM((64, LENGTH), BF),
            pltpu.VMEM((128, 768), F32),
            pltpu.SemaphoreType.DMA((2, 4)),
            pltpu.SemaphoreType.DMA((count, 5, 4)),
            pltpu.SemaphoreType.DMA((8,)),
            pltpu.SemaphoreType.DMA((4, 3)),
        ],
        compiler_params=params(1),
        name="forward",
    )(*operands)
    return dict(zip(stored, results)), {
        name: result for (name, _, _), result in zip(KEPT, results[8:])
    }


def attend_back_block(
    exchange, at, length, rows, out_grad, out_turned, log_total, keys_turned, key_grad, outgoing, incoming
):
    cut = slice(at * BLOCK, (at + 1) * BLOCK)
    four = slice(4 * at, 4 * at + 4)
    queries = unpack_block(rows[four, 64:96], True)
    outs = unpack_block(out_grad[four], False)
    outs_turned = outs.astype(F32).T[64:128]
    delta = jnp.sum(outs_turned * out_turned[:, cut], axis=0, keepdims=True)
    shift = log_total[0:1, cut]
    query_grad = jnp.zeros((64, BLOCK), F32)
    for part in range(at + 1):
        span = slice(part * BLOCK, (part + 1) * BLOCK)
        keys = rows[4 * part : 4 * part + 4, 0:64].reshape(BLOCK, 128)
        scores = lax.dot_general(keys, queries, LAST_DIMS, preferred_element_type=F32)
        allowed = allowed_keys(part * BLOCK, at * BLOCK, BLOCK, BLOCK, length)
        probs = jnp.where(allowed, jnp.exp(scores - shift), 0.0)
        probs_grad = lax.dot_general(keys, outs, LAST_DIMS, preferred_element_type=F32)
        score_grad = (probs * (probs_grad - delta)).astype(BF)
        key_grad[span, :] += jnp.dot(score_grad, queries, preferred_element_type=F32) + jnp.dot(
            probs.astype(BF), outs, preferred_element_type=F32
        )
        query_grad += jnp.dot(keys_turned[:, span], score_grad, preferred_element_type=F32)
    outgoing[four, 0:64] = key_grad[cut, :].reshape(4, SPAN, 128).astype(BF)
    outgoing[four, 64:96] = pack_turned(query_grad)
    for there in range(4 * at, 4 * at + 4):
        exchange.to(there, outgoing.at[there], incoming.at[exchange.pair])


def collect_projections(incoming, cosine, sine, result):
    front = front_lanes(64)
    for slot in range(2):
        span = slice(64 * slot, 64 * slot + 64)
        for tile in range(6):
            cut = slice(128 * tile, 128 * tile + 128)
            at = slot * HEADS + 2 * tile
            first, second = (incoming[at + n, 0:64].astype(F32) for n in (0, 1))
            q = unpack_heads(incoming[at, 64:96], incoming[at + 1, 64:96])
            k = jnp.where(front, first, pltpu.roll(second, 64, 1))
            v = jnp.where(front, pltpu.roll(first, 64, 1), second)
            q = turned(q * (1.0 / math.sqrt(HEAD_DIM)), cosine, -sine)
            result[0, span, cut] = q.astype(BF)
            result[1, span, cut] = turned(k, cosine, -sine).astype(BF)
            result[2, span, cut] = v.astype(BF)


def norm_backward(incoming, values, norm_gain):
    inverse = lax.rsqrt(jnp.mean(values * values, axis=-1, keepdims=True) + EPSILON)
    scaled = incoming * norm_gain
    outgoing = inverse * scaled - values * (inverse * inverse * inverse) * jnp.mean(
        scaled * values, axis=-1, keepdims=True
    )
    return outgoing, jnp.sum(incoming * values * inverse, axis=0, keepdims=True)


def feed_back(incoming, paired, gate_up, down, gate_grads, up_grads, hidden_turned):
    source_grad = jnp.zeros((128, 768), F32)
    for z in range(4):
        cut = slice(512 * z, 512 * z + 512)
        hidden_grad = lax.dot_general(
            incoming, down[z].reshape(512, 768), LAST_DIMS, preferred_element_type=F32
        )
        gate, up = paired[0, :, cut], paired[1, :, cut]
        sigmoid = jax.nn.sigmoid(gate)
        hidden = (gate * sigmoid * up).T.astype(BF).reshape(4, 2, 64, 128)
        hidden_turned[0, z] = hidden[:, 0]
        hidden_turned[1, z] = hidden[:, 1]
        gate_grad = (hidden_grad * up * sigmoid * (1.0 + gate * (1.0 - sigmoid))).astype(BF)
        up_grad = (hidden_grad * gate * sigmoid).astype(BF)
        part = slice(512 * (z % 2), 512 * (z % 2) + 512)
        gate_grads[z // 2, :, part] = gate_grad
        up_grads[z // 2, :, part] = up_grad
        for at, value in enumerate((gate_grad, up_grad)):
            source_grad = source_grad + lax.dot_general(
                value, gate_up[at, :, :, :, cut].reshape(768, 512), LAST_DIMS, preferred_element_type=F32
            )
    return source_grad


def turned_low(values):
    return values.astype(F32).T.astype(BF)


def fill_part(part, rows, left_of, right):
    for z in range(4):
        value = jnp.dot(left_of(z), right, preferred_element_type=F32).astype(BF)
        part.fill(z, value.reshape(4, rows, right.shape[1]))


def beside(first, second, rows):
    def left_of(z):
        cut = slice(4 * rows * z, 4 * rows * (z + 1))
        return jnp.concatenate([first[cut], second[cut]], axis=1)

    return left_of


SHARED = {
    "source": ((768, 128), (768, 128)),
    "gate": ((2, 128, 1024), (128, 1024)),
    "up": ((2, 128, 1024), (128, 1024)),
    "hidden": ((2, 4, 4, 64, 128), (4, 4, 64, 128)),
    "fed": ((128, 768), (128, 768)),
    "merged": ((768, 128), (768, 128)),
    "mixed": ((2, 128, 384), (128, 384)),
    "norm": ((768, 128), (768, 128)),
    "low": ((2, 3, 128, 384), (3, 128, 384)),
}
KEPT_NAMES = ("paired", "rows", "merged", "turned", "total")
KEPT_TYPES = {name: (shape, kind) for name, shape, kind in KEPT}
WEIGHT_ORDER = ("down", "wide", "out", "qkv")


def backward_kernel(lengths, *refs):
    refs = list(refs)

    def take(count):
        taken = refs[:count]
        del refs[:count]
        return taken

    cotangent, stream, residual_0, summed_0, residual_1, gains, cosine, sine = take(8)
    far = [dict(zip(KEPT_NAMES, take(len(KEPT_NAMES)))) for _ in range(2)]
    stored = dict(zip(GATHERED[:-1], take(8)))
    (input_grad,) = take(1)
    sums = dict(zip(SUMS, take(len(SUMS))))
    kept = dict(zip(KEPT_NAMES, take(len(KEPT_NAMES))))
    weights = dict(zip(WEIGHT_ORDER, take(4)))
    shared, own = part_scratch()
    shared, own = take(len(shared)), take(len(own))
    given = dict(zip(SHARED, take(len(SHARED))))
    got = [dict(zip(SHARED, take(len(SHARED)))) for _ in range(2)]
    out_grads, to_pairs, to_places, incoming = take(4)
    keys_turned, key_grad, gain_grads, their_gains, stacked = take(5)
    part_sems, give_sems, load_sems, pair_sems = take(4)
    parts = build_parts(shared, own, part_sems, sums)
    axes = Axes(True)
    core = axes.core
    x, me = lax.axis_index(BATCH), lax.axis_index(SEQ)
    barrier = pltpu.get_barrier_semaphore()
    neighbours = [(x, lax.rem(me + by, 32)) for by in range(1, 32)]
    neighbours += [device(shifted(x, by), axes.z, axes.y, core) for by in (1, 2, 3)]
    for where in neighbours:
        pl.semaphore_signal(barrier, inc=1, device_id=where, device_id_type=MESH)

    def load(name, layer):
        at = WEIGHT_ORDER.index(name)
        return pltpu.make_async_copy(stored[name, layer], weights[name], load_sems.at[at])

    def recall(name, layer):
        at = KEPT_NAMES.index(name)
        return pltpu.make_async_copy(far[layer][name], kept[name], load_sems.at[4 + at])

    recall("paired", 1).start()
    for name in WEIGHT_ORDER:
        load(name, 1).start()
    for name in KEPT_NAMES[1:]:
        recall(name, 1).start()

    def gain(at):
        return gains[at : at + 1, :]

    def stages(*work):
        for names, layer, number in work:
            for name in names:
                parts[name, layer].stage(number)

    def share(layer, names):
        copies = []
        for name in names:
            at = list(SHARED).index(name)
            source = given[name]
            if SHARED[name][0] != SHARED[name][1]:
                source = source.at[1 - core]
            copies.append(
                remote(
                    source,
                    got[layer][name],
                    give_sems.at[layer, at, 0],
                    give_sems.at[layer, at, 1],
                    axes.partner,
                )
            )
        return copies

    def start(copies):
        for copy in copies:
            copy.start()

    def finish(copies):
        for copy in copies:
            copy.wait()

    wide, narrow, down = ("gate", "up"), ("left", "right", "o"), ("left", "right")

    def wide_grads(layer):
        left_of = beside(given["source"], got[layer]["source"], 48)
        for name in wide:
            right = jnp.concatenate([given[name][core], got[layer][name][...]], axis=0)
            fill_part(parts[name, layer], 48, left_of, right)

    def narrow_grads(layer):
        def left_of(z):
            mine = given["hidden"][core, z].reshape(256, 128)
            return jnp.concatenate([mine, got[layer]["hidden"][z].reshape(256, 128)], axis=1)

        right = jnp.concatenate([given["fed"][...], got[layer]["fed"][...]], axis=0)
        fill_part(parts["left", layer], 64, left_of, right[:, :384])
        fill_part(parts["right", layer], 64, left_of, right[:, 384:])
        right = jnp.concatenate([given["mixed"][core], got[layer]["mixed"][...]], axis=0)
        left_of = beside(given["merged"], got[layer]["merged"], 48)
        fill_part(parts["o", layer], 48, left_of, right)

    def projection_grads(layer):
        left_of = beside(given["norm"], got[layer]["norm"], 48)
        for at, name in enumerate("qkv"):
            right = jnp.concatenate([given["low"][core, at], got[layer]["low"][at]], axis=0)
            fill_part(parts[name, layer], 48, left_of, right)

    FED = ("source", "gate", "up", "hidden", "fed")
    MIXED = ("merged", "mixed")
    PROJECTED = ("norm", "low")

    def feed(layer, source, grad):
        load("down", layer).wait()
        load("wide", layer).wait()
        recall("paired", layer).wait()
        low = grad.astype(BF)
        given["fed"][...] = low
        given["source"][...] = turned_low(source.astype(BF))
        return feed_back(
            low,
            kept["paired"],
            weights["wide"],
            weights["down"],
            given["gate"],
            given["up"],
            given["hidden"],
        )

    def send_out_grad(layer, grad):
        load("out", layer).wait()
        low = grad.astype(BF)
        given["mixed"][0] = low[:, :384]
        given["mixed"][1] = low[:, 384:]
        for name in KEPT_NAMES[1:]:
            recall(name, layer).wait()
        given["merged"][...] = turned_low(kept["merged"][...])
        merged_grad = (
            lax.dot_general(
                low, weights["out"][...].reshape(768, 768), LAST_DIMS, preferred_element_type=F32
            )
            .astype(BF)
            .astype(F32)
        )
        exchange = Exchange(pair_sems.at[2 * layer])
        to = to_pairs
        for slot in range(2):
            for tile in range(6):
                at = slot * HEADS + 2 * tile
                both = merged_grad[64 * slot : 64 * slot + 64, 128 * tile : 128 * tile + 128]
                to[at], to[at + 1] = pack_heads(both)
        for pair in range(PAIRS):
            exchange.to(pair_device(pair), to.at[pair], out_grads.at[layer, me])
        return exchange

    def attention(layer, exchange, between):
        rows = kept["rows"]
        length = slot_length(lengths, exchange.pair)

        @pl.when(exchange.has_pair)
        def _():
            all_rows = rows[:, 0:64].reshape(LENGTH, 128).astype(F32)
            keys_turned[...] = all_rows.T[0:64].astype(BF)
            key_grad[...] = jnp.zeros_like(key_grad)

        exchange.wait(to_pairs, out_grads.at[layer], "pairs")
        back = Exchange(pair_sems.at[2 * layer + 1])
        for at in reversed(range(BLOCKS)):

            @pl.when(exchange.has_pair)
            def _(at=at):
                attend_back_block(
                    back,
                    at,
                    length,
                    rows,
                    out_grads.at[layer],
                    kept["turned"],
                    kept["total"],
                    keys_turned,
                    key_grad,
                    to_places,
                    incoming.at[layer],
                )

            stages(*between.get(at, ()))
        stages(*between.get("sent", ()))
        back.wait(to_places, incoming.at[layer], "places")
        collect_projections(incoming.at[layer], cosine[...], sine[...], stacked)

    def source_gradient(layer, source):
        load("qkv", layer).wait()
        given["norm"][...] = turned_low(source.astype(BF))
        for at in range(3):
            given["low"][0, at] = stacked[at, :, 0:384]
            given["low"][1, at] = stacked[at, :, 384:768]
        copies = share(layer, PROJECTED)
        start(copies)
        result = jnp.zeros((128, 768), F32)
        for at in range(3):
            result = result + lax.dot_general(
                stacked[at],
                weights["qkv"][at].reshape(768, 768),
                LAST_DIMS,
                preferred_element_type=F32,
            )
        return result, copies

    normed_two, _ = norm_forward(residual_1[...], gain(3))
    fed_grad = feed(1, normed_two, cotangent[...])
    for name in ("down", "wide"):
        load(name, 0).start()
    recall("paired", 0).start()
    through, gain_grad = norm_backward(fed_grad, residual_1[...], gain(3))
    gain_grads[...] = jnp.zeros_like(gain_grads)
    gain_grads[3:4, :] = gain_grad
    residual_grad = cotangent[...] + through
    pl.semaphore_wait(barrier, len(neighbours))
    exchange = send_out_grad(1, residual_grad)
    load("out", 0).start()
    copies = share(1, FED + MIXED)
    start(copies)
    finish(copies)
    wide_grads(1)
    stages((wide, 1, 0))
    narrow_grads(1)
    stages((narrow, 1, 1))
    attention(1, exchange, {6: [(narrow, 1, 2)], "sent": [(narrow, 1, 3)]})
    for name in KEPT_NAMES[1:]:
        recall(name, 0).start()
    shallow, _ = norm_forward(summed_0[...], gain(1))
    normed, _ = norm_forward(shallow, gain(2))
    normed_grad, copies = source_gradient(1, normed)
    load("qkv", 0).start()
    stages((narrow, 1, 4))
    through, gain_grad = norm_backward(normed_grad, shallow, gain(2))
    gain_grads[2:3, :] = gain_grad
    shallow_grad = residual_grad + through
    summed_grad, gain_grad = norm_backward(shallow_grad, summed_0[...], gain(1))
    gain_grads[1:2, :] = gain_grad

    finish(copies)
    projection_grads(1)
    stages(("qkv", 1, 1))
    middle, _ = norm_forward(residual_0[...], gain(0))
    fed_grad = feed(0, middle, summed_grad)
    middle_grad = summed_grad + fed_grad
    residual_grad, gain_grad = norm_backward(middle_grad, residual_0[...], gain(0))
    gain_grads[0:1, :] = gain_grad
    exchange = send_out_grad(0, residual_grad)
    copies = share(0, FED + MIXED)
    start(copies)
    stages(("qkv", 1, 2))
    finish(copies)
    narrow_grads(0)
    stages((down, 0, 0))
    stages((wide, 1, 1))
    wide_grads(0)
    stages((wide, 0, 1), ("o", 0, 1))
    attention(
        0,
        exchange,
        {
            6: [("qkv", 1, 3)],
            3: [(wide, 1, 2)],
            0: [("qkv", 1, 4), (narrow, 1, 5)],
            "sent": [(wide, 0, 2), ("o", 0, 2), (wide, 1, 3)],
        },
    )
    source_grad, copies = source_gradient(0, stream[...])
    swap = remote(
        gain_grads, their_gains, give_sems.at[0, len(SHARED), 0], give_sems.at[0, len(SHARED), 1], axes.partner
    )
    swap.start()
    input_grad[...] = residual_grad + source_grad
    stages(("qkv", 1, 5), (wide, 1, 4))
    finish(copies)
    projection_grads(0)
    swap.wait()
    gain_total = gain_grads[...] + their_gains[...]
    gain_total = jnp.concatenate([gain_total, jnp.zeros((8, 128), F32)], axis=1)
    for z in range(4):
        for y in range(4):
            first, second = (24 * (8 * z + 2 * y + which) // 128 * 128 for which in (0, 1))
            parts["gain", 0].total[y, z] = jnp.where(
                core == 0, gain_total[:, first : first + 256], gain_total[:, second : second + 256]
            )
    last = ("q", "k", "v", "gain")
    stages((last, 0, 1), (down, 0, 1), (wide, 0, 3), ("o", 0, 3), ("qkv", 1, 6))
    stages((wide, 1, 5), (narrow, 1, 6))
    stages((last, 0, 2), (down, 0, 2), (wide, 0, 4), ("o", 0, 4), (down, 0, 3))
    stages((wide, 1, 6), (last, 0, 4), (down, 0, 4), (wide, 0, 5), ("o", 0, 5), (last, 0, 5), (down, 0, 5))
    stages((wide, 0, 6), ("o", 0, 6), (last, 0, 6), (down, 0, 6))


def run_backward(lengths, kept, store, cosine, sine):
    near = [kept["cotangent"], kept["stream"]] + [
        kept[name] for name in ("mid_0", "summed_0", "mid_1", "gain")
    ]
    near += [cosine, sine]
    away = [kept[name + layer] for layer in ("_0", "_1") for name in KEPT_NAMES]
    away += [store[key] for key in GATHERED[:-1]]
    shared, own = part_scratch()
    results = pl.pallas_call(
        backward_kernel,
        out_shape=[jax.ShapeDtypeStruct((128, 768), F32)]
        + [jax.ShapeDtypeStruct(*shape) for shape in SUMS.values()],
        in_specs=[SMEM] + [VMEM] * len(near) + [ANY] * len(away),
        out_specs=[VMEM] * (1 + len(SUMS)),
        scratch_shapes=[pltpu.VMEM(*KEPT_TYPES[name + "_0"]) for name in KEPT_NAMES]
        + [pltpu.VMEM(*WEIGHTS[name]) for name in WEIGHT_ORDER]
        + shared
        + own
        + [pltpu.VMEM(here, BF) for here, _ in SHARED.values()]
        + [pltpu.VMEM(there, BF) for _, there in SHARED.values()] * 2
        + [
            pltpu.VMEM((2, 32, 32, 128), BF),
            pltpu.VMEM((PAIRS, 32, 128), BF),
            pltpu.VMEM((32, MESSAGE, 128), BF),
            pltpu.VMEM((2, PAIRS, MESSAGE, 128), BF),
            pltpu.VMEM((64, LENGTH), BF),
            pltpu.VMEM((LENGTH, 128), F32),
            pltpu.VMEM((8, 768), F32),
            pltpu.VMEM((8, 768), F32),
            pltpu.VMEM((3, 128, 768), BF),
            pltpu.SemaphoreType.DMA((2 * len(PARTS), SCATTER_SEMAPHORES)),
            pltpu.SemaphoreType.DMA((2, len(SHARED) + 1, 2)),
            pltpu.SemaphoreType.DMA((9,)),
            pltpu.SemaphoreType.DMA((4, 3)),
        ],
        compiler_params=params(2),
        name="backward",
    )(lengths, *near, *away)
    return results[0], dict(zip(SUMS, results[1:]))


def angles(places):
    half_dim = HEAD_DIM // 2
    frequency = jnp.exp(-math.log(10000.0) * jnp.arange(half_dim).astype(F32) / half_dim)
    phases = places.astype(F32)[:, None] * frequency[None, :]
    cosine, sine = jnp.cos(phases), jnp.sin(phases)
    return (
        jnp.concatenate([cosine] * 4, axis=1),
        jnp.concatenate([-sine, sine] * 2, axis=1),
    )


def update(weight_matrix, moment, average, gradient, step_size):
    moment_new = MOMENTUM * moment + gradient
    weight_new = weight_matrix - step_size * (gradient + MOMENTUM * moment_new)
    return (moment_new, weight_new, AVERAGING * average + (1.0 - AVERAGING) * weight_new)


STEPPED = ("qkv", "out", "wide", "down")


def update_kernel(step_size, *refs):
    count = len(STEPPED)
    sources, refs = refs[: 4 * count + 2], refs[4 * count + 2 :]
    targets, refs = refs[: 3 * count + 2], refs[3 * count + 2 :]
    held, (loads, stores) = refs[:-2], refs[-2:]
    placed, held = held[-2:], held[:-2]
    fetches = [
        pltpu.make_async_copy(source, here, loads.at[at])
        for at, (source, here) in enumerate(zip(sources, held))
    ]
    for copy in fetches:
        copy.start()
    saves = []

    def save(here, at):
        copy = pltpu.make_async_copy(here, targets[at], stores.at[at])
        copy.start()
        saves.append(copy)

    for at in range(count):
        for copy in fetches[4 * at : 4 * at + 4]:
            copy.wait()
        gradient, weight_matrix, moment, average = held[4 * at : 4 * at + 4]
        stepped = update(weight_matrix[...], moment[...], average[...], gradient[...], step_size)
        for n, (here, value) in enumerate(zip((moment, weight_matrix, average), stepped)):
            here[...] = value
            save(here, 3 * at + n)
    for at in range(2):
        fetches[4 * count + at].wait()
        for slot in range(2):
            placed[at][:, slot, :] = held[4 * count + at][64 * slot : 64 * slot + 64]
        save(placed[at], 3 * count + at)
    for copy in saves:
        copy.wait()


def run_update(step_size, sums, states, activations):
    shapes = {name: jax.ShapeDtypeStruct(*SUMS[name]) for name in STEPPED}
    operands = []
    for name in STEPPED:
        operands += [sums[name], *states[name]]
    operands += activations
    by_place = jax.ShapeDtypeStruct((SPAN, 2, 768), F32)
    results = pl.pallas_call(
        functools.partial(update_kernel, step_size),
        out_shape=[shapes[name] for name in STEPPED for _ in range(3)] + [by_place] * 2,
        in_specs=[ANY] * len(operands),
        out_specs=[ANY] * (3 * len(STEPPED) + 2),
        scratch_shapes=[pltpu.VMEM(operand.shape, F32) for operand in operands]
        + [pltpu.VMEM((SPAN, 2, 768), F32)] * 2
        + [
            pltpu.SemaphoreType.DMA((len(operands),)),
            pltpu.SemaphoreType.DMA((3 * len(STEPPED) + 2,)),
        ],
        compiler_params=pltpu.CompilerParams(vmem_limit_bytes=VMEM_BYTES),
        name="step",
    )(*operands)
    return results[: 3 * len(STEPPED)], results[3 * len(STEPPED) :]


def on_device(
    inputs,
    cotangent,
    lengths,
    qkv_weight,
    qkv_moment,
    qkv_average,
    out_weight,
    out_moment,
    out_average,
    gate_up_weight,
    gate_up_moment,
    gate_up_average,
    down_weight,
    down_moment,
    down_average,
    norm_gains,
    gain_moment,
    gain_average,
):
    places = lax.axis_index(SEQ) * SPAN + jnp.arange(SPAN)
    cosine, sine = angles(places)
    seq = lax.axis_index(SEQ)
    own_gains = lax.dynamic_update_slice(
        jnp.zeros((8, 256), F32),
        norm_gains.astype(BF).astype(F32).reshape(4, 24),
        (0, lax.rem(24 * seq, 128)),
    )
    store, kept = run_forward(
        lengths[0],
        qkv_weight,
        out_weight,
        gate_up_weight,
        down_weight,
        own_gains,
        inputs[0],
        cotangent[0],
        cosine,
        sine,
    )
    input_grad, sums = run_backward(
        lengths[0], kept, store, cosine, sine
    )
    gain_sum = lax.dynamic_slice(
        sums["gain"][0], (0, lax.rem(24 * seq, 128)), (4, 24)
    ).reshape(2, 2, 24)

    step_size = STEP_RATE / math.sqrt(
        lax.axis_size(BATCH) * SPAN * lax.axis_size(SEQ) * 2
    )
    stepped, (result, input_grad) = run_update(
        step_size,
        sums,
        {
            "qkv": (qkv_weight, qkv_moment, qkv_average),
            "out": (out_weight, out_moment, out_average),
            "wide": (gate_up_weight, gate_up_moment, gate_up_average),
            "down": (down_weight, down_moment, down_average),
        },
        [kept["result"], input_grad],
    )
    gain_new = update(norm_gains, gain_moment, gain_average, gain_sum, step_size)
    return (result[None], input_grad[None], *stepped, *gain_new)


def solution(mesh):
    rows = P(BATCH, SEQ, None, None)
    wide = P(None, None, SEQ, None)
    flat = P(None, SEQ, None)
    gains = P(None, None, SEQ)
    state = (wide,) * 3 + (flat,) * 3 + (wide,) * 3 + (flat,) * 3 + (gains,) * 3
    return jax.shard_map(
        on_device,
        mesh=mesh,
        in_specs=(rows, rows, P(BATCH, None)) + state,
        out_specs=(rows, rows) + state,
        check_vma=False,
    )
```

```python
import functools
import math

import jax
import jax.numpy as jnp
from jax import lax
from jax.experimental import pallas as pl
from jax.experimental.pallas import tpu as pltpu
from jax.sharding import PartitionSpec as P

MESH = pl.DeviceIdType.MESH
BF = jnp.bfloat16
F32 = jnp.float32
BATCH, SEQ = "batch", "seq"
HEAD_DIM = 64
HEADS = 12
PAIRS = 24
SPAN = 64
LENGTH = 2048
BLOCK = 256
EPSILON = 1e-06
MOMENTUM = 0.5
AVERAGING = 0.5
STEP_RATE = 0.1
MASKED = -1e30
VMEM_BYTES = 62 * 2**20
VMEM = pl.BlockSpec(memory_space=pltpu.VMEM)
ANY = pl.BlockSpec(memory_space=pl.ANY)
SMEM = pl.BlockSpec(memory_space=pltpu.SMEM)
ALL = pl.ds(0, 4)


def params(collective_id):
    return pltpu.CompilerParams(
        collective_id=collective_id, has_side_effects=True, vmem_limit_bytes=VMEM_BYTES
    )


def coordinates():
    seq = lax.axis_index(SEQ)
    return (
        lax.axis_index(BATCH),
        lax.div(seq, 8),
        lax.rem(lax.div(seq, 2), 4),
        lax.rem(seq, 2),
    )


def device(x, z, y, core):
    return (x, (z * 4 + y) * 2 + core)


def shifted(value, by):
    return lax.rem(value + by, 4)


def signal(partners):
    barrier = pltpu.get_barrier_semaphore()
    for partner in partners:
        pl.semaphore_signal(barrier, inc=1, device_id=partner, device_id_type=MESH)


def greet(partners):
    signal(partners)
    pl.semaphore_wait(pltpu.get_barrier_semaphore(), len(partners))


def remote(source, target, send, receive, where):
    return pltpu.make_async_remote_copy(
        src_ref=source,
        dst_ref=target,
        send_sem=send,
        recv_sem=receive,
        device_id=where,
        device_id_type=MESH,
    )


class Axes:
    def __init__(self, first_is_y):
        x, z, y, core = coordinates()
        self.first_is_y = first_is_y
        self.x, self.z, self.y, self.core = x, z, y, core
        self.m1, self.m2 = (y, z) if first_is_y else (z, y)
        self.partner = device(x, z, y, 1 - core)

    def along_y(self, by):
        return device(self.x, self.z, shifted(self.y, by), self.core)

    def along_z(self, by):
        return device(self.x, shifted(self.z, by), self.y, self.core)

    def first(self, by):
        return self.along_y(by) if self.first_is_y else self.along_z(by)

    def second(self, by):
        return self.along_z(by) if self.first_is_y else self.along_y(by)

    def order(self, i1, i2):
        return (i2, i1) if self.first_is_y else (i1, i2)


class GatherSegment:
    def __init__(self, first_is_y, view, semaphores, own=None):
        self.axes = Axes(first_is_y)
        self.view, self.own, self.semaphores = view, own, semaphores

    def block(self, i1, i2):
        return self.view(*self.axes.order(i1, i2))

    def row(self, by, part=ALL):
        return self.block(part, shifted(self.axes.m2, by))

    def keep(self):
        here = self.block(self.axes.m1, self.axes.m2)
        return pltpu.make_async_copy(self.own, here, self.semaphores.at[3, 0])

    def begin(self, phase):
        axes = self.axes
        sem = [self.semaphores.at[phase, at] for at in range(4)]

        def send(part, where):
            remote(part, part, sem[0], sem[1], where).start()

        def share(part):
            remote(part, part, sem[2], sem[3], axes.partner).start()

        if phase == 0:
            here = self.block(axes.m1, axes.m2)
            source = here if self.own is None else self.own
            for by in (1, 3, 2):
                remote(source, here, sem[0], sem[1], axes.first(by)).start()
        elif phase == 1:
            send(self.row(0), axes.second(1))
            send(self.row(0), axes.second(3))
            share(self.row(0))
        elif phase == 2:
            send(self.row(3, pl.ds(0, 2)), axes.second(1))
            send(self.row(1, pl.ds(2, 2)), axes.second(3))
            share(self.row(3))
            share(self.row(1))
        else:
            share(self.row(2))

    def end(self, phase):
        axes = self.axes
        sem = [self.semaphores.at[phase, at] for at in range(4)]
        one, two = self.row(0), self.block(ALL, pl.ds(0, 2))
        moved = (self.block(pl.ds(0, 3), axes.m2), two, one, None)[phase]
        shared = (None, one, two, one)[phase]
        if moved is not None:
            remote(moved, moved, sem[0], sem[1], axes.partner).wait()
        if shared is not None:
            remote(shared, shared, sem[2], sem[3], axes.partner).wait()


class AcrossSegment(GatherSegment):
    def __init__(self, first_is_y, quarters, semaphores, own):
        x = lax.axis_index(BATCH)
        super().__init__(first_is_y, lambda z, y: quarters(z, y, x, 1), semaphores, own)
        self.quarters = quarters

    def begin(self, phase):
        axes = self.axes
        sem = [self.semaphores.at[phase, at] for at in range(4)]

        def send(part, where):
            remote(part, part, sem[0], sem[1], where).start()

        def share(part):
            remote(part, part, sem[2], sem[3], axes.partner).start()

        if phase == 0:
            here = self.block(axes.m1, axes.m2)
            for by in (1, 3, 2):
                remote(self.own, here, sem[0], sem[1], axes.first(by)).start()
        elif phase == 1:
            send(self.row(0), axes.second(1))
            send(self.row(0), axes.second(3))
        elif phase == 2:
            send(self.row(3, pl.ds(0, 2)), axes.second(1))
            send(self.row(1, pl.ds(2, 2)), axes.second(3))
        elif phase == 3:
            mine = self.block(ALL, ALL)
            for by in (1, 3):
                send(mine, self.plane(by))
            far = [self.semaphores.at[4, at] for at in range(2)]
            remote(mine, mine, far[0], far[1], self.plane(2)).start()
            share(mine)
        elif phase == 4:
            for by in (1, 3):
                share(self.quarters(ALL, ALL, shifted(axes.x, by), 1))
        else:
            self.last_share().start()

    def plane(self, by):
        axes = self.axes
        return device(shifted(axes.x, by), axes.z, axes.y, axes.core)

    def last_share(self):
        part = self.quarters(ALL, ALL, shifted(self.axes.x, 2), 1)
        sem = [self.semaphores.at[2, at] for at in (2, 3)]
        return remote(part, part, sem[0], sem[1], self.axes.partner)

    def end(self, phase):
        axes = self.axes
        if phase == 5:
            self.last_share().wait()
            return
        sem = [self.semaphores.at[phase, at] for at in range(4)]
        two = self.quarters(ALL, ALL, 0, 2)
        mine = self.block(ALL, ALL)
        moved = (
            self.block(pl.ds(0, 3), axes.m2),
            self.block(ALL, pl.ds(0, 2)),
            self.row(0),
            two,
            mine,
        )[phase]
        shared = (None, None, None, mine, two)[phase]
        remote(moved, moved, sem[0], sem[1], axes.partner).wait()
        if shared is not None:
            remote(shared, shared, sem[2], sem[3], axes.partner).wait()


def across_views(name, ref):
    core = Axes(True).core

    def columns(first, count):
        return pl.ds(pl.multiple_of(core * 1024 + first * 256, 128), 256 * count)

    def rows(first, count):
        return pl.ds(pl.multiple_of(first * 16, 16), 16 * count)

    if name == "wide":
        return [
            (True, lambda z, y, first, count: ref.at[0, z, y, :, columns(first, count)]),
            (False, lambda z, y, first, count: ref.at[1, z, y, :, columns(first, count)]),
        ]
    return [
        (True, lambda z, y, first, count: ref.at[z, y, core, rows(first, count), pl.ds(0, 384)]),
        (False, lambda z, y, first, count: ref.at[z, y, core, rows(first, count), pl.ds(384, 384)]),
    ]


def across_owns(name, ref):
    axes = Axes(True)
    if name == "wide":
        columns = pl.ds(pl.multiple_of(axes.core * 1024 + axes.x * 256, 128), 256)
        return [ref.at[0, :, columns], ref.at[1, :, columns]]
    rows = pl.ds(pl.multiple_of(axes.x * 16, 16), 16)
    return [ref.at[rows, pl.ds(0, 384)], ref.at[rows, pl.ds(384, 384)]]


ACROSS = (("wide", 1), ("down", 0))


def halves(core, width):
    return pl.ds(pl.multiple_of(core * (width // 2), 128), width // 2)


def weight_views(name, ref):
    core = Axes(True).core
    narrow, wide = halves(core, 768), halves(core, 2048)
    if name == "qkv":
        return [
            (True, lambda z, y: ref.at[pl.ds(0, 2), z, y, :, narrow]),
            (False, lambda z, y: ref.at[2, z, y, :, narrow]),
        ]
    if name == "out":
        return [(False, lambda z, y: ref.at[z, y, :, narrow])]
    if name == "wide":
        return [
            (True, lambda z, y: ref.at[0, z, y, :, wide]),
            (False, lambda z, y: ref.at[1, z, y, :, wide]),
        ]
    if name == "down":
        return [
            (True, lambda z, y: ref.at[z, y, core, :, pl.ds(0, 384)]),
            (False, lambda z, y: ref.at[z, y, core, :, pl.ds(384, 384)]),
        ]
    return [(True, lambda z, y: ref.at[z, y, core])]


def own_views(name, ref):
    core = Axes(True).core
    narrow, wide = halves(core, 768), halves(core, 2048)
    if name == "qkv":
        return [ref.at[pl.ds(0, 2), :, narrow], ref.at[2, :, narrow]]
    if name == "out":
        return [ref.at[:, narrow]]
    if name == "wide":
        return [ref.at[0, :, wide], ref.at[1, :, wide]]
    if name == "down":
        return [ref.at[:, pl.ds(0, 384)], ref.at[:, pl.ds(384, 384)]]
    return [ref]


WEIGHTS = {
    "qkv": ((3, 4, 4, 48, 768), BF),
    "out": ((4, 4, 48, 768), BF),
    "wide": ((2, 4, 4, 48, 2048), BF),
    "down": ((4, 4, 2, 64, 768), BF),
    "gain": ((4, 4, 2, 8, 256), F32),
}
SEGMENTS = {"qkv": 2, "out": 1, "wide": 2, "down": 2, "gain": 1}
GATHERED = [(name, layer) for layer in range(2) for name in ("qkv", "out", "wide", "down")] + [
    ("gain", 0)
]


def weight_shape(key):
    return jax.ShapeDtypeStruct(*WEIGHTS[key[0]])


class ScatterPart:
    def __init__(self, first_is_y, total, rows, ring, blocks, groups, semaphores, finish):
        self.axes = Axes(first_is_y)
        self.total, self.rows, self.ring, self.blocks, self.groups = total, rows, ring, blocks, groups
        self.semaphores, self.finish = semaphores, finish

    def fill(self, z, value):
        if self.axes.first_is_y:
            self.total[z] = value
        else:
            self.total[:, z] = value

    def spread(self):
        axes, sem = self.axes, self.semaphores
        for by in (1, 3, 2):
            remote(
                self.total.at[axes.m2, shifted(axes.m1, by)],
                self.blocks.at[by - 1],
                sem.at[4],
                sem.at[5],
                axes.first(by),
            ).start()

    def stage(self, number):
        axes, sem, total = self.axes, self.semaphores, self.total
        m1, m2 = axes.m1, axes.m2
        before, after, across = shifted(m2, 3), shifted(m2, 1), shifted(m2, 2)
        low, high = pl.ds(0, 2), pl.ds(2, 2)

        def add(target, source):
            target[...] = (target[...].astype(F32) + source[...].astype(F32)).astype(target.dtype)

        if number == 1:
            remote(
                total.at[across, low], self.ring.at[0], sem.at[0], sem.at[1], axes.second(1)
            ).start()
            remote(
                total.at[across, high], self.ring.at[1], sem.at[0], sem.at[1], axes.second(3)
            ).start()
        elif number == 2:
            row = total.at[m2]
            remote(row, self.ring, sem.at[0], sem.at[1], axes.partner).wait()
            add(total.at[after, low], self.ring.at[0])
            add(total.at[before, high], self.ring.at[1])
            remote(
                total.at[after], self.rows.at[0], sem.at[2], sem.at[3], axes.second(1)
            ).start()
            remote(
                total.at[before], self.rows.at[1], sem.at[2], sem.at[3], axes.second(3)
            ).start()
        elif number == 3:
            remote(self.rows, self.rows, sem.at[2], sem.at[3], axes.partner).wait()
            for at in range(4):
                total[m2, at] = (
                    total[m2, at].astype(F32)
                    + self.rows[0, at].astype(F32)
                    + self.rows[1, at].astype(F32)
                ).astype(total.dtype)
            self.spread()
        elif number == 4:
            remote(self.blocks, self.blocks, sem.at[4], sem.at[5], axes.partner).wait()
            self.groups[axes.x] = (
                total[m2, m1].astype(F32)
                + self.blocks[0].astype(F32)
                + self.blocks[1].astype(F32)
                + self.blocks[2].astype(F32)
            ).astype(total.dtype)
            mine = self.groups.at[axes.x]
            for by in (1, 3, 2):
                remote(
                    mine,
                    mine,
                    sem.at[6],
                    sem.at[7],
                    device(shifted(axes.x, by), axes.z, axes.y, axes.core),
                ).start()
        elif number == 5:
            three = self.groups.at[pl.ds(0, 3)]
            remote(three, three, sem.at[6], sem.at[7], axes.partner).wait()
            summed = self.groups[0].astype(F32)
            for at in range(1, 4):
                summed = summed + self.groups[at].astype(F32)
            self.finish(0, summed)
        else:
            self.finish(1, None)


class AcrossPart(ScatterPart):
    def __init__(self, first_is_y, whole, quarter, came, rows, ring, blocks, groups, semaphores, finish):
        super().__init__(first_is_y, quarter, rows, ring, blocks, groups, semaphores, finish)
        self.whole, self.came = whole, came
        self.by_rows = whole.shape[2] == 64

    def fill(self, z, value):
        if self.axes.first_is_y:
            self.whole[z] = value
        else:
            self.whole[:, z] = value

    def quarter(self, at):
        if self.by_rows:
            return pl.ds(pl.multiple_of(at * 16, 16), 16), slice(None)
        return slice(None), pl.ds(pl.multiple_of(at * 256, 128), 256)

    def stage(self, number):
        axes, sem = self.axes, self.semaphores
        if number == 0:
            for by in (1, 3, 2):
                there = shifted(axes.x, by)
                remote(
                    self.whole.at[(slice(None), slice(None)) + self.quarter(there)],
                    self.came.at[by - 1],
                    sem.at[10],
                    sem.at[11],
                    device(there, axes.z, axes.y, axes.core),
                ).start()
            return
        if number == 1:
            remote(self.came, self.came, sem.at[10], sem.at[11], axes.partner).wait()
            for at in range(4):
                summed = self.whole[(at, slice(None)) + self.quarter(axes.x)].astype(F32)
                for by in range(3):
                    summed = summed + self.came[by, at].astype(F32)
                self.total[at] = summed.astype(BF)
        if number == 5:
            three = self.groups.at[pl.ds(0, 3)]
            remote(three, three, sem.at[6], sem.at[7], axes.partner).wait()
            quarters = [self.groups[at].astype(F32) for at in range(4)]
            self.finish(0, jnp.concatenate(quarters, axis=0 if self.by_rows else 1))
            return
        super().stage(number)


class StraightPart(ScatterPart):
    def stage(self, number):
        axes, sem = self.axes, self.semaphores
        m2 = axes.m2
        if number == 1:
            for by in (1, 3, 2):
                remote(
                    self.total.at[shifted(m2, by)],
                    self.rows.at[by - 1],
                    sem.at[2],
                    sem.at[3],
                    axes.second(by),
                ).start()
        elif number == 2:
            remote(self.rows, self.rows, sem.at[2], sem.at[3], axes.partner).wait()
            for at in range(4):
                summed = self.total[m2, at].astype(F32)
                for by in range(3):
                    summed = summed + self.rows[by, at].astype(F32)
                self.total[m2, at] = summed.astype(self.total.dtype)
            self.spread()
        elif number != 3:
            super().stage(number)


SCATTER_SEMAPHORES = 12
ACROSS_PARTS = (("left", 0), ("right", 0), ("gate", 1), ("up", 1))
LAST_PARTS = (("q", 0), ("k", 0), ("v", 0), ("w", 0), ("gain", 0))
PARTS = {
    "gate": (True, 48, 1024, BF),
    "up": (False, 48, 1024, BF),
    "left": (True, 64, 384, BF),
    "right": (False, 64, 384, BF),
    "o": (False, 48, 384, BF),
    "q": (True, 48, 384, BF),
    "k": (False, 48, 384, BF),
    "v": (True, 48, 128, BF),
    "w": (False, 48, 256, BF),
    "gain": (False, 8, 256, F32),
}
SOURCE = {
    "q": "qkv", "k": "qkv", "v": "qkv", "w": "qkv", "o": "out", "gate": "wide", "up": "wide",
    "left": "down", "right": "down", "gain": "gain",
}
SUMS = {
    "qkv": ((2, 3, 24, 768), F32),
    "out": ((2, 24, 768), F32),
    "wide": ((2, 2, 24, 2048), F32),
    "down": ((2, 64, 768), F32),
    "gain": ((1, 8, 256), F32),
}
LEFT, RIGHT = pl.ds(0, 384), pl.ds(384, 384)


def part_target(part, ref):
    if part in ("q", "k", "v", "w"):
        return ref.at[min("qkvw".index(part), 2)]
    if part in ("gate", "up"):
        return ref.at[int(part == "up")]
    if part in ("left", "right"):
        return ref.at[:, LEFT if part == "left" else RIGHT]
    return ref


def rows_swapped(target, mine, theirs, sem, first):
    axes = Axes(True)
    core = axes.core

    def finish(part, summed):
        own_rows = pl.ds(pl.multiple_of(core * 24, 8), 24)
        other_rows = pl.ds(pl.multiple_of((1 - core) * 24, 8), 24)
        copy = remote(mine.at[other_rows, :], theirs, sem.at[8], sem.at[9], axes.partner)
        if part == 0:
            mine[...] = summed
            copy.start()
        else:
            copy.wait()
            kept = mine[own_rows, :]
            got = theirs[...]
            width, half = kept.shape[-1], target.shape[-1] // 2
            target[:, first : first + width] = jnp.where(core == 0, kept, got)
            target[:, half + first : half + first + width] = jnp.where(core == 0, got, kept)

    return finish


def direct(target):
    def finish(part, summed):
        if part == 0:
            target[...] = summed

    return finish


def part_scratch():
    shared, own = [], []
    for part, (_, rows, width, kind) in PARTS.items():
        shared += [
            pltpu.VMEM((4, 4, rows, width), kind),
            pltpu.VMEM((8, 128) if part == "gain" else (2, 4, rows, width), kind),
            pltpu.VMEM((48, width), F32) if rows == 48 else pltpu.VMEM((8, 128), F32),
        ]
        for layer in range(1 if part == "gain" else 2):
            across = (part, layer) in ACROSS_PARTS
            block = (rows, width)
            if across:
                block = (16, width) if rows == 64 else (rows, width // 4)
                own += [
                    pltpu.VMEM((4, 4) + block, kind),
                    pltpu.VMEM((3, 4, 4) + block, kind),
                    pltpu.VMEM((2, 4) + block, kind),
                ]
            straight = (part, layer) in LAST_PARTS
            own += [
                pltpu.VMEM(((3, 4) if straight else (2, 2)) + block, kind),
                pltpu.VMEM((3,) + block, kind),
                pltpu.VMEM((4,) + block, kind),
                pltpu.VMEM((24, width), F32) if rows == 48 else pltpu.VMEM((8, 128), F32),
            ]
    return shared, own


def build_parts(shared, own, sems, sums):
    parts = {}
    count = 0
    own = list(own)

    def take(number):
        taken = own[:number]
        del own[:number]
        return taken

    for at, (part, (first_is_y, rows, _, _)) in enumerate(PARTS.items()):
        total, rows_in, mine = shared[3 * at : 3 * at + 3]
        for layer in (0,) if part == "gain" else (0, 1):
            if (part, layer) in ACROSS_PARTS:
                quarter, came, rows_here = take(3)
            ring, blocks, groups, theirs = take(4)
            target = part_target(part, sums[SOURCE[part]].at[layer])
            sem = sems.at[count]
            first = 128 if part == "w" else 0
            if rows == 48:
                finish = rows_swapped(target, mine, theirs, sem, first)
            else:
                finish = direct(target)
            if (part, layer) in ACROSS_PARTS:
                parts[part, layer] = AcrossPart(
                    first_is_y, total, quarter, came, rows_here, ring, blocks, groups, sem, finish
                )
            elif (part, layer) in LAST_PARTS:
                parts[part, layer] = StraightPart(
                    first_is_y, total, ring, None, blocks, groups, sem, finish
                )
            else:
                parts[part, layer] = ScatterPart(
                    first_is_y, total, rows_in, ring, blocks, groups, sem, finish
                )
            count += 1
    return parts


def pair_device(pair):
    if pair < 16:
        return 2 * pair
    z = (pair - 16) // 2
    return 2 * (4 * z + 2 * ((pair - 16) % 2) + z % 2) + 1


def own_pair():
    _, z, y, core = coordinates()
    has_pair = (core == 0) | (lax.rem(z + y, 2) == 0)
    pair = jnp.where(core == 0, 4 * z + y, 16 + 2 * z + lax.div(y, 2))
    return has_pair, pair


def lanes(shape):
    return lax.broadcasted_iota(jnp.int32, shape, len(shape) - 1)


def turned(values, cosine, sine):
    here = lax.rem(lanes(values.shape), 64) < 32
    width = values.shape[-1]
    other = jnp.where(here, pltpu.roll(values, width - 32, 1), pltpu.roll(values, 32, 1))
    return values * cosine + other * sine


def twice(table):
    return jnp.concatenate([table, table], axis=0)


def allowed_keys(first_key, first_query, keys, queries, length):
    key = first_key + lax.broadcasted_iota(jnp.int32, (keys, queries), 0)
    query = first_query + lax.broadcasted_iota(jnp.int32, (keys, queries), 1)
    return (key <= query) & (key < length)


def slot_length(lengths, pair):
    return jnp.where(pair < HEADS, lengths[0], lengths[1])


LAST_DIMS = (((1,), (1,)), ((), ()))
BLOCKS = LENGTH // BLOCK
MESSAGE = 96


def front_lanes(rows):
    return lanes((rows, 128)) < 64


def pack_heads(both):
    front = front_lanes(32)
    top, bottom = both[0:32], both[32:64]
    return (
        jnp.where(front, top, pltpu.roll(bottom, 64, 1)).astype(BF),
        jnp.where(front, pltpu.roll(top, 64, 1), bottom).astype(BF),
    )


def unpack_heads(first, second):
    front = front_lanes(32)
    first, second = first.astype(F32), second.astype(F32)
    return jnp.concatenate(
        [
            jnp.where(front, first, pltpu.roll(second, 64, 1)),
            jnp.where(front, pltpu.roll(first, 64, 1), second),
        ],
        axis=0,
    )


def unpack_block(packed, to_front):
    packed = packed.astype(F32).reshape(128, 128)
    other = pltpu.roll(packed, 64, 1)
    front = front_lanes(128)
    if to_front:
        top, bottom = jnp.where(front, packed, 0.0), jnp.where(front, other, 0.0)
    else:
        top, bottom = jnp.where(front, 0.0, other), jnp.where(front, 0.0, packed)
    joined = jnp.concatenate([top.reshape(4, 32, 128), bottom.reshape(4, 32, 128)], axis=1)
    return joined.reshape(256, 128).astype(BF)


def pack_turned(turned_values):
    rows = jnp.concatenate([turned_values, turned_values], axis=0).T.reshape(4, 64, 128)
    front = lanes((4, 32, 128)) < 64
    return jnp.where(front, rows[:, 0:32], rows[:, 32:64]).astype(BF)


class Exchange:
    def __init__(self, semaphores):
        self.x, self.me = lax.axis_index(BATCH), lax.axis_index(SEQ)
        self.has_pair, self.pair = own_pair()
        self.send, self.receive, self.local = (semaphores.at[at] for at in range(3))

    def to(self, there, source, target):
        @pl.when(self.me != there)
        def _():
            remote(source, target, self.send, self.receive, (self.x, there)).start()

        @pl.when(self.me == there)
        def _():
            pltpu.make_async_copy(source, target, self.local).start()

    def wait(self, sent, got, where):
        if where == "pairs":
            sends, gets = (sent.shape[0], sent.shape[0] - 1), (None, got.shape[0] - 1)
        else:
            sends, gets = (None, sent.shape[0] - 1), (got.shape[0], got.shape[0] - 1)

        def wait_for(n_sent, n_got):
            if n_got is not None:
                part = got.at[pl.ds(0, n_got)]
                remote(part, part, self.send, self.receive, (self.x, self.me)).wait_recv()
            if n_sent is not None:
                part = sent.at[pl.ds(0, n_sent)]
                remote(part, part, self.send, self.receive, (self.x, self.me)).wait_send()

        @pl.when(self.has_pair)
        def _():
            pltpu.make_async_copy(sent.at[0], got.at[0], self.local).wait()
            wait_for(sends[1], gets[1])

        @pl.when(jnp.logical_not(self.has_pair))
        def _():
            wait_for(sends[0], gets[0])


def send_projections(exchange, query, key, value, cosine, sine, outgoing, rows):
    cosine, sine = twice(cosine), twice(sine)
    front = front_lanes(64)
    for tile in range(6):
        cut = slice(128 * tile, 128 * tile + 128)
        q = turned(query[:, cut], cosine, sine) * (1.0 / math.sqrt(HEAD_DIM))
        k = turned(key[:, cut], cosine, sine)
        v = value[:, cut]
        for slot in range(2):
            span = slice(64 * slot, 64 * slot + 64)
            at = slot * HEADS + 2 * tile
            ks, vs = k[span], v[span]
            outgoing[at, 0:64] = jnp.where(front, ks, pltpu.roll(vs, 64, 1)).astype(BF)
            outgoing[at + 1, 0:64] = jnp.where(front, pltpu.roll(ks, 64, 1), vs).astype(BF)
            outgoing[at, 64:96], outgoing[at + 1, 64:96] = pack_heads(q[span])
    for pair in range(PAIRS):
        exchange.to(pair_device(pair), outgoing.at[pair], rows.at[exchange.me])


def attend_block(exchange, at, length, rows, values_turned, out_turned, log_total, outgoing, incoming):
    count = (at + 1) * BLOCK
    queries = unpack_block(rows[4 * at : 4 * at + 4, 64:96], True)
    keys = rows[0 : 4 * at + 4, 0:64].reshape(count, 128)
    scores = lax.dot_general(keys, queries, LAST_DIMS, preferred_element_type=F32)
    scores = jnp.where(allowed_keys(0, at * BLOCK, count, BLOCK, length), scores, MASKED)
    highest = jnp.max(scores, axis=0, keepdims=True)
    raised = jnp.exp(scores - highest)
    total = jnp.sum(raised, axis=0, keepdims=True)
    result = (
        jnp.dot(values_turned[:, 0:count], raised.astype(BF), preferred_element_type=F32) / total
    )
    cut = slice(at * BLOCK, count)
    out_turned[:, cut] = result
    log_total[:, cut] = jnp.broadcast_to(highest + jnp.log(total), (8, BLOCK))
    outgoing[4 * at : 4 * at + 4] = pack_turned(result)
    for there in range(4 * at, 4 * at + 4):
        exchange.to(there, outgoing.at[there], incoming.at[exchange.pair])


def merge_heads(incoming, merged):
    for slot in range(2):
        for tile in range(6):
            at = slot * HEADS + 2 * tile
            merged[64 * slot : 64 * slot + 64, 128 * tile : 128 * tile + 128] = unpack_heads(
                incoming[at], incoming[at + 1]
            ).astype(BF)


def norm_forward(values, norm_gain):
    inverse = lax.rsqrt(jnp.mean(values * values, axis=-1, keepdims=True) + EPSILON)
    return (values * inverse * norm_gain, inverse)


def feed_forward(rows_in, gate_up, down, paired):
    fed = jnp.zeros((128, 768), F32)
    for z in range(4):
        cut = slice(512 * z, 512 * z + 512)
        gate = jnp.dot(rows_in, gate_up[0, :, :, :, cut].reshape(768, 512), preferred_element_type=F32)
        up = jnp.dot(rows_in, gate_up[1, :, :, :, cut].reshape(768, 512), preferred_element_type=F32)
        paired[0, :, cut] = gate
        paired[1, :, cut] = up
        hidden = (jax.nn.silu(gate) * up).astype(BF)
        fed = fed + jnp.dot(hidden, down[z].reshape(512, 768), preferred_element_type=F32)
    return fed


KEPT = (
    [("result", (128, 768), F32), ("mid_0", (128, 768), F32), ("summed_0", (128, 768), F32)]
    + [("mid_1", (128, 768), F32), ("gain", (8, 768), F32)]
    + [("stream", (128, 768), BF), ("cotangent", (128, 768), F32)]
    + [
        (name + "_" + layer, shape, kind)
        for layer in "01"
        for name, shape, kind in (
            ("paired", (2, 128, 2048), F32),
            ("rows", (32, MESSAGE, 128), BF),
            ("merged", (128, 768), BF),
            ("turned", (64, LENGTH), F32),
            ("total", (8, LENGTH), F32),
        )
    ]
)


def forward_kernel(
    lengths, qkv, out, gate_up, down, gains, inputs, cotangents, cosine, sine, *refs
):
    stored = dict(zip(GATHERED[:-1], refs[:8]))
    kept = {name: ref for (name, _, _), ref in zip(KEPT, refs[8:])}
    refs = refs[8 + len(KEPT) :]
    store, refs = dict(zip(GATHERED, refs[:9])), refs[9:]
    their_qkv, their_out, their_gate_up, b_qkv, b_out, b_gate_up, b_down = refs[:7]
    outgoing, places, incoming, values_turned, stream, swap, sems, local, pair_sems = refs[7:]
    axes = Axes(True)
    core = axes.core
    x, me = lax.axis_index(BATCH), lax.axis_index(SEQ)
    greet(
        [(x, lax.rem(me + by, 32)) for by in range(1, 32)]
        + [device(shifted(x, by), axes.z, axes.y, core) for by in (1, 2, 3)]
    )
    swaps = [
        remote(mine, theirs, swap.at[0, at], swap.at[1, at], axes.partner)
        for at, (mine, theirs) in enumerate(
            (
                (qkv.at[0], their_qkv.at[0]),
                (qkv.at[1], their_qkv.at[1]),
                (out, their_out),
                (gate_up, their_gate_up),
            )
        )
    ]
    for copy in swaps:
        copy.start()
    for slot in range(2):
        stream[64 * slot : 64 * slot + 64] = inputs[:, slot, :]
        kept["cotangent"][64 * slot : 64 * slot + 64] = cotangents[:, slot, :]
    kept["stream"][...] = stream[...].astype(BF)

    def joined(mine, theirs):
        upper = jnp.where(core == 0, mine, theirs)
        lower = jnp.where(core == 0, theirs, mine)
        return jnp.concatenate([upper, lower], axis=0).astype(BF)

    segments = {}
    at = 0
    for key in GATHERED:
        name, layer = key
        block = {"qkv": b_qkv, "out": b_out, "wide": b_gate_up, "down": b_down}.get(name)
        block = gains if block is None else block.at[layer]
        kind, views, owns = GatherSegment, weight_views, own_views
        if key in ACROSS:
            kind, views, owns = AcrossSegment, across_views, across_owns
        segments[key] = []
        for (first_is_y, view), own in zip(views(name, store[key]), owns(name, block)):
            segments[key].append(kind(first_is_y, view, sems.at[at], own))
            at += 1

    def each(keys, act):
        for key in keys:
            for segment in segments[key]:
                act(segment)

    def keep(*keys):
        each(keys, lambda segment: segment.keep().start())
        each(keys, lambda segment: segment.keep().wait())

    def begin(phase, *keys):
        each(keys, lambda segment: segment.begin(phase))

    def end(phase, *keys):
        each(keys, lambda segment: segment.end(phase))

    saves = []

    def save(*keys):
        for key in keys:
            copy = pltpu.make_async_copy(store[key], stored[key], local.at[len(saves)])
            copy.start()
            saves.append(copy)

    qkv_0, out_0, wide_0, down_0 = GATHERED[0:4]
    qkv_1, out_1, wide_1, down_1 = GATHERED[4:8]
    gains_0 = GATHERED[8]

    swaps[0].wait()
    for at in range(3):
        b_qkv[0, at] = joined(qkv[0, at], their_qkv[0, at])
    begin(0, qkv_0)
    keep(qkv_0)
    b_down[0] = down[0].astype(BF)
    begin(0, down_0)
    keep(down_0)
    for copy in swaps[1:]:
        copy.wait()
    for at in range(2):
        b_gate_up[0, at] = joined(gate_up[0, at], their_gate_up[0, at])
    begin(0, wide_0)
    keep(wide_0)
    end(0, qkv_0)
    begin(1, qkv_0)
    end(0, down_0)
    begin(1, down_0)
    b_out[0] = joined(out[0], their_out[0])
    for at in range(2):
        b_gate_up[1, at] = joined(gate_up[1, at], their_gate_up[1, at])
    begin(0, out_0, gains_0, wide_1)
    keep(out_0, gains_0, wide_1)
    for at in range(3):
        b_qkv[1, at] = joined(qkv[1, at], their_qkv[1, at])
    b_out[1] = joined(out[1], their_out[1])
    b_down[1] = down[1].astype(BF)
    end(1, qkv_0)
    begin(2, qkv_0)
    end(1, down_0)
    begin(2, down_0)
    end(0, wide_0)
    begin(1, wide_0)
    end(2, qkv_0)
    begin(3, qkv_0)
    keep(qkv_1, out_1, down_1)
    begin(0, qkv_1)
    end(2, down_0)
    begin(3, down_0)
    end(0, out_0, gains_0, wide_1)
    begin(1, wide_1)
    end(3, qkv_0)
    save(qkv_0)

    def attention(layer, source, before, between):
        weights = store["qkv", layer]
        name = "_" + str(layer)
        rows, merged = kept["rows" + name], kept["merged" + name]
        there = Exchange(pair_sems.at[2 * layer])
        back = Exchange(pair_sems.at[2 * layer + 1])
        low = source.astype(BF)
        query, key, value = (
            jnp.dot(low, weights[at].reshape(768, 768), preferred_element_type=F32)
            for at in range(3)
        )
        send_projections(
            there, query, key, value, cosine[...], sine[...], outgoing.at[layer], rows
        )
        before()
        there.wait(outgoing.at[layer], rows, "pairs")
        length = slot_length(lengths, there.pair)

        @pl.when(there.has_pair)
        def _():
            all_rows = rows[:, 0:64].reshape(LENGTH, 128).astype(F32)
            values_turned[...] = all_rows.T[64:128].astype(BF)

        for at in range(BLOCKS):

            @pl.when(there.has_pair)
            def _(at=at):
                attend_block(
                    back,
                    at,
                    length,
                    rows,
                    values_turned,
                    kept["turned" + name],
                    kept["total" + name],
                    places.at[layer],
                    incoming.at[layer],
                )

            if at in between:
                between[at]()
        back.wait(places.at[layer], incoming.at[layer], "places")
        merge_heads(incoming.at[layer], merged)
        between["after"]()
        out_matrix = store["out", layer][...].reshape(768, 768)
        return jnp.dot(merged[...], out_matrix, preferred_element_type=F32)

    def before_0():
        begin(1, out_0, gains_0)
        end(1, wide_1)
        begin(2, wide_1)
        end(0, qkv_1)
        begin(1, qkv_1)

    def within_0():
        end(1, wide_0)
        begin(2, wide_0)
        end(2, wide_1)
        begin(3, wide_1)

    def later_0():
        end(1, out_0, gains_0)
        begin(2, out_0, gains_0)

    def last_0():
        end(1, qkv_1)
        begin(2, qkv_1)
        end(3, down_0)
        begin(4, down_0)

    def after_0():
        end(4, down_0)
        begin(5, down_0)
        end(2, wide_0, out_0, gains_0)
        begin(3, out_0, wide_0, gains_0)
        begin(0, out_1, down_1)
        end(3, out_0, wide_0, gains_0)
        end(5, down_0)
        save(out_0, wide_0, down_0)
        for device_at in range(32):
            piece = store[gains_0][device_at // 8, device_at // 2 % 4, device_at % 2]
            first = 24 * device_at // 128
            if device_at == 0:
                kept["gain"][...] = jnp.zeros((8, 768), F32)
            width = min(256, 768 - 128 * first)
            kept["gain"][:, 128 * first : 128 * first + width] += piece[:, :width]

    def gain(at):
        return kept["gain"][at : at + 1, :]

    mixed = attention(
        0, stream[...], before_0, {1: within_0, 4: later_0, 7: last_0, "after": after_0}
    )
    residual = stream[...] + mixed
    kept["mid_0"][...] = residual
    middle, _ = norm_forward(residual, gain(0))
    end(2, qkv_1)
    begin(3, qkv_1)
    fed = feed_forward(middle.astype(BF), store[wide_0], store[down_0], kept["paired_0"])
    end(0, out_1, down_1)
    summed = middle + fed
    kept["summed_0"][...] = summed
    shallow, _ = norm_forward(summed, gain(1))
    normed, _ = norm_forward(shallow, gain(2))
    end(3, qkv_1)
    save(qkv_1)

    def before_1():
        begin(1, out_1, down_1)

    def within_1():
        end(3, wide_1)
        begin(4, wide_1)

    def later_1():
        end(1, out_1, down_1)
        begin(2, out_1, down_1)
        end(4, wide_1)
        begin(5, wide_1)

    def after_1():
        end(2, out_1, down_1)
        begin(3, out_1, down_1)
        end(3, out_1, down_1)
        end(5, wide_1)
        save(out_1, wide_1, down_1)

    mixed = attention(1, normed, before_1, {1: within_1, 7: later_1, "after": after_1})
    residual = shallow + mixed
    kept["mid_1"][...] = residual
    normed_two, _ = norm_forward(residual, gain(3))
    fed = feed_forward(normed_two.astype(BF), store[wide_1], store[down_1], kept["paired_1"])
    kept["result"][...] = residual + fed
    for copy in saves:
        copy.wait()


def run_forward(*operands):
    count = sum(SEGMENTS[name] for name, _ in GATHERED)
    stored = GATHERED[:-1]
    results = pl.pallas_call(
        forward_kernel,
        out_shape=[weight_shape(key) for key in stored]
        + [jax.ShapeDtypeStruct(shape, kind) for _, shape, kind in KEPT],
        in_specs=[SMEM] + [VMEM] * 9,
        out_specs=[ANY] * 8 + [VMEM] * len(KEPT),
        scratch_shapes=[pltpu.VMEM(*WEIGHTS[name]) for name, _ in GATHERED]
        + [
            pltpu.VMEM((2, 3, 24, 768), F32),
            pltpu.VMEM((2, 24, 768), F32),
            pltpu.VMEM((2, 2, 24, 2048), F32),
            pltpu.VMEM((2, 3, 48, 768), BF),
            pltpu.VMEM((2, 48, 768), BF),
            pltpu.VMEM((2, 2, 48, 2048), BF),
            pltpu.VMEM((2, 64, 768), BF),
            pltpu.VMEM((2, PAIRS, MESSAGE, 128), BF),
            pltpu.VMEM((2, 32, 32, 128), BF),
            pltpu.VMEM((2, PAIRS, 32, 128), BF),
            pltpu.VMEM((64, LENGTH), BF),
            pltpu.VMEM((128, 768), F32),
            pltpu.SemaphoreType.DMA((2, 4)),
            pltpu.SemaphoreType.DMA((count, 5, 4)),
            pltpu.SemaphoreType.DMA((8,)),
            pltpu.SemaphoreType.DMA((4, 3)),
        ],
        compiler_params=params(1),
        name="forward",
    )(*operands)
    return dict(zip(stored, results)), {
        name: result for (name, _, _), result in zip(KEPT, results[8:])
    }


def attend_back_block(
    exchange, at, length, rows, out_grad, out_turned, log_total, keys_turned, key_grad, outgoing, incoming
):
    cut = slice(at * BLOCK, (at + 1) * BLOCK)
    four = slice(4 * at, 4 * at + 4)
    queries = unpack_block(rows[four, 64:96], True)
    outs = unpack_block(out_grad[four], False)
    outs_turned = outs.astype(F32).T[64:128]
    delta = jnp.sum(outs_turned * out_turned[:, cut], axis=0, keepdims=True)
    shift = log_total[0:1, cut]
    query_grad = jnp.zeros((64, BLOCK), F32)
    for part in range(at + 1):
        span = slice(part * BLOCK, (part + 1) * BLOCK)
        keys = rows[4 * part : 4 * part + 4, 0:64].reshape(BLOCK, 128)
        scores = lax.dot_general(keys, queries, LAST_DIMS, preferred_element_type=F32)
        allowed = allowed_keys(part * BLOCK, at * BLOCK, BLOCK, BLOCK, length)
        probs = jnp.where(allowed, jnp.exp(scores - shift), 0.0)
        probs_grad = lax.dot_general(keys, outs, LAST_DIMS, preferred_element_type=F32)
        score_grad = (probs * (probs_grad - delta)).astype(BF)
        key_grad[span, :] += jnp.dot(score_grad, queries, preferred_element_type=F32) + jnp.dot(
            probs.astype(BF), outs, preferred_element_type=F32
        )
        query_grad += jnp.dot(keys_turned[:, span], score_grad, preferred_element_type=F32)
    outgoing[four, 0:64] = key_grad[cut, :].reshape(4, SPAN, 128).astype(BF)
    outgoing[four, 64:96] = pack_turned(query_grad)
    for there in range(4 * at, 4 * at + 4):
        exchange.to(there, outgoing.at[there], incoming.at[exchange.pair])


def collect_projections(incoming, cosine, sine, result):
    front = front_lanes(64)
    for slot in range(2):
        span = slice(64 * slot, 64 * slot + 64)
        for tile in range(6):
            cut = slice(128 * tile, 128 * tile + 128)
            at = slot * HEADS + 2 * tile
            first, second = (incoming[at + n, 0:64].astype(F32) for n in (0, 1))
            q = unpack_heads(incoming[at, 64:96], incoming[at + 1, 64:96])
            k = jnp.where(front, first, pltpu.roll(second, 64, 1))
            v = jnp.where(front, pltpu.roll(first, 64, 1), second)
            q = turned(q * (1.0 / math.sqrt(HEAD_DIM)), cosine, -sine)
            result[0, span, cut] = q.astype(BF)
            result[1, span, cut] = turned(k, cosine, -sine).astype(BF)
            result[2, span, cut] = v.astype(BF)


def norm_backward(incoming, values, norm_gain):
    inverse = lax.rsqrt(jnp.mean(values * values, axis=-1, keepdims=True) + EPSILON)
    scaled = incoming * norm_gain
    outgoing = inverse * scaled - values * (inverse * inverse * inverse) * jnp.mean(
        scaled * values, axis=-1, keepdims=True
    )
    return outgoing, jnp.sum(incoming * values * inverse, axis=0, keepdims=True)


def feed_back(incoming, paired, gate_up, down, gate_grads, up_grads, hidden_turned):
    source_grad = jnp.zeros((128, 768), F32)
    for z in range(4):
        cut = slice(512 * z, 512 * z + 512)
        hidden_grad = lax.dot_general(
            incoming, down[z].reshape(512, 768), LAST_DIMS, preferred_element_type=F32
        )
        gate, up = paired[0, :, cut], paired[1, :, cut]
        sigmoid = jax.nn.sigmoid(gate)
        hidden = (gate * sigmoid * up).T.astype(BF).reshape(4, 2, 64, 128)
        hidden_turned[0, z] = hidden[:, 0]
        hidden_turned[1, z] = hidden[:, 1]
        gate_grad = (hidden_grad * up * sigmoid * (1.0 + gate * (1.0 - sigmoid))).astype(BF)
        up_grad = (hidden_grad * gate * sigmoid).astype(BF)
        part = slice(512 * (z % 2), 512 * (z % 2) + 512)
        gate_grads[z // 2, :, part] = gate_grad
        up_grads[z // 2, :, part] = up_grad
        for at, value in enumerate((gate_grad, up_grad)):
            source_grad = source_grad + lax.dot_general(
                value, gate_up[at, :, :, :, cut].reshape(768, 512), LAST_DIMS, preferred_element_type=F32
            )
    return source_grad


def turned_low(values):
    return values.astype(F32).T.astype(BF)


def fill_part(part, rows, left_of, right):
    for z in range(4):
        value = jnp.dot(left_of(z), right, preferred_element_type=F32).astype(BF)
        part.fill(z, value.reshape(4, rows, right.shape[1]))


def beside(first, second, rows):
    def left_of(z):
        cut = slice(4 * rows * z, 4 * rows * (z + 1))
        return jnp.concatenate([first[cut], second[cut]], axis=1)

    return left_of


SHARED = {
    "source": ((768, 128), (768, 128)),
    "gate": ((2, 128, 1024), (128, 1024)),
    "up": ((2, 128, 1024), (128, 1024)),
    "hidden": ((2, 4, 4, 64, 128), (4, 4, 64, 128)),
    "fed": ((128, 768), (128, 768)),
    "merged": ((768, 128), (768, 128)),
    "mixed": ((2, 128, 384), (128, 384)),
    "norm": ((768, 128), (768, 128)),
    "low": ((2, 3, 128, 384), (3, 128, 384)),
}
KEPT_NAMES = ("paired", "rows", "merged", "turned", "total")
KEPT_TYPES = {name: (shape, kind) for name, shape, kind in KEPT}
WEIGHT_ORDER = ("down", "wide", "out", "qkv")


def backward_kernel(lengths, *refs):
    refs = list(refs)

    def take(count):
        taken = refs[:count]
        del refs[:count]
        return taken

    cotangent, stream, residual_0, summed_0, residual_1, gains, cosine, sine = take(8)
    far = [dict(zip(KEPT_NAMES, take(len(KEPT_NAMES)))) for _ in range(2)]
    stored = dict(zip(GATHERED[:-1], take(8)))
    (input_grad,) = take(1)
    sums = dict(zip(SUMS, take(len(SUMS))))
    kept = dict(zip(KEPT_NAMES, take(len(KEPT_NAMES))))
    weights = dict(zip(WEIGHT_ORDER, take(4)))
    shared, own = part_scratch()
    shared, own = take(len(shared)), take(len(own))
    given = dict(zip(SHARED, take(len(SHARED))))
    got = [dict(zip(SHARED, take(len(SHARED)))) for _ in range(2)]
    out_grads, to_pairs, to_places, incoming = take(4)
    keys_turned, key_grad, gain_grads, their_gains, stacked = take(5)
    part_sems, give_sems, load_sems, pair_sems = take(4)
    parts = build_parts(shared, own, part_sems, sums)
    axes = Axes(True)
    core = axes.core
    x, me = lax.axis_index(BATCH), lax.axis_index(SEQ)
    barrier = pltpu.get_barrier_semaphore()
    neighbours = [(x, lax.rem(me + by, 32)) for by in range(1, 32)]
    neighbours += [device(shifted(x, by), axes.z, axes.y, core) for by in (1, 2, 3)]
    for where in neighbours:
        pl.semaphore_signal(barrier, inc=1, device_id=where, device_id_type=MESH)

    def load(name, layer):
        at = WEIGHT_ORDER.index(name)
        return pltpu.make_async_copy(stored[name, layer], weights[name], load_sems.at[at])

    def recall(name, layer):
        at = KEPT_NAMES.index(name)
        return pltpu.make_async_copy(far[layer][name], kept[name], load_sems.at[4 + at])

    recall("paired", 1).start()
    for name in WEIGHT_ORDER:
        load(name, 1).start()
    for name in KEPT_NAMES[1:]:
        recall(name, 1).start()

    def gain(at):
        return gains[at : at + 1, :]

    def stages(*work):
        for names, layer, number in work:
            for name in names:
                parts[name, layer].stage(number)

    def share(layer, names):
        copies = []
        for name in names:
            at = list(SHARED).index(name)
            source = given[name]
            if SHARED[name][0] != SHARED[name][1]:
                source = source.at[1 - core]
            copies.append(
                remote(
                    source,
                    got[layer][name],
                    give_sems.at[layer, at, 0],
                    give_sems.at[layer, at, 1],
                    axes.partner,
                )
            )
        return copies

    def start(copies):
        for copy in copies:
            copy.start()

    def finish(copies):
        for copy in copies:
            copy.wait()

    PROJECTIONS = "qkvw"
    wide, narrow, down = ("gate", "up"), ("left", "right", "o"), ("left", "right")

    def wide_grads(layer):
        left_of = beside(given["source"], got[layer]["source"], 48)
        for name in wide:
            right = jnp.concatenate([given[name][core], got[layer][name][...]], axis=0)
            fill_part(parts[name, layer], 48, left_of, right)

    def narrow_grads(layer):
        def left_of(z):
            mine = given["hidden"][core, z].reshape(256, 128)
            return jnp.concatenate([mine, got[layer]["hidden"][z].reshape(256, 128)], axis=1)

        right = jnp.concatenate([given["fed"][...], got[layer]["fed"][...]], axis=0)
        fill_part(parts["left", layer], 64, left_of, right[:, :384])
        fill_part(parts["right", layer], 64, left_of, right[:, 384:])
        right = jnp.concatenate([given["mixed"][core], got[layer]["mixed"][...]], axis=0)
        left_of = beside(given["merged"], got[layer]["merged"], 48)
        fill_part(parts["o", layer], 48, left_of, right)

    def projection_grads(layer):
        left_of = beside(given["norm"], got[layer]["norm"], 48)
        for at, name in enumerate("qkv"):
            right = jnp.concatenate([given["low"][core, at], got[layer]["low"][at]], axis=0)
            if name == "v":
                fill_part(parts["w", layer], 48, left_of, right[:, 128:])
                right = right[:, :128]
            fill_part(parts[name, layer], 48, left_of, right)

    FED = ("source", "gate", "up", "hidden", "fed")
    MIXED = ("merged", "mixed")
    PROJECTED = ("norm", "low")

    def feed(layer, source, grad):
        load("down", layer).wait()
        load("wide", layer).wait()
        recall("paired", layer).wait()
        low = grad.astype(BF)
        given["fed"][...] = low
        given["source"][...] = turned_low(source.astype(BF))
        return feed_back(
            low,
            kept["paired"],
            weights["wide"],
            weights["down"],
            given["gate"],
            given["up"],
            given["hidden"],
        )

    def send_out_grad(layer, grad):
        load("out", layer).wait()
        low = grad.astype(BF)
        given["mixed"][0] = low[:, :384]
        given["mixed"][1] = low[:, 384:]
        for name in KEPT_NAMES[1:]:
            recall(name, layer).wait()
        given["merged"][...] = turned_low(kept["merged"][...])
        merged_grad = (
            lax.dot_general(
                low, weights["out"][...].reshape(768, 768), LAST_DIMS, preferred_element_type=F32
            )
            .astype(BF)
            .astype(F32)
        )
        exchange = Exchange(pair_sems.at[2 * layer])
        to = to_pairs
        for slot in range(2):
            for tile in range(6):
                at = slot * HEADS + 2 * tile
                both = merged_grad[64 * slot : 64 * slot + 64, 128 * tile : 128 * tile + 128]
                to[at], to[at + 1] = pack_heads(both)
        for pair in range(PAIRS):
            exchange.to(pair_device(pair), to.at[pair], out_grads.at[layer, me])
        return exchange

    def attention(layer, exchange, between):
        rows = kept["rows"]
        length = slot_length(lengths, exchange.pair)

        @pl.when(exchange.has_pair)
        def _():
            all_rows = rows[:, 0:64].reshape(LENGTH, 128).astype(F32)
            keys_turned[...] = all_rows.T[0:64].astype(BF)
            key_grad[...] = jnp.zeros_like(key_grad)

        exchange.wait(to_pairs, out_grads.at[layer], "pairs")
        back = Exchange(pair_sems.at[2 * layer + 1])
        for at in reversed(range(BLOCKS)):

            @pl.when(exchange.has_pair)
            def _(at=at):
                attend_back_block(
                    back,
                    at,
                    length,
                    rows,
                    out_grads.at[layer],
                    kept["turned"],
                    kept["total"],
                    keys_turned,
                    key_grad,
                    to_places,
                    incoming.at[layer],
                )

            stages(*between.get(at, ()))
        stages(*between.get("sent", ()))
        back.wait(to_places, incoming.at[layer], "places")
        collect_projections(incoming.at[layer], cosine[...], sine[...], stacked)

    def source_gradient(layer, source):
        load("qkv", layer).wait()
        given["norm"][...] = turned_low(source.astype(BF))
        for at in range(3):
            given["low"][0, at] = stacked[at, :, 0:384]
            given["low"][1, at] = stacked[at, :, 384:768]
        copies = share(layer, PROJECTED)
        start(copies)
        result = jnp.zeros((128, 768), F32)
        for at in range(3):
            result = result + lax.dot_general(
                stacked[at],
                weights["qkv"][at].reshape(768, 768),
                LAST_DIMS,
                preferred_element_type=F32,
            )
        return result, copies

    normed_two, _ = norm_forward(residual_1[...], gain(3))
    fed_grad = feed(1, normed_two, cotangent[...])
    for name in ("down", "wide"):
        load(name, 0).start()
    recall("paired", 0).start()
    through, gain_grad = norm_backward(fed_grad, residual_1[...], gain(3))
    gain_grads[...] = jnp.zeros_like(gain_grads)
    gain_grads[3:4, :] = gain_grad
    residual_grad = cotangent[...] + through
    pl.semaphore_wait(barrier, len(neighbours))
    exchange = send_out_grad(1, residual_grad)
    load("out", 0).start()
    copies = share(1, FED + MIXED)
    start(copies)
    finish(copies)
    wide_grads(1)
    stages((wide, 1, 0))
    narrow_grads(1)
    stages((narrow, 1, 1))
    attention(1, exchange, {6: [(narrow, 1, 2)], "sent": [(narrow, 1, 3)]})
    for name in KEPT_NAMES[1:]:
        recall(name, 0).start()
    shallow, _ = norm_forward(summed_0[...], gain(1))
    normed, _ = norm_forward(shallow, gain(2))
    normed_grad, copies = source_gradient(1, normed)
    load("qkv", 0).start()
    stages((narrow, 1, 4))
    through, gain_grad = norm_backward(normed_grad, shallow, gain(2))
    gain_grads[2:3, :] = gain_grad
    shallow_grad = residual_grad + through
    summed_grad, gain_grad = norm_backward(shallow_grad, summed_0[...], gain(1))
    gain_grads[1:2, :] = gain_grad

    finish(copies)
    projection_grads(1)
    stages((PROJECTIONS, 1, 1))
    middle, _ = norm_forward(residual_0[...], gain(0))
    fed_grad = feed(0, middle, summed_grad)
    middle_grad = summed_grad + fed_grad
    residual_grad, gain_grad = norm_backward(middle_grad, residual_0[...], gain(0))
    gain_grads[0:1, :] = gain_grad
    exchange = send_out_grad(0, residual_grad)
    copies = share(0, FED + MIXED)
    start(copies)
    stages((PROJECTIONS, 1, 2))
    finish(copies)
    narrow_grads(0)
    stages((down, 0, 0))
    stages((wide, 1, 1))
    wide_grads(0)
    stages((wide, 0, 1), ("o", 0, 1))
    attention(
        0,
        exchange,
        {
            6: [(PROJECTIONS, 1, 3)],
            3: [(wide, 1, 2)],
            0: [(PROJECTIONS, 1, 4), (narrow, 1, 5)],
            "sent": [(wide, 0, 2), ("o", 0, 2), (wide, 1, 3)],
        },
    )
    source_grad, copies = source_gradient(0, stream[...])
    swap = remote(
        gain_grads, their_gains, give_sems.at[0, len(SHARED), 0], give_sems.at[0, len(SHARED), 1], axes.partner
    )
    swap.start()
    input_grad[...] = residual_grad + source_grad
    stages((PROJECTIONS, 1, 5), (wide, 1, 4))
    finish(copies)
    projection_grads(0)
    swap.wait()
    gain_total = gain_grads[...] + their_gains[...]
    gain_total = jnp.concatenate([gain_total, jnp.zeros((8, 128), F32)], axis=1)
    for z in range(4):
        for y in range(4):
            first, second = (24 * (8 * z + 2 * y + which) // 128 * 128 for which in (0, 1))
            parts["gain", 0].total[y, z] = jnp.where(
                core == 0, gain_total[:, first : first + 256], gain_total[:, second : second + 256]
            )
    last = ("q", "k", "v", "w", "gain")
    stages((last, 0, 1), (down, 0, 1), (wide, 0, 3), ("o", 0, 3), (PROJECTIONS, 1, 6))
    stages((wide, 1, 5), (narrow, 1, 6))
    stages((last, 0, 2), (down, 0, 2), (wide, 0, 4), ("o", 0, 4), (down, 0, 3))
    stages((wide, 1, 6), (last, 0, 4), (down, 0, 4), (wide, 0, 5), ("o", 0, 5), (last, 0, 5), (down, 0, 5))
    stages((wide, 0, 6), ("o", 0, 6), (last, 0, 6), (down, 0, 6))


def run_backward(lengths, kept, store, cosine, sine):
    near = [kept["cotangent"], kept["stream"]] + [
        kept[name] for name in ("mid_0", "summed_0", "mid_1", "gain")
    ]
    near += [cosine, sine]
    away = [kept[name + layer] for layer in ("_0", "_1") for name in KEPT_NAMES]
    away += [store[key] for key in GATHERED[:-1]]
    shared, own = part_scratch()
    results = pl.pallas_call(
        backward_kernel,
        out_shape=[jax.ShapeDtypeStruct((128, 768), F32)]
        + [jax.ShapeDtypeStruct(*shape) for shape in SUMS.values()],
        in_specs=[SMEM] + [VMEM] * len(near) + [ANY] * len(away),
        out_specs=[VMEM] * (1 + len(SUMS)),
        scratch_shapes=[pltpu.VMEM(*KEPT_TYPES[name + "_0"]) for name in KEPT_NAMES]
        + [pltpu.VMEM(*WEIGHTS[name]) for name in WEIGHT_ORDER]
        + shared
        + own
        + [pltpu.VMEM(here, BF) for here, _ in SHARED.values()]
        + [pltpu.VMEM(there, BF) for _, there in SHARED.values()] * 2
        + [
            pltpu.VMEM((2, 32, 32, 128), BF),
            pltpu.VMEM((PAIRS, 32, 128), BF),
            pltpu.VMEM((32, MESSAGE, 128), BF),
            pltpu.VMEM((2, PAIRS, MESSAGE, 128), BF),
            pltpu.VMEM((64, LENGTH), BF),
            pltpu.VMEM((LENGTH, 128), F32),
            pltpu.VMEM((8, 768), F32),
            pltpu.VMEM((8, 768), F32),
            pltpu.VMEM((3, 128, 768), BF),
            pltpu.SemaphoreType.DMA((2 * len(PARTS), SCATTER_SEMAPHORES)),
            pltpu.SemaphoreType.DMA((2, len(SHARED) + 1, 2)),
            pltpu.SemaphoreType.DMA((9,)),
            pltpu.SemaphoreType.DMA((4, 3)),
        ],
        compiler_params=params(2),
        name="backward",
    )(lengths, *near, *away)
    return results[0], dict(zip(SUMS, results[1:]))


def angles(places):
    half_dim = HEAD_DIM // 2
    frequency = jnp.exp(-math.log(10000.0) * jnp.arange(half_dim).astype(F32) / half_dim)
    phases = places.astype(F32)[:, None] * frequency[None, :]
    cosine, sine = jnp.cos(phases), jnp.sin(phases)
    return (
        jnp.concatenate([cosine] * 4, axis=1),
        jnp.concatenate([-sine, sine] * 2, axis=1),
    )


def update(weight_matrix, moment, average, gradient, step_size):
    moment_new = MOMENTUM * moment + gradient
    weight_new = weight_matrix - step_size * (gradient + MOMENTUM * moment_new)
    return (moment_new, weight_new, AVERAGING * average + (1.0 - AVERAGING) * weight_new)


STEPPED = ("qkv", "out", "wide", "down")


def update_kernel(step_size, *refs):
    count = len(STEPPED)
    sources, refs = refs[: 4 * count + 2], refs[4 * count + 2 :]
    targets, refs = refs[: 3 * count + 2], refs[3 * count + 2 :]
    held, (loads, stores) = refs[:-2], refs[-2:]
    placed, held = held[-2:], held[:-2]
    fetches = [
        pltpu.make_async_copy(source, here, loads.at[at])
        for at, (source, here) in enumerate(zip(sources, held))
    ]
    for copy in fetches:
        copy.start()
    saves = []

    def save(here, at):
        copy = pltpu.make_async_copy(here, targets[at], stores.at[at])
        copy.start()
        saves.append(copy)

    for at in range(count):
        for copy in fetches[4 * at : 4 * at + 4]:
            copy.wait()
        gradient, weight_matrix, moment, average = held[4 * at : 4 * at + 4]
        stepped = update(weight_matrix[...], moment[...], average[...], gradient[...], step_size)
        for n, (here, value) in enumerate(zip((moment, weight_matrix, average), stepped)):
            here[...] = value
            save(here, 3 * at + n)
    for at in range(2):
        fetches[4 * count + at].wait()
        for slot in range(2):
            placed[at][:, slot, :] = held[4 * count + at][64 * slot : 64 * slot + 64]
        save(placed[at], 3 * count + at)
    for copy in saves:
        copy.wait()


def run_update(step_size, sums, states, activations):
    shapes = {name: jax.ShapeDtypeStruct(*SUMS[name]) for name in STEPPED}
    operands = []
    for name in STEPPED:
        operands += [sums[name], *states[name]]
    operands += activations
    by_place = jax.ShapeDtypeStruct((SPAN, 2, 768), F32)
    results = pl.pallas_call(
        functools.partial(update_kernel, step_size),
        out_shape=[shapes[name] for name in STEPPED for _ in range(3)] + [by_place] * 2,
        in_specs=[ANY] * len(operands),
        out_specs=[ANY] * (3 * len(STEPPED) + 2),
        scratch_shapes=[pltpu.VMEM(operand.shape, F32) for operand in operands]
        + [pltpu.VMEM((SPAN, 2, 768), F32)] * 2
        + [
            pltpu.SemaphoreType.DMA((len(operands),)),
            pltpu.SemaphoreType.DMA((3 * len(STEPPED) + 2,)),
        ],
        compiler_params=pltpu.CompilerParams(vmem_limit_bytes=VMEM_BYTES),
        name="step",
    )(*operands)
    return results[: 3 * len(STEPPED)], results[3 * len(STEPPED) :]


def on_device(
    inputs,
    cotangent,
    lengths,
    qkv_weight,
    qkv_moment,
    qkv_average,
    out_weight,
    out_moment,
    out_average,
    gate_up_weight,
    gate_up_moment,
    gate_up_average,
    down_weight,
    down_moment,
    down_average,
    norm_gains,
    gain_moment,
    gain_average,
):
    places = lax.axis_index(SEQ) * SPAN + jnp.arange(SPAN)
    cosine, sine = angles(places)
    seq = lax.axis_index(SEQ)
    own_gains = lax.dynamic_update_slice(
        jnp.zeros((8, 256), F32),
        norm_gains.astype(BF).astype(F32).reshape(4, 24),
        (0, lax.rem(24 * seq, 128)),
    )
    store, kept = run_forward(
        lengths[0],
        qkv_weight,
        out_weight,
        gate_up_weight,
        down_weight,
        own_gains,
        inputs[0],
        cotangent[0],
        cosine,
        sine,
    )
    input_grad, sums = run_backward(
        lengths[0], kept, store, cosine, sine
    )
    gain_sum = lax.dynamic_slice(
        sums["gain"][0], (0, lax.rem(24 * seq, 128)), (4, 24)
    ).reshape(2, 2, 24)

    step_size = STEP_RATE / math.sqrt(
        lax.axis_size(BATCH) * SPAN * lax.axis_size(SEQ) * 2
    )
    stepped, (result, input_grad) = run_update(
        step_size,
        sums,
        {
            "qkv": (qkv_weight, qkv_moment, qkv_average),
            "out": (out_weight, out_moment, out_average),
            "wide": (gate_up_weight, gate_up_moment, gate_up_average),
            "down": (down_weight, down_moment, down_average),
        },
        [kept["result"], input_grad],
    )
    gain_new = update(norm_gains, gain_moment, gain_average, gain_sum, step_size)
    return (result[None], input_grad[None], *stepped, *gain_new)


def solution(mesh):
    rows = P(BATCH, SEQ, None, None)
    wide = P(None, None, SEQ, None)
    flat = P(None, SEQ, None)
    gains = P(None, None, SEQ)
    state = (wide,) * 3 + (flat,) * 3 + (wide,) * 3 + (flat,) * 3 + (gains,) * 3
    return jax.shard_map(
        on_device,
        mesh=mesh,
        in_specs=(rows, rows, P(BATCH, None)) + state,
        out_specs=(rows, rows) + state,
        check_vma=False,
    )
```

```python
import functools
import math

import jax
import jax.numpy as jnp
from jax import lax
from jax.experimental import pallas as pl
from jax.experimental.pallas import tpu as pltpu
from jax.sharding import PartitionSpec as P

MESH = pl.DeviceIdType.MESH
BF = jnp.bfloat16
F32 = jnp.float32
BATCH, SEQ = "batch", "seq"
HEAD_DIM = 64
HEADS = 12
PAIRS = 24
SPAN = 64
LENGTH = 2048
BLOCK = 256
EPSILON = 1e-06
MOMENTUM = 0.5
AVERAGING = 0.5
STEP_RATE = 0.1
MASKED = -1e30
VMEM_BYTES = 62 * 2**20
VMEM = pl.BlockSpec(memory_space=pltpu.VMEM)
ANY = pl.BlockSpec(memory_space=pl.ANY)
SMEM = pl.BlockSpec(memory_space=pltpu.SMEM)
ALL = pl.ds(0, 4)


def params(collective_id):
    return pltpu.CompilerParams(
        collective_id=collective_id, has_side_effects=True, vmem_limit_bytes=VMEM_BYTES
    )


def coordinates():
    seq = lax.axis_index(SEQ)
    return (
        lax.axis_index(BATCH),
        lax.div(seq, 8),
        lax.rem(lax.div(seq, 2), 4),
        lax.rem(seq, 2),
    )


def device(x, z, y, core):
    return (x, (z * 4 + y) * 2 + core)


def shifted(value, by):
    return lax.rem(value + by, 4)


def signal(partners):
    barrier = pltpu.get_barrier_semaphore()
    for partner in partners:
        pl.semaphore_signal(barrier, inc=1, device_id=partner, device_id_type=MESH)


def greet(partners):
    signal(partners)
    pl.semaphore_wait(pltpu.get_barrier_semaphore(), len(partners))


def remote(source, target, send, receive, where):
    return pltpu.make_async_remote_copy(
        src_ref=source,
        dst_ref=target,
        send_sem=send,
        recv_sem=receive,
        device_id=where,
        device_id_type=MESH,
    )


class Axes:
    def __init__(self, first_is_y):
        x, z, y, core = coordinates()
        self.first_is_y = first_is_y
        self.x, self.z, self.y, self.core = x, z, y, core
        self.m1, self.m2 = (y, z) if first_is_y else (z, y)
        self.partner = device(x, z, y, 1 - core)

    def along_y(self, by):
        return device(self.x, self.z, shifted(self.y, by), self.core)

    def along_z(self, by):
        return device(self.x, shifted(self.z, by), self.y, self.core)

    def first(self, by):
        return self.along_y(by) if self.first_is_y else self.along_z(by)

    def second(self, by):
        return self.along_z(by) if self.first_is_y else self.along_y(by)

    def order(self, i1, i2):
        return (i2, i1) if self.first_is_y else (i1, i2)


class GatherSegment:
    def __init__(self, first_is_y, view, semaphores, own=None):
        self.axes = Axes(first_is_y)
        self.view, self.own, self.semaphores = view, own, semaphores

    def block(self, i1, i2):
        return self.view(*self.axes.order(i1, i2))

    def row(self, by, part=ALL):
        return self.block(part, shifted(self.axes.m2, by))

    def keep(self):
        here = self.block(self.axes.m1, self.axes.m2)
        return pltpu.make_async_copy(self.own, here, self.semaphores.at[3, 0])

    def begin(self, phase):
        axes = self.axes
        sem = [self.semaphores.at[phase, at] for at in range(4)]

        def send(part, where):
            remote(part, part, sem[0], sem[1], where).start()

        def share(part):
            remote(part, part, sem[2], sem[3], axes.partner).start()

        if phase == 0:
            here = self.block(axes.m1, axes.m2)
            source = here if self.own is None else self.own
            for by in (1, 3, 2):
                remote(source, here, sem[0], sem[1], axes.first(by)).start()
        elif phase == 1:
            send(self.row(0), axes.second(1))
            send(self.row(0), axes.second(3))
            share(self.row(0))
        elif phase == 2:
            send(self.row(3, pl.ds(0, 2)), axes.second(1))
            send(self.row(1, pl.ds(2, 2)), axes.second(3))
            share(self.row(3))
            share(self.row(1))
        else:
            share(self.row(2))

    def end(self, phase):
        axes = self.axes
        sem = [self.semaphores.at[phase, at] for at in range(4)]
        one, two = self.row(0), self.block(ALL, pl.ds(0, 2))
        moved = (self.block(pl.ds(0, 3), axes.m2), two, one, None)[phase]
        shared = (None, one, two, one)[phase]
        if moved is not None:
            remote(moved, moved, sem[0], sem[1], axes.partner).wait()
        if shared is not None:
            remote(shared, shared, sem[2], sem[3], axes.partner).wait()


class AcrossSegment(GatherSegment):
    def __init__(self, first_is_y, quarters, semaphores, own):
        x = lax.axis_index(BATCH)
        super().__init__(first_is_y, lambda z, y: quarters(z, y, x, 1), semaphores, own)
        self.quarters = quarters

    def begin(self, phase):
        axes = self.axes
        sem = [self.semaphores.at[phase, at] for at in range(4)]

        def send(part, where):
            remote(part, part, sem[0], sem[1], where).start()

        def share(part):
            remote(part, part, sem[2], sem[3], axes.partner).start()

        if phase == 0:
            here = self.block(axes.m1, axes.m2)
            for by in (1, 3, 2):
                remote(self.own, here, sem[0], sem[1], axes.first(by)).start()
        elif phase == 1:
            send(self.row(0), axes.second(1))
            send(self.row(0), axes.second(3))
        elif phase == 2:
            send(self.row(3, pl.ds(0, 2)), axes.second(1))
            send(self.row(1, pl.ds(2, 2)), axes.second(3))
        elif phase == 3:
            mine = self.block(ALL, ALL)
            for by in (1, 3):
                send(mine, self.plane(by))
            far = [self.semaphores.at[4, at] for at in range(2)]
            remote(mine, mine, far[0], far[1], self.plane(2)).start()
            share(mine)
        elif phase == 4:
            for by in (1, 3):
                share(self.quarters(ALL, ALL, shifted(axes.x, by), 1))
        else:
            self.last_share().start()

    def plane(self, by):
        axes = self.axes
        return device(shifted(axes.x, by), axes.z, axes.y, axes.core)

    def last_share(self):
        part = self.quarters(ALL, ALL, shifted(self.axes.x, 2), 1)
        sem = [self.semaphores.at[2, at] for at in (2, 3)]
        return remote(part, part, sem[0], sem[1], self.axes.partner)

    def end(self, phase):
        axes = self.axes
        if phase == 5:
            self.last_share().wait()
            return
        sem = [self.semaphores.at[phase, at] for at in range(4)]
        two = self.quarters(ALL, ALL, 0, 2)
        mine = self.block(ALL, ALL)
        moved = (
            self.block(pl.ds(0, 3), axes.m2),
            self.block(ALL, pl.ds(0, 2)),
            self.row(0),
            two,
            mine,
        )[phase]
        shared = (None, None, None, mine, two)[phase]
        remote(moved, moved, sem[0], sem[1], axes.partner).wait()
        if shared is not None:
            remote(shared, shared, sem[2], sem[3], axes.partner).wait()


def across_views(name, ref):
    core = Axes(True).core

    def columns(first, count):
        return pl.ds(pl.multiple_of(core * 1024 + first * 256, 128), 256 * count)

    def rows(first, count):
        return pl.ds(pl.multiple_of(first * 16, 16), 16 * count)

    if name == "wide":
        return [
            (True, lambda z, y, first, count: ref.at[0, z, y, :, columns(first, count)]),
            (False, lambda z, y, first, count: ref.at[1, z, y, :, columns(first, count)]),
        ]
    return [
        (True, lambda z, y, first, count: ref.at[z, y, core, rows(first, count), pl.ds(0, 384)]),
        (False, lambda z, y, first, count: ref.at[z, y, core, rows(first, count), pl.ds(384, 384)]),
    ]


def across_owns(name, ref):
    axes = Axes(True)
    if name == "wide":
        columns = pl.ds(pl.multiple_of(axes.core * 1024 + axes.x * 256, 128), 256)
        return [ref.at[0, :, columns], ref.at[1, :, columns]]
    rows = pl.ds(pl.multiple_of(axes.x * 16, 16), 16)
    return [ref.at[rows, pl.ds(0, 384)], ref.at[rows, pl.ds(384, 384)]]


ACROSS = (("wide", 1), ("down", 0))


def halves(core, width):
    return pl.ds(pl.multiple_of(core * (width // 2), 128), width // 2)


def weight_views(name, ref):
    core = Axes(True).core
    narrow, wide = halves(core, 768), halves(core, 2048)
    if name == "qkv":
        return [
            (True, lambda z, y: ref.at[pl.ds(0, 2), z, y, :, narrow]),
            (False, lambda z, y: ref.at[2, z, y, :, narrow]),
        ]
    if name == "out":
        return [(False, lambda z, y: ref.at[z, y, :, narrow])]
    if name == "wide":
        return [
            (True, lambda z, y: ref.at[0, z, y, :, wide]),
            (False, lambda z, y: ref.at[1, z, y, :, wide]),
        ]
    if name == "down":
        return [
            (True, lambda z, y: ref.at[z, y, core, :, pl.ds(0, 384)]),
            (False, lambda z, y: ref.at[z, y, core, :, pl.ds(384, 384)]),
        ]
    return [(True, lambda z, y: ref.at[z, y, core])]


def own_views(name, ref):
    core = Axes(True).core
    narrow, wide = halves(core, 768), halves(core, 2048)
    if name == "qkv":
        return [ref.at[pl.ds(0, 2), :, narrow], ref.at[2, :, narrow]]
    if name == "out":
        return [ref.at[:, narrow]]
    if name == "wide":
        return [ref.at[0, :, wide], ref.at[1, :, wide]]
    if name == "down":
        return [ref.at[:, pl.ds(0, 384)], ref.at[:, pl.ds(384, 384)]]
    return [ref]


WEIGHTS = {
    "qkv": ((3, 4, 4, 48, 768), BF),
    "out": ((4, 4, 48, 768), BF),
    "wide": ((2, 4, 4, 48, 2048), BF),
    "down": ((4, 4, 2, 64, 768), BF),
    "gain": ((4, 4, 2, 8, 256), F32),
}
SEGMENTS = {"qkv": 2, "out": 1, "wide": 2, "down": 2, "gain": 1}
GATHERED = [(name, layer) for layer in range(2) for name in ("qkv", "out", "wide", "down")] + [
    ("gain", 0)
]


def weight_shape(key):
    return jax.ShapeDtypeStruct(*WEIGHTS[key[0]])


class ScatterPart:
    def __init__(self, first_is_y, total, rows, ring, blocks, groups, semaphores, finish):
        self.axes = Axes(first_is_y)
        self.total, self.rows, self.ring, self.blocks, self.groups = total, rows, ring, blocks, groups
        self.semaphores, self.finish = semaphores, finish

    def fill(self, z, value):
        if self.axes.first_is_y:
            self.total[z] = value
        else:
            self.total[:, z] = value

    def spread(self):
        axes, sem = self.axes, self.semaphores
        for by in (1, 3, 2):
            remote(
                self.total.at[axes.m2, shifted(axes.m1, by)],
                self.blocks.at[by - 1],
                sem.at[4],
                sem.at[5],
                axes.first(by),
            ).start()

    def stage(self, number):
        axes, sem, total = self.axes, self.semaphores, self.total
        m1, m2 = axes.m1, axes.m2
        before, after, across = shifted(m2, 3), shifted(m2, 1), shifted(m2, 2)
        low, high = pl.ds(0, 2), pl.ds(2, 2)

        def add(target, source):
            target[...] = (target[...].astype(F32) + source[...].astype(F32)).astype(target.dtype)

        if number == 1:
            remote(
                total.at[across, low], self.ring.at[0], sem.at[0], sem.at[1], axes.second(1)
            ).start()
            remote(
                total.at[across, high], self.ring.at[1], sem.at[0], sem.at[1], axes.second(3)
            ).start()
        elif number == 2:
            row = total.at[m2]
            remote(row, self.ring, sem.at[0], sem.at[1], axes.partner).wait()
            add(total.at[after, low], self.ring.at[0])
            add(total.at[before, high], self.ring.at[1])
            remote(
                total.at[after], self.rows.at[0], sem.at[2], sem.at[3], axes.second(1)
            ).start()
            remote(
                total.at[before], self.rows.at[1], sem.at[2], sem.at[3], axes.second(3)
            ).start()
        elif number == 3:
            remote(self.rows, self.rows, sem.at[2], sem.at[3], axes.partner).wait()
            for at in range(4):
                total[m2, at] = (
                    total[m2, at].astype(F32)
                    + self.rows[0, at].astype(F32)
                    + self.rows[1, at].astype(F32)
                ).astype(total.dtype)
            self.spread()
        elif number == 4:
            remote(self.blocks, self.blocks, sem.at[4], sem.at[5], axes.partner).wait()
            self.groups[axes.x] = (
                total[m2, m1].astype(F32)
                + self.blocks[0].astype(F32)
                + self.blocks[1].astype(F32)
                + self.blocks[2].astype(F32)
            ).astype(total.dtype)
            mine = self.groups.at[axes.x]
            for by in (1, 3, 2):
                remote(
                    mine,
                    mine,
                    sem.at[6],
                    sem.at[7],
                    device(shifted(axes.x, by), axes.z, axes.y, axes.core),
                ).start()
        elif number == 5:
            three = self.groups.at[pl.ds(0, 3)]
            remote(three, three, sem.at[6], sem.at[7], axes.partner).wait()
            summed = self.groups[0].astype(F32)
            for at in range(1, 4):
                summed = summed + self.groups[at].astype(F32)
            self.finish(0, summed)
        else:
            self.finish(1, None)


class AcrossPart(ScatterPart):
    def __init__(self, first_is_y, whole, quarter, came, rows, ring, blocks, groups, semaphores, finish):
        super().__init__(first_is_y, quarter, rows, ring, blocks, groups, semaphores, finish)
        self.whole, self.came = whole, came
        self.by_rows = whole.shape[2] == 64

    def fill(self, z, value):
        if self.axes.first_is_y:
            self.whole[z] = value
        else:
            self.whole[:, z] = value

    def quarter(self, at):
        if self.by_rows:
            return pl.ds(pl.multiple_of(at * 16, 16), 16), slice(None)
        return slice(None), pl.ds(pl.multiple_of(at * 256, 128), 256)

    def stage(self, number):
        axes, sem = self.axes, self.semaphores
        if number == 0:
            for by in (1, 3, 2):
                there = shifted(axes.x, by)
                remote(
                    self.whole.at[(slice(None), slice(None)) + self.quarter(there)],
                    self.came.at[by - 1],
                    sem.at[10],
                    sem.at[11],
                    device(there, axes.z, axes.y, axes.core),
                ).start()
            return
        if number == 1:
            remote(self.came, self.came, sem.at[10], sem.at[11], axes.partner).wait()
            for at in range(4):
                summed = self.whole[(at, slice(None)) + self.quarter(axes.x)].astype(F32)
                for by in range(3):
                    summed = summed + self.came[by, at].astype(F32)
                self.total[at] = summed.astype(BF)
        if number == 5:
            three = self.groups.at[pl.ds(0, 3)]
            remote(three, three, sem.at[6], sem.at[7], axes.partner).wait()
            quarters = [self.groups[at].astype(F32) for at in range(4)]
            self.finish(0, jnp.concatenate(quarters, axis=0 if self.by_rows else 1))
            return
        super().stage(number)


class StraightPart(ScatterPart):
    def stage(self, number):
        axes, sem = self.axes, self.semaphores
        m2 = axes.m2
        if number == 1:
            for by in (1, 3, 2):
                remote(
                    self.total.at[shifted(m2, by)],
                    self.rows.at[by - 1],
                    sem.at[2],
                    sem.at[3],
                    axes.second(by),
                ).start()
        elif number == 2:
            remote(self.rows, self.rows, sem.at[2], sem.at[3], axes.partner).wait()
            for at in range(4):
                summed = self.total[m2, at].astype(F32)
                for by in range(3):
                    summed = summed + self.rows[by, at].astype(F32)
                self.total[m2, at] = summed.astype(self.total.dtype)
            self.spread()
        elif number != 3:
            super().stage(number)


SCATTER_SEMAPHORES = 12
ACROSS_PARTS = (("left", 0), ("right", 0), ("gate", 1), ("up", 1))
LAST_PARTS = (("q", 0), ("k", 0), ("v", 0), ("gain", 0))
PARTS = {
    "gate": (True, 48, 1024, BF),
    "up": (False, 48, 1024, BF),
    "left": (True, 64, 384, BF),
    "right": (False, 64, 384, BF),
    "o": (False, 48, 384, BF),
    "q": (True, 48, 384, BF),
    "k": (False, 48, 384, BF),
    "v": (True, 48, 384, BF),
    "gain": (False, 8, 256, F32),
}
SOURCE = {
    "q": "qkv", "k": "qkv", "v": "qkv", "o": "out", "gate": "wide", "up": "wide",
    "left": "down", "right": "down", "gain": "gain",
}
SUMS = {
    "qkv": ((2, 3, 24, 768), F32),
    "out": ((2, 24, 768), F32),
    "wide": ((2, 2, 24, 2048), F32),
    "down": ((2, 64, 768), F32),
    "gain": ((1, 8, 256), F32),
}
LEFT, RIGHT = pl.ds(0, 384), pl.ds(384, 384)


def part_target(part, ref):
    if part in ("q", "k", "v"):
        return ref.at["qkv".index(part)]
    if part in ("gate", "up"):
        return ref.at[int(part == "up")]
    if part in ("left", "right"):
        return ref.at[:, LEFT if part == "left" else RIGHT]
    return ref


def rows_swapped(target, mine, theirs, sem):
    axes = Axes(True)
    core = axes.core

    def finish(part, summed):
        own_rows = pl.ds(pl.multiple_of(core * 24, 8), 24)
        other_rows = pl.ds(pl.multiple_of((1 - core) * 24, 8), 24)
        copy = remote(mine.at[other_rows, :], theirs, sem.at[8], sem.at[9], axes.partner)
        if part == 0:
            mine[...] = summed
            copy.start()
        else:
            copy.wait()
            kept = mine[own_rows, :]
            got = theirs[...]
            width = kept.shape[-1]
            target[:, :width] = jnp.where(core == 0, kept, got)
            target[:, width:] = jnp.where(core == 0, got, kept)

    return finish


def direct(target):
    def finish(part, summed):
        if part == 0:
            target[...] = summed

    return finish


def part_scratch():
    shared, own = [], []
    for part, (_, rows, width, kind) in PARTS.items():
        shared += [
            pltpu.VMEM((4, 4, rows, width), kind),
            pltpu.VMEM((8, 128) if part == "gain" else (2, 4, rows, width), kind),
            pltpu.VMEM((48, width), F32) if rows == 48 else pltpu.VMEM((8, 128), F32),
        ]
        for layer in range(1 if part == "gain" else 2):
            across = (part, layer) in ACROSS_PARTS
            block = (rows, width)
            if across:
                block = (16, width) if rows == 64 else (rows, width // 4)
                own += [
                    pltpu.VMEM((4, 4) + block, kind),
                    pltpu.VMEM((3, 4, 4) + block, kind),
                    pltpu.VMEM((2, 4) + block, kind),
                ]
            straight = (part, layer) in LAST_PARTS
            own += [
                pltpu.VMEM(((3, 4) if straight else (2, 2)) + block, kind),
                pltpu.VMEM((3,) + block, kind),
                pltpu.VMEM((4,) + block, kind),
                pltpu.VMEM((24, width), F32) if rows == 48 else pltpu.VMEM((8, 128), F32),
            ]
    return shared, own


def build_parts(shared, own, sems, sums):
    parts = {}
    count = 0
    own = list(own)

    def take(number):
        taken = own[:number]
        del own[:number]
        return taken

    for at, (part, (first_is_y, rows, _, _)) in enumerate(PARTS.items()):
        total, rows_in, mine = shared[3 * at : 3 * at + 3]
        for layer in (0,) if part == "gain" else (0, 1):
            if (part, layer) in ACROSS_PARTS:
                quarter, came, rows_here = take(3)
            ring, blocks, groups, theirs = take(4)
            target = part_target(part, sums[SOURCE[part]].at[layer])
            sem = sems.at[count]
            finish = rows_swapped(target, mine, theirs, sem) if rows == 48 else direct(target)
            if (part, layer) in ACROSS_PARTS:
                parts[part, layer] = AcrossPart(
                    first_is_y, total, quarter, came, rows_here, ring, blocks, groups, sem, finish
                )
            elif (part, layer) in LAST_PARTS:
                parts[part, layer] = StraightPart(
                    first_is_y, total, ring, None, blocks, groups, sem, finish
                )
            else:
                parts[part, layer] = ScatterPart(
                    first_is_y, total, rows_in, ring, blocks, groups, sem, finish
                )
            count += 1
    return parts


def pair_device(pair):
    if pair < 16:
        return 2 * pair
    z = (pair - 16) // 2
    return 2 * (4 * z + 2 * ((pair - 16) % 2) + z % 2) + 1


def own_pair():
    _, z, y, core = coordinates()
    has_pair = (core == 0) | (lax.rem(z + y, 2) == 0)
    pair = jnp.where(core == 0, 4 * z + y, 16 + 2 * z + lax.div(y, 2))
    return has_pair, pair


def lanes(shape):
    return lax.broadcasted_iota(jnp.int32, shape, len(shape) - 1)


def turned(values, cosine, sine):
    here = lax.rem(lanes(values.shape), 64) < 32
    width = values.shape[-1]
    other = jnp.where(here, pltpu.roll(values, width - 32, 1), pltpu.roll(values, 32, 1))
    return values * cosine + other * sine


def twice(table):
    return jnp.concatenate([table, table], axis=0)


def allowed_keys(first_key, first_query, keys, queries, length):
    key = first_key + lax.broadcasted_iota(jnp.int32, (keys, queries), 0)
    query = first_query + lax.broadcasted_iota(jnp.int32, (keys, queries), 1)
    return (key <= query) & (key < length)


def slot_length(lengths, pair):
    return jnp.where(pair < HEADS, lengths[0], lengths[1])


LAST_DIMS = (((1,), (1,)), ((), ()))
BLOCKS = LENGTH // BLOCK
MESSAGE = 96


def front_lanes(rows):
    return lanes((rows, 128)) < 64


def pack_heads(both):
    front = front_lanes(32)
    top, bottom = both[0:32], both[32:64]
    return (
        jnp.where(front, top, pltpu.roll(bottom, 64, 1)).astype(BF),
        jnp.where(front, pltpu.roll(top, 64, 1), bottom).astype(BF),
    )


def unpack_heads(first, second):
    front = front_lanes(32)
    first, second = first.astype(F32), second.astype(F32)
    return jnp.concatenate(
        [
            jnp.where(front, first, pltpu.roll(second, 64, 1)),
            jnp.where(front, pltpu.roll(first, 64, 1), second),
        ],
        axis=0,
    )


def unpack_block(packed, to_front):
    packed = packed.astype(F32).reshape(128, 128)
    other = pltpu.roll(packed, 64, 1)
    front = front_lanes(128)
    if to_front:
        top, bottom = jnp.where(front, packed, 0.0), jnp.where(front, other, 0.0)
    else:
        top, bottom = jnp.where(front, 0.0, other), jnp.where(front, 0.0, packed)
    joined = jnp.concatenate([top.reshape(4, 32, 128), bottom.reshape(4, 32, 128)], axis=1)
    return joined.reshape(256, 128).astype(BF)


def pack_turned(turned_values):
    rows = jnp.concatenate([turned_values, turned_values], axis=0).T.reshape(4, 64, 128)
    front = lanes((4, 32, 128)) < 64
    return jnp.where(front, rows[:, 0:32], rows[:, 32:64]).astype(BF)


class Exchange:
    def __init__(self, semaphores):
        self.x, self.me = lax.axis_index(BATCH), lax.axis_index(SEQ)
        self.has_pair, self.pair = own_pair()
        self.send, self.receive, self.local = (semaphores.at[at] for at in range(3))

    def to(self, there, source, target):
        @pl.when(self.me != there)
        def _():
            remote(source, target, self.send, self.receive, (self.x, there)).start()

        @pl.when(self.me == there)
        def _():
            pltpu.make_async_copy(source, target, self.local).start()

    def wait(self, sent, got, where):
        if where == "pairs":
            sends, gets = (sent.shape[0], sent.shape[0] - 1), (None, got.shape[0] - 1)
        else:
            sends, gets = (None, sent.shape[0] - 1), (got.shape[0], got.shape[0] - 1)

        def wait_for(n_sent, n_got):
            if n_got is not None:
                part = got.at[pl.ds(0, n_got)]
                remote(part, part, self.send, self.receive, (self.x, self.me)).wait_recv()
            if n_sent is not None:
                part = sent.at[pl.ds(0, n_sent)]
                remote(part, part, self.send, self.receive, (self.x, self.me)).wait_send()

        @pl.when(self.has_pair)
        def _():
            pltpu.make_async_copy(sent.at[0], got.at[0], self.local).wait()
            wait_for(sends[1], gets[1])

        @pl.when(jnp.logical_not(self.has_pair))
        def _():
            wait_for(sends[0], gets[0])


def send_projections(exchange, query, key, value, cosine, sine, outgoing, rows):
    cosine, sine = twice(cosine), twice(sine)
    front = front_lanes(64)
    for tile in range(6):
        cut = slice(128 * tile, 128 * tile + 128)
        q = turned(query[:, cut], cosine, sine) * (1.0 / math.sqrt(HEAD_DIM))
        k = turned(key[:, cut], cosine, sine)
        v = value[:, cut]
        for slot in range(2):
            span = slice(64 * slot, 64 * slot + 64)
            at = slot * HEADS + 2 * tile
            ks, vs = k[span], v[span]
            outgoing[at, 0:64] = jnp.where(front, ks, pltpu.roll(vs, 64, 1)).astype(BF)
            outgoing[at + 1, 0:64] = jnp.where(front, pltpu.roll(ks, 64, 1), vs).astype(BF)
            outgoing[at, 64:96], outgoing[at + 1, 64:96] = pack_heads(q[span])
            for pair in (at, at + 1):
                exchange.to(pair_device(pair), outgoing.at[pair], rows.at[exchange.me])


def attend_block(exchange, at, length, rows, values_turned, out_turned, log_total, outgoing, incoming):
    count = (at + 1) * BLOCK
    queries = unpack_block(rows[4 * at : 4 * at + 4, 64:96], True)
    keys = rows[0 : 4 * at + 4, 0:64].reshape(count, 128)
    scores = lax.dot_general(keys, queries, LAST_DIMS, preferred_element_type=F32)
    scores = jnp.where(allowed_keys(0, at * BLOCK, count, BLOCK, length), scores, MASKED)
    highest = jnp.max(scores, axis=0, keepdims=True)
    raised = jnp.exp(scores - highest)
    total = jnp.sum(raised, axis=0, keepdims=True)
    result = (
        jnp.dot(values_turned[:, 0:count], raised.astype(BF), preferred_element_type=F32) / total
    )
    cut = slice(at * BLOCK, count)
    out_turned[:, cut] = result
    log_total[:, cut] = jnp.broadcast_to(highest + jnp.log(total), (8, BLOCK))
    outgoing[4 * at : 4 * at + 4] = pack_turned(result)
    for there in range(4 * at, 4 * at + 4):
        exchange.to(there, outgoing.at[there], incoming.at[exchange.pair])


def merge_heads(incoming, merged):
    for slot in range(2):
        for tile in range(6):
            at = slot * HEADS + 2 * tile
            merged[64 * slot : 64 * slot + 64, 128 * tile : 128 * tile + 128] = unpack_heads(
                incoming[at], incoming[at + 1]
            ).astype(BF)


def norm_forward(values, norm_gain):
    inverse = lax.rsqrt(jnp.mean(values * values, axis=-1, keepdims=True) + EPSILON)
    return (values * inverse * norm_gain, inverse)


def feed_forward(rows_in, gate_up, down, paired):
    fed = jnp.zeros((128, 768), F32)
    for z in range(4):
        cut = slice(512 * z, 512 * z + 512)
        gate = jnp.dot(rows_in, gate_up[0, :, :, :, cut].reshape(768, 512), preferred_element_type=F32)
        up = jnp.dot(rows_in, gate_up[1, :, :, :, cut].reshape(768, 512), preferred_element_type=F32)
        paired[0, :, cut] = gate
        paired[1, :, cut] = up
        hidden = (jax.nn.silu(gate) * up).astype(BF)
        fed = fed + jnp.dot(hidden, down[z].reshape(512, 768), preferred_element_type=F32)
    return fed


KEPT = (
    [("result", (128, 768), F32), ("mid_0", (128, 768), F32), ("summed_0", (128, 768), F32)]
    + [("mid_1", (128, 768), F32), ("gain", (8, 768), F32)]
    + [("stream", (128, 768), BF), ("cotangent", (128, 768), F32)]
    + [
        (name + "_" + layer, shape, kind)
        for layer in "01"
        for name, shape, kind in (
            ("paired", (2, 128, 2048), F32),
            ("rows", (32, MESSAGE, 128), BF),
            ("merged", (128, 768), BF),
            ("turned", (64, LENGTH), F32),
            ("total", (8, LENGTH), F32),
        )
    ]
)


def forward_kernel(
    lengths, qkv, out, gate_up, down, gains, inputs, cotangents, cosine, sine, *refs
):
    stored = dict(zip(GATHERED[:-1], refs[:8]))
    kept = {name: ref for (name, _, _), ref in zip(KEPT, refs[8:])}
    refs = refs[8 + len(KEPT) :]
    store, refs = dict(zip(GATHERED, refs[:9])), refs[9:]
    their_qkv, their_out, their_gate_up, b_qkv, b_out, b_gate_up, b_down = refs[:7]
    outgoing, places, incoming, values_turned, stream, swap, sems, local, pair_sems = refs[7:]
    axes = Axes(True)
    core = axes.core
    x, me = lax.axis_index(BATCH), lax.axis_index(SEQ)
    greet(
        [(x, lax.rem(me + by, 32)) for by in range(1, 32)]
        + [device(shifted(x, by), axes.z, axes.y, core) for by in (1, 2, 3)]
    )
    swaps = [
        remote(mine, theirs, swap.at[0, at], swap.at[1, at], axes.partner)
        for at, (mine, theirs) in enumerate(
            (
                (qkv.at[0], their_qkv.at[0]),
                (qkv.at[1], their_qkv.at[1]),
                (out, their_out),
                (gate_up, their_gate_up),
            )
        )
    ]
    for copy in swaps:
        copy.start()
    for slot in range(2):
        stream[64 * slot : 64 * slot + 64] = inputs[:, slot, :]
        kept["cotangent"][64 * slot : 64 * slot + 64] = cotangents[:, slot, :]
    kept["stream"][...] = stream[...].astype(BF)

    def joined(mine, theirs):
        upper = jnp.where(core == 0, mine, theirs)
        lower = jnp.where(core == 0, theirs, mine)
        return jnp.concatenate([upper, lower], axis=0).astype(BF)

    segments = {}
    at = 0
    for key in GATHERED:
        name, layer = key
        block = {"qkv": b_qkv, "out": b_out, "wide": b_gate_up, "down": b_down}.get(name)
        block = gains if block is None else block.at[layer]
        kind, views, owns = GatherSegment, weight_views, own_views
        if key in ACROSS:
            kind, views, owns = AcrossSegment, across_views, across_owns
        segments[key] = []
        for (first_is_y, view), own in zip(views(name, store[key]), owns(name, block)):
            segments[key].append(kind(first_is_y, view, sems.at[at], own))
            at += 1

    def each(keys, act):
        for key in keys:
            for segment in segments[key]:
                act(segment)

    def keep(*keys):
        each(keys, lambda segment: segment.keep().start())
        each(keys, lambda segment: segment.keep().wait())

    def begin(phase, *keys):
        each(keys, lambda segment: segment.begin(phase))

    def end(phase, *keys):
        each(keys, lambda segment: segment.end(phase))

    saves = []

    def save(*keys):
        for key in keys:
            copy = pltpu.make_async_copy(store[key], stored[key], local.at[len(saves)])
            copy.start()
            saves.append(copy)

    qkv_0, out_0, wide_0, down_0 = GATHERED[0:4]
    qkv_1, out_1, wide_1, down_1 = GATHERED[4:8]
    gains_0 = GATHERED[8]

    swaps[0].wait()
    for at in range(3):
        b_qkv[0, at] = joined(qkv[0, at], their_qkv[0, at])
    begin(0, qkv_0)
    keep(qkv_0)
    b_down[0] = down[0].astype(BF)
    begin(0, down_0)
    keep(down_0)
    for copy in swaps[1:]:
        copy.wait()
    for at in range(2):
        b_gate_up[0, at] = joined(gate_up[0, at], their_gate_up[0, at])
    begin(0, wide_0)
    keep(wide_0)
    end(0, qkv_0)
    begin(1, qkv_0)
    end(0, down_0)
    begin(1, down_0)
    b_out[0] = joined(out[0], their_out[0])
    for at in range(2):
        b_gate_up[1, at] = joined(gate_up[1, at], their_gate_up[1, at])
    begin(0, out_0, gains_0, wide_1)
    keep(out_0, gains_0, wide_1)
    for at in range(3):
        b_qkv[1, at] = joined(qkv[1, at], their_qkv[1, at])
    b_out[1] = joined(out[1], their_out[1])
    b_down[1] = down[1].astype(BF)
    end(1, qkv_0)
    begin(2, qkv_0)
    end(1, down_0)
    begin(2, down_0)
    end(0, wide_0)
    begin(1, wide_0)
    end(2, qkv_0)
    begin(3, qkv_0)
    keep(qkv_1, out_1, down_1)
    begin(0, qkv_1)
    end(2, down_0)
    begin(3, down_0)
    end(0, out_0, gains_0, wide_1)
    begin(1, wide_1)
    end(3, qkv_0)
    save(qkv_0)

    def attention(layer, source, before, between):
        weights = store["qkv", layer]
        name = "_" + str(layer)
        rows, merged = kept["rows" + name], kept["merged" + name]
        there = Exchange(pair_sems.at[2 * layer])
        back = Exchange(pair_sems.at[2 * layer + 1])
        low = source.astype(BF)
        query, key, value = (
            jnp.dot(low, weights[at].reshape(768, 768), preferred_element_type=F32)
            for at in range(3)
        )
        send_projections(
            there, query, key, value, cosine[...], sine[...], outgoing.at[layer], rows
        )
        before()
        there.wait(outgoing.at[layer], rows, "pairs")
        length = slot_length(lengths, there.pair)

        @pl.when(there.has_pair)
        def _():
            all_rows = rows[:, 0:64].reshape(LENGTH, 128).astype(F32)
            values_turned[...] = all_rows.T[64:128].astype(BF)

        for at in range(BLOCKS):

            @pl.when(there.has_pair)
            def _(at=at):
                attend_block(
                    back,
                    at,
                    length,
                    rows,
                    values_turned,
                    kept["turned" + name],
                    kept["total" + name],
                    places.at[layer],
                    incoming.at[layer],
                )

            if at in between:
                between[at]()
        back.wait(places.at[layer], incoming.at[layer], "places")
        merge_heads(incoming.at[layer], merged)
        between["after"]()
        out_matrix = store["out", layer][...].reshape(768, 768)
        return jnp.dot(merged[...], out_matrix, preferred_element_type=F32)

    def before_0():
        begin(1, out_0, gains_0)
        end(1, wide_1)
        begin(2, wide_1)
        end(0, qkv_1)
        begin(1, qkv_1)

    def within_0():
        end(1, wide_0)
        begin(2, wide_0)
        end(2, wide_1)
        begin(3, wide_1)

    def later_0():
        end(1, out_0, gains_0)
        begin(2, out_0, gains_0)

    def last_0():
        end(1, qkv_1)
        begin(2, qkv_1)
        end(3, down_0)
        begin(4, down_0)

    def after_0():
        end(4, down_0)
        begin(5, down_0)
        end(2, wide_0, out_0, gains_0)
        begin(3, out_0, wide_0, gains_0)
        begin(0, out_1, down_1)
        end(3, out_0, wide_0, gains_0)
        end(5, down_0)
        save(out_0, wide_0, down_0)
        for device_at in range(32):
            piece = store[gains_0][device_at // 8, device_at // 2 % 4, device_at % 2]
            first = 24 * device_at // 128
            if device_at == 0:
                kept["gain"][...] = jnp.zeros((8, 768), F32)
            width = min(256, 768 - 128 * first)
            kept["gain"][:, 128 * first : 128 * first + width] += piece[:, :width]

    def gain(at):
        return kept["gain"][at : at + 1, :]

    mixed = attention(
        0, stream[...], before_0, {1: within_0, 4: later_0, 7: last_0, "after": after_0}
    )
    residual = stream[...] + mixed
    kept["mid_0"][...] = residual
    middle, _ = norm_forward(residual, gain(0))
    end(2, qkv_1)
    begin(3, qkv_1)
    fed = feed_forward(middle.astype(BF), store[wide_0], store[down_0], kept["paired_0"])
    end(0, out_1, down_1)
    summed = middle + fed
    kept["summed_0"][...] = summed
    shallow, _ = norm_forward(summed, gain(1))
    normed, _ = norm_forward(shallow, gain(2))
    end(3, qkv_1)
    save(qkv_1)

    def before_1():
        begin(1, out_1, down_1)

    def within_1():
        end(3, wide_1)
        begin(4, wide_1)

    def later_1():
        end(1, out_1, down_1)
        begin(2, out_1, down_1)
        end(4, wide_1)
        begin(5, wide_1)

    def after_1():
        end(2, out_1, down_1)
        begin(3, out_1, down_1)
        end(3, out_1, down_1)
        end(5, wide_1)
        save(out_1, wide_1, down_1)

    mixed = attention(1, normed, before_1, {1: within_1, 7: later_1, "after": after_1})
    residual = shallow + mixed
    kept["mid_1"][...] = residual
    normed_two, _ = norm_forward(residual, gain(3))
    fed = feed_forward(normed_two.astype(BF), store[wide_1], store[down_1], kept["paired_1"])
    kept["result"][...] = residual + fed
    for copy in saves:
        copy.wait()


def run_forward(*operands):
    count = sum(SEGMENTS[name] for name, _ in GATHERED)
    stored = GATHERED[:-1]
    results = pl.pallas_call(
        forward_kernel,
        out_shape=[weight_shape(key) for key in stored]
        + [jax.ShapeDtypeStruct(shape, kind) for _, shape, kind in KEPT],
        in_specs=[SMEM] + [VMEM] * 9,
        out_specs=[ANY] * 8 + [VMEM] * len(KEPT),
        scratch_shapes=[pltpu.VMEM(*WEIGHTS[name]) for name, _ in GATHERED]
        + [
            pltpu.VMEM((2, 3, 24, 768), F32),
            pltpu.VMEM((2, 24, 768), F32),
            pltpu.VMEM((2, 2, 24, 2048), F32),
            pltpu.VMEM((2, 3, 48, 768), BF),
            pltpu.VMEM((2, 48, 768), BF),
            pltpu.VMEM((2, 2, 48, 2048), BF),
            pltpu.VMEM((2, 64, 768), BF),
            pltpu.VMEM((2, PAIRS, MESSAGE, 128), BF),
            pltpu.VMEM((2, 32, 32, 128), BF),
            pltpu.VMEM((2, PAIRS, 32, 128), BF),
            pltpu.VMEM((64, LENGTH), BF),
            pltpu.VMEM((128, 768), F32),
            pltpu.SemaphoreType.DMA((2, 4)),
            pltpu.SemaphoreType.DMA((count, 5, 4)),
            pltpu.SemaphoreType.DMA((8,)),
            pltpu.SemaphoreType.DMA((4, 3)),
        ],
        compiler_params=params(1),
        name="forward",
    )(*operands)
    return dict(zip(stored, results)), {
        name: result for (name, _, _), result in zip(KEPT, results[8:])
    }


def attend_back_block(
    exchange, at, length, rows, out_grad, out_turned, log_total, keys_turned, key_grad, outgoing, incoming
):
    cut = slice(at * BLOCK, (at + 1) * BLOCK)
    four = slice(4 * at, 4 * at + 4)
    queries = unpack_block(rows[four, 64:96], True)
    outs = unpack_block(out_grad[four], False)
    outs_turned = outs.astype(F32).T[64:128]
    delta = jnp.sum(outs_turned * out_turned[:, cut], axis=0, keepdims=True)
    shift = log_total[0:1, cut]
    query_grad = jnp.zeros((64, BLOCK), F32)
    for part in range(at + 1):
        span = slice(part * BLOCK, (part + 1) * BLOCK)
        keys = rows[4 * part : 4 * part + 4, 0:64].reshape(BLOCK, 128)
        scores = lax.dot_general(keys, queries, LAST_DIMS, preferred_element_type=F32)
        allowed = allowed_keys(part * BLOCK, at * BLOCK, BLOCK, BLOCK, length)
        probs = jnp.where(allowed, jnp.exp(scores - shift), 0.0)
        probs_grad = lax.dot_general(keys, outs, LAST_DIMS, preferred_element_type=F32)
        score_grad = (probs * (probs_grad - delta)).astype(BF)
        key_grad[span, :] += jnp.dot(score_grad, queries, preferred_element_type=F32) + jnp.dot(
            probs.astype(BF), outs, preferred_element_type=F32
        )
        query_grad += jnp.dot(keys_turned[:, span], score_grad, preferred_element_type=F32)
    outgoing[four, 0:64] = key_grad[cut, :].reshape(4, SPAN, 128).astype(BF)
    outgoing[four, 64:96] = pack_turned(query_grad)
    for there in range(4 * at, 4 * at + 4):
        exchange.to(there, outgoing.at[there], incoming.at[exchange.pair])


def collect_projections(incoming, cosine, sine, result):
    front = front_lanes(64)
    for slot in range(2):
        span = slice(64 * slot, 64 * slot + 64)
        for tile in range(6):
            cut = slice(128 * tile, 128 * tile + 128)
            at = slot * HEADS + 2 * tile
            first, second = (incoming[at + n, 0:64].astype(F32) for n in (0, 1))
            q = unpack_heads(incoming[at, 64:96], incoming[at + 1, 64:96])
            k = jnp.where(front, first, pltpu.roll(second, 64, 1))
            v = jnp.where(front, pltpu.roll(first, 64, 1), second)
            q = turned(q * (1.0 / math.sqrt(HEAD_DIM)), cosine, -sine)
            result[0, span, cut] = q.astype(BF)
            result[1, span, cut] = turned(k, cosine, -sine).astype(BF)
            result[2, span, cut] = v.astype(BF)


def norm_backward(incoming, values, norm_gain):
    inverse = lax.rsqrt(jnp.mean(values * values, axis=-1, keepdims=True) + EPSILON)
    scaled = incoming * norm_gain
    outgoing = inverse * scaled - values * (inverse * inverse * inverse) * jnp.mean(
        scaled * values, axis=-1, keepdims=True
    )
    return outgoing, jnp.sum(incoming * values * inverse, axis=0, keepdims=True)


def feed_back(incoming, paired, gate_up, down, gate_grads, up_grads, hidden_turned):
    source_grad = jnp.zeros((128, 768), F32)
    for z in range(4):
        cut = slice(512 * z, 512 * z + 512)
        hidden_grad = lax.dot_general(
            incoming, down[z].reshape(512, 768), LAST_DIMS, preferred_element_type=F32
        )
        gate, up = paired[0, :, cut], paired[1, :, cut]
        sigmoid = jax.nn.sigmoid(gate)
        hidden = (gate * sigmoid * up).T.astype(BF).reshape(4, 2, 64, 128)
        hidden_turned[0, z] = hidden[:, 0]
        hidden_turned[1, z] = hidden[:, 1]
        gate_grad = (hidden_grad * up * sigmoid * (1.0 + gate * (1.0 - sigmoid))).astype(BF)
        up_grad = (hidden_grad * gate * sigmoid).astype(BF)
        part = slice(512 * (z % 2), 512 * (z % 2) + 512)
        gate_grads[z // 2, :, part] = gate_grad
        up_grads[z // 2, :, part] = up_grad
        for at, value in enumerate((gate_grad, up_grad)):
            source_grad = source_grad + lax.dot_general(
                value, gate_up[at, :, :, :, cut].reshape(768, 512), LAST_DIMS, preferred_element_type=F32
            )
    return source_grad


def turned_low(values):
    return values.astype(F32).T.astype(BF)


def fill_part(part, rows, left_of, right):
    for z in range(4):
        value = jnp.dot(left_of(z), right, preferred_element_type=F32).astype(BF)
        part.fill(z, value.reshape(4, rows, right.shape[1]))


def beside(first, second, rows):
    def left_of(z):
        cut = slice(4 * rows * z, 4 * rows * (z + 1))
        return jnp.concatenate([first[cut], second[cut]], axis=1)

    return left_of


SHARED = {
    "source": ((768, 128), (768, 128)),
    "gate": ((2, 128, 1024), (128, 1024)),
    "up": ((2, 128, 1024), (128, 1024)),
    "hidden": ((2, 4, 4, 64, 128), (4, 4, 64, 128)),
    "fed": ((128, 768), (128, 768)),
    "merged": ((768, 128), (768, 128)),
    "mixed": ((2, 128, 384), (128, 384)),
    "norm": ((768, 128), (768, 128)),
    "low": ((2, 3, 128, 384), (3, 128, 384)),
}
KEPT_NAMES = ("paired", "rows", "merged", "turned", "total")
KEPT_TYPES = {name: (shape, kind) for name, shape, kind in KEPT}
WEIGHT_ORDER = ("down", "wide", "out", "qkv")


def backward_kernel(lengths, *refs):
    refs = list(refs)

    def take(count):
        taken = refs[:count]
        del refs[:count]
        return taken

    cotangent, stream, residual_0, summed_0, residual_1, gains, cosine, sine = take(8)
    far = [dict(zip(KEPT_NAMES, take(len(KEPT_NAMES)))) for _ in range(2)]
    stored = dict(zip(GATHERED[:-1], take(8)))
    (input_grad,) = take(1)
    sums = dict(zip(SUMS, take(len(SUMS))))
    kept = dict(zip(KEPT_NAMES, take(len(KEPT_NAMES))))
    weights = dict(zip(WEIGHT_ORDER, take(4)))
    shared, own = part_scratch()
    shared, own = take(len(shared)), take(len(own))
    given = dict(zip(SHARED, take(len(SHARED))))
    got = [dict(zip(SHARED, take(len(SHARED)))) for _ in range(2)]
    out_grads, to_pairs, to_places, incoming = take(4)
    keys_turned, key_grad, gain_grads, their_gains, stacked = take(5)
    part_sems, give_sems, load_sems, pair_sems = take(4)
    parts = build_parts(shared, own, part_sems, sums)
    axes = Axes(True)
    core = axes.core
    x, me = lax.axis_index(BATCH), lax.axis_index(SEQ)
    barrier = pltpu.get_barrier_semaphore()
    neighbours = [(x, lax.rem(me + by, 32)) for by in range(1, 32)]
    neighbours += [device(shifted(x, by), axes.z, axes.y, core) for by in (1, 2, 3)]
    for where in neighbours:
        pl.semaphore_signal(barrier, inc=1, device_id=where, device_id_type=MESH)

    def load(name, layer):
        at = WEIGHT_ORDER.index(name)
        return pltpu.make_async_copy(stored[name, layer], weights[name], load_sems.at[at])

    def recall(name, layer):
        at = KEPT_NAMES.index(name)
        return pltpu.make_async_copy(far[layer][name], kept[name], load_sems.at[4 + at])

    recall("paired", 1).start()
    for name in WEIGHT_ORDER:
        load(name, 1).start()
    for name in KEPT_NAMES[1:]:
        recall(name, 1).start()

    def gain(at):
        return gains[at : at + 1, :]

    def stages(*work):
        for names, layer, number in work:
            for name in names:
                parts[name, layer].stage(number)

    def share(layer, names):
        copies = []
        for name in names:
            at = list(SHARED).index(name)
            source = given[name]
            if SHARED[name][0] != SHARED[name][1]:
                source = source.at[1 - core]
            copies.append(
                remote(
                    source,
                    got[layer][name],
                    give_sems.at[layer, at, 0],
                    give_sems.at[layer, at, 1],
                    axes.partner,
                )
            )
        return copies

    def start(copies):
        for copy in copies:
            copy.start()

    def finish(copies):
        for copy in copies:
            copy.wait()

    wide, narrow, down = ("gate", "up"), ("left", "right", "o"), ("left", "right")

    def wide_grads(layer):
        left_of = beside(given["source"], got[layer]["source"], 48)
        for name in wide:
            right = jnp.concatenate([given[name][core], got[layer][name][...]], axis=0)
            fill_part(parts[name, layer], 48, left_of, right)

    def narrow_grads(layer):
        def left_of(z):
            mine = given["hidden"][core, z].reshape(256, 128)
            return jnp.concatenate([mine, got[layer]["hidden"][z].reshape(256, 128)], axis=1)

        right = jnp.concatenate([given["fed"][...], got[layer]["fed"][...]], axis=0)
        fill_part(parts["left", layer], 64, left_of, right[:, :384])
        fill_part(parts["right", layer], 64, left_of, right[:, 384:])
        right = jnp.concatenate([given["mixed"][core], got[layer]["mixed"][...]], axis=0)
        left_of = beside(given["merged"], got[layer]["merged"], 48)
        fill_part(parts["o", layer], 48, left_of, right)

    def projection_grads(layer):
        left_of = beside(given["norm"], got[layer]["norm"], 48)
        for at, name in enumerate("qkv"):
            right = jnp.concatenate([given["low"][core, at], got[layer]["low"][at]], axis=0)
            fill_part(parts[name, layer], 48, left_of, right)

    FED = ("source", "gate", "up", "hidden", "fed")
    MIXED = ("merged", "mixed")
    PROJECTED = ("norm", "low")

    def feed(layer, source, grad):
        load("down", layer).wait()
        load("wide", layer).wait()
        recall("paired", layer).wait()
        low = grad.astype(BF)
        given["fed"][...] = low
        given["source"][...] = turned_low(source.astype(BF))
        return feed_back(
            low,
            kept["paired"],
            weights["wide"],
            weights["down"],
            given["gate"],
            given["up"],
            given["hidden"],
        )

    def send_out_grad(layer, grad):
        load("out", layer).wait()
        low = grad.astype(BF)
        given["mixed"][0] = low[:, :384]
        given["mixed"][1] = low[:, 384:]
        for name in KEPT_NAMES[1:]:
            recall(name, layer).wait()
        given["merged"][...] = turned_low(kept["merged"][...])
        merged_grad = (
            lax.dot_general(
                low, weights["out"][...].reshape(768, 768), LAST_DIMS, preferred_element_type=F32
            )
            .astype(BF)
            .astype(F32)
        )
        exchange = Exchange(pair_sems.at[2 * layer])
        to = to_pairs
        for slot in range(2):
            for tile in range(6):
                at = slot * HEADS + 2 * tile
                both = merged_grad[64 * slot : 64 * slot + 64, 128 * tile : 128 * tile + 128]
                to[at], to[at + 1] = pack_heads(both)
                for pair in (at, at + 1):
                    exchange.to(pair_device(pair), to.at[pair], out_grads.at[layer, me])
        return exchange

    def attention(layer, exchange, between):
        rows = kept["rows"]
        length = slot_length(lengths, exchange.pair)

        @pl.when(exchange.has_pair)
        def _():
            all_rows = rows[:, 0:64].reshape(LENGTH, 128).astype(F32)
            keys_turned[...] = all_rows.T[0:64].astype(BF)
            key_grad[...] = jnp.zeros_like(key_grad)

        exchange.wait(to_pairs, out_grads.at[layer], "pairs")
        back = Exchange(pair_sems.at[2 * layer + 1])
        for at in reversed(range(BLOCKS)):

            @pl.when(exchange.has_pair)
            def _(at=at):
                attend_back_block(
                    back,
                    at,
                    length,
                    rows,
                    out_grads.at[layer],
                    kept["turned"],
                    kept["total"],
                    keys_turned,
                    key_grad,
                    to_places,
                    incoming.at[layer],
                )

            stages(*between.get(at, ()))
        stages(*between.get("sent", ()))
        back.wait(to_places, incoming.at[layer], "places")
        collect_projections(incoming.at[layer], cosine[...], sine[...], stacked)

    def source_gradient(layer, source):
        load("qkv", layer).wait()
        given["norm"][...] = turned_low(source.astype(BF))
        for at in range(3):
            given["low"][0, at] = stacked[at, :, 0:384]
            given["low"][1, at] = stacked[at, :, 384:768]
        copies = share(layer, PROJECTED)
        start(copies)
        result = jnp.zeros((128, 768), F32)
        for at in range(3):
            result = result + lax.dot_general(
                stacked[at],
                weights["qkv"][at].reshape(768, 768),
                LAST_DIMS,
                preferred_element_type=F32,
            )
        return result, copies

    normed_two, _ = norm_forward(residual_1[...], gain(3))
    fed_grad = feed(1, normed_two, cotangent[...])
    for name in ("down", "wide"):
        load(name, 0).start()
    recall("paired", 0).start()
    through, gain_grad = norm_backward(fed_grad, residual_1[...], gain(3))
    gain_grads[...] = jnp.zeros_like(gain_grads)
    gain_grads[3:4, :] = gain_grad
    residual_grad = cotangent[...] + through
    pl.semaphore_wait(barrier, len(neighbours))
    exchange = send_out_grad(1, residual_grad)
    load("out", 0).start()
    copies = share(1, FED + MIXED)
    start(copies)
    finish(copies)
    wide_grads(1)
    stages((wide, 1, 0))
    narrow_grads(1)
    stages((narrow, 1, 1))
    attention(1, exchange, {6: [(narrow, 1, 2)], "sent": [(narrow, 1, 3)]})
    for name in KEPT_NAMES[1:]:
        recall(name, 0).start()
    shallow, _ = norm_forward(summed_0[...], gain(1))
    normed, _ = norm_forward(shallow, gain(2))
    normed_grad, copies = source_gradient(1, normed)
    load("qkv", 0).start()
    stages((narrow, 1, 4))
    through, gain_grad = norm_backward(normed_grad, shallow, gain(2))
    gain_grads[2:3, :] = gain_grad
    shallow_grad = residual_grad + through
    summed_grad, gain_grad = norm_backward(shallow_grad, summed_0[...], gain(1))
    gain_grads[1:2, :] = gain_grad

    finish(copies)
    projection_grads(1)
    stages(("qkv", 1, 1))
    middle, _ = norm_forward(residual_0[...], gain(0))
    fed_grad = feed(0, middle, summed_grad)
    middle_grad = summed_grad + fed_grad
    residual_grad, gain_grad = norm_backward(middle_grad, residual_0[...], gain(0))
    gain_grads[0:1, :] = gain_grad
    exchange = send_out_grad(0, residual_grad)
    copies = share(0, FED + MIXED)
    start(copies)
    stages(("qkv", 1, 2))
    finish(copies)
    narrow_grads(0)
    stages((down, 0, 0))
    stages((wide, 1, 1))
    wide_grads(0)
    stages((wide, 0, 1), ("o", 0, 1))
    attention(
        0,
        exchange,
        {
            6: [("qkv", 1, 3)],
            3: [(wide, 1, 2)],
            0: [("qkv", 1, 4), (narrow, 1, 5)],
            "sent": [(wide, 0, 2), ("o", 0, 2), (wide, 1, 3)],
        },
    )
    source_grad, copies = source_gradient(0, stream[...])
    swap = remote(
        gain_grads, their_gains, give_sems.at[0, len(SHARED), 0], give_sems.at[0, len(SHARED), 1], axes.partner
    )
    swap.start()
    input_grad[...] = residual_grad + source_grad
    stages(("qkv", 1, 5), (wide, 1, 4))
    finish(copies)
    projection_grads(0)
    swap.wait()
    gain_total = gain_grads[...] + their_gains[...]
    gain_total = jnp.concatenate([gain_total, jnp.zeros((8, 128), F32)], axis=1)
    for z in range(4):
        for y in range(4):
            first, second = (24 * (8 * z + 2 * y + which) // 128 * 128 for which in (0, 1))
            parts["gain", 0].total[y, z] = jnp.where(
                core == 0, gain_total[:, first : first + 256], gain_total[:, second : second + 256]
            )
    last = ("q", "k", "v", "gain")
    stages((last, 0, 1), (down, 0, 1), (wide, 0, 3), ("o", 0, 3), ("qkv", 1, 6))
    stages((wide, 1, 5), (narrow, 1, 6))
    stages((last, 0, 2), (down, 0, 2), (wide, 0, 4), ("o", 0, 4), (down, 0, 3))
    stages((wide, 1, 6), (last, 0, 4), (down, 0, 4), (wide, 0, 5), ("o", 0, 5), (last, 0, 5), (down, 0, 5))
    stages((wide, 0, 6), ("o", 0, 6), (last, 0, 6), (down, 0, 6))


def run_backward(lengths, kept, store, cosine, sine):
    near = [kept["cotangent"], kept["stream"]] + [
        kept[name] for name in ("mid_0", "summed_0", "mid_1", "gain")
    ]
    near += [cosine, sine]
    away = [kept[name + layer] for layer in ("_0", "_1") for name in KEPT_NAMES]
    away += [store[key] for key in GATHERED[:-1]]
    shared, own = part_scratch()
    results = pl.pallas_call(
        backward_kernel,
        out_shape=[jax.ShapeDtypeStruct((128, 768), F32)]
        + [jax.ShapeDtypeStruct(*shape) for shape in SUMS.values()],
        in_specs=[SMEM] + [VMEM] * len(near) + [ANY] * len(away),
        out_specs=[VMEM] * (1 + len(SUMS)),
        scratch_shapes=[pltpu.VMEM(*KEPT_TYPES[name + "_0"]) for name in KEPT_NAMES]
        + [pltpu.VMEM(*WEIGHTS[name]) for name in WEIGHT_ORDER]
        + shared
        + own
        + [pltpu.VMEM(here, BF) for here, _ in SHARED.values()]
        + [pltpu.VMEM(there, BF) for _, there in SHARED.values()] * 2
        + [
            pltpu.VMEM((2, 32, 32, 128), BF),
            pltpu.VMEM((PAIRS, 32, 128), BF),
            pltpu.VMEM((32, MESSAGE, 128), BF),
            pltpu.VMEM((2, PAIRS, MESSAGE, 128), BF),
            pltpu.VMEM((64, LENGTH), BF),
            pltpu.VMEM((LENGTH, 128), F32),
            pltpu.VMEM((8, 768), F32),
            pltpu.VMEM((8, 768), F32),
            pltpu.VMEM((3, 128, 768), BF),
            pltpu.SemaphoreType.DMA((2 * len(PARTS), SCATTER_SEMAPHORES)),
            pltpu.SemaphoreType.DMA((2, len(SHARED) + 1, 2)),
            pltpu.SemaphoreType.DMA((9,)),
            pltpu.SemaphoreType.DMA((4, 3)),
        ],
        compiler_params=params(2),
        name="backward",
    )(lengths, *near, *away)
    return results[0], dict(zip(SUMS, results[1:]))


def angles(places):
    half_dim = HEAD_DIM // 2
    frequency = jnp.exp(-math.log(10000.0) * jnp.arange(half_dim).astype(F32) / half_dim)
    phases = places.astype(F32)[:, None] * frequency[None, :]
    cosine, sine = jnp.cos(phases), jnp.sin(phases)
    return (
        jnp.concatenate([cosine] * 4, axis=1),
        jnp.concatenate([-sine, sine] * 2, axis=1),
    )


def update(weight_matrix, moment, average, gradient, step_size):
    moment_new = MOMENTUM * moment + gradient
    weight_new = weight_matrix - step_size * (gradient + MOMENTUM * moment_new)
    return (moment_new, weight_new, AVERAGING * average + (1.0 - AVERAGING) * weight_new)


STEPPED = ("qkv", "out", "wide", "down")


def update_kernel(step_size, *refs):
    count = len(STEPPED)
    sources, refs = refs[: 4 * count + 2], refs[4 * count + 2 :]
    targets, refs = refs[: 3 * count + 2], refs[3 * count + 2 :]
    held, (loads, stores) = refs[:-2], refs[-2:]
    placed, held = held[-2:], held[:-2]
    fetches = [
        pltpu.make_async_copy(source, here, loads.at[at])
        for at, (source, here) in enumerate(zip(sources, held))
    ]
    for copy in fetches:
        copy.start()
    saves = []

    def save(here, at):
        copy = pltpu.make_async_copy(here, targets[at], stores.at[at])
        copy.start()
        saves.append(copy)

    for at in range(count):
        for copy in fetches[4 * at : 4 * at + 4]:
            copy.wait()
        gradient, weight_matrix, moment, average = held[4 * at : 4 * at + 4]
        stepped = update(weight_matrix[...], moment[...], average[...], gradient[...], step_size)
        for n, (here, value) in enumerate(zip((moment, weight_matrix, average), stepped)):
            here[...] = value
            save(here, 3 * at + n)
    for at in range(2):
        fetches[4 * count + at].wait()
        for slot in range(2):
            placed[at][:, slot, :] = held[4 * count + at][64 * slot : 64 * slot + 64]
        save(placed[at], 3 * count + at)
    for copy in saves:
        copy.wait()


def run_update(step_size, sums, states, activations):
    shapes = {name: jax.ShapeDtypeStruct(*SUMS[name]) for name in STEPPED}
    operands = []
    for name in STEPPED:
        operands += [sums[name], *states[name]]
    operands += activations
    by_place = jax.ShapeDtypeStruct((SPAN, 2, 768), F32)
    results = pl.pallas_call(
        functools.partial(update_kernel, step_size),
        out_shape=[shapes[name] for name in STEPPED for _ in range(3)] + [by_place] * 2,
        in_specs=[ANY] * len(operands),
        out_specs=[ANY] * (3 * len(STEPPED) + 2),
        scratch_shapes=[pltpu.VMEM(operand.shape, F32) for operand in operands]
        + [pltpu.VMEM((SPAN, 2, 768), F32)] * 2
        + [
            pltpu.SemaphoreType.DMA((len(operands),)),
            pltpu.SemaphoreType.DMA((3 * len(STEPPED) + 2,)),
        ],
        compiler_params=pltpu.CompilerParams(vmem_limit_bytes=VMEM_BYTES),
        name="step",
    )(*operands)
    return results[: 3 * len(STEPPED)], results[3 * len(STEPPED) :]


def on_device(
    inputs,
    cotangent,
    lengths,
    qkv_weight,
    qkv_moment,
    qkv_average,
    out_weight,
    out_moment,
    out_average,
    gate_up_weight,
    gate_up_moment,
    gate_up_average,
    down_weight,
    down_moment,
    down_average,
    norm_gains,
    gain_moment,
    gain_average,
):
    places = lax.axis_index(SEQ) * SPAN + jnp.arange(SPAN)
    cosine, sine = angles(places)
    seq = lax.axis_index(SEQ)
    own_gains = lax.dynamic_update_slice(
        jnp.zeros((8, 256), F32),
        norm_gains.astype(BF).astype(F32).reshape(4, 24),
        (0, lax.rem(24 * seq, 128)),
    )
    store, kept = run_forward(
        lengths[0],
        qkv_weight,
        out_weight,
        gate_up_weight,
        down_weight,
        own_gains,
        inputs[0],
        cotangent[0],
        cosine,
        sine,
    )
    input_grad, sums = run_backward(
        lengths[0], kept, store, cosine, sine
    )
    gain_sum = lax.dynamic_slice(
        sums["gain"][0], (0, lax.rem(24 * seq, 128)), (4, 24)
    ).reshape(2, 2, 24)

    step_size = STEP_RATE / math.sqrt(
        lax.axis_size(BATCH) * SPAN * lax.axis_size(SEQ) * 2
    )
    stepped, (result, input_grad) = run_update(
        step_size,
        sums,
        {
            "qkv": (qkv_weight, qkv_moment, qkv_average),
            "out": (out_weight, out_moment, out_average),
            "wide": (gate_up_weight, gate_up_moment, gate_up_average),
            "down": (down_weight, down_moment, down_average),
        },
        [kept["result"], input_grad],
    )
    gain_new = update(norm_gains, gain_moment, gain_average, gain_sum, step_size)
    return (result[None], input_grad[None], *stepped, *gain_new)


def solution(mesh):
    rows = P(BATCH, SEQ, None, None)
    wide = P(None, None, SEQ, None)
    flat = P(None, SEQ, None)
    gains = P(None, None, SEQ)
    state = (wide,) * 3 + (flat,) * 3 + (wide,) * 3 + (flat,) * 3 + (gains,) * 3
    return jax.shard_map(
        on_device,
        mesh=mesh,
        in_specs=(rows, rows, P(BATCH, None)) + state,
        out_specs=(rows, rows) + state,
        check_vma=False,
    )
```
